32 devices in a mesh: seq: 8 (over z, x), tensor: 4 (over y, core).
Axes of the slice: x: 2, y: 2, z: 4, core: 2. Of those that a mesh axis runs over, the one named last changes fastest.
Arguments:
- tokens: bfloat16 [4, 1024, 768], P(None, 'seq'), may hold values from -6 to 6
- lengths: int32 [4], replicated, may hold values from 513 to 1024, as said below
- query_weight: bfloat16 [768, 768], P(None, 'tensor'), may hold values from -0.875 to 0.875
- query_bias: float32 [768], P('tensor'), may hold values from -3 to 3
- key_weight: bfloat16 [768, 768], P(None, 'tensor'), may hold values from -0.875 to 0.875
- value_weight: bfloat16 [768, 768], P(None, 'tensor'), may hold values from -0.21875 to 0.21875
- value_bias: float32 [768], P('tensor'), may hold values from -2 to 2
- conv_kernel: float32 [12, 33], P('tensor'), may hold values from -0.6 to 0.6
- out_weight: bfloat16 [768, 768], P('tensor'), may hold values from -0.4375 to 0.4375
- out_bias: float32 [768], replicated, may hold values from -2 to 2
- first_gain: float32 [768], replicated, may hold values from 0.5 to 1.5
- first_shift: float32 [768], replicated, may hold values from -2 to 2
- up_weight: bfloat16 [768, 3072], P(None, 'tensor'), may hold values from -0.21875 to 0.21875
- up_bias: float32 [3072], P('tensor'), may hold values from -3 to 3
- down_weight: bfloat16 [3072, 768], P('tensor'), may hold values from -0.109375 to 0.109375
- down_bias: float32 [768], replicated, may hold values from -2 to 2
- second_gain: float32 [768], replicated, may hold values from 0.5 to 1.5
- second_shift: float32 [768], replicated, may hold values from -2 to 2
- out_grad: bfloat16 [4, 1024, 768], P(None, 'seq'), may hold values from -6 to 6
Outputs:
- output: bfloat16 [4, 1024, 768], P(None, 'seq')
- grad_tokens: float32 [4, 1024, 768], P(None, 'seq')
- grad_query_weight: float32 [768, 768], P('seq', 'tensor')
- grad_query_bias: float32 [768], P('tensor')
- grad_key_weight: float32 [768, 768], P('seq', 'tensor')
- grad_value_weight: float32 [768, 768], P('seq', 'tensor')
- grad_value_bias: float32 [768], P('tensor')
- grad_conv_kernel: float32 [12, 33], P('tensor')
- grad_out_weight: float32 [768, 768], P('tensor', 'seq')
- grad_out_bias: float32 [768], replicated
- grad_first_gain: float32 [768], replicated
- grad_first_shift: float32 [768], replicated
- grad_up_weight: float32 [768, 3072], P('seq', 'tensor')
- grad_up_bias: float32 [3072], P('tensor')
- grad_down_weight: float32 [3072, 768], P('tensor', 'seq')
- grad_down_bias: float32 [768], replicated
- grad_second_gain: float32 [768], replicated
- grad_second_shift: float32 [768], replicated
- proxy_norm: float32 [], replicated
The draws below stay inside these ranges and needn't reach their ends.
Inputs may be any that keep to these rules, and one draw needn't show every extreme that they name: True lengths of the 4 sequences, each more than half of the bucket of 1024 tokens; in every draw one of them is 1024.
All inputs are finite; a program needn't handle non-finite values.
Results may differ from the reference program's by a relative error of at most 0.018.
The reference program's roundings to bfloat16 on the way count: a program that leaves them out, or rounds other values in their place, can miss the bound.
Values may be sent and summed in bfloat16 or wider, within the bound.
A program may use at most 192 MiB of HBM per device.

```python
import jax
import jax.numpy as jnp
from jax import lax

D = 768
HEADS = 12
HEAD_DIM = 64
FF = 3072
LAND = 64
CONV = 33
NS_ITERS = 6
LMIN = 128
BATCH = 4
SEQ_LEN = 1024


def draw_lengths(key, part):
    key = jax.random.fold_in(key, 11)
    first_key, second_key = jax.random.split(key)
    least = max(LMIN, SEQ_LEN // 2 + 1)
    drawn = jax.random.randint(first_key, (BATCH,), least, SEQ_LEN + 1)
    longest = jax.random.randint(second_key, (), 0, BATCH)
    return jnp.where(jnp.arange(BATCH) == longest, SEQ_LEN, drawn).astype(jnp.int32)


def strengthened(entries, rng, source, target, parts, factor):
    def block_of(dim):
        return (jnp.arange(entries.shape[dim]) // (entries.shape[dim] // parts)).reshape((-1,) + (1,) * (entries.ndim - 1 - dim))

    near = jax.random.permutation(rng, parts)[block_of(target)]
    other_side = (block_of(target) + parts // 2) % parts
    return jnp.where((block_of(source) == near) | (block_of(source) == other_side), factor * entries, entries)


def block_scale(own_key, dims, shards, low, largest):
    gain, own = 1.0, jax.random.fold_in(own_key, 6)
    for dim, shards_of in shards:
        draws = jnp.exp(jax.random.uniform(jax.random.fold_in(own, dim), (shards_of,), jnp.float32, low / len(shards), largest / len(shards)))
        gain = gain * jnp.repeat(draws, dims[dim] // shards_of).reshape([-1 if axis == dim else 1 for axis in range(len(dims))])
    return gain


def scatter_about(rng, dims, scale, limit, cuts=(), kind=jnp.bfloat16):
    entries = jax.random.normal(rng, dims, jnp.float32) * scale
    if len(cuts) > 0:
        entries = block_scale(rng, dims, cuts, -0.22, 0.18) * entries
    return jnp.clip(entries, min=-limit, max=limit).astype(kind)


def gaussian_with(key, dims, scale, most, cuts, heavy, held_as=jnp.bfloat16):
    array = scale * jax.random.normal(key, dims, jnp.float32)
    if cuts:
        array = array * block_scale(key, dims, cuts, -0.22, 0.18)
    return jnp.clip(strengthened(array, jax.random.fold_in(key, 3), *heavy), -most, most).astype(held_as)


def setup_inputs(seed: int = 0) -> dict:
    streams_of = jax.random.split(jax.random.key(seed), 20)
    tokens = gaussian_with(streams_of[0], (BATCH, SEQ_LEN, D), 1.0, 6.0, ((1, 8),), (1, 2, 8, 2.0))
    lengths = draw_lengths(jax.random.fold_in(streams_of[19], 71), 0)
    query_weight = scatter_about(streams_of[2], (D, D), (D // 16) ** -0.5, 0.875, ((1, 4),))
    query_bias = scatter_about(streams_of[3], (D,), 0.5, 3.0, ((0, 4),), jnp.float32)
    key_weight = scatter_about(streams_of[4], (D, D), (D // 16) ** -0.5, 0.875, ((1, 4),))
    value_weight = scatter_about(streams_of[5], (D, D), D ** -0.5, 0.21875, ((1, 4),))
    value_bias = scatter_about(streams_of[6], (D,), 0.3, 2.0, ((0, 4),), jnp.float32)
    conv_kernel = scatter_about(streams_of[7], (HEADS, CONV), 0.1, 0.6, ((0, 4),), jnp.float32)
    out_weight = scatter_about(streams_of[8], (D, D), (D // 4) ** -0.5, 0.4375, ((0, 4),))
    out_bias = scatter_about(streams_of[9], (D,), 0.3, 2.0, (), jnp.float32)
    first_gain = jnp.clip(1.0 + 0.1 * jax.random.normal(streams_of[10], (D,), jnp.float32), 0.5, 1.5)
    first_shift = scatter_about(streams_of[11], (D,), 0.3, 2.0, (), jnp.float32)
    up_weight = scatter_about(streams_of[12], (D, FF), D ** -0.5, 0.21875, ((1, 4),))
    up_bias = scatter_about(streams_of[13], (FF,), 0.5, 3.0, ((0, 4),), jnp.float32)
    down_weight = scatter_about(streams_of[14], (FF, D), FF ** -0.5, 0.109375, ((0, 4),))
    down_bias = scatter_about(streams_of[15], (D,), 0.3, 2.0, (), jnp.float32)
    second_gain = jnp.clip(1.0 + 0.1 * jax.random.normal(streams_of[16], (D,), jnp.float32), 0.5, 1.5)
    second_shift = scatter_about(streams_of[17], (D,), 0.3, 2.0, (), jnp.float32)
    out_grad = gaussian_with(streams_of[18], (BATCH, SEQ_LEN, D), 1.0, 6.0, ((1, 8),), (1, 2, 8, 2.0))
    return {"tokens": tokens, "lengths": lengths, "query_weight": query_weight, "query_bias": query_bias, "key_weight": key_weight, "value_weight": value_weight, "value_bias": value_bias, "conv_kernel": conv_kernel, "out_weight": out_weight, "out_bias": out_bias, "first_gain": first_gain, "first_shift": first_shift, "up_weight": up_weight, "up_bias": up_bias, "down_weight": down_weight, "down_bias": down_bias, "second_gain": second_gain, "second_shift": second_shift, "out_grad": out_grad}


@jax.custom_vjp
def low(v):
    return lax.optimization_barrier(v.astype(jnp.bfloat16)).astype(jnp.float32)

@jax.custom_vjp
def low_back(v):
    return v

def low_keep(v):
    return (low(v), None)

def low_pass(kept, grad):
    return (grad,)

def back_keep(v):
    return (v, None)

def back_low(kept, grad):
    return (low(grad),)
low.defvjp(low_keep, low_pass)
low_back.defvjp(back_keep, back_low)
highest = lax.Precision.HIGHEST
epsilon = 1e-05
negative = -1e+30

def layer_norm(summed, scale_vec, shift_vec):
    middle = lax.optimization_barrier(jnp.mean(summed, axis=-1, keepdims=True))
    centred = summed - middle
    inverse_std = lax.rsqrt(lax.optimization_barrier(jnp.mean(centred * centred, axis=-1, keepdims=True)) + epsilon)
    return centred * inverse_std * scale_vec + shift_vec

def newton_inverse(kernel):
    identity = jnp.eye(kernel.shape[-1], dtype=jnp.float32)
    inverse = jnp.swapaxes(kernel, -1, -2) / lax.optimization_barrier(jnp.sum(kernel * kernel, axis=(-2, -1), keepdims=True))
    for _ in range(NS_ITERS):
        product = jnp.matmul(kernel, inverse, precision=highest)
        inner_term = jnp.matmul(product, 7.0 * identity - product, precision=highest)
        inner_term = jnp.matmul(product, 15.0 * identity - inner_term, precision=highest)
        inverse = 0.25 * jnp.matmul(inverse, 13.0 * identity - inner_term, precision=highest)
    return inverse

def sequence_forward(inputs, length, params):
    query_weight, query_bias, key_weight, value_weight, value_bias, conv_kernel, out_weight, out_bias, first_gain, first_shift, up_weight, up_bias, down_weight, down_bias, second_gain, second_shift = params
    score_scale = HEAD_DIM ** (-0.5)
    position = jnp.arange(SEQ_LEN, dtype=jnp.int32)
    inside = position < length
    living = inside.astype(jnp.float32)
    segment = position * LAND // length
    onehot = ((segment[:, None] == jnp.arange(LAND, dtype=jnp.int32)[None, :]) & inside[:, None]).astype(jnp.float32)
    counts = lax.optimization_barrier(jnp.sum(onehot, axis=0))
    queries = low_back(low(jnp.dot(inputs, query_weight, precision=highest) + query_bias))
    key_vectors = low_back(low(jnp.dot(inputs, key_weight, precision=highest)))
    values = low_back(low((jnp.dot(inputs, value_weight, precision=highest) + value_bias) * living[:, None]))
    query_heads = queries.reshape(SEQ_LEN, HEADS, HEAD_DIM)
    key_heads = key_vectors.reshape(SEQ_LEN, HEADS, HEAD_DIM)
    value_heads = values.reshape(SEQ_LEN, HEADS, HEAD_DIM)
    query_marks = jnp.einsum('tj,thd->hjd', onehot, query_heads, precision=highest) / counts[None, :, None]
    key_marks = jnp.einsum('tj,thd->hjd', onehot, key_heads, precision=highest) / counts[None, :, None]
    kernel_two = jax.nn.softmax(jnp.einsum('hjd,hid->hji', query_marks, key_marks, precision=highest) * score_scale, axis=-1)
    inverse = newton_inverse(kernel_two)
    identity = jnp.eye(LAND, dtype=jnp.float32)
    deviation = identity - jnp.matmul(kernel_two, inverse, precision=highest)
    proxy_norm = jnp.mean(jnp.sqrt(lax.optimization_barrier(jnp.sum(deviation * deviation, axis=(1, 2)))))
    kernel_one = jax.nn.softmax(jnp.einsum('thd,hjd->htj', query_heads, key_marks, precision=highest) * score_scale, axis=-1)
    third_scores = jnp.einsum('hjd,thd->hjt', query_marks, key_heads, precision=highest) * score_scale
    third_scores = jnp.where(inside[None, None, :], third_scores, negative)
    third_prob = jax.nn.softmax(third_scores, axis=-1)
    third_out = jnp.einsum('hjt,thd->hjd', third_prob, value_heads, precision=highest)
    carried = jnp.matmul(inverse, third_out, precision=highest)
    nystrom = jnp.einsum('htj,hjd->thd', kernel_one, carried, precision=highest).reshape(SEQ_LEN, D)
    half_width = CONV // 2
    padded = jnp.pad(values, ((half_width, half_width), (0, 0)))
    kernel_wide = jnp.repeat(conv_kernel, HEAD_DIM, axis=0)
    convolved = jnp.zeros((SEQ_LEN, D), jnp.float32)
    for i in range(CONV):
        convolved = convolved + padded[i:i + SEQ_LEN] * kernel_wide[:, i]
    attention = low(nystrom + convolved)
    branch = low_back(jnp.dot(attention, out_weight, precision=highest) + out_bias)
    hidden_one = layer_norm(inputs + branch, first_gain, first_shift)
    up_value = low_back(jnp.dot(low(hidden_one), up_weight, precision=highest) + up_bias)
    activated = low(jax.nn.gelu(up_value, approximate=False))
    down_value = low_back(jnp.dot(activated, down_weight, precision=highest) + down_bias)
    return (layer_norm(hidden_one + down_value, second_gain, second_shift), proxy_norm)

def reference(tokens, lengths, query_weight, query_bias, key_weight, value_weight, value_bias, conv_kernel, out_weight, out_bias, first_gain, first_shift, up_weight, up_bias, down_weight, down_bias, second_gain, second_shift, out_grad):
    params = tuple((w.astype(jnp.float32) for w in (query_weight, query_bias, key_weight, value_weight, value_bias, conv_kernel, out_weight, out_bias, first_gain, first_shift, up_weight, up_bias, down_weight, down_bias, second_gain, second_shift)))

    def forward(inputs, weights):

        def per_sequence(running, item_pair):
            sequence, length = item_pair
            result, proxy_norm = jax.checkpoint(sequence_forward)(sequence, length, weights)
            return (running + proxy_norm, result)
        proxy_sum, outputs = lax.scan(per_sequence, jnp.zeros((), jnp.float32), (inputs, lengths))
        return (outputs, proxy_sum / BATCH)
    outputs, backward, proxy_norm = jax.vjp(forward, tokens.astype(jnp.float32), params, has_aux=True)
    grad_tokens, gradients = backward(out_grad.astype(jnp.float32))
    grad_query_weight, grad_query_bias, grad_key_weight, grad_value_weight, grad_value_bias, grad_conv_kernel, grad_out_weight, grad_out_bias, grad_first_gain, grad_first_shift, grad_up_weight, grad_up_bias, grad_down_weight, grad_down_bias, grad_second_gain, grad_second_shift = gradients
    return (outputs.astype(jnp.bfloat16), grad_tokens, grad_query_weight, grad_query_bias, grad_key_weight, grad_value_weight, grad_value_bias, grad_conv_kernel, grad_out_weight, grad_out_bias, grad_first_gain, grad_first_shift, grad_up_weight, grad_up_bias, grad_down_weight, grad_down_bias, grad_second_gain, grad_second_shift, proxy_norm)
```

```python
import functools

import jax
import jax.numpy as jnp
from jax import lax
from jax.experimental import pallas as pl
from jax.experimental.pallas import tpu as pltpu
from jax.sharding import PartitionSpec as P

HEADS = 12
HEAD_DIM = 64
LAND = 64
CONV = 33
NS_ITERS = 6


highest = lax.Precision.HIGHEST
epsilon = 1e-05
negative = -1e30


def joined(x, axis, combine):
    everything = jax.tree.map(lambda part: lax.all_gather(part, axis), x)
    first = jax.tree.map(lambda part: part[0], everything)

    def hop(k, so_far):
        return combine(so_far, jax.tree.map(lambda part: part[k], everything))

    return lax.fori_loop(1, lax.axis_size(axis), hop, first)


def with_halo(block, sides, width):
    for axis, dim in sides:
        count = lax.axis_size(axis)
        forward = [(i, i + 1) for i in range(count - 1)]
        backward = [(target, source) for source, target in forward]
        low = lax.ppermute(
            lax.slice_in_dim(block, block.shape[dim] - width, None, axis=dim), axis, forward
        )
        high = lax.ppermute(lax.slice_in_dim(block, 0, width, axis=dim), axis, backward)
        block = jnp.concatenate([low, block, high], axis=dim)
    return block


def newton_inverse(kernel):
    identity = jnp.eye(kernel.shape[-1], dtype=jnp.float32)
    inverse = jnp.swapaxes(kernel, -1, -2) / jnp.sum(kernel * kernel, axis=(-2, -1), keepdims=True)
    for _ in range(NS_ITERS):
        product = jnp.matmul(kernel, inverse, precision=highest)
        inner_term = jnp.matmul(product, 7.0 * identity - product, precision=highest)
        inner_term = jnp.matmul(product, 15.0 * identity - inner_term, precision=highest)
        inverse = 0.25 * jnp.matmul(inverse, 13.0 * identity - inner_term, precision=highest)
    return inverse


def landmark_core(query_marks, key_marks):
    scores = jnp.einsum(
        "bhjd,bhid->bhji", query_marks, key_marks, precision=highest
    ) * HEAD_DIM ** (-0.5)
    kernel_two = jax.nn.softmax(scores, axis=-1)
    return (kernel_two, newton_inverse(kernel_two))


def normalize(summed, gain_vec, shift_vec):
    middle = jnp.mean(summed, axis=-1, keepdims=True)
    centred = summed - middle
    inverse_std = lax.rsqrt(jnp.mean(centred * centred, axis=-1, keepdims=True) + epsilon)
    normal = centred * inverse_std
    return (normal * gain_vec + shift_vec, normal, inverse_std)


def add_norm(partial_sum, residual, bias_vec, gain_vec, shift_vec):
    summed = lax.psum(partial_sum.astype(jnp.bfloat16), "tensor").astype(jnp.float32)
    return normalize(residual + summed + bias_vec, gain_vec, shift_vec)


def norm_back(grad_hidden, normal, inverse_std, gain_vec):
    grad_normal = grad_hidden * gain_vec
    grad_summed = inverse_std * (
        grad_normal
        - jnp.mean(grad_normal, axis=-1, keepdims=True)
        - normal * jnp.mean(grad_normal * normal, axis=-1, keepdims=True)
    )
    return (grad_summed, jnp.sum(grad_hidden * normal, axis=0), jnp.sum(grad_hidden, axis=0))


def combine_soft(earlier, later):
    top_score = jnp.maximum(earlier[0], later[0])
    weight_first = jnp.exp(earlier[0] - top_score)
    weight_second = jnp.exp(later[0] - top_score)
    return (
        top_score,
        earlier[1] * weight_first + later[1] * weight_second,
        earlier[2] * weight_first[..., None] + later[2] * weight_second[..., None],
    )


def general_plan(
    tokens,
    lengths,
    query_weight,
    query_bias,
    key_weight,
    value_weight,
    value_bias,
    conv_kernel,
    out_weight,
    out_bias,
    first_gain,
    first_shift,
    up_weight,
    up_bias,
    down_weight,
    down_bias,
    second_gain,
    second_shift,
    out_grad,
):
    batch, tok_local, width = tokens.shape
    local_width = query_weight.shape[1]
    local_heads = conv_kernel.shape[0]
    head_dim = local_width // local_heads
    score_scale = HEAD_DIM ** (-0.5)
    rows = batch * tok_local
    half_width = CONV // 2
    f32 = jnp.float32
    bf16 = jnp.bfloat16
    position = lax.axis_index("seq") * tok_local + jnp.arange(tok_local, dtype=jnp.int32)
    inside = position[None, :] < lengths[:, None]
    living = inside.astype(f32)
    segment = position[None, :] * LAND // lengths[:, None]
    onehot = (
        (segment[:, :, None] == jnp.arange(LAND, dtype=jnp.int32)[None, None, :])
        & inside[:, :, None]
    ).astype(f32)
    marks_index = jnp.arange(LAND, dtype=jnp.int32)
    upper = ((marks_index[None, :] + 1) * lengths[:, None] + LAND - 1) // LAND
    lower = (marks_index[None, :] * lengths[:, None] + LAND - 1) // LAND
    counts = (upper - lower).astype(f32)
    flat = tokens.reshape(rows, width)
    flat_wide = flat.astype(f32)
    queries = (jnp.dot(flat, query_weight, preferred_element_type=f32) + query_bias).astype(bf16)
    key_vectors = jnp.dot(flat, key_weight, preferred_element_type=f32).astype(bf16)
    values = (
        (jnp.dot(flat, value_weight, preferred_element_type=f32) + value_bias)
        * living.reshape(rows, 1)
    ).astype(bf16)
    query_three = queries.reshape(batch, tok_local, local_width)
    key_three = key_vectors.reshape(batch, tok_local, local_width)
    value_three = values.reshape(batch, tok_local, local_width)
    onehot_low = onehot.astype(bf16)
    query_sum = jnp.einsum("btj,btf->bjf", onehot_low, query_three, preferred_element_type=f32)
    key_sum = jnp.einsum("btj,btf->bjf", onehot_low, key_three, preferred_element_type=f32)
    query_sum, key_sum = lax.psum((query_sum, key_sum), "seq")
    query_marks = (
        (query_sum / counts[:, :, None])
        .reshape(batch, LAND, local_heads, head_dim)
        .transpose(0, 2, 1, 3)
    )
    key_marks = (
        (key_sum / counts[:, :, None])
        .reshape(batch, LAND, local_heads, head_dim)
        .transpose(0, 2, 1, 3)
    )
    (kernel_two, inverse), core_back = jax.vjp(landmark_core, query_marks, key_marks)
    identity = jnp.eye(LAND, dtype=f32)
    deviation = identity - jnp.matmul(kernel_two, inverse, precision=highest)
    proxy_part = jnp.sum(jnp.sqrt(jnp.sum(deviation * deviation, axis=(-2, -1)))) / (batch * HEADS)
    query_heads = query_three.reshape(batch, tok_local, local_heads, head_dim).astype(f32)
    key_heads = key_three.reshape(batch, tok_local, local_heads, head_dim).astype(f32)
    value_heads = value_three.reshape(batch, tok_local, local_heads, head_dim).astype(f32)
    first_scores = (
        jnp.einsum("bthd,bhjd->bhtj", query_heads, key_marks, precision=highest) * score_scale
    )
    kernel_one = jax.nn.softmax(first_scores, axis=-1)
    third_scores = (
        jnp.einsum("bhjd,bthd->bhjt", query_marks, key_heads, precision=highest) * score_scale
    )
    key_alive = inside[:, None, None, :]
    third_scores = jnp.where(key_alive, third_scores, negative)
    local_top = jnp.max(third_scores, axis=-1)
    local_weights = jnp.where(key_alive, jnp.exp(third_scores - local_top[..., None]), 0.0)
    local_total = jnp.sum(local_weights, axis=-1)
    local_mix = jnp.einsum("bhjt,bthd->bhjd", local_weights, value_heads, precision=highest)
    top_score, total_weight, mixed = joined(
        (local_top, local_total, local_mix), "seq", combine_soft
    )
    third_out = mixed / total_weight[..., None]
    carried = jnp.matmul(inverse, third_out, precision=highest)
    nystrom = jnp.einsum("bhtj,bhjd->bthd", kernel_one, carried, precision=highest).reshape(
        batch, tok_local, local_width
    )
    padded_values = with_halo(value_three, (("seq", 1),), half_width)
    kernel_wide = jnp.repeat(conv_kernel, head_dim, axis=0)
    convolved = jnp.zeros((batch, tok_local, local_width), f32)
    for i in range(CONV):
        convolved = (
            convolved + padded_values[:, i : i + tok_local, :].astype(f32) * kernel_wide[:, i]
        )
    attention = (nystrom + convolved).astype(bf16).reshape(rows, local_width)
    out_part = jnp.dot(attention, out_weight, preferred_element_type=f32)
    hidden_one, normal_one, inverse_one = add_norm(
        out_part, flat_wide, out_bias, first_gain, first_shift
    )
    hidden_low = hidden_one.astype(bf16)
    up_value = jnp.dot(hidden_low, up_weight, preferred_element_type=f32) + up_bias
    activated, gelu_back = jax.vjp(lambda z: jax.nn.gelu(z, approximate=False), up_value)
    activated = activated.astype(bf16)
    down_part = jnp.dot(activated, down_weight, preferred_element_type=f32)
    hidden_two, normal_two, inverse_two = add_norm(
        down_part, hidden_one, down_bias, second_gain, second_shift
    )
    output = hidden_two.astype(bf16).reshape(batch, tok_local, width)
    grad_output = out_grad.reshape(rows, width).astype(f32)
    grad_second_total, grad_second_gain, grad_second_shift = norm_back(
        grad_output, normal_two, inverse_two, second_gain
    )
    down_in = grad_second_total.astype(bf16)
    grad_down_bias = jnp.sum(down_in.astype(f32), axis=0)
    grad_down_weight = jnp.einsum("rf,rd->fd", activated, down_in, preferred_element_type=f32)
    grad_activated = jnp.einsum("rd,fd->rf", down_in, down_weight, preferred_element_type=f32)
    up_in = gelu_back(grad_activated)[0].astype(bf16)
    grad_up_bias = jnp.sum(up_in.astype(f32), axis=0)
    grad_up_weight = jnp.einsum("rd,rf->df", hidden_low, up_in, preferred_element_type=f32)
    hidden_part = jnp.einsum("rf,df->rd", up_in, up_weight, preferred_element_type=f32)
    grad_hidden_one = (
        lax.psum(hidden_part.astype(jnp.bfloat16), "tensor").astype(jnp.float32) + grad_second_total
    )
    grad_first_total, grad_first_gain, grad_first_shift = norm_back(
        grad_hidden_one, normal_one, inverse_one, first_gain
    )
    out_in = grad_first_total.astype(bf16)
    grad_out_bias = jnp.sum(out_in.astype(f32), axis=0)
    grad_out_weight = jnp.einsum("rf,rd->fd", attention, out_in, preferred_element_type=f32)
    grad_attention = jnp.einsum(
        "rd,fd->rf", out_in, out_weight, preferred_element_type=f32
    ).reshape(batch, tok_local, local_width)
    padded_grad = with_halo(grad_attention.astype(jnp.bfloat16), (("seq", 1),), half_width).astype(
        grad_attention.dtype
    )
    grad_conv_values = jnp.zeros((batch, tok_local, local_width), f32)
    conv_columns = []
    for i in range(CONV):
        conv_columns.append(
            jnp.sum(
                grad_attention * padded_values[:, i : i + tok_local, :].astype(f32), axis=(0, 1)
            )
        )
        start_index = 2 * half_width - i
        grad_conv_values = (
            grad_conv_values
            + padded_grad[:, start_index : start_index + tok_local, :] * kernel_wide[:, i]
        )
    grad_conv_kernel = (
        jnp.stack(conv_columns, axis=0).reshape(CONV, local_heads, head_dim).sum(axis=-1).T
    )
    grad_nystrom = grad_attention.reshape(batch, tok_local, local_heads, head_dim)
    grad_kernel_one = jnp.einsum("bthd,bhjd->bhtj", grad_nystrom, carried, precision=highest)
    grad_carried_part = jnp.einsum("bhtj,bthd->bhjd", kernel_one, grad_nystrom, precision=highest)
    grad_first_scores = kernel_one * (
        grad_kernel_one - jnp.sum(kernel_one * grad_kernel_one, axis=-1, keepdims=True)
    )
    grad_query_one = (
        jnp.einsum("bhtj,bhjd->bthd", grad_first_scores, key_marks, precision=highest) * score_scale
    )
    grad_key_marks_part = (
        jnp.einsum("bhtj,bthd->bhjd", grad_first_scores, query_heads, precision=highest)
        * score_scale
    )
    grad_carried, grad_key_marks_one = lax.psum((grad_carried_part, grad_key_marks_part), "seq")
    grad_third_out = jnp.matmul(jnp.swapaxes(inverse, -1, -2), grad_carried, precision=highest)
    grad_inverse = jnp.matmul(grad_carried, jnp.swapaxes(third_out, -1, -2), precision=highest)
    grad_query_marks_two, grad_key_marks_two = core_back((jnp.zeros_like(kernel_two), grad_inverse))
    third_prob = local_weights * jnp.exp(local_top - top_score)[..., None] / total_weight[..., None]
    delta_term = jnp.sum(grad_third_out * third_out, axis=-1)
    grad_prob_value = jnp.einsum("bhjd,bthd->bhjt", grad_third_out, value_heads, precision=highest)
    grad_third_scores = third_prob * (grad_prob_value - delta_term[..., None])
    grad_value_three = jnp.einsum("bhjt,bhjd->bthd", third_prob, grad_third_out, precision=highest)
    grad_key_three = (
        jnp.einsum("bhjt,bhjd->bthd", grad_third_scores, query_marks, precision=highest)
        * score_scale
    )
    grad_query_marks_part = (
        jnp.einsum("bhjt,bthd->bhjd", grad_third_scores, key_heads, precision=highest) * score_scale
    )
    grad_query_marks_three = lax.psum(grad_query_marks_part, "seq")
    grad_query_marks = (grad_query_marks_two + grad_query_marks_three) / counts[:, None, :, None]
    grad_key_marks = (grad_key_marks_one + grad_key_marks_two) / counts[:, None, :, None]
    grad_query_marks = grad_query_marks.transpose(0, 2, 1, 3).reshape(batch, LAND, local_width)
    grad_key_marks = grad_key_marks.transpose(0, 2, 1, 3).reshape(batch, LAND, local_width)
    grad_query_seg = jnp.einsum("btj,bjf->btf", onehot, grad_query_marks, precision=highest)
    grad_key_seg = jnp.einsum("btj,bjf->btf", onehot, grad_key_marks, precision=highest)
    query_in = (
        (grad_query_one.reshape(batch, tok_local, local_width) + grad_query_seg)
        .astype(bf16)
        .reshape(rows, local_width)
    )
    key_in = (
        (grad_key_three.reshape(batch, tok_local, local_width) + grad_key_seg)
        .astype(bf16)
        .reshape(rows, local_width)
    )
    value_in = (grad_value_three.reshape(batch, tok_local, local_width) + grad_conv_values).astype(
        bf16
    )
    value_in = jnp.where(inside[:, :, None], value_in, jnp.zeros_like(value_in)).reshape(
        rows, local_width
    )
    grad_query_bias = jnp.sum(query_in.astype(f32), axis=0)
    grad_value_bias = jnp.sum(value_in.astype(f32), axis=0)
    grad_query_weight = jnp.einsum("rd,rf->df", flat, query_in, preferred_element_type=f32)
    grad_key_weight = jnp.einsum("rd,rf->df", flat, key_in, preferred_element_type=f32)
    grad_value_weight = jnp.einsum("rd,rf->df", flat, value_in, preferred_element_type=f32)
    input_part = (
        jnp.einsum("rf,df->rd", query_in, query_weight, preferred_element_type=f32)
        + jnp.einsum("rf,df->rd", key_in, key_weight, preferred_element_type=f32)
        + jnp.einsum("rf,df->rd", value_in, value_weight, preferred_element_type=f32)
    )
    input_sum, proxy_norm = (
        lax.psum(input_part.astype(jnp.bfloat16), "tensor").astype(jnp.float32),
        lax.psum(proxy_part.astype(jnp.bfloat16), "tensor").astype(jnp.float32),
    )
    grad_tokens = (grad_first_total + input_sum).reshape(batch, tok_local, width)
    (
        grad_query_weight,
        grad_key_weight,
        grad_value_weight,
        grad_out_weight,
        grad_up_weight,
        grad_down_weight,
    ) = (
        lax.psum_scatter(grad_query_weight, "seq", scatter_dimension=0, tiled=True),
        lax.psum_scatter(grad_key_weight, "seq", scatter_dimension=0, tiled=True),
        lax.psum_scatter(grad_value_weight, "seq", scatter_dimension=0, tiled=True),
        lax.psum_scatter(grad_out_weight, "seq", scatter_dimension=1, tiled=True),
        lax.psum_scatter(grad_up_weight, "seq", scatter_dimension=0, tiled=True),
        lax.psum_scatter(grad_down_weight, "seq", scatter_dimension=1, tiled=True),
    )
    (
        grad_query_bias,
        grad_value_bias,
        grad_conv_kernel,
        grad_out_bias,
        grad_first_gain,
        grad_first_shift,
        grad_up_bias,
        grad_down_bias,
        grad_second_gain,
        grad_second_shift,
    ) = lax.psum(
        (
            grad_query_bias,
            grad_value_bias,
            grad_conv_kernel,
            grad_out_bias,
            grad_first_gain,
            grad_first_shift,
            grad_up_bias,
            grad_down_bias,
            grad_second_gain,
            grad_second_shift,
        ),
        "seq",
    )
    return (
        output,
        grad_tokens,
        grad_query_weight,
        grad_query_bias,
        grad_key_weight,
        grad_value_weight,
        grad_value_bias,
        grad_conv_kernel,
        grad_out_weight,
        grad_out_bias,
        grad_first_gain,
        grad_first_shift,
        grad_up_weight,
        grad_up_bias,
        grad_down_weight,
        grad_down_bias,
        grad_second_gain,
        grad_second_shift,
        proxy_norm,
    )


MESH = pl.DeviceIdType.MESH
LANES = 2 * HEAD_DIM
f32 = jnp.float32
bf16 = jnp.bfloat16
NN = (1, 0)
NT = (1, 1)
TN = (0, 0)


def dot(a, b, dims=NN):
    return lax.dot_general(
        a, b, (((dims[0],), (dims[1],)), ((), ())), preferred_element_type=f32
    )


def split(x):
    if x.dtype == bf16:
        return (x,)
    top = x.astype(bf16)
    return (top, (x - top.astype(f32)).astype(bf16))


def fine(a, b, dims=NN):
    a, b = split(a), split(b)
    total = dot(a[0], b[0], dims)
    if len(b) > 1:
        total = total + dot(a[0], b[1], dims)
    if len(a) > 1:
        total = total + dot(a[1], b[0], dims)
    return total


def iota(shape, dim):
    return lax.broadcasted_iota(jnp.int32, shape, dim)


def block_mask():
    shape = (LANES, LANES)
    return (iota(shape, 0) < HEAD_DIM) == (iota(shape, 1) < HEAD_DIM)


def eye():
    return jnp.where(iota((LANES, LANES), 0) == iota((LANES, LANES), 1), 1.0, 0.0).astype(f32)


def block_sums(x, same_head):
    ones = jnp.where(same_head, 1.0, 0.0).astype(bf16)
    return jnp.where(same_head, fine(fine(ones, x), ones), 1.0)


def taps_matrix(row, tok):
    return pltpu.roll(jnp.broadcast_to(row, (tok, 2 * tok)), 0, 1, stride=1, stride_axis=0)


def taps_row(taps, head, tok):
    row = taps[pl.ds(head, 1), :]
    return jnp.concatenate([row, jnp.zeros((1, 2 * tok - CONV), f32)], axis=1)


def conv_block(matrices, window):
    first = fine(matrices[0], window)
    second = fine(matrices[1], window)
    return jnp.where(iota(first.shape, 1) < HEAD_DIM, first, second)


def greet(n, me, tensor):
    barrier = pltpu.get_barrier_semaphore()
    for d in range(1, n):
        pl.semaphore_signal(
            barrier, inc=1, device_id=(lax.rem(me + d, n), tensor), device_id_type=MESH
        )
    return barrier


def paired(y):
    return y[:, :LANES], jnp.concatenate(
        [y[:, LANES : LANES + HEAD_DIM], y[:, HEAD_DIM:LANES]], axis=1
    )


def remote(src, dst, send, recv, device):
    return pltpu.make_async_remote_copy(
        src_ref=src, dst_ref=dst, send_sem=send, recv_sem=recv, device_id=device,
        device_id_type=MESH,
    )


def member_rows(length, total):
    j = iota((LANES, total), 0) % LAND
    t = iota((LANES, total), 1)
    inside = (t * LAND >= j * length) & (t * LAND < (j + 1) * length) & (t < length)
    return jnp.where(inside, 1.0, 0.0).astype(bf16)


def member_columns(length, total):
    j = iota((total, LANES), 1) % LAND
    t = iota((total, LANES), 0)
    inside = (t * LAND >= j * length) & (t * LAND < (j + 1) * length) & (t < length)
    return jnp.where(inside, 1.0, 0.0).astype(bf16)


def segment_counts(length):
    j = iota((LANES, LANES), 0) % LAND
    upper = ((j + 1) * length + LAND - 1) // LAND
    lower = (j * length + LAND - 1) // LAND
    return (upper - lower).astype(f32)


def forward_kernel(
    n, lengths, x, wq, qb, wk, wv, vb, taps,
    attn, qs, ks, vs, k1, p3, newton, mats, proxy,
    stage, out_stage, send, recv, out_send, out_recv,
):
    me = lax.axis_index("seq")
    tensor = lax.axis_index("tensor")
    rows = x.shape[0]
    batch = n // 2
    tok = rows // batch
    total = n * tok
    half = CONV // 2
    own, side = me // 2, me % 2
    scale = HEAD_DIM ** (-0.5)
    barrier = greet(n, me, tensor)

    copies = []
    owned = (ks, qs, vs)
    offsets = (0, 0, half)
    vs[0:half] = jnp.zeros((half, LANES), bf16)
    vs[half + total : total + tok] = jnp.zeros((tok - half, LANES), bf16)
    for i in range(3):
        y = dot(x[...], (wk, wq, wv)[i][...])
        if i == 1:
            y = y + qb[...]
        if i == 2:
            y = y + vb[...]
            pieces = []
            position = me * tok + iota((tok, y.shape[1]), 0)
            for b in range(batch):
                part = y[b * tok : (b + 1) * tok]
                pieces.append(jnp.where(position < lengths[b], part, 0.0))
            y = jnp.concatenate(pieces, axis=0)
        low = y.astype(bf16)
        stage[i, 0], stage[i, 1] = paired(low)
        if i == 0:
            pl.semaphore_wait(barrier, n - 1)
        here = pl.ds(pl.multiple_of(offsets[i] + me * tok, 16), tok)
        for d in range(1, n):
            peer = lax.rem(me + d, n)
            copy = remote(
                stage.at[i, peer % 2, pl.ds(pl.multiple_of((peer // 2) * tok, tok), tok)],
                owned[i].at[here],
                send.at[i, d - 1],
                recv.at[i, d - 1],
                (peer, tensor),
            )
            copy.start()
            copies.append(copy)
        owned[i][here] = stage[i, side, pl.ds(pl.multiple_of(own * tok, tok), tok)]

    length = lengths[own]
    same_head = block_mask()
    identity = eye()
    ones = jnp.where(same_head, 1.0, 0.0).astype(bf16)
    members = member_rows(length, total)
    counts = segment_counts(length)
    for copy in copies[: n - 1]:
        copy.wait_recv()
    keys = ks[...]
    key_marks = jnp.where(same_head, dot(members, keys) / counts, 0.0)
    for copy in copies[n - 1 : 2 * (n - 1)]:
        copy.wait_recv()
    queries = qs[...]
    query_marks = jnp.where(same_head, dot(members, queries) / counts, 0.0)

    scores = jnp.where(same_head, fine(query_marks, key_marks, NT) * scale, negative)
    weights = jnp.exp(scores - jnp.max(scores, axis=1, keepdims=True))
    kernel_two = weights / jnp.sum(weights, axis=1, keepdims=True)
    inverse = jnp.where(
        same_head, kernel_two.T / block_sums(kernel_two * kernel_two, same_head), 0.0
    )
    for step in range(NS_ITERS):
        product = fine(kernel_two, inverse)
        inner_one = fine(product, 7.0 * identity - product)
        inner_two = fine(product, 15.0 * identity - inner_one)
        newton[4 * step] = inverse
        newton[4 * step + 1] = product
        newton[4 * step + 2] = inner_one
        newton[4 * step + 3] = inner_two
        inverse = 0.25 * fine(inverse, 13.0 * identity - inner_two)

    deviation = identity - fine(kernel_two, inverse)
    norms = jnp.sqrt(block_sums(deviation * deviation, same_head))
    proxy[...] = norms

    first_scores = fine(queries, key_marks, NT) * scale
    left = iota(first_scores.shape, 1) < HEAD_DIM
    top_left = jnp.max(jnp.where(left, first_scores, negative), axis=1, keepdims=True)
    top_right = jnp.max(jnp.where(left, negative, first_scores), axis=1, keepdims=True)
    weights = jnp.exp(first_scores - jnp.where(left, top_left, top_right))
    kernel_one = weights / fine(weights, ones)
    k1[...] = kernel_one

    third_scores = fine(keys, query_marks, NT) * scale
    alive = iota(third_scores.shape, 0) < length
    third_scores = jnp.where(alive, third_scores, negative)
    weights = jnp.exp(third_scores - jnp.max(third_scores, axis=0, keepdims=True))
    weights = jnp.where(alive, weights, 0.0)
    third_prob = weights / jnp.sum(weights, axis=0, keepdims=True)
    p3[...] = third_prob

    for copy in copies[2 * (n - 1) :]:
        copy.wait_recv()
    values = vs[half : half + total]
    third_out = jnp.where(same_head, fine(third_prob, values, TN), 0.0)
    carried = fine(inverse, third_out)
    mats[0] = query_marks
    mats[1] = key_marks
    mats[2] = kernel_two
    mats[3] = inverse
    mats[4] = third_out
    mats[5] = carried

    matrices = [taps_matrix(taps_row(taps, h, tok), tok) for h in (2 * side, 1)]
    there = pl.ds(pl.multiple_of(own * tok, tok), tok)
    for d in range(1, n + 1):
        peer = lax.rem(me + d, n)
        start = pl.multiple_of(peer * tok, tok)
        nystrom = fine(k1[pl.ds(start, tok)], carried)
        convolved = conv_block(matrices, vs[pl.ds(start, 2 * tok)])
        low = (nystrom + convolved).astype(bf16)
        if d == n:
            attn[side, there] = low
        else:
            out_stage[d - 1] = low
            copy = remote(
                out_stage.at[d - 1],
                attn.at[side, there],
                out_send.at[d - 1],
                out_recv.at[d - 1],
                (peer, tensor),
            )
            copy.start()
            copies.append(copy)
    for copy in copies[: 3 * (n - 1)]:
        copy.wait_send()
    for copy in copies[3 * (n - 1) :]:
        copy.wait()


def backward_kernel(
    n, lengths, out_in, out_weight, taps, qs, ks, vs, k1, p3, newton, mats,
    rin, conv_grad,
    stage, gs, out_stage, send, recv, out_send, out_recv,
):
    me = lax.axis_index("seq")
    tensor = lax.axis_index("tensor")
    rows = out_in.shape[0]
    batch = n // 2
    tok = rows // batch
    total = n * tok
    half = CONV // 2
    own, side = me // 2, me % 2
    scale = HEAD_DIM ** (-0.5)
    barrier = greet(n, me, tensor)

    gs[0:half] = jnp.zeros((half, LANES), bf16)
    gs[half + total : total + tok] = jnp.zeros((tok - half, LANES), bf16)
    grad = dot(out_in[...], out_weight[...], NT).astype(bf16)
    stage[0], stage[1] = paired(grad)
    pl.semaphore_wait(barrier, n - 1)
    here = pl.ds(pl.multiple_of(half + me * tok, 16), tok)
    copies = []
    for d in range(1, n):
        peer = lax.rem(me + d, n)
        copy = remote(
            stage.at[peer % 2, pl.ds(pl.multiple_of((peer // 2) * tok, tok), tok)],
            gs.at[here],
            send.at[d - 1],
            recv.at[d - 1],
            (peer, tensor),
        )
        copy.start()
        copies.append(copy)
    gs[here] = stage[side, pl.ds(pl.multiple_of(own * tok, tok), tok)]

    length = lengths[own]
    same_head = block_mask()
    identity = eye()
    ones = jnp.where(same_head, 1.0, 0.0).astype(bf16)
    members = member_columns(length, total)
    counts = segment_counts(length)
    query_marks, key_marks, kernel_two, inverse, third_out, carried = [mats[i] for i in range(6)]
    matrices = [taps_matrix(taps_row(taps, h, tok), tok) for h in (2 * side, 1)]
    flip = jnp.where(
        iota((2 * tok, 2 * tok), 0) + iota((2 * tok, 2 * tok), 1) == CONV - 1, 1.0, 0.0
    ).astype(bf16)
    reverse = [
        taps_matrix(
            fine(jnp.broadcast_to(taps_row(taps, h, tok), (8, 2 * tok)), flip)[0:1], tok
        )
        for h in (2 * side, 1)
    ]
    queries, keys, values = qs[...], ks[...], vs[half : half + total]
    for copy in copies:
        copy.wait_recv()

    grad = gs[half : half + total]
    kernel_one = k1[...]
    grad_carried = jnp.where(same_head, fine(kernel_one, grad, TN), 0.0)
    grad_third = fine(inverse, grad_carried, TN)
    grad_inverse = fine(grad_carried, third_out, NT)

    third_prob = p3[...]
    grad_values = fine(third_prob, grad_third)
    alive = iota((tok, LANES), 0)
    outs = []

    return_blocks = {}
    full = []
    for m in range(n):
        block = grad_values[m * tok : (m + 1) * tok] + conv_block(
            reverse, gs[m * tok : (m + 2) * tok]
        )
        full.append(jnp.where(alive + m * tok < length, block, 0.0))
    return_blocks[2] = jnp.concatenate(full, axis=0)

    kernel_back = jnp.zeros((LANES, LANES), f32)
    grad_state = grad_inverse
    for step in reversed(range(NS_ITERS)):
        state, product, inner_one, inner_two = [newton[4 * step + i] for i in range(4)]
        grad_next = 0.25 * fine(grad_state, 13.0 * identity - inner_two, NT)
        grad_two = -0.25 * fine(state, grad_state, TN)
        grad_product = fine(grad_two, 15.0 * identity - inner_one, NT)
        grad_one = -fine(product, grad_two, TN)
        grad_product = (
            grad_product
            + fine(grad_one, 7.0 * identity - product, NT)
            - fine(product, grad_one, TN)
        )
        grad_state = grad_next + fine(kernel_two, grad_product, TN)
        kernel_back = kernel_back + fine(grad_product, state, NT)
    squares = block_sums(kernel_two * kernel_two, same_head)
    spread = jnp.where(same_head, block_sums(grad_state * newton[0], same_head), 0.0)
    kernel_back = kernel_back + (grad_state.T - 2.0 * kernel_two * spread) / squares
    grad_scores = scale * kernel_two * (
        kernel_back - jnp.sum(kernel_two * kernel_back, axis=1, keepdims=True)
    )
    query_two = fine(grad_scores, key_marks)
    key_two = fine(grad_scores, query_marks, TN)

    grad_one = fine(grad, carried, NT)
    both = kernel_one * grad_one
    first_scores = scale * (both - kernel_one * fine(both, ones))
    key_one = jnp.where(same_head, fine(first_scores, queries, TN), 0.0)
    delta = fine(jnp.ones((8, LANES), bf16), grad_third * third_out, NT)[0:1]
    third_scores = scale * third_prob * (fine(values, grad_third, NT) - delta)
    query_three = jnp.where(same_head, fine(third_scores, keys, TN), 0.0)
    return_blocks[0] = fine(third_scores, query_marks) + fine(
        members, (key_one + key_two) / counts
    )
    return_blocks[1] = fine(first_scores, key_marks) + fine(
        members, (query_two + query_three) / counts
    )
    for i in (2, 0, 1):
        low = return_blocks[i].astype(bf16)
        for m in range(n):
            out_stage[i, m] = low[m * tok : (m + 1) * tok]
        there = pl.ds(pl.multiple_of(own * tok, tok), tok)
        for d in range(1, n):
            peer = lax.rem(me + d, n)
            copy = remote(
                out_stage.at[i, peer],
                rin.at[i, side, there],
                out_send.at[i, d - 1],
                out_recv.at[i, d - 1],
                (peer, tensor),
            )
            copy.start()
            outs.append(copy)
        rin[i, side, there] = out_stage[i, me]

    position = iota((tok, tok), 0) + iota((tok, tok), 1)
    upside = jnp.where(position == tok - 1, 1.0, 0.0).astype(bf16)
    lane = iota((tok, LANES), 1)
    for h in range(2):
        mine = (lane < HEAD_DIM) if h == 0 else (lane >= HEAD_DIM)
        table = jnp.zeros((tok, 2 * tok), f32)
        for m in range(n):
            block = gs[half + m * tok : half + (m + 1) * tok]
            block = jnp.where(mine, block, jnp.zeros_like(block))
            table = table + dot(block, vs[m * tok : (m + 2) * tok], NT)
        table = pltpu.roll(fine(upside, table), 0, 1, stride=1, stride_axis=0)
        row = jnp.sum(table, axis=0, keepdims=True)
        row = pltpu.roll(jnp.broadcast_to(row, (8, 2 * tok)), tok + 1, 1)
        conv_grad[h] = row
    for copy in copies:
        copy.wait_send()
    for copy in outs:
        copy.wait()


def whole(shape, dtype):
    return jax.ShapeDtypeStruct(shape, dtype)


VMEM = pl.BlockSpec(memory_space=pltpu.VMEM)
SMEM = pl.BlockSpec(memory_space=pltpu.SMEM)


def attention_forward(n, lengths, flat, wq, qb, wk, wv, vb, taps):
    rows = flat.shape[0]
    tok = rows // (n // 2)
    total = n * tok
    return pl.pallas_call(
        functools.partial(forward_kernel, n),
        out_shape=(
            whole((2, rows, LANES), bf16),
            whole((total, LANES), bf16),
            whole((total, LANES), bf16),
            whole((total + tok, LANES), bf16),
            whole((total, LANES), f32),
            whole((total, LANES), f32),
            whole((4 * NS_ITERS, LANES, LANES), f32),
            whole((6, LANES, LANES), f32),
            whole((LANES, LANES), f32),
        ),
        in_specs=[SMEM] + [VMEM] * 7,
        out_specs=(VMEM,) * 9,
        scratch_shapes=[
            pltpu.VMEM((3, 2, rows, LANES), bf16),
            pltpu.VMEM((n - 1, tok, LANES), bf16),
            pltpu.SemaphoreType.DMA((3, n - 1)),
            pltpu.SemaphoreType.DMA((3, n - 1)),
            pltpu.SemaphoreType.DMA((n - 1,)),
            pltpu.SemaphoreType.DMA((n - 1,)),
        ],
        compiler_params=pltpu.CompilerParams(
            collective_id=0, has_side_effects=True, vmem_limit_bytes=48 * 2**20
        ),
        name="attention_forward",
    )(lengths, flat, wq, qb, wk, wv, vb, taps)


def attention_backward(n, lengths, out_in, out_weight, taps, saved):
    rows = out_in.shape[0]
    tok = rows // (n // 2)
    total = n * tok
    return pl.pallas_call(
        functools.partial(backward_kernel, n),
        out_shape=(whole((3, 2, rows, LANES), bf16), whole((2, 8, 2 * tok), f32)),
        in_specs=[SMEM] + [VMEM] * 10,
        out_specs=(VMEM,) * 2,
        scratch_shapes=[
            pltpu.VMEM((2, rows, LANES), bf16),
            pltpu.VMEM((total + tok, LANES), bf16),
            pltpu.VMEM((3, n, tok, LANES), bf16),
            pltpu.SemaphoreType.DMA((n - 1,)),
            pltpu.SemaphoreType.DMA((n - 1,)),
            pltpu.SemaphoreType.DMA((3, n - 1)),
            pltpu.SemaphoreType.DMA((3, n - 1)),
        ],
        compiler_params=pltpu.CompilerParams(
            collective_id=1, has_side_effects=True, vmem_limit_bytes=48 * 2**20
        ),
        name="attention_backward",
    )(lengths, out_in, out_weight, taps, *saved)


def gathered_plan(
    n, tokens, lengths, query_weight, query_bias, key_weight, value_weight, value_bias,
    conv_kernel, out_weight, out_bias, first_gain, first_shift, up_weight, up_bias, down_weight,
    down_bias, second_gain, second_shift, out_grad,
):
    batch, tok, width = tokens.shape
    rows = batch * tok
    flat = tokens.reshape(rows, width)
    flat_wide = flat.astype(f32)
    attn, *saved, proxy = attention_forward(
        n, lengths, flat, query_weight, query_bias[None], key_weight, value_weight,
        value_bias[None], conv_kernel,
    )
    side = lax.axis_index("seq") % 2
    proxy_part = jnp.where(side == 0, proxy[0, 0] + proxy[-1, -1], proxy[0, 0]) / (batch * HEADS)
    attention = jnp.concatenate([attn[0], attn[1, :, :HEAD_DIM]], axis=1)
    out_part = jnp.dot(attention, out_weight, preferred_element_type=f32)
    hidden_one, normal_one, inverse_one = add_norm(
        out_part, flat_wide, out_bias, first_gain, first_shift
    )
    hidden_low = hidden_one.astype(bf16)
    up_value = jnp.dot(hidden_low, up_weight, preferred_element_type=f32) + up_bias
    activated, gelu_back = jax.vjp(lambda z: jax.nn.gelu(z, approximate=False), up_value)
    activated = activated.astype(bf16)
    down_part = jnp.dot(activated, down_weight, preferred_element_type=f32)
    hidden_two, normal_two, inverse_two = add_norm(
        down_part, hidden_one, down_bias, second_gain, second_shift
    )
    output = hidden_two.astype(bf16).reshape(batch, tok, width)
    grad_output = out_grad.reshape(rows, width).astype(f32)
    grad_second_total, grad_second_gain, grad_second_shift = norm_back(
        grad_output, normal_two, inverse_two, second_gain
    )
    down_in = grad_second_total.astype(bf16)
    grad_down_bias = jnp.sum(down_in.astype(f32), axis=0)
    grad_down_weight = jnp.einsum("rf,rd->fd", activated, down_in, preferred_element_type=f32)
    grad_activated = jnp.einsum("rd,fd->rf", down_in, down_weight, preferred_element_type=f32)
    up_in = gelu_back(grad_activated)[0].astype(bf16)
    grad_up_bias = jnp.sum(up_in.astype(f32), axis=0)
    grad_up_weight = jnp.einsum("rd,rf->df", hidden_low, up_in, preferred_element_type=f32)
    hidden_part = jnp.einsum("rf,df->rd", up_in, up_weight, preferred_element_type=f32)
    grad_hidden_one = (
        lax.psum(hidden_part.astype(bf16), "tensor").astype(f32) + grad_second_total
    )
    grad_first_total, grad_first_gain, grad_first_shift = norm_back(
        grad_hidden_one, normal_one, inverse_one, first_gain
    )
    out_in = grad_first_total.astype(bf16)
    grad_out_bias = jnp.sum(out_in.astype(f32), axis=0)
    grad_out_weight = jnp.einsum("rf,rd->fd", attention, out_in, preferred_element_type=f32)
    rin, conv_grad = attention_backward(n, lengths, out_in, out_weight, conv_kernel, saved)
    first, second = conv_grad[0, 0, :CONV], conv_grad[1, 0, :CONV]
    nothing = jnp.zeros_like(first)
    grad_conv_kernel = jnp.where(
        side == 0, jnp.stack([first, second, nothing]), jnp.stack([nothing, nothing, first])
    )
    key_in, query_in, value_in = [
        jnp.concatenate([rin[i, 0], rin[i, 1, :, :HEAD_DIM]], axis=1) for i in range(3)
    ]
    grad_query_bias = jnp.sum(query_in.astype(f32), axis=0)
    grad_value_bias = jnp.sum(value_in.astype(f32), axis=0)
    grad_query_weight = jnp.einsum("rd,rf->df", flat, query_in, preferred_element_type=f32)
    grad_key_weight = jnp.einsum("rd,rf->df", flat, key_in, preferred_element_type=f32)
    grad_value_weight = jnp.einsum("rd,rf->df", flat, value_in, preferred_element_type=f32)
    input_part = (
        jnp.einsum("rf,df->rd", query_in, query_weight, preferred_element_type=f32)
        + jnp.einsum("rf,df->rd", key_in, key_weight, preferred_element_type=f32)
        + jnp.einsum("rf,df->rd", value_in, value_weight, preferred_element_type=f32)
    )
    input_sum = lax.psum(input_part.astype(bf16), "tensor").astype(f32)
    proxy_norm = lax.psum(proxy_part, ("seq", "tensor"))
    grad_tokens = (grad_first_total + input_sum).reshape(batch, tok, width)
    scattered = [
        lax.psum_scatter(g, "seq", scatter_dimension=dim, tiled=True)
        for g, dim in (
            (grad_query_weight, 0), (grad_key_weight, 0), (grad_value_weight, 0),
            (grad_out_weight, 1), (grad_up_weight, 0), (grad_down_weight, 1),
        )
    ]
    summed = lax.psum(
        (
            grad_query_bias, grad_value_bias, grad_conv_kernel, grad_out_bias, grad_first_gain,
            grad_first_shift, grad_up_bias, grad_down_bias, grad_second_gain, grad_second_shift,
        ),
        "seq",
    )
    return (
        output, grad_tokens, scattered[0], summed[0], scattered[1], scattered[2], summed[1],
        summed[2], scattered[3], summed[3], summed[4], summed[5], scattered[4], summed[6],
        scattered[5], summed[7], summed[8], summed[9], proxy_norm,
    )


def per_device(seq, tensor, *args):
    batch, tok, _ = args[0].shape
    local_heads = args[7].shape[0]
    if seq == 2 * batch and local_heads == 3 and tok % 128 == 0:
        return gathered_plan(seq, *args)
    return general_plan(*args)


def solution(mesh):
    return jax.shard_map(
        functools.partial(per_device, mesh.shape["seq"], mesh.shape["tensor"]),
        mesh=mesh,
        in_specs=(
            P(None, "seq", None),
            P(),
            P(None, "tensor"),
            P("tensor"),
            P(None, "tensor"),
            P(None, "tensor"),
            P("tensor"),
            P("tensor", None),
            P("tensor", None),
            P(),
            P(),
            P(),
            P(None, "tensor"),
            P("tensor"),
            P("tensor", None),
            P(),
            P(),
            P(),
            P(None, "seq", None),
        ),
        out_specs=(
            P(None, "seq", None),
            P(None, "seq", None),
            P("seq", "tensor"),
            P("tensor"),
            P("seq", "tensor"),
            P("seq", "tensor"),
            P("tensor"),
            P("tensor", None),
            P("tensor", "seq"),
            P(),
            P(),
            P(),
            P("seq", "tensor"),
            P("tensor"),
            P("tensor", "seq"),
            P(),
            P(),
            P(),
            P(),
        ),
        check_vma=False,
    )
```

```python
import functools

import jax
import jax.numpy as jnp
from jax import lax
from jax.experimental import pallas as pl
from jax.experimental.pallas import tpu as pltpu
from jax.sharding import PartitionSpec as P

HEADS = 12
HEAD_DIM = 64
LAND = 64
CONV = 33
NS_ITERS = 6


highest = lax.Precision.HIGHEST
epsilon = 1e-05
negative = -1e30


def joined(x, axis, combine):
    everything = jax.tree.map(lambda part: lax.all_gather(part, axis), x)
    first = jax.tree.map(lambda part: part[0], everything)

    def hop(k, so_far):
        return combine(so_far, jax.tree.map(lambda part: part[k], everything))

    return lax.fori_loop(1, lax.axis_size(axis), hop, first)


def with_halo(block, sides, width):
    for axis, dim in sides:
        count = lax.axis_size(axis)
        forward = [(i, i + 1) for i in range(count - 1)]
        backward = [(target, source) for source, target in forward]
        low = lax.ppermute(
            lax.slice_in_dim(block, block.shape[dim] - width, None, axis=dim), axis, forward
        )
        high = lax.ppermute(lax.slice_in_dim(block, 0, width, axis=dim), axis, backward)
        block = jnp.concatenate([low, block, high], axis=dim)
    return block


def newton_inverse(kernel):
    identity = jnp.eye(kernel.shape[-1], dtype=jnp.float32)
    inverse = jnp.swapaxes(kernel, -1, -2) / jnp.sum(kernel * kernel, axis=(-2, -1), keepdims=True)
    for _ in range(NS_ITERS):
        product = jnp.matmul(kernel, inverse, precision=highest)
        inner_term = jnp.matmul(product, 7.0 * identity - product, precision=highest)
        inner_term = jnp.matmul(product, 15.0 * identity - inner_term, precision=highest)
        inverse = 0.25 * jnp.matmul(inverse, 13.0 * identity - inner_term, precision=highest)
    return inverse


def landmark_core(query_marks, key_marks):
    scores = jnp.einsum(
        "bhjd,bhid->bhji", query_marks, key_marks, precision=highest
    ) * HEAD_DIM ** (-0.5)
    kernel_two = jax.nn.softmax(scores, axis=-1)
    return (kernel_two, newton_inverse(kernel_two))


def normalize(summed, gain_vec, shift_vec):
    middle = jnp.mean(summed, axis=-1, keepdims=True)
    centred = summed - middle
    inverse_std = lax.rsqrt(jnp.mean(centred * centred, axis=-1, keepdims=True) + epsilon)
    normal = centred * inverse_std
    return (normal * gain_vec + shift_vec, normal, inverse_std)


def add_norm(partial_sum, residual, bias_vec, gain_vec, shift_vec):
    summed = lax.psum(partial_sum.astype(jnp.bfloat16), "tensor").astype(jnp.float32)
    return normalize(residual + summed + bias_vec, gain_vec, shift_vec)


def norm_back(grad_hidden, normal, inverse_std, gain_vec):
    grad_normal = grad_hidden * gain_vec
    grad_summed = inverse_std * (
        grad_normal
        - jnp.mean(grad_normal, axis=-1, keepdims=True)
        - normal * jnp.mean(grad_normal * normal, axis=-1, keepdims=True)
    )
    return (grad_summed, jnp.sum(grad_hidden * normal, axis=0), jnp.sum(grad_hidden, axis=0))


def combine_soft(earlier, later):
    top_score = jnp.maximum(earlier[0], later[0])
    weight_first = jnp.exp(earlier[0] - top_score)
    weight_second = jnp.exp(later[0] - top_score)
    return (
        top_score,
        earlier[1] * weight_first + later[1] * weight_second,
        earlier[2] * weight_first[..., None] + later[2] * weight_second[..., None],
    )


def general_plan(
    tokens,
    lengths,
    query_weight,
    query_bias,
    key_weight,
    value_weight,
    value_bias,
    conv_kernel,
    out_weight,
    out_bias,
    first_gain,
    first_shift,
    up_weight,
    up_bias,
    down_weight,
    down_bias,
    second_gain,
    second_shift,
    out_grad,
):
    batch, tok_local, width = tokens.shape
    local_width = query_weight.shape[1]
    local_heads = conv_kernel.shape[0]
    head_dim = local_width // local_heads
    score_scale = HEAD_DIM ** (-0.5)
    rows = batch * tok_local
    half_width = CONV // 2
    f32 = jnp.float32
    bf16 = jnp.bfloat16
    position = lax.axis_index("seq") * tok_local + jnp.arange(tok_local, dtype=jnp.int32)
    inside = position[None, :] < lengths[:, None]
    living = inside.astype(f32)
    segment = position[None, :] * LAND // lengths[:, None]
    onehot = (
        (segment[:, :, None] == jnp.arange(LAND, dtype=jnp.int32)[None, None, :])
        & inside[:, :, None]
    ).astype(f32)
    marks_index = jnp.arange(LAND, dtype=jnp.int32)
    upper = ((marks_index[None, :] + 1) * lengths[:, None] + LAND - 1) // LAND
    lower = (marks_index[None, :] * lengths[:, None] + LAND - 1) // LAND
    counts = (upper - lower).astype(f32)
    flat = tokens.reshape(rows, width)
    flat_wide = flat.astype(f32)
    queries = (jnp.dot(flat, query_weight, preferred_element_type=f32) + query_bias).astype(bf16)
    key_vectors = jnp.dot(flat, key_weight, preferred_element_type=f32).astype(bf16)
    values = (
        (jnp.dot(flat, value_weight, preferred_element_type=f32) + value_bias)
        * living.reshape(rows, 1)
    ).astype(bf16)
    query_three = queries.reshape(batch, tok_local, local_width)
    key_three = key_vectors.reshape(batch, tok_local, local_width)
    value_three = values.reshape(batch, tok_local, local_width)
    onehot_low = onehot.astype(bf16)
    query_sum = jnp.einsum("btj,btf->bjf", onehot_low, query_three, preferred_element_type=f32)
    key_sum = jnp.einsum("btj,btf->bjf", onehot_low, key_three, preferred_element_type=f32)
    query_sum, key_sum = lax.psum((query_sum, key_sum), "seq")
    query_marks = (
        (query_sum / counts[:, :, None])
        .reshape(batch, LAND, local_heads, head_dim)
        .transpose(0, 2, 1, 3)
    )
    key_marks = (
        (key_sum / counts[:, :, None])
        .reshape(batch, LAND, local_heads, head_dim)
        .transpose(0, 2, 1, 3)
    )
    (kernel_two, inverse), core_back = jax.vjp(landmark_core, query_marks, key_marks)
    identity = jnp.eye(LAND, dtype=f32)
    deviation = identity - jnp.matmul(kernel_two, inverse, precision=highest)
    proxy_part = jnp.sum(jnp.sqrt(jnp.sum(deviation * deviation, axis=(-2, -1)))) / (batch * HEADS)
    query_heads = query_three.reshape(batch, tok_local, local_heads, head_dim).astype(f32)
    key_heads = key_three.reshape(batch, tok_local, local_heads, head_dim).astype(f32)
    value_heads = value_three.reshape(batch, tok_local, local_heads, head_dim).astype(f32)
    first_scores = (
        jnp.einsum("bthd,bhjd->bhtj", query_heads, key_marks, precision=highest) * score_scale
    )
    kernel_one = jax.nn.softmax(first_scores, axis=-1)
    third_scores = (
        jnp.einsum("bhjd,bthd->bhjt", query_marks, key_heads, precision=highest) * score_scale
    )
    key_alive = inside[:, None, None, :]
    third_scores = jnp.where(key_alive, third_scores, negative)
    local_top = jnp.max(third_scores, axis=-1)
    local_weights = jnp.where(key_alive, jnp.exp(third_scores - local_top[..., None]), 0.0)
    local_total = jnp.sum(local_weights, axis=-1)
    local_mix = jnp.einsum("bhjt,bthd->bhjd", local_weights, value_heads, precision=highest)
    top_score, total_weight, mixed = joined(
        (local_top, local_total, local_mix), "seq", combine_soft
    )
    third_out = mixed / total_weight[..., None]
    carried = jnp.matmul(inverse, third_out, precision=highest)
    nystrom = jnp.einsum("bhtj,bhjd->bthd", kernel_one, carried, precision=highest).reshape(
        batch, tok_local, local_width
    )
    padded_values = with_halo(value_three, (("seq", 1),), half_width)
    kernel_wide = jnp.repeat(conv_kernel, head_dim, axis=0)
    convolved = jnp.zeros((batch, tok_local, local_width), f32)
    for i in range(CONV):
        convolved = (
            convolved + padded_values[:, i : i + tok_local, :].astype(f32) * kernel_wide[:, i]
        )
    attention = (nystrom + convolved).astype(bf16).reshape(rows, local_width)
    out_part = jnp.dot(attention, out_weight, preferred_element_type=f32)
    hidden_one, normal_one, inverse_one = add_norm(
        out_part, flat_wide, out_bias, first_gain, first_shift
    )
    hidden_low = hidden_one.astype(bf16)
    up_value = jnp.dot(hidden_low, up_weight, preferred_element_type=f32) + up_bias
    activated, gelu_back = jax.vjp(lambda z: jax.nn.gelu(z, approximate=False), up_value)
    activated = activated.astype(bf16)
    down_part = jnp.dot(activated, down_weight, preferred_element_type=f32)
    hidden_two, normal_two, inverse_two = add_norm(
        down_part, hidden_one, down_bias, second_gain, second_shift
    )
    output = hidden_two.astype(bf16).reshape(batch, tok_local, width)
    grad_output = out_grad.reshape(rows, width).astype(f32)
    grad_second_total, grad_second_gain, grad_second_shift = norm_back(
        grad_output, normal_two, inverse_two, second_gain
    )
    down_in = grad_second_total.astype(bf16)
    grad_down_bias = jnp.sum(down_in.astype(f32), axis=0)
    grad_down_weight = jnp.einsum("rf,rd->fd", activated, down_in, preferred_element_type=f32)
    grad_activated = jnp.einsum("rd,fd->rf", down_in, down_weight, preferred_element_type=f32)
    up_in = gelu_back(grad_activated)[0].astype(bf16)
    grad_up_bias = jnp.sum(up_in.astype(f32), axis=0)
    grad_up_weight = jnp.einsum("rd,rf->df", hidden_low, up_in, preferred_element_type=f32)
    hidden_part = jnp.einsum("rf,df->rd", up_in, up_weight, preferred_element_type=f32)
    grad_hidden_one = (
        lax.psum(hidden_part.astype(jnp.bfloat16), "tensor").astype(jnp.float32) + grad_second_total
    )
    grad_first_total, grad_first_gain, grad_first_shift = norm_back(
        grad_hidden_one, normal_one, inverse_one, first_gain
    )
    out_in = grad_first_total.astype(bf16)
    grad_out_bias = jnp.sum(out_in.astype(f32), axis=0)
    grad_out_weight = jnp.einsum("rf,rd->fd", attention, out_in, preferred_element_type=f32)
    grad_attention = jnp.einsum(
        "rd,fd->rf", out_in, out_weight, preferred_element_type=f32
    ).reshape(batch, tok_local, local_width)
    padded_grad = with_halo(grad_attention.astype(jnp.bfloat16), (("seq", 1),), half_width).astype(
        grad_attention.dtype
    )
    grad_conv_values = jnp.zeros((batch, tok_local, local_width), f32)
    conv_columns = []
    for i in range(CONV):
        conv_columns.append(
            jnp.sum(
                grad_attention * padded_values[:, i : i + tok_local, :].astype(f32), axis=(0, 1)
            )
        )
        start_index = 2 * half_width - i
        grad_conv_values = (
            grad_conv_values
            + padded_grad[:, start_index : start_index + tok_local, :] * kernel_wide[:, i]
        )
    grad_conv_kernel = (
        jnp.stack(conv_columns, axis=0).reshape(CONV, local_heads, head_dim).sum(axis=-1).T
    )
    grad_nystrom = grad_attention.reshape(batch, tok_local, local_heads, head_dim)
    grad_kernel_one = jnp.einsum("bthd,bhjd->bhtj", grad_nystrom, carried, precision=highest)
    grad_carried_part = jnp.einsum("bhtj,bthd->bhjd", kernel_one, grad_nystrom, precision=highest)
    grad_first_scores = kernel_one * (
        grad_kernel_one - jnp.sum(kernel_one * grad_kernel_one, axis=-1, keepdims=True)
    )
    grad_query_one = (
        jnp.einsum("bhtj,bhjd->bthd", grad_first_scores, key_marks, precision=highest) * score_scale
    )
    grad_key_marks_part = (
        jnp.einsum("bhtj,bthd->bhjd", grad_first_scores, query_heads, precision=highest)
        * score_scale
    )
    grad_carried, grad_key_marks_one = lax.psum((grad_carried_part, grad_key_marks_part), "seq")
    grad_third_out = jnp.matmul(jnp.swapaxes(inverse, -1, -2), grad_carried, precision=highest)
    grad_inverse = jnp.matmul(grad_carried, jnp.swapaxes(third_out, -1, -2), precision=highest)
    grad_query_marks_two, grad_key_marks_two = core_back((jnp.zeros_like(kernel_two), grad_inverse))
    third_prob = local_weights * jnp.exp(local_top - top_score)[..., None] / total_weight[..., None]
    delta_term = jnp.sum(grad_third_out * third_out, axis=-1)
    grad_prob_value = jnp.einsum("bhjd,bthd->bhjt", grad_third_out, value_heads, precision=highest)
    grad_third_scores = third_prob * (grad_prob_value - delta_term[..., None])
    grad_value_three = jnp.einsum("bhjt,bhjd->bthd", third_prob, grad_third_out, precision=highest)
    grad_key_three = (
        jnp.einsum("bhjt,bhjd->bthd", grad_third_scores, query_marks, precision=highest)
        * score_scale
    )
    grad_query_marks_part = (
        jnp.einsum("bhjt,bthd->bhjd", grad_third_scores, key_heads, precision=highest) * score_scale
    )
    grad_query_marks_three = lax.psum(grad_query_marks_part, "seq")
    grad_query_marks = (grad_query_marks_two + grad_query_marks_three) / counts[:, None, :, None]
    grad_key_marks = (grad_key_marks_one + grad_key_marks_two) / counts[:, None, :, None]
    grad_query_marks = grad_query_marks.transpose(0, 2, 1, 3).reshape(batch, LAND, local_width)
    grad_key_marks = grad_key_marks.transpose(0, 2, 1, 3).reshape(batch, LAND, local_width)
    grad_query_seg = jnp.einsum("btj,bjf->btf", onehot, grad_query_marks, precision=highest)
    grad_key_seg = jnp.einsum("btj,bjf->btf", onehot, grad_key_marks, precision=highest)
    query_in = (
        (grad_query_one.reshape(batch, tok_local, local_width) + grad_query_seg)
        .astype(bf16)
        .reshape(rows, local_width)
    )
    key_in = (
        (grad_key_three.reshape(batch, tok_local, local_width) + grad_key_seg)
        .astype(bf16)
        .reshape(rows, local_width)
    )
    value_in = (grad_value_three.reshape(batch, tok_local, local_width) + grad_conv_values).astype(
        bf16
    )
    value_in = jnp.where(inside[:, :, None], value_in, jnp.zeros_like(value_in)).reshape(
        rows, local_width
    )
    grad_query_bias = jnp.sum(query_in.astype(f32), axis=0)
    grad_value_bias = jnp.sum(value_in.astype(f32), axis=0)
    grad_query_weight = jnp.einsum("rd,rf->df", flat, query_in, preferred_element_type=f32)
    grad_key_weight = jnp.einsum("rd,rf->df", flat, key_in, preferred_element_type=f32)
    grad_value_weight = jnp.einsum("rd,rf->df", flat, value_in, preferred_element_type=f32)
    input_part = (
        jnp.einsum("rf,df->rd", query_in, query_weight, preferred_element_type=f32)
        + jnp.einsum("rf,df->rd", key_in, key_weight, preferred_element_type=f32)
        + jnp.einsum("rf,df->rd", value_in, value_weight, preferred_element_type=f32)
    )
    input_sum, proxy_norm = (
        lax.psum(input_part.astype(jnp.bfloat16), "tensor").astype(jnp.float32),
        lax.psum(proxy_part.astype(jnp.bfloat16), "tensor").astype(jnp.float32),
    )
    grad_tokens = (grad_first_total + input_sum).reshape(batch, tok_local, width)
    (
        grad_query_weight,
        grad_key_weight,
        grad_value_weight,
        grad_out_weight,
        grad_up_weight,
        grad_down_weight,
    ) = (
        lax.psum_scatter(grad_query_weight, "seq", scatter_dimension=0, tiled=True),
        lax.psum_scatter(grad_key_weight, "seq", scatter_dimension=0, tiled=True),
        lax.psum_scatter(grad_value_weight, "seq", scatter_dimension=0, tiled=True),
        lax.psum_scatter(grad_out_weight, "seq", scatter_dimension=1, tiled=True),
        lax.psum_scatter(grad_up_weight, "seq", scatter_dimension=0, tiled=True),
        lax.psum_scatter(grad_down_weight, "seq", scatter_dimension=1, tiled=True),
    )
    (
        grad_query_bias,
        grad_value_bias,
        grad_conv_kernel,
        grad_out_bias,
        grad_first_gain,
        grad_first_shift,
        grad_up_bias,
        grad_down_bias,
        grad_second_gain,
        grad_second_shift,
    ) = lax.psum(
        (
            grad_query_bias,
            grad_value_bias,
            grad_conv_kernel,
            grad_out_bias,
            grad_first_gain,
            grad_first_shift,
            grad_up_bias,
            grad_down_bias,
            grad_second_gain,
            grad_second_shift,
        ),
        "seq",
    )
    return (
        output,
        grad_tokens,
        grad_query_weight,
        grad_query_bias,
        grad_key_weight,
        grad_value_weight,
        grad_value_bias,
        grad_conv_kernel,
        grad_out_weight,
        grad_out_bias,
        grad_first_gain,
        grad_first_shift,
        grad_up_weight,
        grad_up_bias,
        grad_down_weight,
        grad_down_bias,
        grad_second_gain,
        grad_second_shift,
        proxy_norm,
    )


MESH = pl.DeviceIdType.MESH
LANES = 2 * HEAD_DIM
f32 = jnp.float32
bf16 = jnp.bfloat16
NN = (1, 0)
NT = (1, 1)
TN = (0, 0)


def dot(a, b, dims=NN):
    return lax.dot_general(
        a, b, (((dims[0],), (dims[1],)), ((), ())), preferred_element_type=f32
    )


def split(x):
    if x.dtype == bf16:
        return (x,)
    top = x.astype(bf16)
    return (top, (x - top.astype(f32)).astype(bf16))


def fine(a, b, dims=NN):
    a, b = split(a), split(b)
    total = dot(a[0], b[0], dims)
    if len(b) > 1:
        total = total + dot(a[0], b[1], dims)
    if len(a) > 1:
        total = total + dot(a[1], b[0], dims)
    return total


def iota(shape, dim):
    return lax.broadcasted_iota(jnp.int32, shape, dim)


def block_mask():
    shape = (LANES, LANES)
    return (iota(shape, 0) < HEAD_DIM) == (iota(shape, 1) < HEAD_DIM)


def eye():
    return jnp.where(iota((LANES, LANES), 0) == iota((LANES, LANES), 1), 1.0, 0.0).astype(f32)


def block_sums(x, same_head):
    ones = jnp.where(same_head, 1.0, 0.0).astype(bf16)
    return jnp.where(same_head, fine(fine(ones, x), ones), 1.0)


def taps_matrix(row, tok):
    return pltpu.roll(jnp.broadcast_to(row, (tok, 2 * tok)), 0, 1, stride=1, stride_axis=0)


def taps_row(taps, head, tok):
    row = taps[pl.ds(head, 1), :]
    return jnp.concatenate([row, jnp.zeros((1, 2 * tok - CONV), f32)], axis=1)


def conv_block(matrices, window):
    first = fine(matrices[0], window)
    second = fine(matrices[1], window)
    return jnp.where(iota(first.shape, 1) < HEAD_DIM, first, second)


def greet(devices):
    barrier = pltpu.get_barrier_semaphore()
    for device in devices:
        pl.semaphore_signal(barrier, inc=1, device_id=device, device_id_type=MESH)
    return barrier


def around(n, me, tensor):
    return [(lax.rem(me + d, n), tensor) for d in range(1, n)]


def others(me, tensor):
    core = tensor + 1 - 2 * (tensor % 2)
    return [(me, core), (me, lax.rem(tensor + 2, 4)), (me, lax.rem(core + 2, 4))]


def paired(y):
    return y[:, :LANES], jnp.concatenate(
        [y[:, LANES : LANES + HEAD_DIM], y[:, HEAD_DIM:LANES]], axis=1
    )


def remote(src, dst, send, recv, device):
    return pltpu.make_async_remote_copy(
        src_ref=src, dst_ref=dst, send_sem=send, recv_sem=recv, device_id=device,
        device_id_type=MESH,
    )


def member_rows(length, total):
    j = iota((LANES, total), 0) % LAND
    t = iota((LANES, total), 1)
    inside = (t * LAND >= j * length) & (t * LAND < (j + 1) * length) & (t < length)
    return jnp.where(inside, 1.0, 0.0).astype(bf16)


def member_columns(length, total):
    j = iota((total, LANES), 1) % LAND
    t = iota((total, LANES), 0)
    inside = (t * LAND >= j * length) & (t * LAND < (j + 1) * length) & (t < length)
    return jnp.where(inside, 1.0, 0.0).astype(bf16)


def segment_counts(length):
    j = iota((LANES, LANES), 0) % LAND
    upper = ((j + 1) * length + LAND - 1) // LAND
    lower = (j * length + LAND - 1) // LAND
    return (upper - lower).astype(f32)


def forward_kernel(
    n, lengths, x, wq, qb, wk, wv, vb, taps, out_weight,
    attn, qs, ks, vs, k1, p3, newton, mats, proxy, out_whole,
    stage, out_stage, send, recv, out_send, out_recv, whole_send, whole_recv,
):
    me = lax.axis_index("seq")
    tensor = lax.axis_index("tensor")
    rows = x.shape[0]
    batch = n // 2
    tok = rows // batch
    total = n * tok
    half = CONV // 2
    own, side = me // 2, me % 2
    scale = HEAD_DIM ** (-0.5)
    barrier = greet(around(n, me, tensor) + others(me, tensor))

    copies = []
    owned = (ks, qs, vs)
    width = out_weight.shape[0]
    for t in range(4):
        out_whole[t, width:] = jnp.zeros((2 * LANES - width, x.shape[1]), bf16)
    out_whole[tensor, :width] = out_weight[...]
    offsets = (0, 0, half)
    vs[0:half] = jnp.zeros((half, LANES), bf16)
    vs[half + total : total + tok] = jnp.zeros((tok - half, LANES), bf16)
    for i in range(3):
        y = dot(x[...], (wk, wq, wv)[i][...], NT)
        if i == 1:
            y = y + qb[...]
        if i == 2:
            y = y + vb[...]
            pieces = []
            position = me * tok + iota((tok, y.shape[1]), 0)
            for b in range(batch):
                part = y[b * tok : (b + 1) * tok]
                pieces.append(jnp.where(position < lengths[b], part, 0.0))
            y = jnp.concatenate(pieces, axis=0)
        low = y.astype(bf16)
        stage[i, 0], stage[i, 1] = paired(low)
        if i == 0:
            pl.semaphore_wait(barrier, n + 2)
        here = pl.ds(pl.multiple_of(offsets[i] + me * tok, 16), tok)
        for d in range(1, n):
            peer = lax.rem(me + d, n)
            copy = remote(
                stage.at[i, peer % 2, pl.ds(pl.multiple_of((peer // 2) * tok, tok), tok)],
                owned[i].at[here],
                send.at[i, d - 1],
                recv.at[i, d - 1],
                (peer, tensor),
            )
            copy.start()
            copies.append(copy)
        owned[i][here] = stage[i, side, pl.ds(pl.multiple_of(own * tok, tok), tok)]

    shares = []
    for i, device in enumerate(others(me, tensor)):
        copy = remote(
            out_weight, out_whole.at[tensor, pl.ds(0, width)], whole_send.at[i], whole_recv.at[i],
            device,
        )
        copy.start()
        shares.append(copy)

    length = lengths[own]
    same_head = block_mask()
    identity = eye()
    ones = jnp.where(same_head, 1.0, 0.0).astype(bf16)
    members = member_rows(length, total)
    counts = segment_counts(length)
    for copy in copies[: n - 1]:
        copy.wait_recv()
    keys = ks[...]
    key_marks = jnp.where(same_head, dot(members, keys) / counts, 0.0)
    for copy in copies[n - 1 : 2 * (n - 1)]:
        copy.wait_recv()
    queries = qs[...]
    query_marks = jnp.where(same_head, dot(members, queries) / counts, 0.0)

    scores = jnp.where(same_head, fine(query_marks, key_marks, NT) * scale, negative)
    weights = jnp.exp(scores - jnp.max(scores, axis=1, keepdims=True))
    kernel_two = weights / jnp.sum(weights, axis=1, keepdims=True)
    inverse = jnp.where(
        same_head, kernel_two.T / block_sums(kernel_two * kernel_two, same_head), 0.0
    )
    for step in range(NS_ITERS):
        product = fine(kernel_two, inverse)
        inner_one = fine(product, 7.0 * identity - product)
        inner_two = fine(product, 15.0 * identity - inner_one)
        newton[4 * step] = inverse
        newton[4 * step + 1] = product
        newton[4 * step + 2] = inner_one
        newton[4 * step + 3] = inner_two
        inverse = 0.25 * fine(inverse, 13.0 * identity - inner_two)

    deviation = identity - fine(kernel_two, inverse)
    norms = jnp.sqrt(block_sums(deviation * deviation, same_head))
    first, second = norms[0:1, 0:1], norms[LANES - 1 :, LANES - 1 :]
    norm_sum = jnp.where(side == 0, first + second, first) / (batch * HEADS)
    proxy[...] = jnp.broadcast_to(norm_sum, proxy.shape)

    first_scores = fine(queries, key_marks, NT) * scale
    left = iota(first_scores.shape, 1) < HEAD_DIM
    top_left = jnp.max(jnp.where(left, first_scores, negative), axis=1, keepdims=True)
    top_right = jnp.max(jnp.where(left, negative, first_scores), axis=1, keepdims=True)
    weights = jnp.exp(first_scores - jnp.where(left, top_left, top_right))
    kernel_one = weights / fine(weights, ones)
    k1[...] = kernel_one

    third_scores = fine(keys, query_marks, NT) * scale
    alive = iota(third_scores.shape, 0) < length
    third_scores = jnp.where(alive, third_scores, negative)
    weights = jnp.exp(third_scores - jnp.max(third_scores, axis=0, keepdims=True))
    weights = jnp.where(alive, weights, 0.0)
    third_prob = weights / jnp.sum(weights, axis=0, keepdims=True)
    p3[...] = third_prob

    for copy in copies[2 * (n - 1) :]:
        copy.wait_recv()
    values = vs[half : half + total]
    third_out = jnp.where(same_head, fine(third_prob, values, TN), 0.0)
    carried = fine(inverse, third_out)
    mats[0] = query_marks
    mats[1] = key_marks
    mats[2] = kernel_two
    mats[3] = inverse
    mats[4] = third_out
    mats[5] = carried

    matrices = [taps_matrix(taps_row(taps, h, tok), tok) for h in (2 * side, 1)]
    there = pl.ds(pl.multiple_of(own * tok, tok), tok)
    for d in range(1, n + 1):
        peer = lax.rem(me + d, n)
        start = pl.multiple_of(peer * tok, tok)
        nystrom = fine(k1[pl.ds(start, tok)], carried)
        convolved = conv_block(matrices, vs[pl.ds(start, 2 * tok)])
        low = (nystrom + convolved).astype(bf16)
        if d == n:
            attn[side, there] = low
        else:
            out_stage[d - 1] = low
            copy = remote(
                out_stage.at[d - 1],
                attn.at[side, there],
                out_send.at[d - 1],
                out_recv.at[d - 1],
                (peer, tensor),
            )
            copy.start()
            copies.append(copy)
    for copy in copies[: 3 * (n - 1)]:
        copy.wait_send()
    for copy in copies[3 * (n - 1) :] + shares:
        copy.wait()


def normal_of(summed):
    middle = jnp.mean(summed, axis=-1, keepdims=True)
    centred = summed - middle
    inverse_std = lax.rsqrt(jnp.mean(centred * centred, axis=-1, keepdims=True) + epsilon)
    return centred * inverse_std, inverse_std


def before_norm(grad, normal, inverse_std, gain):
    grad_normal = grad * gain
    return inverse_std * (
        grad_normal
        - jnp.mean(grad_normal, axis=-1, keepdims=True)
        - normal * jnp.mean(grad_normal * normal, axis=-1, keepdims=True)
    )


def block_rows(t, tok):
    return pl.ds(pl.multiple_of(t * tok, tok), tok)


def gather_and_sum(phase, me, tensor, held, work, ring, filler):
    tok = held.shape[0] // 4
    ag_send, ag_recv, sum_send, sum_recv, core_out, core_in, y_out, y_in = ring
    core, across, far = others(me, tensor)
    mine = held.at[block_rows(tensor, tok)]
    to_y = remote(mine, mine, ag_send.at[phase, 0], ag_recv.at[phase, 0], across)
    to_y.start()
    to_core = remote(mine, mine, ag_send.at[phase, 1], ag_recv.at[phase, 1], core)
    to_core.start()
    total = work(tensor)
    to_core.wait_recv()
    core_out[phase, 0] = work(core[1]).astype(bf16)
    near = remote(
        core_out.at[phase, 0], core_in.at[phase, 0], sum_send.at[phase, 0], sum_recv.at[phase, 0],
        core,
    )
    near.start()
    to_y.wait_recv()
    other = held.at[block_rows(across[1], tok)]
    pass_on = remote(other, other, ag_send.at[phase, 2], ag_recv.at[phase, 2], core)
    pass_on.start()
    part = work(across[1])
    pass_on.wait_recv()
    core_out[phase, 1] = work(far[1]).astype(bf16)
    middle = remote(
        core_out.at[phase, 1], core_in.at[phase, 1], sum_send.at[phase, 1], sum_recv.at[phase, 1],
        core,
    )
    middle.start()
    middle.wait_recv()
    y_out[phase] = (part + core_in[phase, 1].astype(f32)).astype(bf16)
    last = remote(
        y_out.at[phase], y_in.at[phase], sum_send.at[phase, 2], sum_recv.at[phase, 2], across
    )
    last.start()
    filler()
    near.wait_recv()
    last.wait_recv()
    total = total + core_in[phase, 0].astype(f32) + y_in[phase].astype(f32)
    return total, [to_y, to_core, pass_on, near, middle, last]


def middle_kernel(
    attn, x, out_whole, out_bias, gain_one, shift_one, up_weight, up_bias, down_weight, down_bias,
    gain_two, shift_two, out_grad,
    grad_attn, grad_first, out_in, out_rows, grad_up, grad_down, sums,
    heads_in, heads_out, hidden, slope, active, down_in, up_in,
    core_out, core_in, y_out, y_in,
    a2a_send, a2a_recv, ag_send, ag_recv, sum_send, sum_recv,
):
    me = lax.axis_index("seq")
    tensor = lax.axis_index("tensor")
    rows = x.shape[0]
    tok = rows // 4
    peers = others(me, tensor)
    ring = (ag_send, ag_recv, sum_send, sum_recv, core_out, core_in, y_out, y_in)
    barrier = greet(peers)
    pl.semaphore_wait(barrier, 3)
    mine = block_rows(tensor, tok)
    pending = []
    for i in (2, 1, 0):
        copy = remote(
            attn.at[:, block_rows(peers[i][1], tok)], heads_in.at[tensor], a2a_send.at[0, i],
            a2a_recv.at[0, i], peers[i],
        )
        copy.start()
        pending.append(copy)
    heads_in[tensor] = attn[:, mine]
    for copy in pending:
        copy.wait_recv()
    branch = jnp.zeros((tok, x.shape[1]), f32)
    for t in range(4):
        branch = branch + dot(heads_in[t, 0], out_whole[t, :LANES])
        branch = branch + dot(heads_in[t, 1], out_whole[t, LANES:])
    first_total = x[mine].astype(f32) + (branch + out_bias[...])
    normal_one, inverse_one = normal_of(first_total)
    hidden_one = normal_one * gain_one[...] + shift_one[...]
    hidden[mine] = hidden_one.astype(bf16)

    def up(t):
        at = block_rows(t, tok)
        value = dot(hidden[at], up_weight[...]) + up_bias[...]
        half = 0.5 * (1.0 + lax.erf(value * (0.5**0.5)))
        density = jnp.exp(-0.5 * value * value) * (0.5 / jnp.pi) ** 0.5
        slope[at] = half + value * density
        low = (value * half).astype(bf16)
        active[at] = low
        return dot(low, down_weight[...])

    down_sum, copies = gather_and_sum(0, me, tensor, hidden, up, ring, lambda: None)
    pending += copies
    second_total = hidden_one + (down_sum + down_bias[...])
    normal_two, inverse_two = normal_of(second_total)
    out_rows[...] = (normal_two * gain_two[...] + shift_two[...]).astype(bf16)
    grad_out = out_grad[mine].astype(f32)
    grad_second = before_norm(grad_out, normal_two, inverse_two, gain_two[...])
    low = grad_second.astype(bf16)
    down_in[mine] = low

    def total_of(v):
        return jnp.sum(v, axis=0, keepdims=True)

    def down(t):
        at = block_rows(t, tok)
        low = (dot(down_in[at], down_weight[...], NT) * slope[at]).astype(bf16)
        up_in[at] = low
        return dot(low, up_weight[...], NT)

    def fill():
        sums[0:1] = total_of(grad_out * normal_two)
        sums[1:2] = total_of(grad_out)
        sums[2:3] = total_of(low.astype(f32))
        grad_down[...] = dot(down_in[...], active[...], TN).astype(bf16)

    up_sum, copies = gather_and_sum(1, me, tensor, down_in, down, ring, fill)
    pending += copies
    grad_hidden = grad_second + up_sum
    grad_total = before_norm(grad_hidden, normal_one, inverse_one, gain_one[...])
    grad_first[...] = grad_total
    low_out = grad_total.astype(bf16)
    out_in[...] = low_out
    sent = []
    for i in (2, 1, 0):
        t = peers[i][1]
        heads_out[i, 0] = dot(low_out, out_whole[t, :LANES], NT).astype(bf16)
        heads_out[i, 1] = turn(dot(low_out, out_whole[t, LANES:], NT), heads_out[i, 0])
        copy = remote(
            heads_out.at[i], grad_attn.at[:, mine], a2a_send.at[1, i], a2a_recv.at[1, i], peers[i]
        )
        copy.start()
        sent.append(copy)
    own_first = dot(low_out, out_whole[tensor, :LANES], NT).astype(bf16)
    grad_attn[0, mine] = own_first
    grad_attn[1, mine] = turn(dot(low_out, out_whole[tensor, LANES:], NT), own_first)
    sums[3:4] = total_of(grad_hidden * normal_one)
    sums[4:5] = total_of(grad_hidden)
    sums[5:6] = total_of(low_out.astype(f32))
    sums[6:7] = dot(jnp.ones((8, rows), bf16), up_in[...])[0:1]
    sums[7:8] = jnp.zeros_like(sums[7:8])
    grad_up[...] = dot(hidden[...], up_in[...], TN).astype(bf16)
    for copy in pending:
        copy.wait_send()
    for copy in sent:
        copy.wait()


def turn(second, first):
    low = second.astype(bf16)
    return jnp.where(iota(low.shape, 1) < HEAD_DIM, low, first)


class Scatter:
    def __init__(self, index, me, tensor, source, buffers, send, recv):
        self.index, self.source = index, source
        self.x_in, self.held, self.z_in, self.pair, self.last_in = buffers
        self.block = source.shape[0] // 8
        self.x, self.z = me % 2, me // 2
        z = self.z
        self.partners = (
            (me + 1 - 2 * self.x, tensor),
            (2 * (z + 1 - 2 * (z % 2)) + self.x, tensor),
            (2 * lax.rem(z + 2, 4) + self.x, tensor),
        )
        self.send, self.recv = send, recv
        self.copies = []

    def rows(self, z, x):
        return pl.ds(pl.multiple_of((2 * z + x) * self.block, 16), self.block)

    def copy(self, src, dst, k, partner):
        copy = remote(
            src, dst, self.send.at[self.index, k], self.recv.at[self.index, k],
            self.partners[partner],
        )
        copy.start()
        self.copies.append(copy)

    def first(self):
        for z in range(4):
            self.copy(self.source.at[self.rows(z, 1 - self.x)], self.x_in.at[z], z, 0)

    def second(self):
        odd = self.z % 2
        for z in range(4):
            self.copies[z].wait_recv()
        for z in range(4):
            both = self.source[self.rows(z, self.x)].astype(f32) + self.x_in[z].astype(f32)
            self.held[z] = both.astype(bf16)
        for k in range(2):
            self.copy(self.held.at[2 * k + 1 - odd], self.z_in.at[k], 4 + k, 1)

    def third(self):
        odd = self.z % 2
        for k in range(2):
            self.copies[4 + k].wait_recv()
        for k in range(2):
            both = self.held[2 * k + odd].astype(f32) + self.z_in[k].astype(f32)
            self.pair[k] = both.astype(bf16)
        self.copy(self.pair.at[1 - self.z // 2], self.last_in, 6, 2)

    def last(self):
        self.copies[6].wait_recv()
        return self.pair[self.z // 2].astype(f32) + self.last_in[...].astype(f32)

    def finish(self):
        for copy in self.copies:
            copy.wait_send()


def scatter_buffers(width, block):
    return [
        pltpu.VMEM((4, block, width), bf16),
        pltpu.VMEM((4, block, width), bf16),
        pltpu.VMEM((2, block, width), bf16),
        pltpu.VMEM((2, block, width), bf16),
        pltpu.VMEM((block, width), bf16),
    ]


def backward_kernel(
    n, lengths, grad_attn, taps, qs, ks, vs, k1, p3, newton, mats, proxy, attn, x, wq, wk, wv,
    grad_first, out_in, out_rows, grad_up, grad_down, sums,
    grad_tokens, output, grad_query, grad_key, grad_value, grad_out, up_result, down_result,
    early_result, late_result,
    gs, out_stage, rin, out_whole, early, early_tensor, early_seq, late_seq, source_out,
    source_heads, tokens_low, tokens_whole, core_out, core_in, y_out, y_in, *rest,
):
    buffers, sems = rest[:20], rest[20:]
    (send, recv, out_send, out_recv, share_send, share_recv, sum_send, sum_recv, small_send,
     small_recv, job_send, job_recv) = sems
    me = lax.axis_index("seq")
    tensor = lax.axis_index("tensor")
    rows, width = x.shape
    batch = n // 2
    tok = rows // batch
    total = n * tok
    half = CONV // 2
    own, side = me // 2, me % 2
    scale = HEAD_DIM ** (-0.5)
    ring_peers = around(n, me, tensor)
    peers = others(me, tensor)
    core, across, far = peers
    mine = block_rows(tensor, tok)
    barrier = greet(ring_peers + peers)
    jobs = [
        Scatter(i, me, tensor, source, buffers[5 * i : 5 * i + 5], job_send, job_recv)
        for i, source in enumerate((grad_down, grad_up, source_out, source_heads))
    ]

    gs[0:half] = jnp.zeros((half, LANES), bf16)
    gs[half + total : total + tok] = jnp.zeros((tok - half, LANES), bf16)
    output[mine] = out_rows[...]
    out_whole[mine] = out_in[...]
    early[0:7] = sums[0:7]
    early[7:8] = jnp.broadcast_to(proxy[0:1, 0:1], (1, width))
    early_tensor[tensor] = early[...]
    pl.semaphore_wait(barrier, n + 2)

    here = pl.ds(pl.multiple_of(half + me * tok, 16), tok)
    copies = []
    for d in range(1, n):
        peer = lax.rem(me + d, n)
        copy = remote(
            grad_attn.at[peer % 2, block_rows(peer // 2, tok)], gs.at[here], send.at[d - 1],
            recv.at[d - 1], (peer, tensor),
        )
        copy.start()
        copies.append(copy)
    gs[here] = grad_attn[side, block_rows(own, tok)]
    shares = []
    for i, held in enumerate((out_whole, output)):
        for j, device in enumerate((across, core)):
            copy = remote(
                held.at[mine], held.at[mine], share_send.at[i, j], share_recv.at[i, j], device
            )
            copy.start()
            shares.append(copy)
    for i, device in enumerate(peers):
        copy = remote(
            early, early_tensor.at[tensor], small_send.at[0, i], small_recv.at[0, i], device
        )
        copy.start()
        shares.append(copy)
    jobs[0].first()
    jobs[1].first()

    length = lengths[own]
    same_head = block_mask()
    identity = eye()
    ones = jnp.where(same_head, 1.0, 0.0).astype(bf16)
    members = member_columns(length, total)
    counts = segment_counts(length)
    query_marks, key_marks, kernel_two, inverse, third_out, carried = [mats[i] for i in range(6)]
    flip = jnp.where(
        iota((2 * tok, 2 * tok), 0) + iota((2 * tok, 2 * tok), 1) == CONV - 1, 1.0, 0.0
    ).astype(bf16)
    reverse = [
        taps_matrix(
            fine(jnp.broadcast_to(taps_row(taps, h, tok), (8, 2 * tok)), flip)[0:1], tok
        )
        for h in (2 * side, 1)
    ]
    queries, keys, values = qs[...], ks[...], vs[half : half + total]
    there = block_rows(own, tok)
    outs = []

    def give(i, block):
        low = block.astype(bf16)
        for m in range(n):
            out_stage[i, m] = low[m * tok : (m + 1) * tok]
        for d in range(1, n):
            peer = lax.rem(me + d, n)
            copy = remote(
                out_stage.at[i, peer], rin.at[i, side, there], out_send.at[i, d - 1],
                out_recv.at[i, d - 1], (peer, tensor),
            )
            copy.start()
            outs.append(copy)
        rin[i, side, there] = out_stage[i, me]

    for copy in copies:
        copy.wait_recv()
    grad = gs[half : half + total]
    kernel_one = k1[...]
    grad_carried = jnp.where(same_head, fine(kernel_one, grad, TN), 0.0)
    grad_third = fine(inverse, grad_carried, TN)
    grad_inverse = fine(grad_carried, third_out, NT)
    third_prob = p3[...]
    convolved = jnp.concatenate(
        [conv_block(reverse, gs[m * tok : (m + 2) * tok]) for m in range(n)], axis=0
    )
    grad_values = fine(third_prob, grad_third) + convolved
    give(2, jnp.where(iota(grad_values.shape, 0) < length, grad_values, 0.0))

    for i, held in enumerate((out_whole, output)):
        shares[2 * i].wait_recv()
        block = held.at[block_rows(across[1], tok)]
        copy = remote(block, block, share_send.at[i, 2], share_recv.at[i, 2], core)
        copy.start()
        shares.append(copy)

    kernel_back = jnp.zeros((LANES, LANES), f32)
    grad_state = grad_inverse
    for step in reversed(range(NS_ITERS)):
        state, product, inner_one, inner_two = [newton[4 * step + i] for i in range(4)]
        grad_next = 0.25 * fine(grad_state, 13.0 * identity - inner_two, NT)
        grad_two = -0.25 * fine(state, grad_state, TN)
        grad_product = fine(grad_two, 15.0 * identity - inner_one, NT)
        grad_one = -fine(product, grad_two, TN)
        grad_product = (
            grad_product
            + fine(grad_one, 7.0 * identity - product, NT)
            - fine(product, grad_one, TN)
        )
        grad_state = grad_next + fine(kernel_two, grad_product, TN)
        kernel_back = kernel_back + fine(grad_product, state, NT)
    squares = block_sums(kernel_two * kernel_two, same_head)
    spread = jnp.where(same_head, block_sums(grad_state * newton[0], same_head), 0.0)
    kernel_back = kernel_back + (grad_state.T - 2.0 * kernel_two * spread) / squares
    grad_scores = scale * kernel_two * (
        kernel_back - jnp.sum(kernel_two * kernel_back, axis=1, keepdims=True)
    )
    query_two = fine(grad_scores, key_marks)
    key_two = fine(grad_scores, query_marks, TN)

    grad_one = fine(grad, carried, NT)
    both = kernel_one * grad_one
    first_scores = scale * (both - kernel_one * fine(both, ones))
    key_one = jnp.where(same_head, fine(first_scores, queries, TN), 0.0)
    delta = fine(jnp.ones((8, LANES), bf16), grad_third * third_out, NT)[0:1]
    third_scores = scale * third_prob * (fine(values, grad_third, NT) - delta)
    query_three = jnp.where(same_head, fine(third_scores, keys, TN), 0.0)
    give(
        0, fine(third_scores, query_marks) + fine(members, (key_one + key_two) / counts)
    )
    give(
        1, fine(first_scores, key_marks) + fine(members, (query_two + query_three) / counts)
    )

    jobs[0].second()
    jobs[1].second()
    for copy in shares[4:7]:
        copy.wait_recv()
    by_tensor = early_tensor[0] + early_tensor[1] + early_tensor[2] + early_tensor[3]
    early_seq[me] = jnp.where(iota(by_tensor.shape, 0) == 6, early[...], by_tensor)
    for d, device in enumerate(ring_peers):
        copy = remote(
            early_seq.at[me], early_seq.at[me], small_send.at[1, d], small_recv.at[1, d], device
        )
        copy.start()
        shares.append(copy)

    shares[1].wait_recv()
    shares[7].wait_recv()
    attention = jnp.concatenate([attn[0], attn[1, :, :HEAD_DIM]], axis=1)
    source_out[...] = dot(out_whole[...], attention, TN).astype(bf16)
    jobs[2].first()

    position = iota((tok, tok), 0) + iota((tok, tok), 1)
    upside = jnp.where(position == tok - 1, 1.0, 0.0).astype(bf16)
    lane = iota((tok, LANES), 1)
    conv_rows = []
    for h in range(2):
        inner = (lane < HEAD_DIM) if h == 0 else (lane >= HEAD_DIM)
        table = jnp.zeros((tok, 2 * tok), f32)
        for m in range(n):
            block = gs[half + m * tok : half + (m + 1) * tok]
            block = jnp.where(inner, block, jnp.zeros_like(block))
            table = table + dot(block, vs[m * tok : (m + 2) * tok], NT)
        table = pltpu.roll(fine(upside, table), 0, 1, stride=1, stride_axis=0)
        row = jnp.sum(table, axis=0, keepdims=True)
        row = pltpu.roll(jnp.broadcast_to(row, (8, 2 * tok)), tok + 1, 1)
        conv_rows.append(row[0:1, :LANES])
    whole_weight = jnp.concatenate(
        [w[:LANES] for w in (wk, wq, wv)] + [w[LANES:] for w in (wk, wq, wv)], axis=0
    )
    jobs[0].third()
    jobs[1].third()

    for copy in outs:
        copy.wait_recv()
    low = jnp.concatenate(
        [rin[i, 0] for i in range(3)] + [rin[i, 1, :, :HEAD_DIM] for i in range(3)], axis=1
    )
    source_heads[...] = dot(x[...], low, TN).astype(bf16)
    jobs[3].first()

    tokens_low[...] = low

    def input_part(t):
        return dot(tokens_low[block_rows(t, tok)], whole_weight)

    def pass_sum(k, value, device):
        core_out[k] = value.astype(bf16)
        copy = remote(core_out.at[k], core_in.at[k], sum_send.at[k], sum_recv.at[k], device)
        copy.start()
        shares.append(copy)
        return copy

    middle = pass_sum(1, input_part(far[1]), core)
    near = pass_sum(0, input_part(core[1]), core)
    part = input_part(across[1])
    middle.wait_recv()
    y_out[...] = (part + core_in[1].astype(f32)).astype(bf16)
    final = remote(y_out, y_in, sum_send.at[2], sum_recv.at[2], across)
    final.start()
    shares.append(final)
    result = input_part(tensor) + grad_first[...]

    head_sums = dot(jnp.ones((8, rows), bf16), low)[0:1]
    late = late_seq.at[me]
    late[...] = jnp.zeros(late.shape, f32)
    inner = HEAD_DIM
    late[0:1, 0:LANES] = head_sums[:, LANES : 2 * LANES]
    late[0:1, LANES : LANES + inner] = head_sums[:, 3 * LANES + inner : 4 * LANES]
    late[1:2, 0:LANES] = head_sums[:, 2 * LANES : 3 * LANES]
    late[1:2, LANES : LANES + inner] = head_sums[:, 4 * LANES : 4 * LANES + inner]
    even = side == 0
    late[2:3, 0:LANES] = jnp.where(even, conv_rows[0], 0.0)
    late[3:4, 0:LANES] = jnp.where(even, conv_rows[1], 0.0)
    late[4:5, 0:LANES] = jnp.where(even, 0.0, conv_rows[0])
    for d, device in enumerate(ring_peers):
        copy = remote(late, late, small_send.at[2, d], small_recv.at[2, d], device)
        copy.start()
        shares.append(copy)

    jobs[2].second()
    down_result[...] = jobs[0].last().T
    up_result[...] = jobs[1].last()

    near.wait_recv()
    final.wait_recv()
    result = result + core_in[0].astype(f32) + y_in[...].astype(f32)
    tokens_whole[mine] = result.astype(bf16)
    ends = []
    for j, device in enumerate((across, core)):
        copy = remote(
            tokens_whole.at[mine], tokens_whole.at[mine], share_send.at[2, j], share_recv.at[2, j],
            device,
        )
        copy.start()
        ends.append(copy)
    jobs[3].second()
    jobs[2].third()
    ends[0].wait_recv()
    block = tokens_whole.at[block_rows(across[1], tok)]
    copy = remote(block, block, share_send.at[2, 2], share_recv.at[2, 2], core)
    copy.start()
    jobs[3].third()
    grad_out[...] = jobs[2].last().T
    for k, device in enumerate(ring_peers):
        shares[9 + k].wait_recv()
    early_result[...] = functools.reduce(lambda a, b: a + b, [early_seq[i] for i in range(n)])
    for k, device in enumerate(ring_peers):
        shares[9 + n - 1 + 3 + k].wait_recv()
    late_result[...] = functools.reduce(lambda a, b: a + b, [late_seq[i] for i in range(n)])
    ends[1].wait_recv()
    copy.wait_recv()
    grad_tokens[...] = tokens_whole[...].astype(f32)
    heads = jobs[3].last()
    for i, ref in enumerate((grad_key, grad_query, grad_value)):
        ref[:, :LANES] = heads[:, i * LANES : (i + 1) * LANES]
        ref[:, LANES:] = heads[:, 3 * LANES + i * inner : 3 * LANES + (i + 1) * inner]
    shares[3].wait_recv()
    shares[8].wait_recv()
    for copy in copies + outs + shares + ends + [copy]:
        copy.wait_send()
    for job in jobs:
        job.finish()


def whole(shape, dtype):
    return jax.ShapeDtypeStruct(shape, dtype)


VMEM = pl.BlockSpec(memory_space=pltpu.VMEM)
SMEM = pl.BlockSpec(memory_space=pltpu.SMEM)


def limits(collective):
    return pltpu.CompilerParams(
        collective_id=collective, has_side_effects=True, vmem_limit_bytes=56 * 2**20
    )


def dma(*shape):
    return pltpu.SemaphoreType.DMA(shape)


def attention_forward(n, lengths, flat, wq, qb, wk, wv, vb, taps, out_weight):
    rows, width = flat.shape
    tok = rows // (n // 2)
    total = n * tok
    return pl.pallas_call(
        functools.partial(forward_kernel, n),
        out_shape=(
            whole((2, rows, LANES), bf16),
            whole((total, LANES), bf16),
            whole((total, LANES), bf16),
            whole((total + tok, LANES), bf16),
            whole((total, LANES), f32),
            whole((total, LANES), f32),
            whole((4 * NS_ITERS, LANES, LANES), f32),
            whole((6, LANES, LANES), f32),
            whole((1, LANES), f32),
            whole((4, 2 * LANES, width), bf16),
        ),
        in_specs=[SMEM] + [VMEM] * 8,
        out_specs=(VMEM,) * 10,
        scratch_shapes=[
            pltpu.VMEM((3, 2, rows, LANES), bf16),
            pltpu.VMEM((n - 1, tok, LANES), bf16),
            dma(3, n - 1), dma(3, n - 1), dma(n - 1), dma(n - 1), dma(3), dma(3),
        ],
        compiler_params=limits(0),
        name="attention_forward",
    )(lengths, flat, wq, qb, wk, wv, vb, taps, out_weight)


def middle(attn, flat, out_whole, *params):
    rows, width = flat.shape
    hidden = params[3].shape[1]
    tok = rows // 4
    return pl.pallas_call(
        middle_kernel,
        out_shape=(
            whole((2, rows, LANES), bf16),
            whole((tok, width), f32),
            whole((tok, width), bf16),
            whole((tok, width), bf16),
            whole((width, hidden), bf16),
            whole((width, hidden), bf16),
            whole((8, width), f32),
        ),
        in_specs=[VMEM] * 13,
        out_specs=(VMEM,) * 7,
        scratch_shapes=[
            pltpu.VMEM((4, 2, tok, LANES), bf16),
            pltpu.VMEM((3, 2, tok, LANES), bf16),
            pltpu.VMEM((rows, width), bf16),
            pltpu.VMEM((rows, hidden), f32),
            pltpu.VMEM((rows, hidden), bf16),
            pltpu.VMEM((rows, width), bf16),
            pltpu.VMEM((rows, hidden), bf16),
            pltpu.VMEM((2, 2, tok, width), bf16),
            pltpu.VMEM((2, 2, tok, width), bf16),
            pltpu.VMEM((2, tok, width), bf16),
            pltpu.VMEM((2, tok, width), bf16),
            dma(2, 3), dma(2, 3), dma(2, 3), dma(2, 3), dma(2, 3), dma(2, 3),
        ],
        compiler_params=limits(1),
        name="middle",
    )(attn, flat, out_whole, *params)


def attention_backward(n, *args):
    rows, width = args[12].shape
    tok = rows // 4
    total = n * tok
    block = width // n
    local = 3 * HEAD_DIM
    hidden = args[20].shape[1]
    return pl.pallas_call(
        functools.partial(backward_kernel, n),
        out_shape=(
            whole((rows, width), f32),
            whole((rows, width), bf16),
            whole((block, local), f32),
            whole((block, local), f32),
            whole((block, local), f32),
            whole((local, block), f32),
            whole((block, hidden), f32),
            whole((hidden, block), f32),
            whole((8, width), f32),
            whole((8, width), f32),
        ),
        in_specs=[SMEM] + [VMEM] * (len(args) - 1),
        out_specs=(VMEM,) * 10,
        scratch_shapes=[
            pltpu.VMEM((total + tok, LANES), bf16),
            pltpu.VMEM((3, n, tok, LANES), bf16),
            pltpu.VMEM((3, 2, rows, LANES), bf16),
            pltpu.VMEM((rows, width), bf16),
            pltpu.VMEM((8, width), f32),
            pltpu.VMEM((4, 8, width), f32),
            pltpu.VMEM((n, 8, width), f32),
            pltpu.VMEM((n, 8, width), f32),
            pltpu.VMEM((width, local), bf16),
            pltpu.VMEM((width, 3 * local), bf16),
            pltpu.VMEM((rows, 3 * local), bf16),
            pltpu.VMEM((rows, width), bf16),
            pltpu.VMEM((2, tok, width), bf16),
            pltpu.VMEM((2, tok, width), bf16),
            pltpu.VMEM((tok, width), bf16),
            pltpu.VMEM((tok, width), bf16),
        ]
        + [b for w in (hidden, hidden, local, 3 * local) for b in scatter_buffers(w, block)]
        + [
            dma(n - 1), dma(n - 1), dma(3, n - 1), dma(3, n - 1), dma(3, 3), dma(3, 3), dma(3),
            dma(3), dma(3, n - 1), dma(3, n - 1), dma(4, 7), dma(4, 7),
        ],
        compiler_params=limits(2),
        name="attention_backward",
    )(*args)


def gathered_plan(
    n, tokens, lengths, query_weight, query_bias, key_weight, value_weight, value_bias,
    conv_kernel, out_weight, out_bias, first_gain, first_shift, up_weight, up_bias, down_weight,
    down_bias, second_gain, second_shift, out_grad,
):
    batch, tok, width = tokens.shape
    rows = batch * tok
    flat = tokens.reshape(rows, width)
    wq, wk, wv = query_weight.T, key_weight.T, value_weight.T
    attn, *saved, out_whole = attention_forward(
        n, lengths, flat, wq, query_bias[None], wk, wv, value_bias[None], conv_kernel, out_weight
    )
    grad_attn, *results = middle(
        attn, flat, out_whole, out_bias[None], first_gain[None], first_shift[None], up_weight,
        up_bias[None], down_weight, down_bias[None], second_gain[None], second_shift[None],
        out_grad.reshape(rows, width),
    )
    (grad_tokens, output, grad_query, grad_key, grad_value, grad_out, grad_up, grad_down, early,
     late) = attention_backward(
        n, lengths, grad_attn, conv_kernel, *saved, attn, flat, wq, wk, wv, *results
    )
    local = wq.shape[0]
    return (
        output.reshape(tokens.shape),
        grad_tokens.reshape(tokens.shape),
        grad_query,
        late[0, :local],
        grad_key,
        grad_value,
        late[1, :local],
        late[2:5, :CONV],
        grad_out,
        early[5],
        early[3],
        early[4],
        grad_up,
        early[6],
        grad_down,
        early[2],
        early[0],
        early[1],
        early[7, 0],
    )


def per_device(seq, tensor, *args):
    batch, tok, width = args[0].shape
    heads = args[7].shape[0]
    if seq == 8 and tensor == 4 and batch == 4 and heads == 3 and tok == 128:
        return gathered_plan(seq, *args)
    return general_plan(*args)


def solution(mesh):
    return jax.shard_map(
        functools.partial(per_device, mesh.shape["seq"], mesh.shape["tensor"]),
        mesh=mesh,
        in_specs=(
            P(None, "seq", None),
            P(),
            P(None, "tensor"),
            P("tensor"),
            P(None, "tensor"),
            P(None, "tensor"),
            P("tensor"),
            P("tensor", None),
            P("tensor", None),
            P(),
            P(),
            P(),
            P(None, "tensor"),
            P("tensor"),
            P("tensor", None),
            P(),
            P(),
            P(),
            P(None, "seq", None),
        ),
        out_specs=(
            P(None, "seq", None),
            P(None, "seq", None),
            P("seq", "tensor"),
            P("tensor"),
            P("seq", "tensor"),
            P("seq", "tensor"),
            P("tensor"),
            P("tensor", None),
            P("tensor", "seq"),
            P(),
            P(),
            P(),
            P("seq", "tensor"),
            P("tensor"),
            P("tensor", "seq"),
            P(),
            P(),
            P(),
            P(),
        ),
        check_vma=False,
    )
```

```python
import functools

import jax
import jax.numpy as jnp
from jax import lax
from jax.experimental import pallas as pl
from jax.experimental.pallas import tpu as pltpu
from jax.sharding import PartitionSpec as P

HEADS = 12
HEAD_DIM = 64
LAND = 64
CONV = 33
NS_ITERS = 6


highest = lax.Precision.HIGHEST
epsilon = 1e-05
negative = -1e30


def joined(x, axis, combine):
    everything = jax.tree.map(lambda part: lax.all_gather(part, axis), x)
    first = jax.tree.map(lambda part: part[0], everything)

    def hop(k, so_far):
        return combine(so_far, jax.tree.map(lambda part: part[k], everything))

    return lax.fori_loop(1, lax.axis_size(axis), hop, first)


def with_halo(block, sides, width):
    for axis, dim in sides:
        count = lax.axis_size(axis)
        forward = [(i, i + 1) for i in range(count - 1)]
        backward = [(target, source) for source, target in forward]
        low = lax.ppermute(
            lax.slice_in_dim(block, block.shape[dim] - width, None, axis=dim), axis, forward
        )
        high = lax.ppermute(lax.slice_in_dim(block, 0, width, axis=dim), axis, backward)
        block = jnp.concatenate([low, block, high], axis=dim)
    return block


def newton_inverse(kernel):
    identity = jnp.eye(kernel.shape[-1], dtype=jnp.float32)
    inverse = jnp.swapaxes(kernel, -1, -2) / jnp.sum(kernel * kernel, axis=(-2, -1), keepdims=True)
    for _ in range(NS_ITERS):
        product = jnp.matmul(kernel, inverse, precision=highest)
        inner_term = jnp.matmul(product, 7.0 * identity - product, precision=highest)
        inner_term = jnp.matmul(product, 15.0 * identity - inner_term, precision=highest)
        inverse = 0.25 * jnp.matmul(inverse, 13.0 * identity - inner_term, precision=highest)
    return inverse


def landmark_core(query_marks, key_marks):
    scores = jnp.einsum(
        "bhjd,bhid->bhji", query_marks, key_marks, precision=highest
    ) * HEAD_DIM ** (-0.5)
    kernel_two = jax.nn.softmax(scores, axis=-1)
    return (kernel_two, newton_inverse(kernel_two))


def normalize(summed, gain_vec, shift_vec):
    middle = jnp.mean(summed, axis=-1, keepdims=True)
    centred = summed - middle
    inverse_std = lax.rsqrt(jnp.mean(centred * centred, axis=-1, keepdims=True) + epsilon)
    normal = centred * inverse_std
    return (normal * gain_vec + shift_vec, normal, inverse_std)


def add_norm(partial_sum, residual, bias_vec, gain_vec, shift_vec):
    summed = lax.psum(partial_sum.astype(jnp.bfloat16), "tensor").astype(jnp.float32)
    return normalize(residual + summed + bias_vec, gain_vec, shift_vec)


def norm_back(grad_hidden, normal, inverse_std, gain_vec):
    grad_normal = grad_hidden * gain_vec
    grad_summed = inverse_std * (
        grad_normal
        - jnp.mean(grad_normal, axis=-1, keepdims=True)
        - normal * jnp.mean(grad_normal * normal, axis=-1, keepdims=True)
    )
    return (grad_summed, jnp.sum(grad_hidden * normal, axis=0), jnp.sum(grad_hidden, axis=0))


def combine_soft(earlier, later):
    top_score = jnp.maximum(earlier[0], later[0])
    weight_first = jnp.exp(earlier[0] - top_score)
    weight_second = jnp.exp(later[0] - top_score)
    return (
        top_score,
        earlier[1] * weight_first + later[1] * weight_second,
        earlier[2] * weight_first[..., None] + later[2] * weight_second[..., None],
    )


def general_plan(
    tokens,
    lengths,
    query_weight,
    query_bias,
    key_weight,
    value_weight,
    value_bias,
    conv_kernel,
    out_weight,
    out_bias,
    first_gain,
    first_shift,
    up_weight,
    up_bias,
    down_weight,
    down_bias,
    second_gain,
    second_shift,
    out_grad,
):
    batch, tok_local, width = tokens.shape
    local_width = query_weight.shape[1]
    local_heads = conv_kernel.shape[0]
    head_dim = local_width // local_heads
    score_scale = HEAD_DIM ** (-0.5)
    rows = batch * tok_local
    half_width = CONV // 2
    f32 = jnp.float32
    bf16 = jnp.bfloat16
    position = lax.axis_index("seq") * tok_local + jnp.arange(tok_local, dtype=jnp.int32)
    inside = position[None, :] < lengths[:, None]
    living = inside.astype(f32)
    segment = position[None, :] * LAND // lengths[:, None]
    onehot = (
        (segment[:, :, None] == jnp.arange(LAND, dtype=jnp.int32)[None, None, :])
        & inside[:, :, None]
    ).astype(f32)
    marks_index = jnp.arange(LAND, dtype=jnp.int32)
    upper = ((marks_index[None, :] + 1) * lengths[:, None] + LAND - 1) // LAND
    lower = (marks_index[None, :] * lengths[:, None] + LAND - 1) // LAND
    counts = (upper - lower).astype(f32)
    flat = tokens.reshape(rows, width)
    flat_wide = flat.astype(f32)
    queries = (jnp.dot(flat, query_weight, preferred_element_type=f32) + query_bias).astype(bf16)
    key_vectors = jnp.dot(flat, key_weight, preferred_element_type=f32).astype(bf16)
    values = (
        (jnp.dot(flat, value_weight, preferred_element_type=f32) + value_bias)
        * living.reshape(rows, 1)
    ).astype(bf16)
    query_three = queries.reshape(batch, tok_local, local_width)
    key_three = key_vectors.reshape(batch, tok_local, local_width)
    value_three = values.reshape(batch, tok_local, local_width)
    onehot_low = onehot.astype(bf16)
    query_sum = jnp.einsum("btj,btf->bjf", onehot_low, query_three, preferred_element_type=f32)
    key_sum = jnp.einsum("btj,btf->bjf", onehot_low, key_three, preferred_element_type=f32)
    query_sum, key_sum = lax.psum((query_sum, key_sum), "seq")
    query_marks = (
        (query_sum / counts[:, :, None])
        .reshape(batch, LAND, local_heads, head_dim)
        .transpose(0, 2, 1, 3)
    )
    key_marks = (
        (key_sum / counts[:, :, None])
        .reshape(batch, LAND, local_heads, head_dim)
        .transpose(0, 2, 1, 3)
    )
    (kernel_two, inverse), core_back = jax.vjp(landmark_core, query_marks, key_marks)
    identity = jnp.eye(LAND, dtype=f32)
    deviation = identity - jnp.matmul(kernel_two, inverse, precision=highest)
    proxy_part = jnp.sum(jnp.sqrt(jnp.sum(deviation * deviation, axis=(-2, -1)))) / (batch * HEADS)
    query_heads = query_three.reshape(batch, tok_local, local_heads, head_dim).astype(f32)
    key_heads = key_three.reshape(batch, tok_local, local_heads, head_dim).astype(f32)
    value_heads = value_three.reshape(batch, tok_local, local_heads, head_dim).astype(f32)
    first_scores = (
        jnp.einsum("bthd,bhjd->bhtj", query_heads, key_marks, precision=highest) * score_scale
    )
    kernel_one = jax.nn.softmax(first_scores, axis=-1)
    third_scores = (
        jnp.einsum("bhjd,bthd->bhjt", query_marks, key_heads, precision=highest) * score_scale
    )
    key_alive = inside[:, None, None, :]
    third_scores = jnp.where(key_alive, third_scores, negative)
    local_top = jnp.max(third_scores, axis=-1)
    local_weights = jnp.where(key_alive, jnp.exp(third_scores - local_top[..., None]), 0.0)
    local_total = jnp.sum(local_weights, axis=-1)
    local_mix = jnp.einsum("bhjt,bthd->bhjd", local_weights, value_heads, precision=highest)
    top_score, total_weight, mixed = joined(
        (local_top, local_total, local_mix), "seq", combine_soft
    )
    third_out = mixed / total_weight[..., None]
    carried = jnp.matmul(inverse, third_out, precision=highest)
    nystrom = jnp.einsum("bhtj,bhjd->bthd", kernel_one, carried, precision=highest).reshape(
        batch, tok_local, local_width
    )
    padded_values = with_halo(value_three, (("seq", 1),), half_width)
    kernel_wide = jnp.repeat(conv_kernel, head_dim, axis=0)
    convolved = jnp.zeros((batch, tok_local, local_width), f32)
    for i in range(CONV):
        convolved = (
            convolved + padded_values[:, i : i + tok_local, :].astype(f32) * kernel_wide[:, i]
        )
    attention = (nystrom + convolved).astype(bf16).reshape(rows, local_width)
    out_part = jnp.dot(attention, out_weight, preferred_element_type=f32)
    hidden_one, normal_one, inverse_one = add_norm(
        out_part, flat_wide, out_bias, first_gain, first_shift
    )
    hidden_low = hidden_one.astype(bf16)
    up_value = jnp.dot(hidden_low, up_weight, preferred_element_type=f32) + up_bias
    activated, gelu_back = jax.vjp(lambda z: jax.nn.gelu(z, approximate=False), up_value)
    activated = activated.astype(bf16)
    down_part = jnp.dot(activated, down_weight, preferred_element_type=f32)
    hidden_two, normal_two, inverse_two = add_norm(
        down_part, hidden_one, down_bias, second_gain, second_shift
    )
    output = hidden_two.astype(bf16).reshape(batch, tok_local, width)
    grad_output = out_grad.reshape(rows, width).astype(f32)
    grad_second_total, grad_second_gain, grad_second_shift = norm_back(
        grad_output, normal_two, inverse_two, second_gain
    )
    down_in = grad_second_total.astype(bf16)
    grad_down_bias = jnp.sum(down_in.astype(f32), axis=0)
    grad_down_weight = jnp.einsum("rf,rd->fd", activated, down_in, preferred_element_type=f32)
    grad_activated = jnp.einsum("rd,fd->rf", down_in, down_weight, preferred_element_type=f32)
    up_in = gelu_back(grad_activated)[0].astype(bf16)
    grad_up_bias = jnp.sum(up_in.astype(f32), axis=0)
    grad_up_weight = jnp.einsum("rd,rf->df", hidden_low, up_in, preferred_element_type=f32)
    hidden_part = jnp.einsum("rf,df->rd", up_in, up_weight, preferred_element_type=f32)
    grad_hidden_one = (
        lax.psum(hidden_part.astype(jnp.bfloat16), "tensor").astype(jnp.float32) + grad_second_total
    )
    grad_first_total, grad_first_gain, grad_first_shift = norm_back(
        grad_hidden_one, normal_one, inverse_one, first_gain
    )
    out_in = grad_first_total.astype(bf16)
    grad_out_bias = jnp.sum(out_in.astype(f32), axis=0)
    grad_out_weight = jnp.einsum("rf,rd->fd", attention, out_in, preferred_element_type=f32)
    grad_attention = jnp.einsum(
        "rd,fd->rf", out_in, out_weight, preferred_element_type=f32
    ).reshape(batch, tok_local, local_width)
    padded_grad = with_halo(grad_attention.astype(jnp.bfloat16), (("seq", 1),), half_width).astype(
        grad_attention.dtype
    )
    grad_conv_values = jnp.zeros((batch, tok_local, local_width), f32)
    conv_columns = []
    for i in range(CONV):
        conv_columns.append(
            jnp.sum(
                grad_attention * padded_values[:, i : i + tok_local, :].astype(f32), axis=(0, 1)
            )
        )
        start_index = 2 * half_width - i
        grad_conv_values = (
            grad_conv_values
            + padded_grad[:, start_index : start_index + tok_local, :] * kernel_wide[:, i]
        )
    grad_conv_kernel = (
        jnp.stack(conv_columns, axis=0).reshape(CONV, local_heads, head_dim).sum(axis=-1).T
    )
    grad_nystrom = grad_attention.reshape(batch, tok_local, local_heads, head_dim)
    grad_kernel_one = jnp.einsum("bthd,bhjd->bhtj", grad_nystrom, carried, precision=highest)
    grad_carried_part = jnp.einsum("bhtj,bthd->bhjd", kernel_one, grad_nystrom, precision=highest)
    grad_first_scores = kernel_one * (
        grad_kernel_one - jnp.sum(kernel_one * grad_kernel_one, axis=-1, keepdims=True)
    )
    grad_query_one = (
        jnp.einsum("bhtj,bhjd->bthd", grad_first_scores, key_marks, precision=highest) * score_scale
    )
    grad_key_marks_part = (
        jnp.einsum("bhtj,bthd->bhjd", grad_first_scores, query_heads, precision=highest)
        * score_scale
    )
    grad_carried, grad_key_marks_one = lax.psum((grad_carried_part, grad_key_marks_part), "seq")
    grad_third_out = jnp.matmul(jnp.swapaxes(inverse, -1, -2), grad_carried, precision=highest)
    grad_inverse = jnp.matmul(grad_carried, jnp.swapaxes(third_out, -1, -2), precision=highest)
    grad_query_marks_two, grad_key_marks_two = core_back((jnp.zeros_like(kernel_two), grad_inverse))
    third_prob = local_weights * jnp.exp(local_top - top_score)[..., None] / total_weight[..., None]
    delta_term = jnp.sum(grad_third_out * third_out, axis=-1)
    grad_prob_value = jnp.einsum("bhjd,bthd->bhjt", grad_third_out, value_heads, precision=highest)
    grad_third_scores = third_prob * (grad_prob_value - delta_term[..., None])
    grad_value_three = jnp.einsum("bhjt,bhjd->bthd", third_prob, grad_third_out, precision=highest)
    grad_key_three = (
        jnp.einsum("bhjt,bhjd->bthd", grad_third_scores, query_marks, precision=highest)
        * score_scale
    )
    grad_query_marks_part = (
        jnp.einsum("bhjt,bthd->bhjd", grad_third_scores, key_heads, precision=highest) * score_scale
    )
    grad_query_marks_three = lax.psum(grad_query_marks_part, "seq")
    grad_query_marks = (grad_query_marks_two + grad_query_marks_three) / counts[:, None, :, None]
    grad_key_marks = (grad_key_marks_one + grad_key_marks_two) / counts[:, None, :, None]
    grad_query_marks = grad_query_marks.transpose(0, 2, 1, 3).reshape(batch, LAND, local_width)
    grad_key_marks = grad_key_marks.transpose(0, 2, 1, 3).reshape(batch, LAND, local_width)
    grad_query_seg = jnp.einsum("btj,bjf->btf", onehot, grad_query_marks, precision=highest)
    grad_key_seg = jnp.einsum("btj,bjf->btf", onehot, grad_key_marks, precision=highest)
    query_in = (
        (grad_query_one.reshape(batch, tok_local, local_width) + grad_query_seg)
        .astype(bf16)
        .reshape(rows, local_width)
    )
    key_in = (
        (grad_key_three.reshape(batch, tok_local, local_width) + grad_key_seg)
        .astype(bf16)
        .reshape(rows, local_width)
    )
    value_in = (grad_value_three.reshape(batch, tok_local, local_width) + grad_conv_values).astype(
        bf16
    )
    value_in = jnp.where(inside[:, :, None], value_in, jnp.zeros_like(value_in)).reshape(
        rows, local_width
    )
    grad_query_bias = jnp.sum(query_in.astype(f32), axis=0)
    grad_value_bias = jnp.sum(value_in.astype(f32), axis=0)
    grad_query_weight = jnp.einsum("rd,rf->df", flat, query_in, preferred_element_type=f32)
    grad_key_weight = jnp.einsum("rd,rf->df", flat, key_in, preferred_element_type=f32)
    grad_value_weight = jnp.einsum("rd,rf->df", flat, value_in, preferred_element_type=f32)
    input_part = (
        jnp.einsum("rf,df->rd", query_in, query_weight, preferred_element_type=f32)
        + jnp.einsum("rf,df->rd", key_in, key_weight, preferred_element_type=f32)
        + jnp.einsum("rf,df->rd", value_in, value_weight, preferred_element_type=f32)
    )
    input_sum, proxy_norm = (
        lax.psum(input_part.astype(jnp.bfloat16), "tensor").astype(jnp.float32),
        lax.psum(proxy_part.astype(jnp.bfloat16), "tensor").astype(jnp.float32),
    )
    grad_tokens = (grad_first_total + input_sum).reshape(batch, tok_local, width)
    (
        grad_query_weight,
        grad_key_weight,
        grad_value_weight,
        grad_out_weight,
        grad_up_weight,
        grad_down_weight,
    ) = (
        lax.psum_scatter(grad_query_weight, "seq", scatter_dimension=0, tiled=True),
        lax.psum_scatter(grad_key_weight, "seq", scatter_dimension=0, tiled=True),
        lax.psum_scatter(grad_value_weight, "seq", scatter_dimension=0, tiled=True),
        lax.psum_scatter(grad_out_weight, "seq", scatter_dimension=1, tiled=True),
        lax.psum_scatter(grad_up_weight, "seq", scatter_dimension=0, tiled=True),
        lax.psum_scatter(grad_down_weight, "seq", scatter_dimension=1, tiled=True),
    )
    (
        grad_query_bias,
        grad_value_bias,
        grad_conv_kernel,
        grad_out_bias,
        grad_first_gain,
        grad_first_shift,
        grad_up_bias,
        grad_down_bias,
        grad_second_gain,
        grad_second_shift,
    ) = lax.psum(
        (
            grad_query_bias,
            grad_value_bias,
            grad_conv_kernel,
            grad_out_bias,
            grad_first_gain,
            grad_first_shift,
            grad_up_bias,
            grad_down_bias,
            grad_second_gain,
            grad_second_shift,
        ),
        "seq",
    )
    return (
        output,
        grad_tokens,
        grad_query_weight,
        grad_query_bias,
        grad_key_weight,
        grad_value_weight,
        grad_value_bias,
        grad_conv_kernel,
        grad_out_weight,
        grad_out_bias,
        grad_first_gain,
        grad_first_shift,
        grad_up_weight,
        grad_up_bias,
        grad_down_weight,
        grad_down_bias,
        grad_second_gain,
        grad_second_shift,
        proxy_norm,
    )


MESH = pl.DeviceIdType.MESH
LANES = 2 * HEAD_DIM
f32 = jnp.float32
bf16 = jnp.bfloat16
NN = (1, 0)
NT = (1, 1)
TN = (0, 0)


def dot(a, b, dims=NN):
    return lax.dot_general(
        a, b, (((dims[0],), (dims[1],)), ((), ())), preferred_element_type=f32
    )


def split(x):
    if x.dtype == bf16:
        return (x,)
    top = x.astype(bf16)
    return (top, (x - top.astype(f32)).astype(bf16))


def fine(a, b, dims=NN):
    a, b = split(a), split(b)
    total = dot(a[0], b[0], dims)
    if len(b) > 1:
        total = total + dot(a[0], b[1], dims)
    if len(a) > 1:
        total = total + dot(a[1], b[0], dims)
    return total


def iota(shape, dim):
    return lax.broadcasted_iota(jnp.int32, shape, dim)


def block_mask():
    shape = (LANES, LANES)
    return (iota(shape, 0) < HEAD_DIM) == (iota(shape, 1) < HEAD_DIM)


def eye():
    return jnp.where(iota((LANES, LANES), 0) == iota((LANES, LANES), 1), 1.0, 0.0).astype(f32)


def block_sums(x, same_head):
    ones = jnp.where(same_head, 1.0, 0.0).astype(bf16)
    return jnp.where(same_head, fine(fine(ones, x), ones), 1.0)


def taps_matrix(row, tok):
    return pltpu.roll(jnp.broadcast_to(row, (tok, 2 * tok)), 0, 1, stride=1, stride_axis=0)


def taps_row(taps, head, tok):
    row = taps[pl.ds(head, 1), :]
    return jnp.concatenate([row, jnp.zeros((1, 2 * tok - CONV), f32)], axis=1)


def conv_block(matrices, window):
    first = fine(matrices[0], window)
    second = fine(matrices[1], window)
    return jnp.where(iota(first.shape, 1) < HEAD_DIM, first, second)


def greet(devices):
    barrier = pltpu.get_barrier_semaphore()
    for device in devices:
        pl.semaphore_signal(barrier, inc=1, device_id=device, device_id_type=MESH)
    return barrier


def around(n, me, tensor):
    return [(lax.rem(me + d, n), tensor) for d in range(1, n)]


def others(me, tensor):
    core = tensor + 1 - 2 * (tensor % 2)
    return [(me, core), (me, lax.rem(tensor + 2, 4)), (me, lax.rem(core + 2, 4))]


def paired(y):
    return y[:, :LANES], jnp.concatenate(
        [y[:, LANES : LANES + HEAD_DIM], y[:, HEAD_DIM:LANES]], axis=1
    )


def remote(src, dst, send, recv, device):
    return pltpu.make_async_remote_copy(
        src_ref=src, dst_ref=dst, send_sem=send, recv_sem=recv, device_id=device,
        device_id_type=MESH,
    )


def member_rows(length, total):
    j = iota((LANES, total), 0) % LAND
    t = iota((LANES, total), 1)
    inside = (t * LAND >= j * length) & (t * LAND < (j + 1) * length) & (t < length)
    return jnp.where(inside, 1.0, 0.0).astype(bf16)


def member_columns(length, total):
    j = iota((total, LANES), 1) % LAND
    t = iota((total, LANES), 0)
    inside = (t * LAND >= j * length) & (t * LAND < (j + 1) * length) & (t < length)
    return jnp.where(inside, 1.0, 0.0).astype(bf16)


def segment_counts(length):
    j = iota((LANES, LANES), 0) % LAND
    upper = ((j + 1) * length + LAND - 1) // LAND
    lower = (j * length + LAND - 1) // LAND
    return (upper - lower).astype(f32)


def normal_of(summed):
    middle = jnp.mean(summed, axis=-1, keepdims=True)
    centred = summed - middle
    inverse_std = lax.rsqrt(jnp.mean(centred * centred, axis=-1, keepdims=True) + epsilon)
    return centred * inverse_std, inverse_std


def before_norm(grad, normal, inverse_std, gain):
    grad_normal = grad * gain
    return inverse_std * (
        grad_normal
        - jnp.mean(grad_normal, axis=-1, keepdims=True)
        - normal * jnp.mean(grad_normal * normal, axis=-1, keepdims=True)
    )


def block_rows(t, tok):
    return pl.ds(pl.multiple_of(t * tok, tok), tok)


def gather_and_sum(phase, me, tensor, held, work, ring, filler):
    tok = held.shape[0] // 4
    ag_send, ag_recv, sum_send, sum_recv, core_out, core_in, y_out, y_in = ring
    core, across, far = others(me, tensor)
    mine = held.at[block_rows(tensor, tok)]
    to_y = remote(mine, mine, ag_send.at[phase, 0], ag_recv.at[phase, 0], across)
    to_y.start()
    to_core = remote(mine, mine, ag_send.at[phase, 1], ag_recv.at[phase, 1], core)
    to_core.start()
    total = work(tensor)
    to_core.wait_recv()
    core_out[phase, 0] = work(core[1]).astype(bf16)
    near = remote(
        core_out.at[phase, 0], core_in.at[phase, 0], sum_send.at[phase, 0], sum_recv.at[phase, 0],
        core,
    )
    near.start()
    to_y.wait_recv()
    other = held.at[block_rows(across[1], tok)]
    pass_on = remote(other, other, ag_send.at[phase, 2], ag_recv.at[phase, 2], core)
    pass_on.start()
    part = work(across[1])
    pass_on.wait_recv()
    core_out[phase, 1] = work(far[1]).astype(bf16)
    middle = remote(
        core_out.at[phase, 1], core_in.at[phase, 1], sum_send.at[phase, 1], sum_recv.at[phase, 1],
        core,
    )
    middle.start()
    middle.wait_recv()
    y_out[phase] = (part + core_in[phase, 1].astype(f32)).astype(bf16)
    last = remote(
        y_out.at[phase], y_in.at[phase], sum_send.at[phase, 2], sum_recv.at[phase, 2], across
    )
    last.start()
    filler()
    near.wait_recv()
    last.wait_recv()
    total = total + core_in[phase, 0].astype(f32) + y_in[phase].astype(f32)
    return total, [to_y, to_core, pass_on, near, middle, last]


class Scatter:
    def __init__(self, index, me, tensor, source, buffers, send, recv, order=(0, 1, 2)):
        self.index, self.source = index, source
        self.first_in, self.held, self.second_in, self.pair, self.last_in = buffers
        self.block = source.shape[0] // 8
        self.weights = [2**bit for bit in order]
        self.bits = [(me // weight) % 2 for weight in self.weights]
        self.partners = [
            (me + weight * (1 - 2 * bit), tensor) for weight, bit in zip(self.weights, self.bits)
        ]
        self.send, self.recv = send, recv
        self.copies = []

    def rows(self, slot, bit):
        index = (slot // 2) * self.weights[2] + (slot % 2) * self.weights[1] + bit * self.weights[0]
        return pl.ds(pl.multiple_of(index * self.block, 16), self.block)

    def copy(self, src, dst, k, stage):
        copy = remote(
            src, dst, self.send.at[self.index, k], self.recv.at[self.index, k],
            self.partners[stage],
        )
        copy.start()
        self.copies.append(copy)

    def first(self, slots=range(4)):
        for slot in slots:
            self.copy(self.source.at[self.rows(slot, 1 - self.bits[0])], self.first_in.at[slot], slot, 0)

    def second(self):
        for slot in range(4):
            self.copies[slot].wait_recv()
        for slot in range(4):
            both = self.source[self.rows(slot, self.bits[0])].astype(f32)
            self.held[slot] = (both + self.first_in[slot].astype(f32)).astype(bf16)
        for k in range(2):
            self.copy(self.held.at[2 * k + 1 - self.bits[1]], self.second_in.at[k], 4 + k, 1)

    def third(self):
        for k in range(2):
            self.copies[4 + k].wait_recv()
        for k in range(2):
            both = self.held[2 * k + self.bits[1]].astype(f32) + self.second_in[k].astype(f32)
            self.pair[k] = both.astype(bf16)
        self.copy(self.pair.at[1 - self.bits[2]], self.last_in, 6, 2)

    def last(self):
        kept, come = self.swapped()
        return kept.astype(f32) + come.astype(f32)

    def swapped(self):
        self.copies[6].wait_recv()
        return self.pair[self.bits[2]], self.last_in[...]

    def finish(self):
        for copy in self.copies:
            copy.wait_send()


def scatter_buffers(width, block):
    return [
        pltpu.VMEM((4, block, width), bf16),
        pltpu.VMEM((4, block, width), bf16),
        pltpu.VMEM((2, block, width), bf16),
        pltpu.VMEM((2, block, width), bf16),
        pltpu.VMEM((block, width), bf16),
    ]


def total_of(v):
    return jnp.sum(v, axis=0, keepdims=True)


def turn(second, first):
    low = second.astype(bf16)
    return jnp.where(iota(low.shape, 1) < HEAD_DIM, low, first)


JOBS = 5
RESULTS = 19


def layer_kernel(
    n, lengths, x_far, wq_far, qb, wk_far, wv_far, vb, taps, out_far, out_bias, gain_one,
    shift_one, up_far, up_bias, down_far, down_bias, gain_two, shift_two, grad_far,
    *rest,
):
    results, rest = rest[:RESULTS], rest[RESULTS:]
    ready, rest = rest[:RESULTS], rest[RESULTS:]
    layer_body(
        n, lengths, x_far, wq_far, qb, wk_far, wv_far, vb, taps, out_far, out_bias, gain_one,
        shift_one, up_far, up_bias, down_far, down_bias, gain_two, shift_two, grad_far, results,
        ready, *rest,
    )


def layer_body(
    n, lengths, x_far, wq_far, qb, wk_far, wv_far, vb, taps, out_far, out_bias, gain_one,
    shift_one, up_far, up_bias, down_far, down_bias, gain_two, shift_two, grad_far, results, ready,
    x, wk, wq, wv, up_weight, down_weight, out_grad, out_whole,
    stage, ks, qs, vs, k1, p3, newton, out_stage, attn,
    heads_in, heads_out, grad_attn, hidden, slope, active, down_in, up_in,
    core_out, core_in, y_out, y_in,
    gs, back_stage, back_single, come_pair, come_single, weight_in, out_in, early, early_tensor, tokens_own, tokens_low, source_up,
    source_down, source_out, source_v, source_kq, early_seq, late_seq, tokens_whole,
    *rest,
):
    buffers, sems = rest[: 5 * JOBS], rest[5 * JOBS :]
    (load, send, recv, out_send, out_recv, whole_send, whole_recv, a2a_send, a2a_recv, ag_send,
     ag_recv, sum_send, sum_recv, grad_send, grad_recv, back_send, back_recv, share_send,
     share_recv, small_send, small_recv, job_send, job_recv, own_send, own_recv, store) = sems
    (output, grad_tokens, grad_query, query_bias, grad_key, grad_value, value_bias, conv, grad_out,
     out_bias_grad, first_gain, first_shift, grad_up, up_bias_grad, grad_down, down_bias_grad,
     second_gain, second_shift, proxy) = ready
    stores = []

    def done(*numbers):
        for i in numbers:
            copy = pltpu.make_async_copy(ready[i], results[i], store.at[i])
            copy.start()
            stores.append(copy)

    me = lax.axis_index("seq")
    tensor = lax.axis_index("tensor")
    rows, width = x.shape
    batch = n // 2
    tok = rows // batch
    total = n * tok
    half = CONV // 2
    own, side = me // 2, me % 2
    scale = HEAD_DIM ** (-0.5)
    ring_peers = around(n, me, tensor)
    peers = others(me, tensor)
    core, across, far = peers
    mine = block_rows(tensor, tok)
    local = wk.shape[0]
    barrier = greet(ring_peers + peers)
    loads = []
    for i, (source, target) in enumerate((
        (x_far, x), (wk_far, wk), (wq_far, wq), (wv_far, wv),
        (out_far, out_whole.at[tensor, pl.ds(0, local)]), (up_far, up_weight),
        (down_far, down_weight), (grad_far, out_grad),
    )):
        copy = pltpu.make_async_copy(source, target, load.at[i])
        copy.start()
        loads.append(copy)
    jobs = [
        Scatter(i, me, tensor, source, buffers[5 * i : 5 * i + 5], job_send, job_recv, order)
        for i, (source, order) in enumerate((
            (source_down, (0, 1, 2)), (source_up, (0, 1, 2)), (source_out, (0, 1, 2)),
            (source_v, (1, 2, 0)), (source_kq, (1, 2, 0)),
        ))
    ]
    job_down, job_up, job_out, job_v, job_kq = jobs
    sent = []

    owned = (ks, qs, vs)
    offsets = (0, 0, half)
    for padded in (vs, gs):
        padded[0:half] = jnp.zeros((half, LANES), bf16)
        padded[half + total : total + tok] = jnp.zeros((tok - half, LANES), bf16)
    for t in range(4):
        out_whole[t, local:] = jnp.zeros((2 * LANES - local, width), bf16)

    arrivals = [[], [], []]

    def spread(i):
        here = pl.ds(pl.multiple_of(offsets[i] + me * tok, 16), tok)
        for d in range(1, n):
            peer = lax.rem(me + d, n)
            copy = remote(
                stage.at[i, peer % 2, block_rows(peer // 2, tok)], owned[i].at[here],
                send.at[i, d - 1], recv.at[i, d - 1], (peer, tensor),
            )
            copy.start()
            arrivals[i].append(copy)
            if i != 1:
                sent.append(copy)
        owned[i][here] = stage[i, side, block_rows(own, tok)]

    loads[0].wait()
    loads[1].wait()
    y = dot(x[...], wk[...], NT)
    stage[0, 0], stage[0, 1] = paired(y.astype(bf16))
    pl.semaphore_wait(barrier, n + 2)
    spread(0)
    loads[2].wait()
    y = dot(x[...], wq[...], NT) + qb[...].reshape(1, local)
    stage[1, 0], stage[1, 1] = paired(y.astype(bf16))
    spread(1)
    loads[3].wait()
    y = dot(x[...], wv[...], NT) + vb[...].reshape(1, local)
    position = me * tok + iota((tok, local), 0)
    y = jnp.concatenate(
        [
            jnp.where(position < lengths[b], y[b * tok : (b + 1) * tok], 0.0)
            for b in range(batch)
        ],
        axis=0,
    )
    stage[2, 0], stage[2, 1] = paired(y.astype(bf16))
    loads[4].wait()
    whole_parts = []
    for i, device in enumerate(peers):
        part = out_whole.at[tensor, pl.ds(0, local)]
        copy = remote(part, part, whole_send.at[i], whole_recv.at[i], device)
        copy.start()
        whole_parts.append(copy)

    length = lengths[own]
    same_head = block_mask()
    identity = eye()
    ones = jnp.where(same_head, 1.0, 0.0).astype(bf16)
    members = member_rows(length, total)
    counts = segment_counts(length)
    matrices = [taps_matrix(taps_row(taps, h, tok), tok) for h in (2 * side, 1)]
    flip = jnp.where(
        iota((2 * tok, 2 * tok), 0) + iota((2 * tok, 2 * tok), 1) == CONV - 1, 1.0, 0.0
    ).astype(bf16)
    reverse = [
        taps_matrix(
            fine(jnp.broadcast_to(taps_row(taps, h, tok), (8, 2 * tok)), flip)[0:1], tok
        )
        for h in (2 * side, 1)
    ]
    even = side == 0
    for i, w in enumerate((wk, wq, wv)):
        pair, single = w[:LANES], w[LANES:]
        weight_in[i * LANES : (i + 1) * LANES] = jnp.where(
            even, pair, jnp.concatenate([single, pair[HEAD_DIM:]], axis=0)
        )
        start = 3 * LANES + i * HEAD_DIM
        weight_in[start : start + HEAD_DIM] = jnp.where(even, single, pair[:HEAD_DIM])
    for copy in arrivals[0]:
        copy.wait_recv()
    keys = ks[...]
    key_marks = jnp.where(same_head, dot(members, keys) / counts, 0.0)
    for copy in arrivals[1]:
        copy.wait_send()
    spread(2)
    for copy in arrivals[1]:
        copy.wait_recv()
    queries = qs[...]
    query_marks = jnp.where(same_head, dot(members, queries) / counts, 0.0)
    scores = jnp.where(same_head, fine(query_marks, key_marks, NT) * scale, negative)
    weights = jnp.exp(scores - jnp.max(scores, axis=1, keepdims=True))
    kernel_two = weights / jnp.sum(weights, axis=1, keepdims=True)
    inverse = jnp.where(
        same_head, kernel_two.T / block_sums(kernel_two * kernel_two, same_head), 0.0
    )
    for step in range(NS_ITERS):
        product = fine(kernel_two, inverse)
        inner_one = fine(product, 7.0 * identity - product)
        inner_two = fine(product, 15.0 * identity - inner_one)
        newton[4 * step] = inverse
        newton[4 * step + 1] = product
        newton[4 * step + 2] = inner_one
        newton[4 * step + 3] = inner_two
        inverse = 0.25 * fine(inverse, 13.0 * identity - inner_two)

    deviation = identity - fine(kernel_two, inverse)
    norms = jnp.sqrt(block_sums(deviation * deviation, same_head))
    first, second = norms[0:1, 0:1], norms[LANES - 1 :, LANES - 1 :]
    norm_sum = jnp.where(side == 0, first + second, first) / (batch * HEADS)
    early[7:8] = jnp.broadcast_to(norm_sum, (1, width))

    first_scores = fine(queries, key_marks, NT) * scale
    left = iota(first_scores.shape, 1) < HEAD_DIM
    top_left = jnp.max(jnp.where(left, first_scores, negative), axis=1, keepdims=True)
    top_right = jnp.max(jnp.where(left, negative, first_scores), axis=1, keepdims=True)
    weights = jnp.exp(first_scores - jnp.where(left, top_left, top_right))
    k1[...] = weights / fine(weights, ones)

    third_scores = fine(keys, query_marks, NT) * scale
    alive = iota(third_scores.shape, 0) < length
    third_scores = jnp.where(alive, third_scores, negative)
    weights = jnp.exp(third_scores - jnp.max(third_scores, axis=0, keepdims=True))
    weights = jnp.where(alive, weights, 0.0)
    third_prob = weights / jnp.sum(weights, axis=0, keepdims=True)
    p3[...] = third_prob

    for copy in arrivals[2]:
        copy.wait_recv()
    values = vs[half : half + total]
    third_out = jnp.where(same_head, fine(third_prob, values, TN), 0.0)
    carried = fine(inverse, third_out)

    there = block_rows(own, tok)
    attn_parts = []
    for d in range(1, n + 1):
        peer = lax.rem(me + d, n)
        start = pl.multiple_of(peer * tok, tok)
        nystrom = fine(k1[pl.ds(start, tok)], carried)
        convolved = conv_block(matrices, vs[pl.ds(start, 2 * tok)])
        low = (nystrom + convolved).astype(bf16)
        if d == n:
            attn[side, there] = low
        else:
            out_stage[d - 1] = low
            copy = remote(
                out_stage.at[d - 1], attn.at[side, there], out_send.at[d - 1], out_recv.at[d - 1],
                (peer, tensor),
            )
            copy.start()
            attn_parts.append(copy)
    for copy in whole_parts + attn_parts:
        copy.wait_recv()
    sent += whole_parts + attn_parts

    parts = []
    for i in (2, 1, 0):
        copy = remote(
            attn.at[:, block_rows(peers[i][1], tok)], heads_in.at[tensor], a2a_send.at[0, i],
            a2a_recv.at[0, i], peers[i],
        )
        copy.start()
        parts.append(copy)
    heads_in[tensor] = attn[:, mine]
    z, side_of_chip = me // 2, tensor % 2
    beside = (me + 1 - 2 * side, tensor)
    token_parts = []

    def give_tokens(src, dst, i, device):
        copy = remote(src, dst, own_send.at[i], own_recv.at[i], device)
        copy.start()
        token_parts.append(copy)

    def half_block(b):
        start = pl.multiple_of(b * tok + side_of_chip * (tok // 2), tok // 2)
        return pl.ds(start, tok // 2)

    tokens_own[me, side_of_chip] = x[half_block(own)]
    for k in range(1, 4):
        peer = lax.rem(z + k, 4)
        give_tokens(
            x.at[half_block(peer)], tokens_own.at[me, side_of_chip], k - 1,
            (2 * peer + side, tensor),
        )
    half_own = tokens_own.at[me, side_of_chip]
    give_tokens(half_own, half_own, 3, beside)

    def pass_tokens():
        for k in range(1, 4):
            token_parts[k - 1].wait_recv()
        for k in range(1, 4):
            come = tokens_own.at[2 * lax.rem(z + 4 - k, 4) + side, side_of_chip]
            give_tokens(come, come, 3 + k, beside)

    for copy in loads[5:]:
        copy.wait()
    for copy in parts:
        copy.wait_recv()
    sent += parts
    branch = jnp.zeros((tok, width), f32)
    for t in range(4):
        branch = branch + dot(heads_in[t, 0], out_whole[t, :LANES])
        branch = branch + dot(heads_in[t, 1], out_whole[t, LANES:])

    def line(vector):
        return vector[...].reshape(1, vector.shape[0])

    first_total = x[mine].astype(f32) + (branch + line(out_bias))
    normal_one, inverse_one = normal_of(first_total)
    hidden_one = normal_one * line(gain_one) + line(shift_one)
    hidden[mine] = hidden_one.astype(bf16)
    ring = (ag_send, ag_recv, sum_send, sum_recv, core_out, core_in, y_out, y_in)

    def up(t):
        at = block_rows(t, tok)
        value = dot(hidden[at], up_weight[...]) + line(up_bias)
        half_erf = 0.5 * (1.0 + lax.erf(value * (0.5**0.5)))
        density = jnp.exp(-0.5 * value * value) * (0.5 / jnp.pi) ** 0.5
        slope[at] = half_erf + value * density
        low = (value * half_erf).astype(bf16)
        active[at] = low
        return dot(low, down_weight[...])

    down_sum, copies = gather_and_sum(0, me, tensor, hidden, up, ring, pass_tokens)
    sent += copies
    second_total = hidden_one + (down_sum + line(down_bias))
    normal_two, inverse_two = normal_of(second_total)
    output[mine] = (normal_two * line(gain_two) + line(shift_two)).astype(bf16)
    grad_output = out_grad[mine].astype(f32)
    grad_second = before_norm(grad_output, normal_two, inverse_two, line(gain_two))
    low = grad_second.astype(bf16)
    down_in[mine] = low

    def down(t):
        at = block_rows(t, tok)
        low = (dot(down_in[at], down_weight[...], NT) * slope[at]).astype(bf16)
        up_in[at] = low
        return dot(low, up_weight[...], NT)

    def fill():
        source_down[...] = dot(down_in[...], active[...], TN).astype(bf16)
        job_down.first()
        source_up[...] = dot(hidden[...], up_in[...], TN).astype(bf16)
        early[0:1] = total_of(grad_output * normal_two)
        early[1:2] = total_of(grad_output)
        early[2:3] = total_of(low.astype(f32))
        early[6:7] = dot(jnp.ones((8, rows), bf16), up_in[...])[0:1]

    for copy in token_parts[3:7]:
        copy.wait_recv()
    half_all = tokens_own.at[:, side_of_chip]
    give_tokens(half_all, half_all, 7, core)
    up_sum, copies = gather_and_sum(1, me, tensor, down_in, down, ring, fill)
    sent += copies
    grad_hidden = grad_second + up_sum
    grad_first = before_norm(grad_hidden, normal_one, inverse_one, line(gain_one))
    low_out = grad_first.astype(bf16)
    out_in[mine] = low_out
    parts = []
    for i in (2, 1, 0):
        t = peers[i][1]
        heads_out[i, 0] = dot(low_out, out_whole[t, :LANES], NT).astype(bf16)
        heads_out[i, 1] = turn(dot(low_out, out_whole[t, LANES:], NT), heads_out[i, 0])
        copy = remote(
            heads_out.at[i], grad_attn.at[:, mine], a2a_send.at[1, i], a2a_recv.at[1, i], peers[i]
        )
        copy.start()
        parts.append(copy)
    own_first = dot(low_out, out_whole[tensor, :LANES], NT).astype(bf16)
    grad_attn[0, mine] = own_first
    grad_attn[1, mine] = turn(dot(low_out, out_whole[tensor, LANES:], NT), own_first)
    sent += parts
    early[3:4] = total_of(grad_hidden * normal_one)
    early[4:5] = total_of(grad_hidden)
    early[5:6] = total_of(low_out.astype(f32))
    early_tensor[tensor] = early[...]
    for copy in parts:
        copy.wait_recv()

    here = pl.ds(pl.multiple_of(half + me * tok, 16), tok)
    parts = []
    for d in range(1, n):
        peer = lax.rem(me + d, n)
        copy = remote(
            grad_attn.at[peer % 2, block_rows(peer // 2, tok)], gs.at[here], grad_send.at[d - 1],
            grad_recv.at[d - 1], (peer, tensor),
        )
        copy.start()
        parts.append(copy)
    gs[here] = grad_attn[side, block_rows(own, tok)]
    shares = []
    for i, held in enumerate((out_in, output)):
        for j, device in enumerate((across, core)):
            copy = remote(
                held.at[mine], held.at[mine], share_send.at[i, j], share_recv.at[i, j], device
            )
            copy.start()
            shares.append(copy)
    smalls = []
    for i, device in enumerate(peers):
        copy = remote(
            early, early_tensor.at[tensor], small_send.at[0, i], small_recv.at[0, i], device
        )
        copy.start()
        smalls.append(copy)
    job_up.first(range(2))

    members = member_columns(length, total)
    outs = []

    def give(i, block):
        low = block.astype(bf16)
        blocks = low.reshape(n, 2, tok // 2, LANES)
        back_stage[i] = low.reshape(n, tok, LANES)
        back_single[i] = jnp.concatenate(
            [blocks[:, 0, :, :HEAD_DIM], blocks[:, 1, :, :HEAD_DIM]], axis=2
        )
        part = []
        for d in range(1, n):
            peer = lax.rem(me + d, n)
            source, target = (back_stage, come_pair) if d % 2 == 0 else (back_single, come_single)
            copy = remote(
                source.at[i, peer], target.at[i, own], back_send.at[i, d - 1],
                back_recv.at[i, d - 1], (peer, tensor),
            )
            copy.start()
            part.append(copy)
        come_pair[i, own] = back_stage[i, me]
        outs.append(part)
        return low

    job_down.second()
    for copy in parts:
        copy.wait_recv()
    sent += parts
    job_up.first(range(2, 4))
    grad = gs[half : half + total]
    kernel_one = k1[...]
    grad_carried = jnp.where(same_head, fine(kernel_one, grad, TN), 0.0)
    grad_third = fine(inverse, grad_carried, TN)
    grad_inverse = fine(grad_carried, third_out, NT)
    third_prob = p3[...]
    convolved = jnp.concatenate(
        [conv_block(reverse, gs[m * tok : (m + 2) * tok]) for m in range(n)], axis=0
    )
    grad_values = fine(third_prob, grad_third) + convolved
    value_in = give(2, jnp.where(iota(grad_values.shape, 0) < length, grad_values, 0.0))


    kernel_back = jnp.zeros((LANES, LANES), f32)
    grad_state = grad_inverse
    for step in reversed(range(NS_ITERS)):
        state, product, inner_one, inner_two = [newton[4 * step + i] for i in range(4)]
        grad_next = 0.25 * fine(grad_state, 13.0 * identity - inner_two, NT)
        grad_two = -0.25 * fine(state, grad_state, TN)
        grad_product = fine(grad_two, 15.0 * identity - inner_one, NT)
        grad_one = -fine(product, grad_two, TN)
        grad_product = (
            grad_product
            + fine(grad_one, 7.0 * identity - product, NT)
            - fine(product, grad_one, TN)
        )
        grad_state = grad_next + fine(kernel_two, grad_product, TN)
        kernel_back = kernel_back + fine(grad_product, state, NT)
    squares = block_sums(kernel_two * kernel_two, same_head)
    spread_sum = jnp.where(same_head, block_sums(grad_state * newton[0], same_head), 0.0)
    kernel_back = kernel_back + (grad_state.T - 2.0 * kernel_two * spread_sum) / squares
    grad_scores = scale * kernel_two * (
        kernel_back - jnp.sum(kernel_two * kernel_back, axis=1, keepdims=True)
    )
    query_two = fine(grad_scores, key_marks)
    key_two = fine(grad_scores, query_marks, TN)

    grad_one = fine(grad, carried, NT)
    both = kernel_one * grad_one
    first_scores = scale * (both - kernel_one * fine(both, ones))
    key_one = jnp.where(same_head, fine(first_scores, queries, TN), 0.0)
    delta = fine(jnp.ones((8, LANES), bf16), grad_third * third_out, NT)[0:1]
    third_scores = scale * third_prob * (fine(values, grad_third, NT) - delta)
    query_three = jnp.where(same_head, fine(third_scores, keys, TN), 0.0)
    key_in = give(0, fine(third_scores, query_marks) + fine(members, (key_one + key_two) / counts))
    query_in = give(1, fine(first_scores, key_marks) + fine(members, (query_two + query_three) / counts))

    for i, held in enumerate((out_in, output)):
        shares[2 * i].wait_recv()
        block = held.at[block_rows(across[1], tok)]
        copy = remote(block, block, share_send.at[i, 2], share_recv.at[i, 2], core)
        copy.start()
        shares.append(copy)
    for copy in smalls:
        copy.wait_recv()
    by_tensor = early_tensor[0] + early_tensor[1] + early_tensor[2] + early_tensor[3]
    early_seq[me] = jnp.where(iota(by_tensor.shape, 0) == 6, early[...], by_tensor)
    smalls_early = []
    for d, device in enumerate(ring_peers):
        copy = remote(
            early_seq.at[me], early_seq.at[me], small_send.at[1, d], small_recv.at[1, d], device
        )
        copy.start()
        smalls_early.append(copy)
    position = iota((tok, tok), 0) + iota((tok, tok), 1)
    upside = jnp.where(position == tok - 1, 1.0, 0.0).astype(bf16)
    lane = iota((tok, LANES), 1)
    conv_rows = []
    for h in range(2):
        inner = (lane < HEAD_DIM) if h == 0 else (lane >= HEAD_DIM)
        table = jnp.zeros((tok, 2 * tok), f32)
        for m in range(n):
            block = gs[half + m * tok : half + (m + 1) * tok]
            block = jnp.where(inner, block, jnp.zeros_like(block))
            table = table + dot(block, vs[m * tok : (m + 2) * tok], NT)
        table = pltpu.roll(fine(upside, table), 0, 1, stride=1, stride_axis=0)
        row = jnp.sum(table, axis=0, keepdims=True)
        row = pltpu.roll(jnp.broadcast_to(row, (8, 2 * tok)), tok + 1, 1)
        conv_rows.append(row[0:1, :LANES])
    shares[1].wait_recv()
    shares[4].wait_recv()
    attention = jnp.concatenate([attn[0], attn[1, :, :HEAD_DIM]], axis=1)
    source_out[...] = dot(out_in[...], attention, TN).astype(bf16)
    job_out.first()
    token_parts[7].wait_recv()
    sent += token_parts
    tokens_all = tokens_own[...].reshape(total, width)
    source_v[...] = dot(tokens_all, value_in, TN).astype(bf16)
    source_kq[:, :LANES] = dot(tokens_all, key_in, TN).astype(bf16)
    source_kq[:, LANES:] = dot(tokens_all, query_in, TN).astype(bf16)
    job_v.first()
    job_kq.first()
    late = late_seq.at[me]
    late[...] = jnp.zeros(late.shape, f32)
    column = jnp.ones((8, total), bf16)
    for row, v in ((0, query_in), (1, value_in)):
        v = dot(column, v)[0:1]
        late[row : row + 1, 0:LANES] = jnp.where(even, v, 0.0)
        late[row : row + 1, LANES:local] = jnp.where(even, 0.0, v[:, :HEAD_DIM])
    late[2:3, 0:LANES] = jnp.where(even, conv_rows[0], 0.0)
    late[3:4, 0:LANES] = jnp.where(even, conv_rows[1], 0.0)
    late[4:5, 0:LANES] = jnp.where(even, 0.0, conv_rows[0])
    smalls_late = []
    for d, device in enumerate(ring_peers):
        copy = remote(late, late, small_send.at[2, d], small_recv.at[2, d], device)
        copy.start()
        smalls_late.append(copy)
    job_up.second()
    job_down.third()

    for part in outs:
        for copy in part:
            copy.wait_recv()
    singles = []
    for i in range(3):
        tokens_low[:, i * LANES : (i + 1) * LANES] = come_pair[i].reshape(rows, LANES)
        packed = come_single[i]
        single = jnp.concatenate([packed[:, :, :HEAD_DIM], packed[:, :, HEAD_DIM:]], axis=1)
        singles.append(single.reshape(rows, HEAD_DIM))
    tokens_low[:, 3 * LANES :] = jnp.concatenate(singles, axis=1)

    def input_part(t):
        return dot(tokens_low[block_rows(t, tok)], weight_in[...])

    def pass_sum(k, value, device):
        core_out[2, k] = value.astype(bf16)
        copy = remote(
            core_out.at[2, k], core_in.at[2, k], sum_send.at[2, k], sum_recv.at[2, k], device
        )
        copy.start()
        sent.append(copy)
        return copy

    middle = pass_sum(1, input_part(far[1]), core)
    near = pass_sum(0, input_part(core[1]), core)
    part = input_part(across[1])
    middle.wait_recv()
    y_out[2] = (part + core_in[2, 1].astype(f32)).astype(bf16)
    final = remote(y_out.at[2], y_in.at[2], sum_send.at[2, 2], sum_recv.at[2, 2], across)
    final.start()
    sent.append(final)
    result = input_part(tensor) + grad_first
    job_out.second()
    job_v.second()
    near.wait_recv()
    final.wait_recv()
    result = result + core_in[2, 0].astype(f32) + y_in[2].astype(f32)
    tokens_whole[mine] = result.astype(bf16)
    ends = []
    for j, device in enumerate((across, core)):
        copy = remote(
            tokens_whole.at[mine], tokens_whole.at[mine], share_send.at[2, j], share_recv.at[2, j],
            device,
        )
        copy.start()
        ends.append(copy)
    job_up.third()
    job_kq.second()
    job_out.third()
    job_v.third()
    grad_down[...] = job_down.last()
    done(14)
    for copy in smalls_early + smalls_late:
        copy.wait_recv()
    by_seq = functools.reduce(lambda a, b: a + b, [early_seq[i] for i in range(n)])
    for ref, row in (
        (second_gain, 0), (second_shift, 1), (down_bias_grad, 2), (first_gain, 3),
        (first_shift, 4), (out_bias_grad, 5), (up_bias_grad, 6),
    ):
        ref[...] = by_seq[row]
    proxy[...] = by_seq[7:8, 0:1]
    by_seq = functools.reduce(lambda a, b: a + b, [late_seq[i] for i in range(n)])
    query_bias[...] = by_seq[0, :local]
    value_bias[...] = by_seq[1, :local]
    conv[...] = by_seq[2:5, :CONV]
    shares[3].wait_recv()
    shares[5].wait_recv()
    done(0, 3, 6, 7, 9, 10, 11, 13, 15, 16, 17, 18)
    ends[0].wait_recv()
    block = tokens_whole.at[block_rows(across[1], tok)]
    copy = remote(block, block, share_send.at[2, 2], share_recv.at[2, 2], core)
    copy.start()
    ends.append(copy)
    job_kq.third()
    grad_up[...] = job_up.last()
    done(12)
    grad_out[...] = job_out.last().T
    done(8)

    def heads(job, *refs):
        kept, come = job.swapped()
        pair, single = jnp.where(even, kept, come), jnp.where(even, come, kept)
        for i, ref in enumerate(refs):
            ref[:, :LANES] = pair[:, i * LANES : (i + 1) * LANES].astype(f32)
            ref[:, LANES:] = single[:, i * LANES : i * LANES + HEAD_DIM].astype(f32)

    heads(job_v, grad_value)
    done(5)
    ends[1].wait_recv()
    ends[2].wait_recv()
    grad_tokens[...] = tokens_whole[...].astype(f32)
    done(1)
    heads(job_kq, grad_key, grad_query)
    done(2, 4)
    for copy in sent + shares + smalls + smalls_early + smalls_late + ends:
        copy.wait_send()
    for part in outs:
        for copy in part:
            copy.wait_send()
    for job in jobs:
        job.finish()
    for copy in stores:
        copy.wait()


def finish_kernel(*refs):
    come, go, held = [refs[i * RESULTS : (i + 1) * RESULTS] for i in range(3)]
    loads, stores = refs[3 * RESULTS :]
    copies = [
        pltpu.make_async_copy(come[i], held[i], loads.at[i]) for i in range(RESULTS)
    ]
    for copy in copies:
        copy.start()
    outs = []
    for i in range(RESULTS):
        copies[i].wait()
        copy = pltpu.make_async_copy(held[i], go[i], stores.at[i])
        copy.start()
        outs.append(copy)
    for copy in outs:
        copy.wait()


def whole(shape, dtype):
    return jax.ShapeDtypeStruct(shape, dtype)


VMEM = pl.BlockSpec(memory_space=pltpu.VMEM)
SMEM = pl.BlockSpec(memory_space=pltpu.SMEM)
HBM = pl.BlockSpec(memory_space=pl.ANY)


def dma(*shape):
    return pltpu.SemaphoreType.DMA(shape)


def gathered_plan(
    n, tokens, lengths, query_weight, query_bias, key_weight, value_weight, value_bias,
    conv_kernel, out_weight, out_bias, first_gain, first_shift, up_weight, up_bias, down_weight,
    down_bias, second_gain, second_shift, out_grad,
):
    batch, tok, width = tokens.shape
    rows = batch * tok
    local = query_weight.shape[1]
    hidden = up_weight.shape[1]
    total = n * tok
    block = width // n

    def low(*shape):
        return pltpu.VMEM(shape, bf16)

    def wide(*shape):
        return pltpu.VMEM(shape, f32)

    results = (
        whole((rows, width), bf16),
        whole((rows, width), f32),
        whole((block, local), f32),
        whole((local,), f32),
        whole((block, local), f32),
        whole((block, local), f32),
        whole((local,), f32),
        whole(conv_kernel.shape, f32),
        whole((local, block), f32),
        whole((width,), f32),
        whole((width,), f32),
        whole((width,), f32),
        whole((block, hidden), f32),
        whole((hidden,), f32),
        whole((block, hidden), f32),
        whole((width,), f32),
        whole((width,), f32),
        whole((width,), f32),
        whole((1, 1), f32),
    )
    outs = pl.pallas_call(
        functools.partial(layer_kernel, n),
        out_shape=results,
        in_specs=[SMEM, HBM, HBM, VMEM, HBM, HBM, VMEM, VMEM, HBM, VMEM, VMEM, VMEM, HBM, VMEM, HBM,
                  VMEM, VMEM, VMEM, HBM],
        out_specs=(HBM,) * RESULTS,
        scratch_shapes=[pltpu.VMEM(r.shape, r.dtype) for r in results]
        + [
            low(rows, width), low(local, width), low(local, width), low(local, width),
            low(width, hidden), low(hidden, width), low(rows, width), low(4, 2 * LANES, width),
            low(3, 2, rows, LANES), low(total, LANES), low(total, LANES), low(total + tok, LANES),
            wide(total, LANES), wide(total, LANES), wide(4 * NS_ITERS, LANES, LANES),
            low(n - 1, tok, LANES), low(2, rows, LANES),
            low(4, 2, tok, LANES), low(3, 2, tok, LANES), low(2, rows, LANES), low(rows, width),
            wide(rows, hidden), low(rows, hidden), low(rows, width), low(rows, hidden),
            low(3, 2, tok, width), low(3, 2, tok, width), low(3, tok, width), low(3, tok, width),
            low(total + tok, LANES), low(3, n, tok, LANES), low(3, n, tok // 2, LANES),
            low(3, batch, tok, LANES), low(3, batch, tok // 2, LANES), low(3 * local, width),
            low(rows, width), wide(8, width), wide(4, 8, width), low(n, 2, tok // 2, width),
            low(rows, 3 * local), low(width, hidden), low(width, hidden), low(width, local),
            low(width, LANES), low(width, 2 * LANES), wide(n, 8, width), wide(n, 8, width),
            low(rows, width),
        ]
        + [
            b
            for w in (hidden, hidden, local, LANES, 2 * LANES)
            for b in scatter_buffers(w, block)
        ]
        + [
            dma(8), dma(3, n - 1), dma(3, n - 1), dma(n - 1), dma(n - 1), dma(3), dma(3),
            dma(2, 3), dma(2, 3), dma(2, 3), dma(2, 3), dma(3, 3), dma(3, 3), dma(n - 1),
            dma(n - 1), dma(3, n - 1), dma(3, n - 1), dma(3, 3), dma(3, 3), dma(3, n - 1),
            dma(3, n - 1), dma(JOBS, 7), dma(JOBS, 7), dma(8), dma(8), dma(RESULTS),
        ],
        compiler_params=pltpu.CompilerParams(
            collective_id=0, has_side_effects=True, vmem_limit_bytes=56 * 2**20
        ),
        name="layer",
    )(
        lengths, tokens.reshape(rows, width), query_weight.T, query_bias, key_weight.T,
        value_weight.T, value_bias, conv_kernel, out_weight, out_bias, first_gain, first_shift,
        up_weight, up_bias, down_weight, down_bias, second_gain, second_shift,
        out_grad.reshape(rows, width),
    )
    outs = pl.pallas_call(
        finish_kernel,
        out_shape=results,
        in_specs=[HBM] * RESULTS,
        out_specs=(HBM,) * RESULTS,
        scratch_shapes=[pltpu.VMEM(r.shape, r.dtype) for r in results]
        + [dma(RESULTS), dma(RESULTS)],
        compiler_params=pltpu.CompilerParams(vmem_limit_bytes=60 * 2**20),
        name="finish",
    )(*outs)
    return (
        outs[0].reshape(tokens.shape),
        outs[1].reshape(tokens.shape),
        *outs[2:14],
        outs[14].T,
        *outs[15:18],
        outs[18].reshape(()),
    )


def per_device(seq, tensor, *args):
    batch, tok, width = args[0].shape
    heads = args[7].shape[0]
    if seq == 8 and tensor == 4 and batch == 4 and heads == 3 and tok == 128:
        return gathered_plan(seq, *args)
    return general_plan(*args)


def solution(mesh):
    return jax.shard_map(
        functools.partial(per_device, mesh.shape["seq"], mesh.shape["tensor"]),
        mesh=mesh,
        in_specs=(
            P(None, "seq", None),
            P(),
            P(None, "tensor"),
            P("tensor"),
            P(None, "tensor"),
            P(None, "tensor"),
            P("tensor"),
            P("tensor", None),
            P("tensor", None),
            P(),
            P(),
            P(),
            P(None, "tensor"),
            P("tensor"),
            P("tensor", None),
            P(),
            P(),
            P(),
            P(None, "seq", None),
        ),
        out_specs=(
            P(None, "seq", None),
            P(None, "seq", None),
            P("seq", "tensor"),
            P("tensor"),
            P("seq", "tensor"),
            P("seq", "tensor"),
            P("tensor"),
            P("tensor", None),
            P("tensor", "seq"),
            P(),
            P(),
            P(),
            P("seq", "tensor"),
            P("tensor"),
            P("tensor", "seq"),
            P(),
            P(),
            P(),
            P(),
        ),
        check_vma=False,
    )
```

```python
import functools

import jax
import jax.numpy as jnp
from jax import lax
from jax.experimental import pallas as pl
from jax.experimental.pallas import tpu as pltpu
from jax.sharding import PartitionSpec as P

HEADS = 12
HEAD_DIM = 64
LAND = 64
CONV = 33
NS_ITERS = 6


highest = lax.Precision.HIGHEST
epsilon = 1e-05
negative = -1e30


def joined(x, axis, combine):
    everything = jax.tree.map(lambda part: lax.all_gather(part, axis), x)
    first = jax.tree.map(lambda part: part[0], everything)

    def hop(k, so_far):
        return combine(so_far, jax.tree.map(lambda part: part[k], everything))

    return lax.fori_loop(1, lax.axis_size(axis), hop, first)


def with_halo(block, sides, width):
    for axis, dim in sides:
        count = lax.axis_size(axis)
        forward = [(i, i + 1) for i in range(count - 1)]
        backward = [(target, source) for source, target in forward]
        low = lax.ppermute(
            lax.slice_in_dim(block, block.shape[dim] - width, None, axis=dim), axis, forward
        )
        high = lax.ppermute(lax.slice_in_dim(block, 0, width, axis=dim), axis, backward)
        block = jnp.concatenate([low, block, high], axis=dim)
    return block


def newton_inverse(kernel):
    identity = jnp.eye(kernel.shape[-1], dtype=jnp.float32)
    inverse = jnp.swapaxes(kernel, -1, -2) / jnp.sum(kernel * kernel, axis=(-2, -1), keepdims=True)
    for _ in range(NS_ITERS):
        product = jnp.matmul(kernel, inverse, precision=highest)
        inner_term = jnp.matmul(product, 7.0 * identity - product, precision=highest)
        inner_term = jnp.matmul(product, 15.0 * identity - inner_term, precision=highest)
        inverse = 0.25 * jnp.matmul(inverse, 13.0 * identity - inner_term, precision=highest)
    return inverse


def landmark_core(query_marks, key_marks):
    scores = jnp.einsum(
        "bhjd,bhid->bhji", query_marks, key_marks, precision=highest
    ) * HEAD_DIM ** (-0.5)
    kernel_two = jax.nn.softmax(scores, axis=-1)
    return (kernel_two, newton_inverse(kernel_two))


def normalize(summed, gain_vec, shift_vec):
    middle = jnp.mean(summed, axis=-1, keepdims=True)
    centred = summed - middle
    inverse_std = lax.rsqrt(jnp.mean(centred * centred, axis=-1, keepdims=True) + epsilon)
    normal = centred * inverse_std
    return (normal * gain_vec + shift_vec, normal, inverse_std)


def add_norm(partial_sum, residual, bias_vec, gain_vec, shift_vec):
    summed = lax.psum(partial_sum.astype(jnp.bfloat16), "tensor").astype(jnp.float32)
    return normalize(residual + summed + bias_vec, gain_vec, shift_vec)


def norm_back(grad_hidden, normal, inverse_std, gain_vec):
    grad_normal = grad_hidden * gain_vec
    grad_summed = inverse_std * (
        grad_normal
        - jnp.mean(grad_normal, axis=-1, keepdims=True)
        - normal * jnp.mean(grad_normal * normal, axis=-1, keepdims=True)
    )
    return (grad_summed, jnp.sum(grad_hidden * normal, axis=0), jnp.sum(grad_hidden, axis=0))


def combine_soft(earlier, later):
    top_score = jnp.maximum(earlier[0], later[0])
    weight_first = jnp.exp(earlier[0] - top_score)
    weight_second = jnp.exp(later[0] - top_score)
    return (
        top_score,
        earlier[1] * weight_first + later[1] * weight_second,
        earlier[2] * weight_first[..., None] + later[2] * weight_second[..., None],
    )


def general_plan(
    tokens,
    lengths,
    query_weight,
    query_bias,
    key_weight,
    value_weight,
    value_bias,
    conv_kernel,
    out_weight,
    out_bias,
    first_gain,
    first_shift,
    up_weight,
    up_bias,
    down_weight,
    down_bias,
    second_gain,
    second_shift,
    out_grad,
):
    batch, tok_local, width = tokens.shape
    local_width = query_weight.shape[1]
    local_heads = conv_kernel.shape[0]
    head_dim = local_width // local_heads
    score_scale = HEAD_DIM ** (-0.5)
    rows = batch * tok_local
    half_width = CONV // 2
    f32 = jnp.float32
    bf16 = jnp.bfloat16
    position = lax.axis_index("seq") * tok_local + jnp.arange(tok_local, dtype=jnp.int32)
    inside = position[None, :] < lengths[:, None]
    living = inside.astype(f32)
    segment = position[None, :] * LAND // lengths[:, None]
    onehot = (
        (segment[:, :, None] == jnp.arange(LAND, dtype=jnp.int32)[None, None, :])
        & inside[:, :, None]
    ).astype(f32)
    marks_index = jnp.arange(LAND, dtype=jnp.int32)
    upper = ((marks_index[None, :] + 1) * lengths[:, None] + LAND - 1) // LAND
    lower = (marks_index[None, :] * lengths[:, None] + LAND - 1) // LAND
    counts = (upper - lower).astype(f32)
    flat = tokens.reshape(rows, width)
    flat_wide = flat.astype(f32)
    queries = (jnp.dot(flat, query_weight, preferred_element_type=f32) + query_bias).astype(bf16)
    key_vectors = jnp.dot(flat, key_weight, preferred_element_type=f32).astype(bf16)
    values = (
        (jnp.dot(flat, value_weight, preferred_element_type=f32) + value_bias)
        * living.reshape(rows, 1)
    ).astype(bf16)
    query_three = queries.reshape(batch, tok_local, local_width)
    key_three = key_vectors.reshape(batch, tok_local, local_width)
    value_three = values.reshape(batch, tok_local, local_width)
    onehot_low = onehot.astype(bf16)
    query_sum = jnp.einsum("btj,btf->bjf", onehot_low, query_three, preferred_element_type=f32)
    key_sum = jnp.einsum("btj,btf->bjf", onehot_low, key_three, preferred_element_type=f32)
    query_sum, key_sum = lax.psum((query_sum, key_sum), "seq")
    query_marks = (
        (query_sum / counts[:, :, None])
        .reshape(batch, LAND, local_heads, head_dim)
        .transpose(0, 2, 1, 3)
    )
    key_marks = (
        (key_sum / counts[:, :, None])
        .reshape(batch, LAND, local_heads, head_dim)
        .transpose(0, 2, 1, 3)
    )
    (kernel_two, inverse), core_back = jax.vjp(landmark_core, query_marks, key_marks)
    identity = jnp.eye(LAND, dtype=f32)
    deviation = identity - jnp.matmul(kernel_two, inverse, precision=highest)
    proxy_part = jnp.sum(jnp.sqrt(jnp.sum(deviation * deviation, axis=(-2, -1)))) / (batch * HEADS)
    query_heads = query_three.reshape(batch, tok_local, local_heads, head_dim).astype(f32)
    key_heads = key_three.reshape(batch, tok_local, local_heads, head_dim).astype(f32)
    value_heads = value_three.reshape(batch, tok_local, local_heads, head_dim).astype(f32)
    first_scores = (
        jnp.einsum("bthd,bhjd->bhtj", query_heads, key_marks, precision=highest) * score_scale
    )
    kernel_one = jax.nn.softmax(first_scores, axis=-1)
    third_scores = (
        jnp.einsum("bhjd,bthd->bhjt", query_marks, key_heads, precision=highest) * score_scale
    )
    key_alive = inside[:, None, None, :]
    third_scores = jnp.where(key_alive, third_scores, negative)
    local_top = jnp.max(third_scores, axis=-1)
    local_weights = jnp.where(key_alive, jnp.exp(third_scores - local_top[..., None]), 0.0)
    local_total = jnp.sum(local_weights, axis=-1)
    local_mix = jnp.einsum("bhjt,bthd->bhjd", local_weights, value_heads, precision=highest)
    top_score, total_weight, mixed = joined(
        (local_top, local_total, local_mix), "seq", combine_soft
    )
    third_out = mixed / total_weight[..., None]
    carried = jnp.matmul(inverse, third_out, precision=highest)
    nystrom = jnp.einsum("bhtj,bhjd->bthd", kernel_one, carried, precision=highest).reshape(
        batch, tok_local, local_width
    )
    padded_values = with_halo(value_three, (("seq", 1),), half_width)
    kernel_wide = jnp.repeat(conv_kernel, head_dim, axis=0)
    convolved = jnp.zeros((batch, tok_local, local_width), f32)
    for i in range(CONV):
        convolved = (
            convolved + padded_values[:, i : i + tok_local, :].astype(f32) * kernel_wide[:, i]
        )
    attention = (nystrom + convolved).astype(bf16).reshape(rows, local_width)
    out_part = jnp.dot(attention, out_weight, preferred_element_type=f32)
    hidden_one, normal_one, inverse_one = add_norm(
        out_part, flat_wide, out_bias, first_gain, first_shift
    )
    hidden_low = hidden_one.astype(bf16)
    up_value = jnp.dot(hidden_low, up_weight, preferred_element_type=f32) + up_bias
    activated, gelu_back = jax.vjp(lambda z: jax.nn.gelu(z, approximate=False), up_value)
    activated = activated.astype(bf16)
    down_part = jnp.dot(activated, down_weight, preferred_element_type=f32)
    hidden_two, normal_two, inverse_two = add_norm(
        down_part, hidden_one, down_bias, second_gain, second_shift
    )
    output = hidden_two.astype(bf16).reshape(batch, tok_local, width)
    grad_output = out_grad.reshape(rows, width).astype(f32)
    grad_second_total, grad_second_gain, grad_second_shift = norm_back(
        grad_output, normal_two, inverse_two, second_gain
    )
    down_in = grad_second_total.astype(bf16)
    grad_down_bias = jnp.sum(down_in.astype(f32), axis=0)
    grad_down_weight = jnp.einsum("rf,rd->fd", activated, down_in, preferred_element_type=f32)
    grad_activated = jnp.einsum("rd,fd->rf", down_in, down_weight, preferred_element_type=f32)
    up_in = gelu_back(grad_activated)[0].astype(bf16)
    grad_up_bias = jnp.sum(up_in.astype(f32), axis=0)
    grad_up_weight = jnp.einsum("rd,rf->df", hidden_low, up_in, preferred_element_type=f32)
    hidden_part = jnp.einsum("rf,df->rd", up_in, up_weight, preferred_element_type=f32)
    grad_hidden_one = (
        lax.psum(hidden_part.astype(jnp.bfloat16), "tensor").astype(jnp.float32) + grad_second_total
    )
    grad_first_total, grad_first_gain, grad_first_shift = norm_back(
        grad_hidden_one, normal_one, inverse_one, first_gain
    )
    out_in = grad_first_total.astype(bf16)
    grad_out_bias = jnp.sum(out_in.astype(f32), axis=0)
    grad_out_weight = jnp.einsum("rf,rd->fd", attention, out_in, preferred_element_type=f32)
    grad_attention = jnp.einsum(
        "rd,fd->rf", out_in, out_weight, preferred_element_type=f32
    ).reshape(batch, tok_local, local_width)
    padded_grad = with_halo(grad_attention.astype(jnp.bfloat16), (("seq", 1),), half_width).astype(
        grad_attention.dtype
    )
    grad_conv_values = jnp.zeros((batch, tok_local, local_width), f32)
    conv_columns = []
    for i in range(CONV):
        conv_columns.append(
            jnp.sum(
                grad_attention * padded_values[:, i : i + tok_local, :].astype(f32), axis=(0, 1)
            )
        )
        start_index = 2 * half_width - i
        grad_conv_values = (
            grad_conv_values
            + padded_grad[:, start_index : start_index + tok_local, :] * kernel_wide[:, i]
        )
    grad_conv_kernel = (
        jnp.stack(conv_columns, axis=0).reshape(CONV, local_heads, head_dim).sum(axis=-1).T
    )
    grad_nystrom = grad_attention.reshape(batch, tok_local, local_heads, head_dim)
    grad_kernel_one = jnp.einsum("bthd,bhjd->bhtj", grad_nystrom, carried, precision=highest)
    grad_carried_part = jnp.einsum("bhtj,bthd->bhjd", kernel_one, grad_nystrom, precision=highest)
    grad_first_scores = kernel_one * (
        grad_kernel_one - jnp.sum(kernel_one * grad_kernel_one, axis=-1, keepdims=True)
    )
    grad_query_one = (
        jnp.einsum("bhtj,bhjd->bthd", grad_first_scores, key_marks, precision=highest) * score_scale
    )
    grad_key_marks_part = (
        jnp.einsum("bhtj,bthd->bhjd", grad_first_scores, query_heads, precision=highest)
        * score_scale
    )
    grad_carried, grad_key_marks_one = lax.psum((grad_carried_part, grad_key_marks_part), "seq")
    grad_third_out = jnp.matmul(jnp.swapaxes(inverse, -1, -2), grad_carried, precision=highest)
    grad_inverse = jnp.matmul(grad_carried, jnp.swapaxes(third_out, -1, -2), precision=highest)
    grad_query_marks_two, grad_key_marks_two = core_back((jnp.zeros_like(kernel_two), grad_inverse))
    third_prob = local_weights * jnp.exp(local_top - top_score)[..., None] / total_weight[..., None]
    delta_term = jnp.sum(grad_third_out * third_out, axis=-1)
    grad_prob_value = jnp.einsum("bhjd,bthd->bhjt", grad_third_out, value_heads, precision=highest)
    grad_third_scores = third_prob * (grad_prob_value - delta_term[..., None])
    grad_value_three = jnp.einsum("bhjt,bhjd->bthd", third_prob, grad_third_out, precision=highest)
    grad_key_three = (
        jnp.einsum("bhjt,bhjd->bthd", grad_third_scores, query_marks, precision=highest)
        * score_scale
    )
    grad_query_marks_part = (
        jnp.einsum("bhjt,bthd->bhjd", grad_third_scores, key_heads, precision=highest) * score_scale
    )
    grad_query_marks_three = lax.psum(grad_query_marks_part, "seq")
    grad_query_marks = (grad_query_marks_two + grad_query_marks_three) / counts[:, None, :, None]
    grad_key_marks = (grad_key_marks_one + grad_key_marks_two) / counts[:, None, :, None]
    grad_query_marks = grad_query_marks.transpose(0, 2, 1, 3).reshape(batch, LAND, local_width)
    grad_key_marks = grad_key_marks.transpose(0, 2, 1, 3).reshape(batch, LAND, local_width)
    grad_query_seg = jnp.einsum("btj,bjf->btf", onehot, grad_query_marks, precision=highest)
    grad_key_seg = jnp.einsum("btj,bjf->btf", onehot, grad_key_marks, precision=highest)
    query_in = (
        (grad_query_one.reshape(batch, tok_local, local_width) + grad_query_seg)
        .astype(bf16)
        .reshape(rows, local_width)
    )
    key_in = (
        (grad_key_three.reshape(batch, tok_local, local_width) + grad_key_seg)
        .astype(bf16)
        .reshape(rows, local_width)
    )
    value_in = (grad_value_three.reshape(batch, tok_local, local_width) + grad_conv_values).astype(
        bf16
    )
    value_in = jnp.where(inside[:, :, None], value_in, jnp.zeros_like(value_in)).reshape(
        rows, local_width
    )
    grad_query_bias = jnp.sum(query_in.astype(f32), axis=0)
    grad_value_bias = jnp.sum(value_in.astype(f32), axis=0)
    grad_query_weight = jnp.einsum("rd,rf->df", flat, query_in, preferred_element_type=f32)
    grad_key_weight = jnp.einsum("rd,rf->df", flat, key_in, preferred_element_type=f32)
    grad_value_weight = jnp.einsum("rd,rf->df", flat, value_in, preferred_element_type=f32)
    input_part = (
        jnp.einsum("rf,df->rd", query_in, query_weight, preferred_element_type=f32)
        + jnp.einsum("rf,df->rd", key_in, key_weight, preferred_element_type=f32)
        + jnp.einsum("rf,df->rd", value_in, value_weight, preferred_element_type=f32)
    )
    input_sum, proxy_norm = (
        lax.psum(input_part.astype(jnp.bfloat16), "tensor").astype(jnp.float32),
        lax.psum(proxy_part.astype(jnp.bfloat16), "tensor").astype(jnp.float32),
    )
    grad_tokens = (grad_first_total + input_sum).reshape(batch, tok_local, width)
    (
        grad_query_weight,
        grad_key_weight,
        grad_value_weight,
        grad_out_weight,
        grad_up_weight,
        grad_down_weight,
    ) = (
        lax.psum_scatter(grad_query_weight, "seq", scatter_dimension=0, tiled=True),
        lax.psum_scatter(grad_key_weight, "seq", scatter_dimension=0, tiled=True),
        lax.psum_scatter(grad_value_weight, "seq", scatter_dimension=0, tiled=True),
        lax.psum_scatter(grad_out_weight, "seq", scatter_dimension=1, tiled=True),
        lax.psum_scatter(grad_up_weight, "seq", scatter_dimension=0, tiled=True),
        lax.psum_scatter(grad_down_weight, "seq", scatter_dimension=1, tiled=True),
    )
    (
        grad_query_bias,
        grad_value_bias,
        grad_conv_kernel,
        grad_out_bias,
        grad_first_gain,
        grad_first_shift,
        grad_up_bias,
        grad_down_bias,
        grad_second_gain,
        grad_second_shift,
    ) = lax.psum(
        (
            grad_query_bias,
            grad_value_bias,
            grad_conv_kernel,
            grad_out_bias,
            grad_first_gain,
            grad_first_shift,
            grad_up_bias,
            grad_down_bias,
            grad_second_gain,
            grad_second_shift,
        ),
        "seq",
    )
    return (
        output,
        grad_tokens,
        grad_query_weight,
        grad_query_bias,
        grad_key_weight,
        grad_value_weight,
        grad_value_bias,
        grad_conv_kernel,
        grad_out_weight,
        grad_out_bias,
        grad_first_gain,
        grad_first_shift,
        grad_up_weight,
        grad_up_bias,
        grad_down_weight,
        grad_down_bias,
        grad_second_gain,
        grad_second_shift,
        proxy_norm,
    )


MESH = pl.DeviceIdType.MESH
LANES = 2 * HEAD_DIM
f32 = jnp.float32
bf16 = jnp.bfloat16
NN = (1, 0)
NT = (1, 1)
TN = (0, 0)


def dot(a, b, dims=NN):
    return lax.dot_general(
        a, b, (((dims[0],), (dims[1],)), ((), ())), preferred_element_type=f32
    )


def split(x):
    if x.dtype == bf16:
        return (x,)
    top = x.astype(bf16)
    return (top, (x - top.astype(f32)).astype(bf16))


def fine(a, b, dims=NN):
    a, b = split(a), split(b)
    total = dot(a[0], b[0], dims)
    if len(b) > 1:
        total = total + dot(a[0], b[1], dims)
    if len(a) > 1:
        total = total + dot(a[1], b[0], dims)
    return total


def iota(shape, dim):
    return lax.broadcasted_iota(jnp.int32, shape, dim)


def block_mask():
    shape = (LANES, LANES)
    return (iota(shape, 0) < HEAD_DIM) == (iota(shape, 1) < HEAD_DIM)


def eye():
    return jnp.where(iota((LANES, LANES), 0) == iota((LANES, LANES), 1), 1.0, 0.0).astype(f32)


def block_sums(x, same_head):
    ones = jnp.where(same_head, 1.0, 0.0).astype(bf16)
    return jnp.where(same_head, fine(fine(ones, x), ones), 1.0)


def taps_matrix(row, tok):
    return pltpu.roll(jnp.broadcast_to(row, (tok, 2 * tok)), 0, 1, stride=1, stride_axis=0)


def taps_row(taps, head, tok):
    row = taps[pl.ds(head, 1), :]
    return jnp.concatenate([row, jnp.zeros((1, 2 * tok - CONV), f32)], axis=1)


def conv_block(matrices, window):
    first = fine(matrices[0], window)
    second = fine(matrices[1], window)
    return jnp.where(iota(first.shape, 1) < HEAD_DIM, first, second)


def greet(devices):
    barrier = pltpu.get_barrier_semaphore()
    for device in devices:
        pl.semaphore_signal(barrier, inc=1, device_id=device, device_id_type=MESH)
    return barrier


def around(n, me, tensor):
    return [(lax.rem(me + d, n), tensor) for d in range(1, n)]


def others(me, tensor):
    core = tensor + 1 - 2 * (tensor % 2)
    return [(me, core), (me, lax.rem(tensor + 2, 4)), (me, lax.rem(core + 2, 4))]


def paired(y):
    return y[:, :LANES], jnp.concatenate(
        [y[:, LANES : LANES + HEAD_DIM], y[:, HEAD_DIM:LANES]], axis=1
    )


def remote(src, dst, send, recv, device):
    return pltpu.make_async_remote_copy(
        src_ref=src, dst_ref=dst, send_sem=send, recv_sem=recv, device_id=device,
        device_id_type=MESH,
    )


def member_rows(length, total):
    j = iota((LANES, total), 0) % LAND
    t = iota((LANES, total), 1)
    inside = (t * LAND >= j * length) & (t * LAND < (j + 1) * length) & (t < length)
    return jnp.where(inside, 1.0, 0.0).astype(bf16)


def member_columns(length, total):
    j = iota((total, LANES), 1) % LAND
    t = iota((total, LANES), 0)
    inside = (t * LAND >= j * length) & (t * LAND < (j + 1) * length) & (t < length)
    return jnp.where(inside, 1.0, 0.0).astype(bf16)


def segment_counts(length):
    j = iota((LANES, LANES), 0) % LAND
    upper = ((j + 1) * length + LAND - 1) // LAND
    lower = (j * length + LAND - 1) // LAND
    return (upper - lower).astype(f32)


def normal_of(summed):
    middle = jnp.mean(summed, axis=-1, keepdims=True)
    centred = summed - middle
    inverse_std = lax.rsqrt(jnp.mean(centred * centred, axis=-1, keepdims=True) + epsilon)
    return centred * inverse_std, inverse_std


def before_norm(grad, normal, inverse_std, gain):
    grad_normal = grad * gain
    return inverse_std * (
        grad_normal
        - jnp.mean(grad_normal, axis=-1, keepdims=True)
        - normal * jnp.mean(grad_normal * normal, axis=-1, keepdims=True)
    )


def block_rows(t, tok):
    return pl.ds(pl.multiple_of(t * tok, tok), tok)


class Scatter:
    def __init__(self, index, me, tensor, source, columns, buffers, send, recv, order):
        self.index, self.source, self.columns = index, source, pl.ds(*columns)
        self.first_in, self.held, self.second_in, self.pair, self.last_in, self.cross_in = buffers
        self.block = source.shape[0] // 8
        self.weights = [2**bit for bit in order]
        self.bits = [(me // weight) % 2 for weight in self.weights]
        self.partners = [
            (me + weight * (1 - 2 * bit), tensor) for weight, bit in zip(self.weights, self.bits)
        ]
        self.send, self.recv = send, recv
        self.copies = []

    def rows(self, slot, bit):
        index = (slot // 2) * self.weights[2] + (slot % 2) * self.weights[1] + bit * self.weights[0]
        return pl.ds(pl.multiple_of(index * self.block, 16), self.block)

    def copy(self, src, dst, k, stage):
        copy = remote(
            src, dst, self.send.at[self.index, k], self.recv.at[self.index, k],
            self.partners[stage],
        )
        copy.start()
        self.copies.append(copy)

    def first(self, slots=range(4)):
        for slot in slots:
            self.copy(self.source.at[self.rows(slot, 1 - self.bits[0]), self.columns], self.first_in.at[slot], slot, 0)

    def second(self):
        for slot in range(4):
            self.copies[slot].wait_recv()
        for slot in range(4):
            mine = self.source[self.rows(slot, self.bits[0]), self.columns]
            self.held[slot] = self.joined(mine, self.first_in[slot])
        for k in range(2):
            self.copy(self.held.at[2 * k + 1 - self.bits[1]], self.second_in.at[k], 4 + k, 1)

    def joined(self, mine, come):
        return (mine.astype(f32) + come.astype(f32)).astype(bf16)

    def third(self):
        for k in range(2):
            self.copies[4 + k].wait_recv()
        for k in range(2):
            both = self.held[2 * k + self.bits[1]].astype(f32) + self.second_in[k].astype(f32)
            self.pair[k] = both.astype(bf16)
        self.copy(self.pair.at[1 - self.bits[2]], self.last_in, 6, 2)

    def last(self, write):
        self.copies[6].wait_recv()
        write(self.pair[self.bits[2]].astype(f32) + self.last_in[...].astype(f32))

    def finish(self):
        for copy in self.copies:
            copy.wait_send()


class Line(Scatter):
    def __init__(self, *args):
        super().__init__(*args)
        z = self.bits[1] + 2 * self.bits[2]
        right = z // 2
        self.end = self.bits[1] == right
        self.inner = self.bits[1] != right
        self.slots = [k * (1 - right) + (3 - k) * right for k in range(4)]
        self.partners[2] = (2 * (3 - z) + self.bits[0], self.partners[0][1])
        self.own = {}

    def step(self, src, dst, k, stage):
        copy = remote(
            src, dst, self.send.at[self.index, k], self.recv.at[self.index, k],
            self.partners[stage],
        )
        self.own[k] = copy
        return copy

    def second(self):
        for slot in range(4):
            self.copies[slot].wait_recv()
        for slot in range(4):
            mine = self.source[self.rows(slot, self.bits[0]), self.columns]
            self.held[slot] = self.joined(mine, self.first_in[slot])
        come = (self.second_in.at[0], self.second_in.at[1], self.last_in)
        sends = [
            self.step(self.held.at[self.slots[3 - k]], come[k], 4 + k, 1) for k in range(3)
        ]

        @pl.when(self.end)
        def _():
            for copy in sends:
                copy.start()

    def third(self):
        sends = [
            self.step(self.pair.at[k], self.cross_in.at[k], 7 + k, 2) for k in range(2)
        ]

        @pl.when(self.inner)
        def _():
            for k in range(2):
                self.own[4 + k].wait_recv()
                self.pair[k] = self.joined(self.held[self.slots[3 - k]], self.second_in[k])
                sends[k].start()

    def fourth(self):
        back = self.step(self.first_in.at[2], self.first_in.at[3], 9, 1)

        @pl.when(self.inner)
        def _():
            self.own[7].wait_recv()
            self.first_in[2] = self.joined(self.held[self.slots[0]], self.cross_in[0])
            back.start()

    def last(self, write):
        @pl.when(self.inner)
        def _():
            self.own[6].wait_recv()
            self.own[8].wait_recv()
            write(
                self.held[self.slots[1]].astype(f32)
                + self.last_in[...].astype(f32)
                + self.cross_in[1].astype(f32)
            )

        @pl.when(self.end)
        def _():
            self.own[9].wait_recv()
            write(self.held[self.slots[0]].astype(f32) + self.first_in[3].astype(f32))

    def finish(self):
        super().finish()

        @pl.when(self.end)
        def _():
            for k in range(4, 7):
                self.own[k].wait_send()

        @pl.when(self.inner)
        def _():
            for k in range(7, 10):
                self.own[k].wait_send()


class Heads(Scatter):
    def joined(self, mine, come):
        even = self.bits[0] == 0
        pair, other = jnp.where(even, mine, come), jnp.where(even, come, mine)
        return jnp.concatenate(
            [pair] + [other[:, k : k + HEAD_DIM] for k in range(0, other.shape[1], LANES)], axis=1
        )


def scatter_buffers(first, width, block):
    return [
        pltpu.VMEM((4, block, first), bf16),
        pltpu.VMEM((4, block, width), bf16),
        pltpu.VMEM((2, block, width), bf16),
        pltpu.VMEM((2, block, width), bf16),
        pltpu.VMEM((block, width), bf16),
        pltpu.VMEM((2, block, width), bf16),
    ]


def total_of(v):
    return jnp.sum(v, axis=0, keepdims=True)


def packed(block):
    middle = block.shape[-2] // 2
    first, second = block[..., :middle, :HEAD_DIM], block[..., middle:, :HEAD_DIM]
    return jnp.concatenate([first, second], axis=-1)


def unpacked(block):
    return jnp.concatenate([block[..., :HEAD_DIM], block[..., HEAD_DIM:]], axis=-2)


class Ring:
    def __init__(
        self, tensor, peers, parts, core_out, core_in, y_out, y_in, ag_send, ag_recv, sum_send,
        sum_recv,
    ):
        self.tensor, self.place = tensor, tensor % 2
        self.core, self.across, self.far = peers
        self.near_pair = tensor - self.place
        self.far_pair = lax.rem(self.near_pair + 2, 4)
        self.parts, self.core_out, self.core_in = parts, core_out, core_in
        self.y_out, self.y_in = y_out, y_in
        self.ag, self.sums = (ag_send, ag_recv), (sum_send, sum_recv)
        self.copies = {}

    def send(self, name, src, dst, sems, at, device):
        copy = remote(src, dst, sems[0].at[at], sems[1].at[at], device)
        copy.start()
        self.copies[name] = copy

    def share(self, phase, c, held):
        mine = held.at[c, self.tensor]
        self.send((phase, c, "y"), mine, mine, self.ag, (phase, c, 0), self.across)
        self.send((phase, c, "core"), mine, mine, self.ag, (phase, c, 1), self.core)

    def work(self, phase, c, side, value):
        self.parts[phase, c, side] = value.reshape(2, -1, value.shape[1])
        self.core_out[phase, c, side] = self.parts[phase, c, side, 1 - self.place].astype(bf16)
        self.send(
            (phase, c, side), self.core_out.at[phase, c, side], self.core_in.at[phase, c, side],
            self.sums, (phase, c, side), self.core,
        )

    def run(self, phase, held, work):
        for c in range(2):
            self.copies[phase, c, "core"].wait_recv()
            self.work(phase, c, 0, work(c, self.near_pair))
        for c in range(2):
            self.copies[phase, c, "y"].wait_recv()
            other = held.at[c, self.across[1]]
            self.send((phase, c, "pass"), other, other, self.ag, (phase, c, 2), self.core)
            if c == 1:
                self.cross(phase, 0)
            self.copies[phase, c, "pass"].wait_recv()
            self.work(phase, c, 1, work(c, self.far_pair))
        self.cross(phase, 1)

    def cross(self, phase, c):
        self.copies[phase, c, 1].wait_recv()
        both = self.parts[phase, c, 1, self.place] + self.core_in[phase, c, 1].astype(f32)
        self.y_out[phase, c] = both.astype(bf16)
        self.send(
            (phase, c, "sum"), self.y_out.at[phase, c], self.y_in.at[phase, c], self.sums,
            (phase, c, 2), self.across,
        )

    def total(self, phase, c):
        self.copies[phase, c, 0].wait_recv()
        self.copies[phase, c, "sum"].wait_recv()
        return (
            self.parts[phase, c, 0, self.place]
            + self.core_in[phase, c, 0].astype(f32)
            + self.y_in[phase, c].astype(f32)
        )


JOBS = 7
RESULTS = 19


def layer_kernel(
    n, lengths, x_far, wq_far, qb, wk_far, wv_far, vb, taps, out_far, out_bias, gain_one,
    shift_one, up_far, up_bias, down_far, down_bias, gain_two, shift_two, grad_far,
    *rest,
):
    results, rest = rest[:RESULTS], rest[RESULTS:]
    ready, rest = rest[:RESULTS], rest[RESULTS:]
    layer_body(
        n, lengths, x_far, wq_far, qb, wk_far, wv_far, vb, taps, out_far, out_bias, gain_one,
        shift_one, up_far, up_bias, down_far, down_bias, gain_two, shift_two, grad_far, results,
        ready, *rest,
    )


def layer_body(
    n, lengths, x_far, wq_far, qb, wk_far, wv_far, vb, taps, out_far, out_bias, gain_one,
    shift_one, up_far, up_bias, down_far, down_bias, gain_two, shift_two, grad_far, results, ready,
    x, wk, wq, wv, up_weight, down_weight, out_grad, out_weight, out_whole,
    stage, ks, qs, vs, k1, p3, newton, out_stage, out_single, attn_pair, attn_single,
    pairs_in, singles_in, heads_out, grad_attn, hidden, slope, active, down_in, up_in,
    core_out, core_in, y_out, y_in, core_last, y_last,
    gs, back_stage, back_single, come_pair, come_single, weight_in, out_in, early, early_tensor, tokens_own, tokens_low, source_up,
    source_down, source_out, source_v, source_kq, early_out, early_in, late_seq, tokens_whole,
    parts_held,
    *rest,
):
    buffers, sems = rest[: 6 * JOBS], rest[6 * JOBS :]
    (load, send, recv, out_send, out_recv, whole_send, whole_recv, a2a_send, a2a_recv, ag_send,
     ag_recv, sum_send, sum_recv, grad_send, grad_recv, back_send, back_recv, share_send,
     share_recv, small_send, small_recv, job_send, job_recv, own_send, own_recv, last_send, last_recv,
     store) = sems
    (output, grad_tokens, grad_query, query_bias, grad_key, grad_value, value_bias, conv, grad_out,
     out_bias_grad, first_gain, first_shift, grad_up, up_bias_grad, grad_down, down_bias_grad,
     second_gain, second_shift, proxy) = ready
    stores = []

    def done(*numbers):
        for i in numbers:
            copy = pltpu.make_async_copy(ready[i], results[i], store.at[i])
            copy.start()
            stores.append(copy)

    me = lax.axis_index("seq")
    tensor = lax.axis_index("tensor")
    rows, width = x.shape
    batch = n // 2
    tok = rows // batch
    total = n * tok
    half = CONV // 2
    own, side = me // 2, me % 2
    scale = HEAD_DIM ** (-0.5)
    ring_peers = around(n, me, tensor)
    peers = others(me, tensor)
    core, across, far = peers
    mine = block_rows(tensor, tok)
    local = wk.shape[0]
    barrier = greet(ring_peers + peers)
    loads = []
    for i, (source, target) in enumerate((
        (x_far, x), (wk_far, wk), (wq_far, wq), (wv_far, wv),
        (out_far, out_weight), (up_far, up_weight),
        (down_far, down_weight), (grad_far, out_grad),
    )):
        copy = pltpu.make_async_copy(source, target, load.at[i])
        copy.start()
        loads.append(copy)
    hidden_width = up_weight.shape[1]
    span = hidden_width // 2
    jobs = [
        kind(i, me, tensor, source, columns, buffers[6 * i : 6 * i + 6], job_send, job_recv, order)
        for i, (kind, source, columns, order) in enumerate((
            (Line, source_down, (0, span), (0, 1, 2)),
            (Scatter, source_down, (span, span), (1, 0, 2)),
            (Line, source_up, (0, span), (0, 1, 2)),
            (Line, source_up, (span, span), (0, 1, 2)),
            (Scatter, source_out, (0, local), (0, 1, 2)),
            (Heads, source_v, (0, LANES), (0, 1, 2)),
            (Heads, source_kq, (0, 2 * LANES), (0, 1, 2)),
        ))
    ]
    job_down, job_up = jobs[0:2], jobs[2:4]
    job_out, job_v, job_kq = jobs[4:]
    sent = []

    owned = (ks, qs, vs)
    offsets = (0, 0, half)
    for padded in (vs, gs):
        padded[0:half] = jnp.zeros((half, LANES), bf16)
        padded[half + total : total + tok] = jnp.zeros((tok - half, LANES), bf16)
    even = side == 0

    arrivals = [[], [], []]

    def spread(i):
        here = pl.ds(pl.multiple_of(offsets[i] + me * tok, 16), tok)
        for d in range(1, n):
            peer = lax.rem(me + d, n)
            copy = remote(
                stage.at[i, peer % 2, block_rows(peer // 2, tok)], owned[i].at[here],
                send.at[i, d - 1], recv.at[i, d - 1], (peer, tensor),
            )
            copy.start()
            arrivals[i].append(copy)
            if i != 1:
                sent.append(copy)
        owned[i][here] = stage[i, side, block_rows(own, tok)]

    loads[0].wait()
    loads[1].wait()
    y = dot(x[...], wk[...], NT)
    stage[0, 0], stage[0, 1] = paired(y.astype(bf16))
    pl.semaphore_wait(barrier, n + 2)
    spread(0)
    loads[2].wait()
    y = dot(x[...], wq[...], NT) + qb[...].reshape(1, local)
    stage[1, 0], stage[1, 1] = paired(y.astype(bf16))
    spread(1)
    loads[3].wait()
    y = dot(x[...], wv[...], NT) + vb[...].reshape(1, local)
    position = me * tok + iota((tok, local), 0)
    y = jnp.concatenate(
        [
            jnp.where(position < lengths[b], y[b * tok : (b + 1) * tok], 0.0)
            for b in range(batch)
        ],
        axis=0,
    )
    stage[2, 0], stage[2, 1] = paired(y.astype(bf16))
    loads[4].wait()
    whole_parts = []
    pair_rows = block_rows(tensor, LANES)
    single_rows = pl.ds(pl.multiple_of(4 * LANES + tensor * HEAD_DIM, HEAD_DIM), HEAD_DIM)
    first, single = out_weight[:LANES], out_weight[LANES:]
    out_whole[pair_rows] = jnp.where(
        even, first, jnp.concatenate([single, first[HEAD_DIM:]], axis=0)
    )
    out_whole[single_rows] = jnp.where(even, single, first[:HEAD_DIM])
    for i, device in enumerate(peers):
        for j, at in enumerate((pair_rows, single_rows)):
            part = out_whole.at[at]
            copy = remote(part, part, whole_send.at[i, j], whole_recv.at[i, j], device)
            copy.start()
            whole_parts.append(copy)

    length = lengths[own]
    same_head = block_mask()
    identity = eye()
    ones = jnp.where(same_head, 1.0, 0.0).astype(bf16)
    members = member_rows(length, total)
    counts = segment_counts(length)
    matrices = [taps_matrix(taps_row(taps, h, tok), tok) for h in (2 * side, 1)]
    flip = jnp.where(
        iota((2 * tok, 2 * tok), 0) + iota((2 * tok, 2 * tok), 1) == CONV - 1, 1.0, 0.0
    ).astype(bf16)
    reverse = [
        taps_matrix(
            fine(jnp.broadcast_to(taps_row(taps, h, tok), (8, 2 * tok)), flip)[0:1], tok
        )
        for h in (2 * side, 1)
    ]
    for i, w in enumerate((wk, wq, wv)):
        pair, single = w[:LANES], w[LANES:]
        weight_in[i * LANES : (i + 1) * LANES] = jnp.where(
            even, pair, jnp.concatenate([single, pair[HEAD_DIM:]], axis=0)
        )
        start = 3 * LANES + i * HEAD_DIM
        weight_in[start : start + HEAD_DIM] = jnp.where(even, single, pair[:HEAD_DIM])
    for copy in arrivals[0]:
        copy.wait_recv()
    keys = ks[...]
    key_marks = jnp.where(same_head, dot(members, keys) / counts, 0.0)
    for copy in arrivals[1]:
        copy.wait_send()
    spread(2)
    for copy in arrivals[1]:
        copy.wait_recv()
    queries = qs[...]
    query_marks = jnp.where(same_head, dot(members, queries) / counts, 0.0)
    scores = jnp.where(same_head, fine(query_marks, key_marks, NT) * scale, negative)
    weights = jnp.exp(scores - jnp.max(scores, axis=1, keepdims=True))
    kernel_two = weights / jnp.sum(weights, axis=1, keepdims=True)
    inverse = jnp.where(
        same_head, kernel_two.T / block_sums(kernel_two * kernel_two, same_head), 0.0
    )
    for step in range(NS_ITERS):
        product = fine(kernel_two, inverse)
        inner_one = fine(product, 7.0 * identity - product)
        inner_two = fine(product, 15.0 * identity - inner_one)
        newton[4 * step] = inverse
        newton[4 * step + 1] = product
        newton[4 * step + 2] = inner_one
        newton[4 * step + 3] = inner_two
        inverse = 0.25 * fine(inverse, 13.0 * identity - inner_two)

    deviation = identity - fine(kernel_two, inverse)
    norms = jnp.sqrt(block_sums(deviation * deviation, same_head))
    first, second = norms[0:1, 0:1], norms[LANES - 1 :, LANES - 1 :]
    norm_sum = jnp.where(side == 0, first + second, first) / (batch * HEADS)
    early[7:8] = jnp.broadcast_to(norm_sum, (1, width))

    first_scores = fine(queries, key_marks, NT) * scale
    left = iota(first_scores.shape, 1) < HEAD_DIM
    top_left = jnp.max(jnp.where(left, first_scores, negative), axis=1, keepdims=True)
    top_right = jnp.max(jnp.where(left, negative, first_scores), axis=1, keepdims=True)
    weights = jnp.exp(first_scores - jnp.where(left, top_left, top_right))
    k1[...] = weights / fine(weights, ones)

    third_scores = fine(keys, query_marks, NT) * scale
    alive = iota(third_scores.shape, 0) < length
    third_scores = jnp.where(alive, third_scores, negative)
    weights = jnp.exp(third_scores - jnp.max(third_scores, axis=0, keepdims=True))
    weights = jnp.where(alive, weights, 0.0)
    third_prob = weights / jnp.sum(weights, axis=0, keepdims=True)
    p3[...] = third_prob

    for copy in arrivals[2]:
        copy.wait_recv()
    values = vs[half : half + total]
    third_out = jnp.where(same_head, fine(third_prob, values, TN), 0.0)
    carried = fine(inverse, third_out)

    attn_parts = []
    for d in range(1, n + 1):
        peer = lax.rem(me + d, n)
        start = pl.multiple_of(peer * tok, tok)
        nystrom = fine(k1[pl.ds(start, tok)], carried)
        convolved = conv_block(matrices, vs[pl.ds(start, 2 * tok)])
        low = (nystrom + convolved).astype(bf16)
        if d == n:
            attn_pair[own] = low
            continue
        if d % 2 == 0:
            source, target = out_stage.at[d - 1], attn_pair.at[own]
            source[...] = low
        else:
            source, target = out_single.at[d - 1], attn_single.at[own]
            source[...] = packed(low)
        copy = remote(source, target, out_send.at[d - 1], out_recv.at[d - 1], (peer, tensor))
        copy.start()
        attn_parts.append(copy)
    for copy in whole_parts + attn_parts:
        copy.wait_recv()
    sent += whole_parts + attn_parts

    parts = []
    for i in (2, 1, 0):
        t = peers[i][1]
        for j, (held, come) in enumerate(((attn_pair, pairs_in), (attn_single, singles_in))):
            copy = remote(
                held.at[t], come.at[tensor], a2a_send.at[0, i, j], a2a_recv.at[0, i, j], peers[i]
            )
            copy.start()
            parts.append(copy)
    pairs_in[tensor] = attn_pair[tensor]
    singles_in[tensor] = attn_single[tensor]
    z, side_of_chip = me // 2, tensor % 2
    beside = (me + 1 - 2 * side, tensor)
    token_parts = []

    def give_tokens(src, dst, i, device):
        copy = remote(src, dst, own_send.at[i], own_recv.at[i], device)
        copy.start()
        token_parts.append(copy)

    def half_block(b):
        start = pl.multiple_of(b * tok + side_of_chip * (tok // 2), tok // 2)
        return pl.ds(start, tok // 2)

    tokens_own[me, side_of_chip] = x[half_block(own)]
    for k in range(1, 4):
        peer = lax.rem(z + k, 4)
        give_tokens(
            x.at[half_block(peer)], tokens_own.at[me, side_of_chip], k - 1,
            (2 * peer + side, tensor),
        )
    half_own = tokens_own.at[me, side_of_chip]
    give_tokens(half_own, half_own, 3, beside)

    def pass_tokens():
        for k in range(1, 4):
            token_parts[k - 1].wait_recv()
        for k in range(1, 4):
            come = tokens_own.at[2 * lax.rem(z + 4 - k, 4) + side, side_of_chip]
            give_tokens(come, come, 3 + k, beside)

    for copy in loads[5:]:
        copy.wait()
    for copy in parts:
        copy.wait_recv()
    sent += parts
    def line(vector):
        return vector[...].reshape(1, vector.shape[0])

    piece = tok // 2
    chunks = range(2)
    ring = Ring(
        tensor, peers, parts_held, core_out, core_in, y_out, y_in, ag_send, ag_recv, sum_send,
        sum_recv,
    )

    def rows_of(c):
        return pl.ds(pl.multiple_of(tensor * tok + c * piece, piece), piece)

    def normed(c):
        at = slice(c * piece, (c + 1) * piece)
        lanes = slice(c * HEAD_DIM, (c + 1) * HEAD_DIM)
        heads = jnp.concatenate(
            [pairs_in[t, at] for t in range(4)] + [singles_in[t, :, lanes] for t in range(4)],
            axis=1,
        )
        branch = dot(heads, out_whole[...])
        first_total = x[rows_of(c)].astype(f32) + (branch + line(out_bias))
        normal, inverse_std = normal_of(first_total)
        whole_row = normal * line(gain_one) + line(shift_one)
        hidden[c, tensor] = whole_row.astype(bf16)
        ring.share(0, c, hidden)
        return normal, inverse_std, whole_row

    def up(c, t):
        at = pl.ds(t, 2)
        value = dot(hidden[c, at].reshape(tok, width), up_weight[...]) + line(up_bias)
        half_erf = 0.5 * (1.0 + lax.erf(value * (0.5**0.5)))
        density = jnp.exp(-0.5 * value * value) * (0.5 / jnp.pi) ** 0.5
        slope[c, at] = (half_erf + value * density).reshape(2, piece, hidden_width)
        low = (value * half_erf).astype(bf16)
        active[c, at] = low.reshape(2, piece, hidden_width)
        return dot(low, down_weight[...])

    def down(c, t):
        at = pl.ds(t, 2)
        grad = dot(down_in[c, at].reshape(tok, width), down_weight[...], NT)
        low = (grad * slope[c, at].reshape(tok, hidden_width)).astype(bf16)
        up_in[c, at] = low.reshape(2, piece, hidden_width)
        return dot(low, up_weight[...], NT)

    after_norm_one = [normed(c) for c in chunks]
    ring.run(0, hidden, up)
    pass_tokens()

    grads_second, sums_second = [], []
    for c in chunks:
        hidden_one = after_norm_one[c][2]
        second_total = hidden_one + (ring.total(0, c) + line(down_bias))
        normal, inverse_std = normal_of(second_total)
        output[rows_of(c)] = (normal * line(gain_two) + line(shift_two)).astype(bf16)
        grad_output = out_grad[rows_of(c)].astype(f32)
        grad_second = before_norm(grad_output, normal, inverse_std, line(gain_two))
        low = grad_second.astype(bf16)
        down_in[c, tensor] = low
        ring.share(1, c, down_in)
        grads_second.append(grad_second)
        sums_second.append(
            (total_of(grad_output * normal), total_of(grad_output), total_of(low.astype(f32)))
        )
    ring.run(1, down_in, down)
    everything = (rows, width)
    every_hidden = (rows, hidden_width)
    source_down[...] = dot(
        down_in[...].reshape(everything), active[...].reshape(every_hidden), TN
    ).astype(bf16)
    for job in job_down:
        job.first()

    grads_first, sums_first = [], []
    parts = []
    for c in chunks:
        normal, inverse_std, _ = after_norm_one[c]
        grad_hidden = grads_second[c] + ring.total(1, c)
        grad_first = before_norm(grad_hidden, normal, inverse_std, line(gain_one))
        low = grad_first.astype(bf16)
        out_in[rows_of(c)] = low
        heads = dot(low, out_whole[...], NT).astype(bf16)
        at = slice(c * piece, (c + 1) * piece)
        for t in range(4):
            start = 4 * LANES + t * HEAD_DIM
            pair = heads[:, t * LANES : (t + 1) * LANES]
            heads_out[t, 0, at] = pair
            heads_out[t, 1, at] = jnp.concatenate(
                [heads[:, start : start + HEAD_DIM], pair[:, HEAD_DIM:]], axis=1
            )
        for i in (2, 1, 0):
            copy = remote(
                heads_out.at[peers[i][1], :, pl.ds(c * piece, piece)],
                grad_attn.at[:, rows_of(c)], a2a_send.at[1, i, c], a2a_recv.at[1, i, c], peers[i],
            )
            copy.start()
            parts.append(copy)
        grads_first.append(grad_first)
        sums_first.append(
            (total_of(grad_hidden * normal), total_of(grad_hidden), total_of(low.astype(f32)))
        )
    grad_attn[:, mine] = heads_out[tensor]
    sent += parts
    source_up[...] = dot(
        hidden[...].reshape(everything), up_in[...].reshape(every_hidden), TN
    ).astype(bf16)
    for i in range(3):
        early[i : i + 1] = sums_second[0][i] + sums_second[1][i]
        early[i + 3 : i + 4] = sums_first[0][i] + sums_first[1][i]
    early[6:7] = dot(jnp.ones((8, rows), bf16), up_in[...].reshape(every_hidden))[0:1]
    early_tensor[tensor] = early[...]
    for copy in parts:
        copy.wait_recv()

    here = pl.ds(pl.multiple_of(half + me * tok, 16), tok)
    parts = []
    for d in range(1, n):
        peer = lax.rem(me + d, n)
        copy = remote(
            grad_attn.at[d % 2, block_rows(peer // 2, tok)], gs.at[here], grad_send.at[d - 1],
            grad_recv.at[d - 1], (peer, tensor),
        )
        copy.start()
        parts.append(copy)
    gs[here] = grad_attn[0, block_rows(own, tok)]
    smalls = []
    for i, device in enumerate(peers):
        copy = remote(
            early, early_tensor.at[tensor], small_send.at[0, i], small_recv.at[0, i], device
        )
        copy.start()
        smalls.append(copy)
    shares = []
    for i, held in enumerate((out_in, output)):
        for j, device in enumerate((across, core)):
            copy = remote(
                held.at[mine], held.at[mine], share_send.at[i, j], share_recv.at[i, j], device
            )
            copy.start()
            shares.append(copy)
    for job in job_down:
        job.second()
    for job in job_up:
        job.first()
    for copy in token_parts[3:7]:
        copy.wait_recv()
    half_all = tokens_own.at[:, side_of_chip]
    give_tokens(half_all, half_all, 7, core)

    members = member_columns(length, total)
    outs = []

    def give(i, block):
        low = block.astype(bf16)
        back_stage[i] = low.reshape(n, tok, LANES)
        back_single[i] = packed(low.reshape(n, tok, LANES))
        part = []
        for d in range(1, n):
            peer = lax.rem(me + d, n)
            source, target = (back_stage, come_pair) if d % 2 == 0 else (back_single, come_single)
            copy = remote(
                source.at[i, peer], target.at[i, own], back_send.at[i, d - 1],
                back_recv.at[i, d - 1], (peer, tensor),
            )
            copy.start()
            part.append(copy)
        come_pair[i, own] = back_stage[i, me]
        outs.append(part)
        return low

    for copy in parts:
        copy.wait_recv()
    sent += parts
    grad = gs[half : half + total]
    kernel_one = k1[...]
    grad_carried = jnp.where(same_head, fine(kernel_one, grad, TN), 0.0)
    grad_third = fine(inverse, grad_carried, TN)
    grad_inverse = fine(grad_carried, third_out, NT)
    third_prob = p3[...]
    convolved = jnp.concatenate(
        [conv_block(reverse, gs[m * tok : (m + 2) * tok]) for m in range(n)], axis=0
    )
    grad_values = fine(third_prob, grad_third) + convolved
    value_in = give(2, jnp.where(iota(grad_values.shape, 0) < length, grad_values, 0.0))


    job_down[0].third()
    token_parts[7].wait_recv()
    sent += token_parts
    tokens_all = tokens_own[...].reshape(total, width)
    source_v[...] = dot(tokens_all, value_in, TN).astype(bf16)
    kernel_back = jnp.zeros((LANES, LANES), f32)
    grad_state = grad_inverse
    for step in reversed(range(NS_ITERS)):
        state, product, inner_one, inner_two = [newton[4 * step + i] for i in range(4)]
        grad_next = 0.25 * fine(grad_state, 13.0 * identity - inner_two, NT)
        grad_two = -0.25 * fine(state, grad_state, TN)
        grad_product = fine(grad_two, 15.0 * identity - inner_one, NT)
        grad_one = -fine(product, grad_two, TN)
        grad_product = (
            grad_product
            + fine(grad_one, 7.0 * identity - product, NT)
            - fine(product, grad_one, TN)
        )
        grad_state = grad_next + fine(kernel_two, grad_product, TN)
        kernel_back = kernel_back + fine(grad_product, state, NT)
    squares = block_sums(kernel_two * kernel_two, same_head)
    spread_sum = jnp.where(same_head, block_sums(grad_state * newton[0], same_head), 0.0)
    kernel_back = kernel_back + (grad_state.T - 2.0 * kernel_two * spread_sum) / squares
    grad_scores = scale * kernel_two * (
        kernel_back - jnp.sum(kernel_two * kernel_back, axis=1, keepdims=True)
    )
    query_two = fine(grad_scores, key_marks)
    key_two = fine(grad_scores, query_marks, TN)

    grad_one = fine(grad, carried, NT)
    both = kernel_one * grad_one
    first_scores = scale * (both - kernel_one * fine(both, ones))
    key_one = jnp.where(same_head, fine(first_scores, queries, TN), 0.0)
    delta = fine(jnp.ones((8, LANES), bf16), grad_third * third_out, NT)[0:1]
    third_scores = scale * third_prob * (fine(values, grad_third, NT) - delta)
    query_three = jnp.where(same_head, fine(third_scores, keys, TN), 0.0)
    job_v.first()
    key_in = give(0, fine(third_scores, query_marks) + fine(members, (key_one + key_two) / counts))
    query_in = give(1, fine(first_scores, key_marks) + fine(members, (query_two + query_three) / counts))

    for i, held in enumerate((out_in, output)):
        shares[2 * i].wait_recv()
        block = held.at[block_rows(across[1], tok)]
        copy = remote(block, block, share_send.at[i, 2], share_recv.at[i, 2], core)
        copy.start()
        shares.append(copy)
    source_kq[:, :LANES] = dot(tokens_all, key_in, TN).astype(bf16)
    source_kq[:, LANES:] = dot(tokens_all, query_in, TN).astype(bf16)
    job_kq.first()
    for copy in smalls:
        copy.wait_recv()
    by_tensor = early_tensor[0] + early_tensor[1] + early_tensor[2] + early_tensor[3]
    early_out[0] = jnp.where(iota(by_tensor.shape, 0) == 6, early[...], by_tensor)
    smalls_early = []

    def early_next(k):
        if k > 0:
            smalls_early[k - 1].wait_recv()
            early_out[k] = early_out[k - 1] + early_in[k - 1]
        if k < 3:
            copy = remote(
                early_out.at[k], early_in.at[k], small_send.at[1, k], small_recv.at[1, k],
                job_out.partners[k],
            )
            copy.start()
            smalls_early.append(copy)

    early_next(0)
    shares[1].wait_recv()
    shares[4].wait_recv()
    pair, single = attn_pair[...].reshape(rows, LANES), unpacked(attn_single[...])
    single = single.reshape(rows, HEAD_DIM)
    attention = jnp.concatenate(
        [
            jnp.where(even, pair, jnp.concatenate([single, pair[:, HEAD_DIM:]], axis=1)),
            jnp.where(even, single, pair[:, :HEAD_DIM]),
        ],
        axis=1,
    )
    source_out[...] = dot(out_in[...], attention, TN).astype(bf16)
    job_out.first()
    position = iota((tok, tok), 0) + iota((tok, tok), 1)
    upside = jnp.where(position == tok - 1, 1.0, 0.0).astype(bf16)
    lane = iota((tok, LANES), 1)
    conv_rows = []
    for h in range(2):
        inner = (lane < HEAD_DIM) if h == 0 else (lane >= HEAD_DIM)
        table = jnp.zeros((tok, 2 * tok), f32)
        for m in range(n):
            block = gs[half + m * tok : half + (m + 1) * tok]
            block = jnp.where(inner, block, jnp.zeros_like(block))
            table = table + dot(block, vs[m * tok : (m + 2) * tok], NT)
        table = pltpu.roll(fine(upside, table), 0, 1, stride=1, stride_axis=0)
        row = jnp.sum(table, axis=0, keepdims=True)
        row = pltpu.roll(jnp.broadcast_to(row, (8, 2 * tok)), tok + 1, 1)
        conv_rows.append(row[0:1, :LANES])
    late = late_seq.at[me]
    late[...] = jnp.zeros(late.shape, f32)
    column = jnp.ones((8, total), bf16)
    for row, v in ((0, query_in), (1, value_in)):
        v = dot(column, v)[0:1]
        late[row : row + 1, 0:LANES] = jnp.where(even, v, 0.0)
        late[row : row + 1, LANES:local] = jnp.where(even, 0.0, v[:, :HEAD_DIM])
    late[2:3, 0:LANES] = jnp.where(even, conv_rows[0], 0.0)
    late[3:4, 0:LANES] = jnp.where(even, conv_rows[1], 0.0)
    late[4:5, 0:LANES] = jnp.where(even, 0.0, conv_rows[0])
    smalls_late = []
    for d, device in enumerate(ring_peers):
        copy = remote(late, late, small_send.at[2, d], small_recv.at[2, d], device)
        copy.start()
        smalls_late.append(copy)
    job_down[1].third()
    job_down[0].fourth()
    job_up[0].second()
    for part in outs:
        for copy in part:
            copy.wait_recv()
    singles = []
    for i in range(3):
        tokens_low[:, i * LANES : (i + 1) * LANES] = come_pair[i].reshape(rows, LANES)
        singles.append(unpacked(come_single[i]).reshape(rows, HEAD_DIM))
    tokens_low[:, 3 * LANES :] = jnp.concatenate(singles, axis=1)

    def input_part(t):
        return dot(tokens_low[block_rows(t, tok)], weight_in[...])

    def pass_sum(k, value, device):
        core_last[0, k] = value.astype(bf16)
        copy = remote(
            core_last.at[0, k], core_last.at[1, k], last_send.at[k], last_recv.at[k], device
        )
        copy.start()
        sent.append(copy)
        return copy

    middle = pass_sum(1, input_part(far[1]), core)
    near = pass_sum(0, input_part(core[1]), core)
    crossing = input_part(across[1])
    middle.wait_recv()
    y_last[0] = (crossing + core_last[1, 1].astype(f32)).astype(bf16)
    final = remote(y_last.at[0], y_last.at[1], last_send.at[2], last_recv.at[2], across)
    final.start()
    sent.append(final)
    result = input_part(tensor) + jnp.concatenate(grads_first, axis=0)
    job_v.second()
    job_up[1].second()
    job_up[0].third()
    near.wait_recv()
    final.wait_recv()
    result = result + core_last[1, 0].astype(f32) + y_last[1].astype(f32)
    tokens_whole[mine] = result.astype(bf16)
    ends = []
    for j, device in enumerate((across, core)):
        copy = remote(
            tokens_whole.at[mine], tokens_whole.at[mine], share_send.at[2, j], share_recv.at[2, j],
            device,
        )
        copy.start()
        ends.append(copy)
    early_next(1)
    job_kq.second()
    job_out.second()
    job_up[0].fourth()
    job_up[1].third()
    early_next(2)
    job_v.third()

    def into(ref, k):
        def write(value):
            ref[:, k * span : (k + 1) * span] = value

        return write

    for k, job in enumerate(job_down):
        job.last(into(grad_down, k))
    done(14)
    ends[0].wait_recv()
    block = tokens_whole.at[block_rows(across[1], tok)]
    copy = remote(block, block, share_send.at[2, 2], share_recv.at[2, 2], core)
    copy.start()
    ends.append(copy)
    job_kq.third()
    job_up[1].fourth()
    job_out.third()
    ends[1].wait_recv()
    ends[2].wait_recv()
    grad_tokens[...] = tokens_whole[...].astype(f32)
    done(1)
    for copy in smalls_late:
        copy.wait_recv()
    early_next(3)
    by_seq = early_out[3]
    for ref, row in (
        (second_gain, 0), (second_shift, 1), (down_bias_grad, 2), (first_gain, 3),
        (first_shift, 4), (out_bias_grad, 5), (up_bias_grad, 6),
    ):
        ref[...] = by_seq[row]
    proxy[...] = by_seq[7:8, 0:1]
    by_seq = functools.reduce(lambda a, b: a + b, [late_seq[i] for i in range(n)])
    query_bias[...] = by_seq[0, :local]
    value_bias[...] = by_seq[1, :local]
    conv[...] = by_seq[2:5, :CONV]
    shares[3].wait_recv()
    shares[5].wait_recv()
    done(0, 3, 6, 7, 9, 10, 11, 13, 15, 16, 17, 18)

    def heads(job, *refs):
        def write(result):
            for i, ref in enumerate(refs):
                start = len(refs) * LANES + i * HEAD_DIM
                ref[:, :LANES] = result[:, i * LANES : (i + 1) * LANES]
                ref[:, LANES:] = result[:, start : start + HEAD_DIM]

        job.last(write)

    heads(job_v, grad_value)
    done(5)
    for k, job in enumerate(job_up):
        job.last(into(grad_up, k))
    done(12)
    heads(job_kq, grad_key, grad_query)
    done(2, 4)

    def write_out(value):
        grad_out[...] = value.T

    job_out.last(write_out)
    done(8)
    for copy in list(ring.copies.values()) + sent + shares + smalls + smalls_early + smalls_late + ends:
        copy.wait_send()
    for part in outs:
        for copy in part:
            copy.wait_send()
    for job in jobs:
        job.finish()
    for copy in stores:
        copy.wait()


def finish_kernel(*refs):
    come, go, held = [refs[i * RESULTS : (i + 1) * RESULTS] for i in range(3)]
    loads, stores = refs[3 * RESULTS :]
    copies = [
        pltpu.make_async_copy(come[i], held[i], loads.at[i]) for i in range(RESULTS)
    ]
    for copy in copies:
        copy.start()
    outs = []
    for i in range(RESULTS):
        copies[i].wait()
        copy = pltpu.make_async_copy(held[i], go[i], stores.at[i])
        copy.start()
        outs.append(copy)
    for copy in outs:
        copy.wait()


def whole(shape, dtype):
    return jax.ShapeDtypeStruct(shape, dtype)


VMEM = pl.BlockSpec(memory_space=pltpu.VMEM)
SMEM = pl.BlockSpec(memory_space=pltpu.SMEM)
HBM = pl.BlockSpec(memory_space=pl.ANY)


def dma(*shape):
    return pltpu.SemaphoreType.DMA(shape)


def gathered_plan(
    n, tokens, lengths, query_weight, query_bias, key_weight, value_weight, value_bias,
    conv_kernel, out_weight, out_bias, first_gain, first_shift, up_weight, up_bias, down_weight,
    down_bias, second_gain, second_shift, out_grad,
):
    batch, tok, width = tokens.shape
    rows = batch * tok
    local = query_weight.shape[1]
    hidden = up_weight.shape[1]
    total = n * tok
    block = width // n
    piece = tok // 2

    def low(*shape):
        return pltpu.VMEM(shape, bf16)

    def wide(*shape):
        return pltpu.VMEM(shape, f32)

    results = (
        whole((rows, width), bf16),
        whole((rows, width), f32),
        whole((block, local), f32),
        whole((local,), f32),
        whole((block, local), f32),
        whole((block, local), f32),
        whole((local,), f32),
        whole(conv_kernel.shape, f32),
        whole((local, block), f32),
        whole((width,), f32),
        whole((width,), f32),
        whole((width,), f32),
        whole((block, hidden), f32),
        whole((hidden,), f32),
        whole((block, hidden), f32),
        whole((width,), f32),
        whole((width,), f32),
        whole((width,), f32),
        whole((1, 1), f32),
    )
    outs = pl.pallas_call(
        functools.partial(layer_kernel, n),
        out_shape=results,
        in_specs=[SMEM, HBM, HBM, VMEM, HBM, HBM, VMEM, VMEM, HBM, VMEM, VMEM, VMEM, HBM, VMEM, HBM,
                  VMEM, VMEM, VMEM, HBM],
        out_specs=(HBM,) * RESULTS,
        scratch_shapes=[pltpu.VMEM(r.shape, r.dtype) for r in results]
        + [
            low(rows, width), low(local, width), low(local, width), low(local, width),
            low(width, hidden), low(hidden, width), low(rows, width), low(local, width),
            low(width, width),
            low(3, 2, rows, LANES), low(total, LANES), low(total, LANES), low(total + tok, LANES),
            wide(total, LANES), wide(total, LANES), wide(4 * NS_ITERS, LANES, LANES),
            low(n - 1, tok, LANES), low(n - 1, piece, LANES), low(batch, tok, LANES),
            low(batch, piece, LANES),
            low(4, tok, LANES), low(4, piece, LANES), low(4, 2, tok, LANES),
            low(2, rows, LANES), low(2, 4, piece, width), wide(2, 4, piece, hidden),
            low(2, 4, piece, hidden), low(2, 4, piece, width), low(2, 4, piece, hidden),
            low(2, 2, 2, piece, width), low(2, 2, 2, piece, width), low(2, 2, piece, width),
            low(2, 2, piece, width), low(2, 2, tok, width), low(2, tok, width),
            low(total + tok, LANES), low(3, n, tok, LANES), low(3, n, tok // 2, LANES),
            low(3, batch, tok, LANES), low(3, batch, tok // 2, LANES), low(3 * local, width),
            low(rows, width), wide(8, width), wide(4, 8, width), low(n, 2, tok // 2, width),
            low(rows, 3 * local), low(width, hidden), low(width, hidden), low(width, local),
            low(width, LANES), low(width, 2 * LANES), wide(4, 8, width), wide(3, 8, width),
            wide(n, 8, 2 * LANES), low(rows, width), wide(2, 2, 2, 2, piece, width),
        ]
        + [
            b
            for first, w in (
                *((hidden // 2, hidden // 2),) * 4, (local, local), (LANES, local), (2 * LANES, 2 * local)
            )
            for b in scatter_buffers(first, w, block)
        ]
        + [
            dma(8), dma(3, n - 1), dma(3, n - 1), dma(n - 1), dma(n - 1), dma(3, 2),
            dma(3, 2), dma(2, 3, 2), dma(2, 3, 2), dma(2, 2, 3), dma(2, 2, 3), dma(2, 2, 3),
            dma(2, 2, 3), dma(n - 1),
            dma(n - 1), dma(3, n - 1), dma(3, n - 1), dma(3, 3), dma(3, 3), dma(3, n - 1),
            dma(3, n - 1), dma(JOBS, 10), dma(JOBS, 10), dma(8), dma(8), dma(3), dma(3), dma(RESULTS),
        ],
        compiler_params=pltpu.CompilerParams(
            collective_id=0, has_side_effects=True, vmem_limit_bytes=56 * 2**20
        ),
        name="layer",
    )(
        lengths, tokens.reshape(rows, width), query_weight.T, query_bias, key_weight.T,
        value_weight.T, value_bias, conv_kernel, out_weight, out_bias, first_gain, first_shift,
        up_weight, up_bias, down_weight, down_bias, second_gain, second_shift,
        out_grad.reshape(rows, width),
    )
    outs = pl.pallas_call(
        finish_kernel,
        out_shape=results,
        in_specs=[HBM] * RESULTS,
        out_specs=(HBM,) * RESULTS,
        scratch_shapes=[pltpu.VMEM(r.shape, r.dtype) for r in results]
        + [dma(RESULTS), dma(RESULTS)],
        compiler_params=pltpu.CompilerParams(vmem_limit_bytes=60 * 2**20),
        name="finish",
    )(*outs)
    return (
        outs[0].reshape(tokens.shape),
        outs[1].reshape(tokens.shape),
        *outs[2:14],
        outs[14].T,
        *outs[15:18],
        outs[18].reshape(()),
    )


def per_device(seq, tensor, *args):
    batch, tok, width = args[0].shape
    heads = args[7].shape[0]
    if seq == 8 and tensor == 4 and batch == 4 and heads == 3 and tok == 128:
        return gathered_plan(seq, *args)
    return general_plan(*args)


def solution(mesh):
    return jax.shard_map(
        functools.partial(per_device, mesh.shape["seq"], mesh.shape["tensor"]),
        mesh=mesh,
        in_specs=(
            P(None, "seq", None),
            P(),
            P(None, "tensor"),
            P("tensor"),
            P(None, "tensor"),
            P(None, "tensor"),
            P("tensor"),
            P("tensor", None),
            P("tensor", None),
            P(),
            P(),
            P(),
            P(None, "tensor"),
            P("tensor"),
            P("tensor", None),
            P(),
            P(),
            P(),
            P(None, "seq", None),
        ),
        out_specs=(
            P(None, "seq", None),
            P(None, "seq", None),
            P("seq", "tensor"),
            P("tensor"),
            P("seq", "tensor"),
            P("seq", "tensor"),
            P("tensor"),
            P("tensor", None),
            P("tensor", "seq"),
            P(),
            P(),
            P(),
            P("seq", "tensor"),
            P("tensor"),
            P("tensor", "seq"),
            P(),
            P(),
            P(),
            P(),
        ),
        check_vma=False,
    )
```

```python
import functools

import jax
import jax.numpy as jnp
from jax import lax
from jax.experimental import pallas as pl
from jax.experimental.pallas import tpu as pltpu
from jax.sharding import PartitionSpec as P

HEADS = 12
HEAD_DIM = 64
LAND = 64
CONV = 33
NS_ITERS = 6


highest = lax.Precision.HIGHEST
epsilon = 1e-05
negative = -1e30


def joined(x, axis, combine):
    everything = jax.tree.map(lambda part: lax.all_gather(part, axis), x)
    first = jax.tree.map(lambda part: part[0], everything)

    def hop(k, so_far):
        return combine(so_far, jax.tree.map(lambda part: part[k], everything))

    return lax.fori_loop(1, lax.axis_size(axis), hop, first)


def with_halo(block, sides, width):
    for axis, dim in sides:
        count = lax.axis_size(axis)
        forward = [(i, i + 1) for i in range(count - 1)]
        backward = [(target, source) for source, target in forward]
        low = lax.ppermute(
            lax.slice_in_dim(block, block.shape[dim] - width, None, axis=dim), axis, forward
        )
        high = lax.ppermute(lax.slice_in_dim(block, 0, width, axis=dim), axis, backward)
        block = jnp.concatenate([low, block, high], axis=dim)
    return block


def newton_inverse(kernel):
    identity = jnp.eye(kernel.shape[-1], dtype=jnp.float32)
    inverse = jnp.swapaxes(kernel, -1, -2) / jnp.sum(kernel * kernel, axis=(-2, -1), keepdims=True)
    for _ in range(NS_ITERS):
        product = jnp.matmul(kernel, inverse, precision=highest)
        inner_term = jnp.matmul(product, 7.0 * identity - product, precision=highest)
        inner_term = jnp.matmul(product, 15.0 * identity - inner_term, precision=highest)
        inverse = 0.25 * jnp.matmul(inverse, 13.0 * identity - inner_term, precision=highest)
    return inverse


def landmark_core(query_marks, key_marks):
    scores = jnp.einsum(
        "bhjd,bhid->bhji", query_marks, key_marks, precision=highest
    ) * HEAD_DIM ** (-0.5)
    kernel_two = jax.nn.softmax(scores, axis=-1)
    return (kernel_two, newton_inverse(kernel_two))


def normalize(summed, gain_vec, shift_vec):
    middle = jnp.mean(summed, axis=-1, keepdims=True)
    centred = summed - middle
    inverse_std = lax.rsqrt(jnp.mean(centred * centred, axis=-1, keepdims=True) + epsilon)
    normal = centred * inverse_std
    return (normal * gain_vec + shift_vec, normal, inverse_std)


def add_norm(partial_sum, residual, bias_vec, gain_vec, shift_vec):
    summed = lax.psum(partial_sum.astype(jnp.bfloat16), "tensor").astype(jnp.float32)
    return normalize(residual + summed + bias_vec, gain_vec, shift_vec)


def norm_back(grad_hidden, normal, inverse_std, gain_vec):
    grad_normal = grad_hidden * gain_vec
    grad_summed = inverse_std * (
        grad_normal
        - jnp.mean(grad_normal, axis=-1, keepdims=True)
        - normal * jnp.mean(grad_normal * normal, axis=-1, keepdims=True)
    )
    return (grad_summed, jnp.sum(grad_hidden * normal, axis=0), jnp.sum(grad_hidden, axis=0))


def combine_soft(earlier, later):
    top_score = jnp.maximum(earlier[0], later[0])
    weight_first = jnp.exp(earlier[0] - top_score)
    weight_second = jnp.exp(later[0] - top_score)
    return (
        top_score,
        earlier[1] * weight_first + later[1] * weight_second,
        earlier[2] * weight_first[..., None] + later[2] * weight_second[..., None],
    )


def general_plan(
    tokens,
    lengths,
    query_weight,
    query_bias,
    key_weight,
    value_weight,
    value_bias,
    conv_kernel,
    out_weight,
    out_bias,
    first_gain,
    first_shift,
    up_weight,
    up_bias,
    down_weight,
    down_bias,
    second_gain,
    second_shift,
    out_grad,
):
    batch, tok_local, width = tokens.shape
    local_width = query_weight.shape[1]
    local_heads = conv_kernel.shape[0]
    head_dim = local_width // local_heads
    score_scale = HEAD_DIM ** (-0.5)
    rows = batch * tok_local
    half_width = CONV // 2
    f32 = jnp.float32
    bf16 = jnp.bfloat16
    position = lax.axis_index("seq") * tok_local + jnp.arange(tok_local, dtype=jnp.int32)
    inside = position[None, :] < lengths[:, None]
    living = inside.astype(f32)
    segment = position[None, :] * LAND // lengths[:, None]
    onehot = (
        (segment[:, :, None] == jnp.arange(LAND, dtype=jnp.int32)[None, None, :])
        & inside[:, :, None]
    ).astype(f32)
    marks_index = jnp.arange(LAND, dtype=jnp.int32)
    upper = ((marks_index[None, :] + 1) * lengths[:, None] + LAND - 1) // LAND
    lower = (marks_index[None, :] * lengths[:, None] + LAND - 1) // LAND
    counts = (upper - lower).astype(f32)
    flat = tokens.reshape(rows, width)
    flat_wide = flat.astype(f32)
    queries = (jnp.dot(flat, query_weight, preferred_element_type=f32) + query_bias).astype(bf16)
    key_vectors = jnp.dot(flat, key_weight, preferred_element_type=f32).astype(bf16)
    values = (
        (jnp.dot(flat, value_weight, preferred_element_type=f32) + value_bias)
        * living.reshape(rows, 1)
    ).astype(bf16)
    query_three = queries.reshape(batch, tok_local, local_width)
    key_three = key_vectors.reshape(batch, tok_local, local_width)
    value_three = values.reshape(batch, tok_local, local_width)
    onehot_low = onehot.astype(bf16)
    query_sum = jnp.einsum("btj,btf->bjf", onehot_low, query_three, preferred_element_type=f32)
    key_sum = jnp.einsum("btj,btf->bjf", onehot_low, key_three, preferred_element_type=f32)
    query_sum, key_sum = lax.psum((query_sum, key_sum), "seq")
    query_marks = (
        (query_sum / counts[:, :, None])
        .reshape(batch, LAND, local_heads, head_dim)
        .transpose(0, 2, 1, 3)
    )
    key_marks = (
        (key_sum / counts[:, :, None])
        .reshape(batch, LAND, local_heads, head_dim)
        .transpose(0, 2, 1, 3)
    )
    (kernel_two, inverse), core_back = jax.vjp(landmark_core, query_marks, key_marks)
    identity = jnp.eye(LAND, dtype=f32)
    deviation = identity - jnp.matmul(kernel_two, inverse, precision=highest)
    proxy_part = jnp.sum(jnp.sqrt(jnp.sum(deviation * deviation, axis=(-2, -1)))) / (batch * HEADS)
    query_heads = query_three.reshape(batch, tok_local, local_heads, head_dim).astype(f32)
    key_heads = key_three.reshape(batch, tok_local, local_heads, head_dim).astype(f32)
    value_heads = value_three.reshape(batch, tok_local, local_heads, head_dim).astype(f32)
    first_scores = (
        jnp.einsum("bthd,bhjd->bhtj", query_heads, key_marks, precision=highest) * score_scale
    )
    kernel_one = jax.nn.softmax(first_scores, axis=-1)
    third_scores = (
        jnp.einsum("bhjd,bthd->bhjt", query_marks, key_heads, precision=highest) * score_scale
    )
    key_alive = inside[:, None, None, :]
    third_scores = jnp.where(key_alive, third_scores, negative)
    local_top = jnp.max(third_scores, axis=-1)
    local_weights = jnp.where(key_alive, jnp.exp(third_scores - local_top[..., None]), 0.0)
    local_total = jnp.sum(local_weights, axis=-1)
    local_mix = jnp.einsum("bhjt,bthd->bhjd", local_weights, value_heads, precision=highest)
    top_score, total_weight, mixed = joined(
        (local_top, local_total, local_mix), "seq", combine_soft
    )
    third_out = mixed / total_weight[..., None]
    carried = jnp.matmul(inverse, third_out, precision=highest)
    nystrom = jnp.einsum("bhtj,bhjd->bthd", kernel_one, carried, precision=highest).reshape(
        batch, tok_local, local_width
    )
    padded_values = with_halo(value_three, (("seq", 1),), half_width)
    kernel_wide = jnp.repeat(conv_kernel, head_dim, axis=0)
    convolved = jnp.zeros((batch, tok_local, local_width), f32)
    for i in range(CONV):
        convolved = (
            convolved + padded_values[:, i : i + tok_local, :].astype(f32) * kernel_wide[:, i]
        )
    attention = (nystrom + convolved).astype(bf16).reshape(rows, local_width)
    out_part = jnp.dot(attention, out_weight, preferred_element_type=f32)
    hidden_one, normal_one, inverse_one = add_norm(
        out_part, flat_wide, out_bias, first_gain, first_shift
    )
    hidden_low = hidden_one.astype(bf16)
    up_value = jnp.dot(hidden_low, up_weight, preferred_element_type=f32) + up_bias
    activated, gelu_back = jax.vjp(lambda z: jax.nn.gelu(z, approximate=False), up_value)
    activated = activated.astype(bf16)
    down_part = jnp.dot(activated, down_weight, preferred_element_type=f32)
    hidden_two, normal_two, inverse_two = add_norm(
        down_part, hidden_one, down_bias, second_gain, second_shift
    )
    output = hidden_two.astype(bf16).reshape(batch, tok_local, width)
    grad_output = out_grad.reshape(rows, width).astype(f32)
    grad_second_total, grad_second_gain, grad_second_shift = norm_back(
        grad_output, normal_two, inverse_two, second_gain
    )
    down_in = grad_second_total.astype(bf16)
    grad_down_bias = jnp.sum(down_in.astype(f32), axis=0)
    grad_down_weight = jnp.einsum("rf,rd->fd", activated, down_in, preferred_element_type=f32)
    grad_activated = jnp.einsum("rd,fd->rf", down_in, down_weight, preferred_element_type=f32)
    up_in = gelu_back(grad_activated)[0].astype(bf16)
    grad_up_bias = jnp.sum(up_in.astype(f32), axis=0)
    grad_up_weight = jnp.einsum("rd,rf->df", hidden_low, up_in, preferred_element_type=f32)
    hidden_part = jnp.einsum("rf,df->rd", up_in, up_weight, preferred_element_type=f32)
    grad_hidden_one = (
        lax.psum(hidden_part.astype(jnp.bfloat16), "tensor").astype(jnp.float32) + grad_second_total
    )
    grad_first_total, grad_first_gain, grad_first_shift = norm_back(
        grad_hidden_one, normal_one, inverse_one, first_gain
    )
    out_in = grad_first_total.astype(bf16)
    grad_out_bias = jnp.sum(out_in.astype(f32), axis=0)
    grad_out_weight = jnp.einsum("rf,rd->fd", attention, out_in, preferred_element_type=f32)
    grad_attention = jnp.einsum(
        "rd,fd->rf", out_in, out_weight, preferred_element_type=f32
    ).reshape(batch, tok_local, local_width)
    padded_grad = with_halo(grad_attention.astype(jnp.bfloat16), (("seq", 1),), half_width).astype(
        grad_attention.dtype
    )
    grad_conv_values = jnp.zeros((batch, tok_local, local_width), f32)
    conv_columns = []
    for i in range(CONV):
        conv_columns.append(
            jnp.sum(
                grad_attention * padded_values[:, i : i + tok_local, :].astype(f32), axis=(0, 1)
            )
        )
        start_index = 2 * half_width - i
        grad_conv_values = (
            grad_conv_values
            + padded_grad[:, start_index : start_index + tok_local, :] * kernel_wide[:, i]
        )
    grad_conv_kernel = (
        jnp.stack(conv_columns, axis=0).reshape(CONV, local_heads, head_dim).sum(axis=-1).T
    )
    grad_nystrom = grad_attention.reshape(batch, tok_local, local_heads, head_dim)
    grad_kernel_one = jnp.einsum("bthd,bhjd->bhtj", grad_nystrom, carried, precision=highest)
    grad_carried_part = jnp.einsum("bhtj,bthd->bhjd", kernel_one, grad_nystrom, precision=highest)
    grad_first_scores = kernel_one * (
        grad_kernel_one - jnp.sum(kernel_one * grad_kernel_one, axis=-1, keepdims=True)
    )
    grad_query_one = (
        jnp.einsum("bhtj,bhjd->bthd", grad_first_scores, key_marks, precision=highest) * score_scale
    )
    grad_key_marks_part = (
        jnp.einsum("bhtj,bthd->bhjd", grad_first_scores, query_heads, precision=highest)
        * score_scale
    )
    grad_carried, grad_key_marks_one = lax.psum((grad_carried_part, grad_key_marks_part), "seq")
    grad_third_out = jnp.matmul(jnp.swapaxes(inverse, -1, -2), grad_carried, precision=highest)
    grad_inverse = jnp.matmul(grad_carried, jnp.swapaxes(third_out, -1, -2), precision=highest)
    grad_query_marks_two, grad_key_marks_two = core_back((jnp.zeros_like(kernel_two), grad_inverse))
    third_prob = local_weights * jnp.exp(local_top - top_score)[..., None] / total_weight[..., None]
    delta_term = jnp.sum(grad_third_out * third_out, axis=-1)
    grad_prob_value = jnp.einsum("bhjd,bthd->bhjt", grad_third_out, value_heads, precision=highest)
    grad_third_scores = third_prob * (grad_prob_value - delta_term[..., None])
    grad_value_three = jnp.einsum("bhjt,bhjd->bthd", third_prob, grad_third_out, precision=highest)
    grad_key_three = (
        jnp.einsum("bhjt,bhjd->bthd", grad_third_scores, query_marks, precision=highest)
        * score_scale
    )
    grad_query_marks_part = (
        jnp.einsum("bhjt,bthd->bhjd", grad_third_scores, key_heads, precision=highest) * score_scale
    )
    grad_query_marks_three = lax.psum(grad_query_marks_part, "seq")
    grad_query_marks = (grad_query_marks_two + grad_query_marks_three) / counts[:, None, :, None]
    grad_key_marks = (grad_key_marks_one + grad_key_marks_two) / counts[:, None, :, None]
    grad_query_marks = grad_query_marks.transpose(0, 2, 1, 3).reshape(batch, LAND, local_width)
    grad_key_marks = grad_key_marks.transpose(0, 2, 1, 3).reshape(batch, LAND, local_width)
    grad_query_seg = jnp.einsum("btj,bjf->btf", onehot, grad_query_marks, precision=highest)
    grad_key_seg = jnp.einsum("btj,bjf->btf", onehot, grad_key_marks, precision=highest)
    query_in = (
        (grad_query_one.reshape(batch, tok_local, local_width) + grad_query_seg)
        .astype(bf16)
        .reshape(rows, local_width)
    )
    key_in = (
        (grad_key_three.reshape(batch, tok_local, local_width) + grad_key_seg)
        .astype(bf16)
        .reshape(rows, local_width)
    )
    value_in = (grad_value_three.reshape(batch, tok_local, local_width) + grad_conv_values).astype(
        bf16
    )
    value_in = jnp.where(inside[:, :, None], value_in, jnp.zeros_like(value_in)).reshape(
        rows, local_width
    )
    grad_query_bias = jnp.sum(query_in.astype(f32), axis=0)
    grad_value_bias = jnp.sum(value_in.astype(f32), axis=0)
    grad_query_weight = jnp.einsum("rd,rf->df", flat, query_in, preferred_element_type=f32)
    grad_key_weight = jnp.einsum("rd,rf->df", flat, key_in, preferred_element_type=f32)
    grad_value_weight = jnp.einsum("rd,rf->df", flat, value_in, preferred_element_type=f32)
    input_part = (
        jnp.einsum("rf,df->rd", query_in, query_weight, preferred_element_type=f32)
        + jnp.einsum("rf,df->rd", key_in, key_weight, preferred_element_type=f32)
        + jnp.einsum("rf,df->rd", value_in, value_weight, preferred_element_type=f32)
    )
    input_sum, proxy_norm = (
        lax.psum(input_part.astype(jnp.bfloat16), "tensor").astype(jnp.float32),
        lax.psum(proxy_part.astype(jnp.bfloat16), "tensor").astype(jnp.float32),
    )
    grad_tokens = (grad_first_total + input_sum).reshape(batch, tok_local, width)
    (
        grad_query_weight,
        grad_key_weight,
        grad_value_weight,
        grad_out_weight,
        grad_up_weight,
        grad_down_weight,
    ) = (
        lax.psum_scatter(grad_query_weight, "seq", scatter_dimension=0, tiled=True),
        lax.psum_scatter(grad_key_weight, "seq", scatter_dimension=0, tiled=True),
        lax.psum_scatter(grad_value_weight, "seq", scatter_dimension=0, tiled=True),
        lax.psum_scatter(grad_out_weight, "seq", scatter_dimension=1, tiled=True),
        lax.psum_scatter(grad_up_weight, "seq", scatter_dimension=0, tiled=True),
        lax.psum_scatter(grad_down_weight, "seq", scatter_dimension=1, tiled=True),
    )
    (
        grad_query_bias,
        grad_value_bias,
        grad_conv_kernel,
        grad_out_bias,
        grad_first_gain,
        grad_first_shift,
        grad_up_bias,
        grad_down_bias,
        grad_second_gain,
        grad_second_shift,
    ) = lax.psum(
        (
            grad_query_bias,
            grad_value_bias,
            grad_conv_kernel,
            grad_out_bias,
            grad_first_gain,
            grad_first_shift,
            grad_up_bias,
            grad_down_bias,
            grad_second_gain,
            grad_second_shift,
        ),
        "seq",
    )
    return (
        output,
        grad_tokens,
        grad_query_weight,
        grad_query_bias,
        grad_key_weight,
        grad_value_weight,
        grad_value_bias,
        grad_conv_kernel,
        grad_out_weight,
        grad_out_bias,
        grad_first_gain,
        grad_first_shift,
        grad_up_weight,
        grad_up_bias,
        grad_down_weight,
        grad_down_bias,
        grad_second_gain,
        grad_second_shift,
        proxy_norm,
    )


MESH = pl.DeviceIdType.MESH
LANES = 2 * HEAD_DIM
f32 = jnp.float32
bf16 = jnp.bfloat16
NN = (1, 0)
NT = (1, 1)
TN = (0, 0)


def dot(a, b, dims=NN):
    return lax.dot_general(
        a, b, (((dims[0],), (dims[1],)), ((), ())), preferred_element_type=f32
    )


def split(x):
    if x.dtype == bf16:
        return (x,)
    top = x.astype(bf16)
    return (top, (x - top.astype(f32)).astype(bf16))


def fine(a, b, dims=NN):
    a, b = split(a), split(b)
    total = dot(a[0], b[0], dims)
    if len(b) > 1:
        total = total + dot(a[0], b[1], dims)
    if len(a) > 1:
        total = total + dot(a[1], b[0], dims)
    return total


def iota(shape, dim):
    return lax.broadcasted_iota(jnp.int32, shape, dim)


def block_mask():
    shape = (LANES, LANES)
    return (iota(shape, 0) < HEAD_DIM) == (iota(shape, 1) < HEAD_DIM)


def eye():
    return jnp.where(iota((LANES, LANES), 0) == iota((LANES, LANES), 1), 1.0, 0.0).astype(f32)


def block_sums(x, same_head):
    ones = jnp.where(same_head, 1.0, 0.0).astype(bf16)
    return jnp.where(same_head, fine(fine(ones, x), ones), 1.0)


def taps_matrix(row, tok):
    return pltpu.roll(jnp.broadcast_to(row, (tok, 2 * tok)), 0, 1, stride=1, stride_axis=0)


def taps_row(taps, head, tok):
    row = taps[pl.ds(head, 1), :]
    return jnp.concatenate([row, jnp.zeros((1, 2 * tok - CONV), f32)], axis=1)


def conv_block(matrices, window):
    first = fine(matrices[0], window)
    second = fine(matrices[1], window)
    return jnp.where(iota(first.shape, 1) < HEAD_DIM, first, second)


def greet(devices):
    barrier = pltpu.get_barrier_semaphore()
    for device in devices:
        pl.semaphore_signal(barrier, inc=1, device_id=device, device_id_type=MESH)
    return barrier


def around(n, me, tensor):
    return [(lax.rem(me + d, n), tensor) for d in range(1, n)]


def others(me, tensor):
    core = tensor + 1 - 2 * (tensor % 2)
    return [(me, core), (me, lax.rem(tensor + 2, 4)), (me, lax.rem(core + 2, 4))]


def paired(y):
    return y[:, :LANES], jnp.concatenate(
        [y[:, LANES : LANES + HEAD_DIM], y[:, HEAD_DIM:LANES]], axis=1
    )


def remote(src, dst, send, recv, device):
    return pltpu.make_async_remote_copy(
        src_ref=src, dst_ref=dst, send_sem=send, recv_sem=recv, device_id=device,
        device_id_type=MESH,
    )


def member_rows(length, total):
    j = iota((LANES, total), 0) % LAND
    t = iota((LANES, total), 1)
    inside = (t * LAND >= j * length) & (t * LAND < (j + 1) * length) & (t < length)
    return jnp.where(inside, 1.0, 0.0).astype(bf16)


def member_columns(length, total):
    j = iota((total, LANES), 1) % LAND
    t = iota((total, LANES), 0)
    inside = (t * LAND >= j * length) & (t * LAND < (j + 1) * length) & (t < length)
    return jnp.where(inside, 1.0, 0.0).astype(bf16)


def segment_counts(length):
    j = iota((LANES, LANES), 0) % LAND
    upper = ((j + 1) * length + LAND - 1) // LAND
    lower = (j * length + LAND - 1) // LAND
    return (upper - lower).astype(f32)


def normal_of(summed):
    middle = jnp.mean(summed, axis=-1, keepdims=True)
    centred = summed - middle
    inverse_std = lax.rsqrt(jnp.mean(centred * centred, axis=-1, keepdims=True) + epsilon)
    return centred * inverse_std, inverse_std


def before_norm(grad, normal, inverse_std, gain):
    grad_normal = grad * gain
    return inverse_std * (
        grad_normal
        - jnp.mean(grad_normal, axis=-1, keepdims=True)
        - normal * jnp.mean(grad_normal * normal, axis=-1, keepdims=True)
    )


def block_rows(t, tok):
    return pl.ds(pl.multiple_of(t * tok, tok), tok)


def settle(ref, sem):
    pltpu.make_async_copy(ref, ref, sem).wait()


class Scatter:
    def __init__(self, index, me, tensor, source, columns, buffers, send, recv, order):
        self.index, self.source, self.columns = index, source, pl.ds(*columns)
        self.first_in, self.held, self.second_in, self.pair, self.last_in, self.cross_in = buffers
        self.block = source.shape[0] // 8
        self.weights = [2**bit for bit in order]
        self.bits = [(me // weight) % 2 for weight in self.weights]
        self.partners = [
            (me + weight * (1 - 2 * bit), tensor) for weight, bit in zip(self.weights, self.bits)
        ]
        self.send, self.recv = send, recv

    def rows(self, slot, bit):
        index = (slot // 2) * self.weights[2] + (slot % 2) * self.weights[1] + bit * self.weights[0]
        return pl.ds(pl.multiple_of(index * self.block, 16), self.block)

    def copy(self, src, dst, k, stage):
        return remote(
            src, dst, self.send.at[self.index, min(k, 1)], self.recv.at[self.index, k],
            self.partners[stage],
        )

    def arrived(self, ref, k):
        settle(ref, self.recv.at[self.index, k])

    def first(self, slots=range(4)):
        for slot in slots:
            source = self.source.at[self.rows(slot, 1 - self.bits[0]), self.columns]
            self.copy(source, self.first_in.at[slot], 0, 0).start()

    def second(self):
        self.arrived(self.first_in, 0)
        for slot in range(4):
            mine = self.source[self.rows(slot, self.bits[0]), self.columns]
            self.held[slot] = self.joined(mine, self.first_in[slot])
        for k in range(2):
            self.copy(self.held.at[2 * k + 1 - self.bits[1]], self.second_in.at[k], 1, 1).start()

    def joined(self, mine, come):
        return (mine.astype(f32) + come.astype(f32)).astype(bf16)

    def third(self):
        self.arrived(self.second_in, 1)
        for k in range(2):
            both = self.held[2 * k + self.bits[1]].astype(f32) + self.second_in[k].astype(f32)
            self.pair[k] = both.astype(bf16)
        self.copy(self.pair.at[1 - self.bits[2]], self.last_in, 2, 2).start()

    def last(self, write):
        self.arrived(self.last_in, 2)
        write(self.pair[self.bits[2]].astype(f32) + self.last_in[...].astype(f32))

    def finish(self):
        settle(self.first_in, self.send.at[self.index, 0])
        settle(self.held.at[pl.ds(0, 3)], self.send.at[self.index, 1])


class Line(Scatter):
    def __init__(self, *args):
        super().__init__(*args)
        z = self.bits[1] + 2 * self.bits[2]
        right = z // 2
        self.end = self.bits[1] == right
        self.inner = self.bits[1] != right
        self.slots = [k * (1 - right) + (3 - k) * right for k in range(4)]
        self.partners[2] = (2 * (3 - z) + self.bits[0], self.partners[0][1])

    def second(self):
        self.arrived(self.first_in, 0)
        for slot in range(4):
            mine = self.source[self.rows(slot, self.bits[0]), self.columns]
            self.held[slot] = self.joined(mine, self.first_in[slot])
        come = (self.second_in.at[0], self.second_in.at[1], self.last_in)
        sends = [
            self.copy(self.held.at[self.slots[3 - k]], come[k], (1, 1, 2)[k], 1)
            for k in range(3)
        ]

        @pl.when(self.end)
        def _():
            for copy in sends:
                copy.start()

    def third(self):
        sends = [
            self.copy(self.pair.at[k], self.cross_in.at[k], 3, 2) for k in range(2)
        ]

        @pl.when(self.inner)
        def _():
            self.arrived(self.second_in, 1)
            for k in range(2):
                self.pair[k] = self.joined(self.held[self.slots[3 - k]], self.second_in[k])
                sends[k].start()

    def fourth(self):
        back = self.copy(self.first_in.at[2], self.first_in.at[3], 4, 1)

        @pl.when(self.inner)
        def _():
            self.arrived(self.cross_in, 3)
            self.first_in[2] = self.joined(self.held[self.slots[0]], self.cross_in[0])
            back.start()

    def last(self, write):
        @pl.when(self.inner)
        def _():
            self.arrived(self.last_in, 2)
            write(
                self.held[self.slots[1]].astype(f32)
                + self.last_in[...].astype(f32)
                + self.cross_in[1].astype(f32)
            )

        @pl.when(self.end)
        def _():
            self.arrived(self.first_in.at[3], 4)
            write(self.held[self.slots[0]].astype(f32) + self.first_in[3].astype(f32))


class Heads(Scatter):
    def joined(self, mine, come):
        even = self.bits[0] == 0
        pair, other = jnp.where(even, mine, come), jnp.where(even, come, mine)
        return jnp.concatenate(
            [pair] + [other[:, k : k + HEAD_DIM] for k in range(0, other.shape[1], LANES)], axis=1
        )


class Pairs(Scatter):
    def second(self):
        self.arrived(self.first_in, 0)
        width = self.first_in.shape[2]
        for slot in range(4):
            at = self.rows(slot, self.bits[0])
            self.held[slot, :, :width] = self.source[at]
            self.held[slot, :, width : 2 * width] = self.shared[at]
            self.held[slot, :, 2 * width :] = self.first_in[slot]
        for k in range(2):
            self.copy(self.held.at[2 * k + 1 - self.bits[1]], self.second_in.at[k], 1, 1).start()


def scatter_buffers(first, width, block):
    return [
        pltpu.VMEM((4, block, first), bf16),
        pltpu.VMEM((4, block, width), bf16),
        pltpu.VMEM((2, block, width), bf16),
        pltpu.VMEM((2, block, width), bf16),
        pltpu.VMEM((block, width), bf16),
        pltpu.VMEM((2, block, width), bf16),
    ]


def total_of(v):
    return jnp.sum(v, axis=0, keepdims=True)


def packed(block):
    middle = block.shape[-2] // 2
    first, second = block[..., :middle, :HEAD_DIM], block[..., middle:, :HEAD_DIM]
    return jnp.concatenate([first, second], axis=-1)


def unpacked(block):
    return jnp.concatenate([block[..., :HEAD_DIM], block[..., HEAD_DIM:]], axis=-2)


class Ring:
    def __init__(
        self, tensor, peers, parts, core_out, core_in, y_out, y_in, ag_send, ag_recv, sum_send,
        sum_recv,
    ):
        self.tensor, self.place = tensor, tensor % 2
        self.core, self.across, self.far = peers
        self.near_pair = tensor - self.place
        self.far_pair = lax.rem(self.near_pair + 2, 4)
        self.parts, self.core_out, self.core_in = parts, core_out, core_in
        self.y_out, self.y_in = y_out, y_in
        self.ag, self.sums = (ag_send, ag_recv), (sum_send, sum_recv)
        self.copies = {}

    def send(self, name, src, dst, sems, at, device):
        copy = remote(src, dst, sems[0].at[0], sems[1].at[at], device)
        copy.start()
        self.copies[name] = copy

    def share(self, phase, c, held):
        mine = held.at[c, self.tensor]
        self.send((phase, c, "y"), mine, mine, self.ag, (phase, c, 0), self.across)
        self.send((phase, c, "core"), mine, mine, self.ag, (phase, c, 1), self.core)

    def work(self, phase, c, side, value):
        self.parts[phase, c, side] = value.reshape(2, -1, value.shape[1])
        self.core_out[phase, c, side] = self.parts[phase, c, side, 1 - self.place].astype(bf16)
        self.send(
            (phase, c, side), self.core_out.at[phase, c, side], self.core_in.at[phase, c, side],
            self.sums, (phase, c, side), self.core,
        )

    def run(self, phase, held, work):
        for c in range(2):
            self.copies[phase, c, "core"].wait_recv()
            self.work(phase, c, 0, work(c, self.near_pair))
        for c in range(2):
            self.copies[phase, c, "y"].wait_recv()
            other = held.at[c, self.across[1]]
            self.send((phase, c, "pass"), other, other, self.ag, (phase, c, 2), self.core)
            if c == 1:
                self.cross(phase, 0)
            self.copies[phase, c, "pass"].wait_recv()
            self.work(phase, c, 1, work(c, self.far_pair))
        self.cross(phase, 1)

    def cross(self, phase, c):
        self.copies[phase, c, 1].wait_recv()
        both = self.parts[phase, c, 1, self.place] + self.core_in[phase, c, 1].astype(f32)
        self.y_out[phase, c] = both.astype(bf16)
        self.send(
            (phase, c, "sum"), self.y_out.at[phase, c], self.y_in.at[phase, c], self.sums,
            (phase, c, 2), self.across,
        )

    def total(self, phase, c):
        self.copies[phase, c, 0].wait_recv()
        self.copies[phase, c, "sum"].wait_recv()
        return (
            self.parts[phase, c, 0, self.place]
            + self.core_in[phase, c, 0].astype(f32)
            + self.y_in[phase, c].astype(f32)
        )


JOBS = 7
RESULTS = 19


def layer_kernel(
    n, lengths, x_far, wq_far, qb, wk_far, wv_far, vb, taps, out_far, out_bias, gain_one,
    shift_one, up_far, up_bias, down_far, down_bias, gain_two, shift_two, grad_far,
    *rest,
):
    results, rest = rest[:RESULTS], rest[RESULTS:]
    ready, rest = rest[:RESULTS], rest[RESULTS:]
    layer_body(
        n, lengths, x_far, wq_far, qb, wk_far, wv_far, vb, taps, out_far, out_bias, gain_one,
        shift_one, up_far, up_bias, down_far, down_bias, gain_two, shift_two, grad_far, results,
        ready, *rest,
    )


def layer_body(
    n, lengths, x_far, wq_far, qb, wk_far, wv_far, vb, taps, out_far, out_bias, gain_one,
    shift_one, up_far, up_bias, down_far, down_bias, gain_two, shift_two, grad_far, results, ready,
    x, wk, wq, wv, up_weight, down_weight, out_grad, out_weight, out_whole,
    stage, ks, qs, vs, k1, p3, newton, out_stage, out_single, attn_pair, attn_single,
    pairs_in, singles_in, heads_out, grad_attn, hidden, slope, active, down_in, up_in,
    core_out, core_in, y_out, y_in, core_last, y_last,
    gs, back_stage, back_single, come_pair, come_single, weight_in, out_in, early, early_tensor, tokens_own, tokens_low, source_up,
    source_down, source_out, source_v, source_kq, shared_kq, early_out, early_in, late_out, late_in, tokens_whole,
    parts_held,
    *rest,
):
    buffers, sems = rest[: 6 * JOBS], rest[6 * JOBS :]
    (load, send, recv, out_send, out_recv, whole_send, whole_recv, a2a_send, a2a_recv, ag_send,
     ag_recv, sum_send, sum_recv, grad_send, grad_recv, back_send, back_recv, share_send,
     share_recv, small_send, small_recv, job_send, job_recv, own_send, own_recv, last_send, last_recv,
     store) = sems
    (output, grad_tokens, grad_query, query_bias, grad_key, grad_value, value_bias, conv, grad_out,
     out_bias_grad, first_gain, first_shift, grad_up, up_bias_grad, grad_down, down_bias_grad,
     second_gain, second_shift, proxy) = ready
    stores = []

    def done(*numbers):
        for i in numbers:
            copy = pltpu.make_async_copy(ready[i], results[i], store.at[i])
            copy.start()
            stores.append(copy)

    me = lax.axis_index("seq")
    tensor = lax.axis_index("tensor")
    rows, width = x.shape
    batch = n // 2
    tok = rows // batch
    total = n * tok
    half = CONV // 2
    own, side = me // 2, me % 2
    scale = HEAD_DIM ** (-0.5)
    ring_peers = around(n, me, tensor)
    peers = others(me, tensor)
    core, across, far = peers
    mine = block_rows(tensor, tok)
    local = wk.shape[0]
    barrier = greet(ring_peers + peers)
    loads = []
    for i, (source, target) in enumerate((
        (x_far, x), (wk_far, wk), (wq_far, wq), (wv_far, wv),
        (out_far, out_weight), (up_far, up_weight),
        (down_far, down_weight), (grad_far, out_grad),
    )):
        copy = pltpu.make_async_copy(source, target, load.at[i])
        copy.start()
        loads.append(copy)
    hidden_width = up_weight.shape[1]
    span = hidden_width // 2
    jobs = [
        kind(i, me, tensor, source, columns, buffers[6 * i : 6 * i + 6], job_send, job_recv, order)
        for i, (kind, source, columns, order) in enumerate((
            (Line, source_down, (0, span), (0, 1, 2)),
            (Scatter, source_down, (span, span), (1, 0, 2)),
            (Line, source_up, (0, span), (0, 1, 2)),
            (Line, source_up, (span, span), (0, 1, 2)),
            (Scatter, source_out, (0, local), (0, 1, 2)),
            (Heads, source_v, (0, LANES), (0, 1, 2)),
            (Pairs, source_kq, (0, LANES), (0, 1, 2)),
        ))
    ]
    job_down, job_up = jobs[0:2], jobs[2:4]
    job_out, job_v, job_kq = jobs[4:]
    job_kq.shared = shared_kq

    owned = (ks, qs, vs)
    offsets = (0, 0, half)
    for padded in (vs, gs):
        padded[0:half] = jnp.zeros((half, LANES), bf16)
        padded[half + total : total + tok] = jnp.zeros((tok - half, LANES), bf16)
    even = side == 0

    seven = pl.ds(0, (n - 1) * tok)

    def spread(i):
        here = pl.ds(pl.multiple_of(offsets[i] + me * tok, 16), tok)
        for d in range(1, n):
            peer = lax.rem(me + d, n)
            copy = remote(
                stage.at[i, peer % 2, block_rows(peer // 2, tok)], owned[i].at[here],
                send.at[i], recv.at[i], (peer, tensor),
            )
            copy.start()
        owned[i][here] = stage[i, side, block_rows(own, tok)]

    loads[0].wait()
    loads[1].wait()
    y = dot(x[...], wk[...], NT)
    stage[0, 0], stage[0, 1] = paired(y.astype(bf16))
    pl.semaphore_wait(barrier, n + 2)
    spread(0)
    loads[2].wait()
    y = dot(x[...], wq[...], NT) + qb[...].reshape(1, local)
    stage[1, 0], stage[1, 1] = paired(y.astype(bf16))
    spread(1)
    loads[3].wait()
    y = dot(x[...], wv[...], NT) + vb[...].reshape(1, local)
    position = me * tok + iota((tok, local), 0)
    y = jnp.concatenate(
        [
            jnp.where(position < lengths[b], y[b * tok : (b + 1) * tok], 0.0)
            for b in range(batch)
        ],
        axis=0,
    )
    stage[2, 0], stage[2, 1] = paired(y.astype(bf16))
    loads[4].wait()
    pair_rows = block_rows(tensor, LANES)
    single_rows = pl.ds(pl.multiple_of(4 * LANES + tensor * HEAD_DIM, HEAD_DIM), HEAD_DIM)
    first, single = out_weight[:LANES], out_weight[LANES:]
    out_whole[pair_rows] = jnp.where(
        even, first, jnp.concatenate([single, first[HEAD_DIM:]], axis=0)
    )
    out_whole[single_rows] = jnp.where(even, single, first[:HEAD_DIM])
    for i, device in enumerate(peers):
        for at in (pair_rows, single_rows):
            part = out_whole.at[at]
            remote(part, part, whole_send.at[0], whole_recv.at[0], device).start()

    length = lengths[own]
    same_head = block_mask()
    identity = eye()
    ones = jnp.where(same_head, 1.0, 0.0).astype(bf16)
    members = member_rows(length, total)
    counts = segment_counts(length)
    matrices = [taps_matrix(taps_row(taps, h, tok), tok) for h in (2 * side, 1)]
    flip = jnp.where(
        iota((2 * tok, 2 * tok), 0) + iota((2 * tok, 2 * tok), 1) == CONV - 1, 1.0, 0.0
    ).astype(bf16)
    reverse = [
        taps_matrix(
            fine(jnp.broadcast_to(taps_row(taps, h, tok), (8, 2 * tok)), flip)[0:1], tok
        )
        for h in (2 * side, 1)
    ]
    for i, w in enumerate((wk, wq, wv)):
        pair, single = w[:LANES], w[LANES:]
        weight_in[i * LANES : (i + 1) * LANES] = jnp.where(
            even, pair, jnp.concatenate([single, pair[HEAD_DIM:]], axis=0)
        )
        start = 3 * LANES + i * HEAD_DIM
        weight_in[start : start + HEAD_DIM] = jnp.where(even, single, pair[:HEAD_DIM])
    settle(ks.at[seven], recv.at[0])
    keys = ks[...]
    key_marks = jnp.where(same_head, dot(members, keys) / counts, 0.0)
    settle(qs.at[seven], send.at[1])
    spread(2)
    settle(qs.at[seven], recv.at[1])
    queries = qs[...]
    query_marks = jnp.where(same_head, dot(members, queries) / counts, 0.0)
    scores = jnp.where(same_head, fine(query_marks, key_marks, NT) * scale, negative)
    weights = jnp.exp(scores - jnp.max(scores, axis=1, keepdims=True))
    kernel_two = weights / jnp.sum(weights, axis=1, keepdims=True)
    inverse = jnp.where(
        same_head, kernel_two.T / block_sums(kernel_two * kernel_two, same_head), 0.0
    )
    product = fine(kernel_two, inverse)
    for step in range(NS_ITERS):
        inner = fine(product, 7.0 * identity - product)
        outer = 13.0 * identity - fine(product, 15.0 * identity - inner)
        newton[5 * step] = inverse
        newton[5 * step + 1] = product
        newton[5 * step + 2] = inner
        newton[5 * step + 3] = outer
        newton[5 * step + 4] = fine(product, kernel_two)
        inverse = 0.25 * fine(inverse, outer)
        product = 0.25 * fine(product, outer)

    deviation = identity - product
    norms = jnp.sqrt(block_sums(deviation * deviation, same_head))
    first, second = norms[0:1, 0:1], norms[LANES - 1 :, LANES - 1 :]
    norm_sum = jnp.where(side == 0, first + second, first) / (batch * HEADS)
    early[7:8] = jnp.broadcast_to(norm_sum, (1, width))

    first_scores = fine(queries, key_marks, NT) * scale
    left = iota(first_scores.shape, 1) < HEAD_DIM
    top_left = jnp.max(jnp.where(left, first_scores, negative), axis=1, keepdims=True)
    top_right = jnp.max(jnp.where(left, negative, first_scores), axis=1, keepdims=True)
    weights = jnp.exp(first_scores - jnp.where(left, top_left, top_right))
    k1[...] = weights / fine(weights, ones)

    third_scores = fine(keys, query_marks, NT) * scale
    alive = iota(third_scores.shape, 0) < length
    third_scores = jnp.where(alive, third_scores, negative)
    weights = jnp.exp(third_scores - jnp.max(third_scores, axis=0, keepdims=True))
    weights = jnp.where(alive, weights, 0.0)
    third_prob = weights / jnp.sum(weights, axis=0, keepdims=True)
    p3[...] = third_prob

    settle(vs.at[seven], recv.at[2])
    values = vs[half : half + total]
    third_out = jnp.where(same_head, fine(third_prob, values, TN), 0.0)
    carried = fine(inverse, third_out)

    for d in range(1, n + 1):
        peer = lax.rem(me + d, n)
        start = pl.multiple_of(peer * tok, tok)
        nystrom = fine(k1[pl.ds(start, tok)], carried)
        convolved = conv_block(matrices, vs[pl.ds(start, 2 * tok)])
        low = (nystrom + convolved).astype(bf16)
        if d == n:
            attn_pair[own] = low
            continue
        if d % 2 == 0:
            source, target = out_stage.at[d - 1], attn_pair.at[own]
            source[...] = low
        else:
            source, target = out_single.at[d - 1], attn_single.at[own]
            source[...] = packed(low)
        remote(source, target, out_send.at[d % 2], out_recv.at[d % 2], (peer, tensor)).start()
    three = pl.ds(0, 3)
    settle(attn_pair.at[three], out_recv.at[0])
    settle(attn_single, out_recv.at[1])
    settle(out_whole.at[pl.ds(0, 3 * local)], whole_recv.at[0])

    for i in (2, 1, 0):
        t = peers[i][1]
        for j, (held, come) in enumerate(((attn_pair, pairs_in), (attn_single, singles_in))):
            remote(
                held.at[t], come.at[tensor], a2a_send.at[j], a2a_recv.at[j], peers[i]
            ).start()
    pairs_in[tensor] = attn_pair[tensor]
    singles_in[tensor] = attn_single[tensor]
    z, side_of_chip = me // 2, tensor % 2
    beside = (me + 1 - 2 * side, tensor)
    def give_tokens(src, dst, i, device):
        remote(src, dst, own_send.at[i // 2], own_recv.at[i], device).start()

    def half_block(b):
        start = pl.multiple_of(b * tok + side_of_chip * (tok // 2), tok // 2)
        return pl.ds(start, tok // 2)

    tokens_own[me, side_of_chip] = x[half_block(own)]
    for k in range(1, 4):
        peer = lax.rem(z + k, 4)
        give_tokens(
            x.at[half_block(peer)], tokens_own.at[me, side_of_chip], 0, (2 * peer + side, tensor)
        )
    half_own = tokens_own.at[me, side_of_chip]
    give_tokens(half_own, half_own, 1, beside)

    def pass_tokens():
        settle(tokens_own.at[pl.ds(0, 3), 0], own_recv.at[0])
        for k in range(1, 4):
            come = tokens_own.at[2 * lax.rem(z + 4 - k, 4) + side, side_of_chip]
            give_tokens(come, come, 1, beside)

    for copy in loads[5:]:
        copy.wait()
    settle(pairs_in.at[three], a2a_recv.at[0])
    settle(singles_in.at[three], a2a_recv.at[1])
    def line(vector):
        return vector[...].reshape(1, vector.shape[0])

    piece = tok // 2
    chunks = range(2)
    ring = Ring(
        tensor, peers, parts_held, core_out, core_in, y_out, y_in, ag_send, ag_recv, sum_send,
        sum_recv,
    )

    def rows_of(c):
        return pl.ds(pl.multiple_of(tensor * tok + c * piece, piece), piece)

    def normed(c):
        at = slice(c * piece, (c + 1) * piece)
        lanes = slice(c * HEAD_DIM, (c + 1) * HEAD_DIM)
        heads = jnp.concatenate(
            [pairs_in[t, at] for t in range(4)] + [singles_in[t, :, lanes] for t in range(4)],
            axis=1,
        )
        branch = dot(heads, out_whole[...])
        first_total = x[rows_of(c)].astype(f32) + (branch + line(out_bias))
        normal, inverse_std = normal_of(first_total)
        whole_row = normal * line(gain_one) + line(shift_one)
        hidden[c, tensor] = whole_row.astype(bf16)
        ring.share(0, c, hidden)
        return normal, inverse_std, whole_row

    def up(c, t):
        at = pl.ds(t, 2)
        value = dot(hidden[c, at].reshape(tok, width), up_weight[...]) + line(up_bias)
        half_erf = 0.5 * (1.0 + lax.erf(value * (0.5**0.5)))
        density = jnp.exp(-0.5 * value * value) * (0.5 / jnp.pi) ** 0.5
        slope[c, at] = (half_erf + value * density).reshape(2, piece, hidden_width)
        low = (value * half_erf).astype(bf16)
        active[c, at] = low.reshape(2, piece, hidden_width)
        return dot(low, down_weight[...])

    def down(c, t):
        at = pl.ds(t, 2)
        grad = dot(down_in[c, at].reshape(tok, width), down_weight[...], NT)
        low = (grad * slope[c, at].reshape(tok, hidden_width)).astype(bf16)
        up_in[c, at] = low.reshape(2, piece, hidden_width)
        return dot(low, up_weight[...], NT)

    after_norm_one = [normed(c) for c in chunks]
    ring.run(0, hidden, up)
    pass_tokens()

    grads_second, sums_second = [], []
    for c in chunks:
        hidden_one = after_norm_one[c][2]
        second_total = hidden_one + (ring.total(0, c) + line(down_bias))
        normal, inverse_std = normal_of(second_total)
        output[rows_of(c)] = (normal * line(gain_two) + line(shift_two)).astype(bf16)
        grad_output = out_grad[rows_of(c)].astype(f32)
        grad_second = before_norm(grad_output, normal, inverse_std, line(gain_two))
        low = grad_second.astype(bf16)
        down_in[c, tensor] = low
        ring.share(1, c, down_in)
        grads_second.append(grad_second)
        sums_second.append(
            (total_of(grad_output * normal), total_of(grad_output), total_of(low.astype(f32)))
        )
    ring.run(1, down_in, down)
    everything = (rows, width)
    every_hidden = (rows, hidden_width)
    source_down[...] = dot(
        down_in[...].reshape(everything), active[...].reshape(every_hidden), TN
    ).astype(bf16)
    for job in job_down:
        job.first()

    grads_first, sums_first = [], []
    for c in chunks:
        normal, inverse_std, _ = after_norm_one[c]
        grad_hidden = grads_second[c] + ring.total(1, c)
        grad_first = before_norm(grad_hidden, normal, inverse_std, line(gain_one))
        low = grad_first.astype(bf16)
        out_in[rows_of(c)] = low
        heads = dot(low, out_whole[...], NT).astype(bf16)
        at = slice(c * piece, (c + 1) * piece)
        for t in range(4):
            start = 4 * LANES + t * HEAD_DIM
            pair = heads[:, t * LANES : (t + 1) * LANES]
            heads_out[t, 0, at] = pair
            heads_out[t, 1, at] = jnp.concatenate(
                [heads[:, start : start + HEAD_DIM], pair[:, HEAD_DIM:]], axis=1
            )
        for i in (2, 1, 0):
            remote(
                heads_out.at[peers[i][1], :, pl.ds(c * piece, piece)],
                grad_attn.at[:, rows_of(c)], a2a_send.at[2], a2a_recv.at[2], peers[i],
            ).start()
        grads_first.append(grad_first)
        sums_first.append(
            (total_of(grad_hidden * normal), total_of(grad_hidden), total_of(low.astype(f32)))
        )
    grad_attn[:, mine] = heads_out[tensor]
    source_up[...] = dot(
        hidden[...].reshape(everything), up_in[...].reshape(every_hidden), TN
    ).astype(bf16)
    for i in range(3):
        early[i : i + 1] = sums_second[0][i] + sums_second[1][i]
        early[i + 3 : i + 4] = sums_first[0][i] + sums_first[1][i]
    early[6:7] = dot(jnp.ones((8, rows), bf16), up_in[...].reshape(every_hidden))[0:1]
    early_tensor[tensor] = early[...]
    job_up[0].first(range(2))
    three_blocks = grad_attn.at[:, pl.ds(0, 3 * tok)]
    settle(three_blocks, a2a_recv.at[2])

    here = pl.ds(pl.multiple_of(half + me * tok, 16), tok)
    for d in range(1, n):
        peer = lax.rem(me + d, n)
        remote(
            grad_attn.at[d % 2, block_rows(peer // 2, tok)], gs.at[here], grad_send.at[0],
            grad_recv.at[0], (peer, tensor),
        ).start()
    gs[here] = grad_attn[0, block_rows(own, tok)]
    for i, device in enumerate(peers):
        remote(
            early, early_tensor.at[tensor], small_send.at[0], small_recv.at[0], device
        ).start()
    shares = []
    for i, held in enumerate((out_in, output)):
        for j, device in enumerate((across, core)):
            copy = remote(
                held.at[mine], held.at[mine], share_send.at[i], share_recv.at[i, j], device
            )
            copy.start()
            shares.append(copy)
    job_down[0].second()
    job_up[0].first(range(2, 4))
    job_down[1].second()
    job_up[1].first()
    settle(tokens_own.at[pl.ds(0, 4), 0], own_recv.at[1])
    half_all = tokens_own.at[:, side_of_chip]
    give_tokens(half_all, half_all, 2, core)

    members = member_columns(length, total)
    def give(i, block):
        low = block.astype(bf16)
        back_stage[i] = low.reshape(n, tok, LANES)
        back_single[i] = packed(low.reshape(n, tok, LANES))
        for d in range(1, n):
            peer = lax.rem(me + d, n)
            source, target = (back_stage, come_pair) if d % 2 == 0 else (back_single, come_single)
            remote(
                source.at[i, peer], target.at[i, own], back_send.at[d % 2],
                back_recv.at[d % 2], (peer, tensor),
            ).start()
        come_pair[i, own] = back_stage[i, me]
        return low

    settle(gs.at[seven], grad_recv.at[0])
    grad = gs[half : half + total]
    kernel_one = k1[...]
    grad_carried = jnp.where(same_head, fine(kernel_one, grad, TN), 0.0)
    grad_third = fine(inverse, grad_carried, TN)
    grad_inverse = fine(grad_carried, third_out, NT)
    third_prob = p3[...]
    convolved = jnp.concatenate(
        [conv_block(reverse, gs[m * tok : (m + 2) * tok]) for m in range(n)], axis=0
    )
    grad_values = fine(third_prob, grad_third) + convolved
    value_in = give(2, jnp.where(iota(grad_values.shape, 0) < length, grad_values, 0.0))


    settle(early_tensor.at[three], small_recv.at[0])
    by_tensor = early_tensor[0] + early_tensor[1] + early_tensor[2] + early_tensor[3]
    early_out[0] = jnp.where(iota(by_tensor.shape, 0) == 6, early[...], by_tensor)
    smalls_early = []

    def early_next(k):
        if k > 0:
            smalls_early[k - 1].wait_recv()
            early_out[k] = early_out[k - 1] + early_in[k - 1]
        if k < 3:
            copy = remote(
                early_out.at[k], early_in.at[k], small_send.at[1], small_recv.at[1 + k],
                job_out.partners[(k + 1) % 3],
            )
            copy.start()
            smalls_early.append(copy)

    early_next(0)
    job_down[0].third()
    settle(half_all, own_recv.at[2])
    tokens_all = tokens_own[...].reshape(total, width)
    source_v[...] = dot(tokens_all, value_in, TN).astype(bf16)
    kernel_back = jnp.zeros((LANES, LANES), f32)
    grad_state = grad_inverse
    for step in reversed(range(NS_ITERS)):
        state, product, inner, outer, shifted = [newton[5 * step + i] for i in range(5)]
        grad_outer = 0.25 * fine(state, grad_state, TN)
        partial = (
            fine(grad_outer, inner, NT)
            - 15.0 * grad_outer
            - fine(7.0 * product - inner, grad_outer, TN)
        )
        rest_part = 7.0 * grad_outer - fine(grad_outer, product, NT)
        grad_state = (
            0.25 * fine(grad_state, outer, NT)
            + fine(kernel_two, partial, TN)
            + fine(shifted, rest_part, TN)
        )
        kernel_back = kernel_back + fine(partial + fine(product, rest_part, TN), state, NT)
    squares = block_sums(kernel_two * kernel_two, same_head)
    spread_sum = jnp.where(same_head, block_sums(grad_state * newton[0], same_head), 0.0)
    kernel_back = kernel_back + (grad_state.T - 2.0 * kernel_two * spread_sum) / squares
    grad_scores = scale * kernel_two * (
        kernel_back - jnp.sum(kernel_two * kernel_back, axis=1, keepdims=True)
    )
    query_two = fine(grad_scores, key_marks)
    key_two = fine(grad_scores, query_marks, TN)

    job_up[0].second()
    grad_one = fine(grad, carried, NT)
    both = kernel_one * grad_one
    first_scores = scale * (both - kernel_one * fine(both, ones))
    key_one = jnp.where(same_head, fine(first_scores, queries, TN), 0.0)
    delta = fine(jnp.ones((8, LANES), bf16), grad_third * third_out, NT)[0:1]
    third_scores = scale * third_prob * (fine(values, grad_third, NT) - delta)
    query_three = jnp.where(same_head, fine(third_scores, keys, TN), 0.0)
    job_v.first()
    key_in = give(0, fine(third_scores, query_marks) + fine(members, (key_one + key_two) / counts))
    query_in = give(1, fine(first_scores, key_marks) + fine(members, (query_two + query_three) / counts))

    for i, held in enumerate((out_in, output)):
        shares[2 * i].wait_recv()
        block = held.at[block_rows(across[1], tok)]
        copy = remote(block, block, share_send.at[i], share_recv.at[i, 2], core)
        copy.start()
        shares.append(copy)
    lanes_own, lanes_both = slice(0, HEAD_DIM), slice(HEAD_DIM, LANES)
    for ref, at in ((source_kq, lanes_own), (shared_kq, lanes_both)):
        ref[...] = dot(
            tokens_all, jnp.concatenate([key_in[:, at], query_in[:, at]], axis=1), TN
        ).astype(bf16)
    job_kq.first()
    shares[1].wait_recv()
    shares[4].wait_recv()
    pair, single = attn_pair[...].reshape(rows, LANES), unpacked(attn_single[...])
    single = single.reshape(rows, HEAD_DIM)
    attention = jnp.concatenate(
        [
            jnp.where(even, pair, jnp.concatenate([single, pair[:, HEAD_DIM:]], axis=1)),
            jnp.where(even, single, pair[:, :HEAD_DIM]),
        ],
        axis=1,
    )
    source_out[...] = dot(out_in[...], attention, TN).astype(bf16)
    job_out.first()
    position = iota((tok, tok), 0) + iota((tok, tok), 1)
    upside = jnp.where(position == tok - 1, 1.0, 0.0).astype(bf16)
    lane = iota((tok, LANES), 1)
    conv_rows = []
    for h in range(2):
        inner = (lane < HEAD_DIM) if h == 0 else (lane >= HEAD_DIM)
        table = jnp.zeros((tok, 2 * tok), f32)
        for m in range(n):
            block = gs[half + m * tok : half + (m + 1) * tok]
            block = jnp.where(inner, block, jnp.zeros_like(block))
            table = table + dot(block, vs[m * tok : (m + 2) * tok], NT)
        table = pltpu.roll(fine(upside, table), 0, 1, stride=1, stride_axis=0)
        row = jnp.sum(table, axis=0, keepdims=True)
        row = pltpu.roll(jnp.broadcast_to(row, (8, 2 * tok)), tok + 1, 1)
        conv_rows.append(row[0:1, :LANES])
    late = late_out.at[0]
    late[...] = jnp.zeros(late.shape, f32)
    column = jnp.ones((8, total), bf16)
    for row, v in ((0, query_in), (1, value_in)):
        v = dot(column, v)[0:1]
        late[row : row + 1, 0:LANES] = jnp.where(even, v, 0.0)
        late[row : row + 1, LANES:local] = jnp.where(even, 0.0, v[:, :HEAD_DIM])
    late[2:3, 0:LANES] = jnp.where(even, conv_rows[0], 0.0)
    late[3:4, 0:LANES] = jnp.where(even, conv_rows[1], 0.0)
    late[4:5, 0:LANES] = jnp.where(even, 0.0, conv_rows[0])
    smalls_late = []

    def late_next(k):
        if k > 0:
            smalls_late[k - 1].wait_recv()
            late_out[k] = late_out[k - 1] + late_in[k - 1]
        if k < 3:
            copy = remote(
                late_out.at[k], late_in.at[k], small_send.at[2], small_recv.at[4 + k],
                job_out.partners[(k + 1) % 3],
            )
            copy.start()
            smalls_late.append(copy)

    late_next(0)
    early_next(1)
    job_down[1].third()
    job_down[0].fourth()
    job_up[0].third()
    job_up[1].second()
    job_v.second()
    settle(come_pair.at[:, three], back_recv.at[0])
    settle(come_single, back_recv.at[1])
    singles = []
    for i in range(3):
        tokens_low[:, i * LANES : (i + 1) * LANES] = come_pair[i].reshape(rows, LANES)
        singles.append(unpacked(come_single[i]).reshape(rows, HEAD_DIM))
    tokens_low[:, 3 * LANES :] = jnp.concatenate(singles, axis=1)

    def input_part(t):
        return dot(tokens_low[block_rows(t, tok)], weight_in[...])

    def pass_sum(k, value, device):
        core_last[0, k] = value.astype(bf16)
        copy = remote(
            core_last.at[0, k], core_last.at[1, k], last_send.at[0], last_recv.at[k], device
        )
        copy.start()
        return copy

    middle = pass_sum(1, input_part(far[1]), core)
    near = pass_sum(0, input_part(core[1]), core)
    crossing = input_part(across[1])
    middle.wait_recv()
    y_last[0] = (crossing + core_last[1, 1].astype(f32)).astype(bf16)
    final = remote(y_last.at[0], y_last.at[1], last_send.at[0], last_recv.at[2], across)
    final.start()
    result = input_part(tensor) + jnp.concatenate(grads_first, axis=0)
    late_next(1)
    job_kq.second()
    early_next(2)
    job_v.third()
    near.wait_recv()
    final.wait_recv()
    result = result + core_last[1, 0].astype(f32) + y_last[1].astype(f32)
    tokens_whole[mine] = result.astype(bf16)
    ends = []
    for j, device in enumerate((across, core)):
        copy = remote(
            tokens_whole.at[mine], tokens_whole.at[mine], share_send.at[2], share_recv.at[2, j],
            device,
        )
        copy.start()
        ends.append(copy)
    job_out.second()
    job_up[0].fourth()
    job_up[1].third()
    late_next(2)

    def into(ref, k):
        def write(value):
            ref[:, k * span : (k + 1) * span] = value

        return write

    for k, job in enumerate(job_down):
        job.last(into(grad_down, k))
    done(14)
    job_kq.third()
    job_up[1].fourth()
    ends[0].wait_recv()
    block = tokens_whole.at[block_rows(across[1], tok)]
    copy = remote(block, block, share_send.at[2], share_recv.at[2, 2], core)
    copy.start()
    ends.append(copy)
    job_out.third()
    ends[1].wait_recv()
    ends[2].wait_recv()
    grad_tokens[...] = tokens_whole[...].astype(f32)
    done(1)
    early_next(3)
    late_next(3)
    by_seq = early_out[3]
    for ref, row in (
        (second_gain, 0), (second_shift, 1), (down_bias_grad, 2), (first_gain, 3),
        (first_shift, 4), (out_bias_grad, 5), (up_bias_grad, 6),
    ):
        ref[...] = by_seq[row]
    proxy[...] = by_seq[7:8, 0:1]
    by_seq = late_out[3]
    query_bias[...] = by_seq[0, :local]
    value_bias[...] = by_seq[1, :local]
    conv[...] = by_seq[2:5, :CONV]
    shares[3].wait_recv()
    shares[5].wait_recv()
    done(0, 3, 6, 7, 9, 10, 11, 13, 15, 16, 17, 18)

    def heads(job, *refs):
        def write(result):
            for i, ref in enumerate(refs):
                start = len(refs) * LANES + i * HEAD_DIM
                ref[:, :LANES] = result[:, i * LANES : (i + 1) * LANES]
                ref[:, LANES:] = result[:, start : start + HEAD_DIM]

        job.last(write)

    heads(job_v, grad_value)
    done(5)
    for k, job in enumerate(job_up):
        job.last(into(grad_up, k))
    done(12)
    def write_kq(result):
        mine, both, come = [result[:, i * LANES : (i + 1) * LANES] for i in range(3)]
        first, third = jnp.where(even, mine, come), jnp.where(even, come, mine)
        for ref, at in ((grad_key, lanes_own), (grad_query, lanes_both)):
            ref[:, :LANES] = jnp.concatenate([first[:, at], both[:, at]], axis=1)
            ref[:, LANES:] = third[:, at]

    job_kq.last(write_kq)
    done(2, 4)

    def write_out(value):
        grad_out[...] = value.T

    job_out.last(write_out)
    done(8)
    three_rows = x.at[pl.ds(0, 3 * tok)]
    for ref, sem in (
        (ks.at[seven], send.at[0]), (vs.at[seven], send.at[2]),
        (attn_pair.at[three], out_send.at[0]), (attn_single, out_send.at[1]),
        (out_whole.at[pl.ds(0, 3 * local)], whole_send.at[0]),
        (pairs_in.at[three], a2a_send.at[0]), (singles_in.at[three], a2a_send.at[1]),
        (three_blocks, a2a_send.at[2]), (out_whole, ag_send.at[0]), (out_whole, sum_send.at[0]),
        (gs.at[seven], grad_send.at[0]), (come_pair.at[:, three], back_send.at[0]),
        (come_single, back_send.at[1]), (three_rows, share_send.at[0]),
        (three_rows, share_send.at[1]), (three_rows, share_send.at[2]),
        (early_tensor.at[three], small_send.at[0]), (early_in, small_send.at[1]),
        (late_in, small_send.at[2]), (tokens_own.at[pl.ds(0, n - 1), 0], own_send.at[0]),
        (half_all, own_send.at[1]), (three_rows, last_send.at[0]),
    ):
        settle(ref, sem)
    for job in jobs:
        job.finish()
    for copy in stores:
        copy.wait()


def finish_kernel(*refs):
    come, go, held = [refs[i * RESULTS : (i + 1) * RESULTS] for i in range(3)]
    loads, stores = refs[3 * RESULTS :]
    copies = [
        pltpu.make_async_copy(come[i], held[i], loads.at[i]) for i in range(RESULTS)
    ]
    for copy in copies:
        copy.start()
    outs = []
    for i in range(RESULTS):
        copies[i].wait()
        copy = pltpu.make_async_copy(held[i], go[i], stores.at[i])
        copy.start()
        outs.append(copy)
    for copy in outs:
        copy.wait()


def whole(shape, dtype):
    return jax.ShapeDtypeStruct(shape, dtype)


VMEM = pl.BlockSpec(memory_space=pltpu.VMEM)
SMEM = pl.BlockSpec(memory_space=pltpu.SMEM)
HBM = pl.BlockSpec(memory_space=pl.ANY)


def dma(*shape):
    return pltpu.SemaphoreType.DMA(shape)


def gathered_plan(
    n, tokens, lengths, query_weight, query_bias, key_weight, value_weight, value_bias,
    conv_kernel, out_weight, out_bias, first_gain, first_shift, up_weight, up_bias, down_weight,
    down_bias, second_gain, second_shift, out_grad,
):
    batch, tok, width = tokens.shape
    rows = batch * tok
    local = query_weight.shape[1]
    hidden = up_weight.shape[1]
    total = n * tok
    block = width // n
    piece = tok // 2

    def low(*shape):
        return pltpu.VMEM(shape, bf16)

    def wide(*shape):
        return pltpu.VMEM(shape, f32)

    results = (
        whole((rows, width), bf16),
        whole((rows, width), f32),
        whole((block, local), f32),
        whole((local,), f32),
        whole((block, local), f32),
        whole((block, local), f32),
        whole((local,), f32),
        whole(conv_kernel.shape, f32),
        whole((local, block), f32),
        whole((width,), f32),
        whole((width,), f32),
        whole((width,), f32),
        whole((block, hidden), f32),
        whole((hidden,), f32),
        whole((block, hidden), f32),
        whole((width,), f32),
        whole((width,), f32),
        whole((width,), f32),
        whole((1, 1), f32),
    )
    outs = pl.pallas_call(
        functools.partial(layer_kernel, n),
        out_shape=results,
        in_specs=[SMEM, HBM, HBM, VMEM, HBM, HBM, VMEM, VMEM, HBM, VMEM, VMEM, VMEM, HBM, VMEM, HBM,
                  VMEM, VMEM, VMEM, HBM],
        out_specs=(HBM,) * RESULTS,
        scratch_shapes=[pltpu.VMEM(r.shape, r.dtype) for r in results]
        + [
            low(rows, width), low(local, width), low(local, width), low(local, width),
            low(width, hidden), low(hidden, width), low(rows, width), low(local, width),
            low(width, width),
            low(3, 2, rows, LANES), low(total, LANES), low(total, LANES), low(total + tok, LANES),
            wide(total, LANES), wide(total, LANES), wide(5 * NS_ITERS, LANES, LANES),
            low(n - 1, tok, LANES), low(n - 1, piece, LANES), low(batch, tok, LANES),
            low(batch, piece, LANES),
            low(4, tok, LANES), low(4, piece, LANES), low(4, 2, tok, LANES),
            low(2, rows, LANES), low(2, 4, piece, width), wide(2, 4, piece, hidden),
            low(2, 4, piece, hidden), low(2, 4, piece, width), low(2, 4, piece, hidden),
            low(2, 2, 2, piece, width), low(2, 2, 2, piece, width), low(2, 2, piece, width),
            low(2, 2, piece, width), low(2, 2, tok, width), low(2, tok, width),
            low(total + tok, LANES), low(3, n, tok, LANES), low(3, n, tok // 2, LANES),
            low(3, batch, tok, LANES), low(3, batch, tok // 2, LANES), low(3 * local, width),
            low(rows, width), wide(8, width), wide(4, 8, width), low(n, 2, tok // 2, width),
            low(rows, 3 * local), low(width, hidden), low(width, hidden), low(width, local),
            low(width, LANES), low(width, LANES), low(width, LANES), wide(4, 8, width), wide(3, 8, width),
            wide(4, 8, 2 * LANES), wide(3, 8, 2 * LANES), low(rows, width), wide(2, 2, 2, 2, piece, width),
        ]
        + [
            b
            for first, w in (
                *((hidden // 2, hidden // 2),) * 4, (local, local), (LANES, local), (LANES, 2 * local)
            )
            for b in scatter_buffers(first, w, block)
        ]
        + [
            dma(8), dma(3), dma(3), dma(2), dma(2), dma(1), dma(1), dma(3), dma(3), dma(1),
            dma(2, 2, 3), dma(1), dma(2, 2, 3), dma(1), dma(1), dma(2), dma(2), dma(3), dma(3, 3),
            dma(3), dma(7), dma(JOBS, 2), dma(JOBS, 5), dma(2), dma(3), dma(1), dma(3),
            dma(RESULTS),
        ],
        compiler_params=pltpu.CompilerParams(
            collective_id=0, has_side_effects=True, vmem_limit_bytes=56 * 2**20
        ),
        name="layer",
    )(
        lengths, tokens.reshape(rows, width), query_weight.T, query_bias, key_weight.T,
        value_weight.T, value_bias, conv_kernel, out_weight, out_bias, first_gain, first_shift,
        up_weight, up_bias, down_weight, down_bias, second_gain, second_shift,
        out_grad.reshape(rows, width),
    )
    outs = pl.pallas_call(
        finish_kernel,
        out_shape=results,
        in_specs=[HBM] * RESULTS,
        out_specs=(HBM,) * RESULTS,
        scratch_shapes=[pltpu.VMEM(r.shape, r.dtype) for r in results]
        + [dma(RESULTS), dma(RESULTS)],
        compiler_params=pltpu.CompilerParams(vmem_limit_bytes=60 * 2**20),
        name="finish",
    )(*outs)
    return (
        outs[0].reshape(tokens.shape),
        outs[1].reshape(tokens.shape),
        *outs[2:14],
        outs[14].T,
        *outs[15:18],
        outs[18].reshape(()),
    )


def per_device(seq, tensor, *args):
    batch, tok, width = args[0].shape
    heads = args[7].shape[0]
    if seq == 8 and tensor == 4 and batch == 4 and heads == 3 and tok == 128:
        return gathered_plan(seq, *args)
    return general_plan(*args)


def solution(mesh):
    return jax.shard_map(
        functools.partial(per_device, mesh.shape["seq"], mesh.shape["tensor"]),
        mesh=mesh,
        in_specs=(
            P(None, "seq", None),
            P(),
            P(None, "tensor"),
            P("tensor"),
            P(None, "tensor"),
            P(None, "tensor"),
            P("tensor"),
            P("tensor", None),
            P("tensor", None),
            P(),
            P(),
            P(),
            P(None, "tensor"),
            P("tensor"),
            P("tensor", None),
            P(),
            P(),
            P(),
            P(None, "seq", None),
        ),
        out_specs=(
            P(None, "seq", None),
            P(None, "seq", None),
            P("seq", "tensor"),
            P("tensor"),
            P("seq", "tensor"),
            P("seq", "tensor"),
            P("tensor"),
            P("tensor", None),
            P("tensor", "seq"),
            P(),
            P(),
            P(),
            P("seq", "tensor"),
            P("tensor"),
            P("tensor", "seq"),
            P(),
            P(),
            P(),
            P(),
        ),
        check_vma=False,
    )
```

```python
import functools

import jax
import jax.numpy as jnp
from jax import lax
from jax.experimental import pallas as pl
from jax.experimental.pallas import tpu as pltpu
from jax.sharding import PartitionSpec as P

HEADS = 12
HEAD_DIM = 64
LAND = 64
CONV = 33
NS_ITERS = 6


highest = lax.Precision.HIGHEST
epsilon = 1e-05
negative = -1e30


def joined(x, axis, combine):
    everything = jax.tree.map(lambda part: lax.all_gather(part, axis), x)
    first = jax.tree.map(lambda part: part[0], everything)

    def hop(k, so_far):
        return combine(so_far, jax.tree.map(lambda part: part[k], everything))

    return lax.fori_loop(1, lax.axis_size(axis), hop, first)


def with_halo(block, sides, width):
    for axis, dim in sides:
        count = lax.axis_size(axis)
        forward = [(i, i + 1) for i in range(count - 1)]
        backward = [(target, source) for source, target in forward]
        low = lax.ppermute(
            lax.slice_in_dim(block, block.shape[dim] - width, None, axis=dim), axis, forward
        )
        high = lax.ppermute(lax.slice_in_dim(block, 0, width, axis=dim), axis, backward)
        block = jnp.concatenate([low, block, high], axis=dim)
    return block


def newton_inverse(kernel):
    identity = jnp.eye(kernel.shape[-1], dtype=jnp.float32)
    inverse = jnp.swapaxes(kernel, -1, -2) / jnp.sum(kernel * kernel, axis=(-2, -1), keepdims=True)
    for _ in range(NS_ITERS):
        product = jnp.matmul(kernel, inverse, precision=highest)
        inner_term = jnp.matmul(product, 7.0 * identity - product, precision=highest)
        inner_term = jnp.matmul(product, 15.0 * identity - inner_term, precision=highest)
        inverse = 0.25 * jnp.matmul(inverse, 13.0 * identity - inner_term, precision=highest)
    return inverse


def landmark_core(query_marks, key_marks):
    scores = jnp.einsum(
        "bhjd,bhid->bhji", query_marks, key_marks, precision=highest
    ) * HEAD_DIM ** (-0.5)
    kernel_two = jax.nn.softmax(scores, axis=-1)
    return (kernel_two, newton_inverse(kernel_two))


def normalize(summed, gain_vec, shift_vec):
    middle = jnp.mean(summed, axis=-1, keepdims=True)
    centred = summed - middle
    inverse_std = lax.rsqrt(jnp.mean(centred * centred, axis=-1, keepdims=True) + epsilon)
    normal = centred * inverse_std
    return (normal * gain_vec + shift_vec, normal, inverse_std)


def add_norm(partial_sum, residual, bias_vec, gain_vec, shift_vec):
    summed = lax.psum(partial_sum.astype(jnp.bfloat16), "tensor").astype(jnp.float32)
    return normalize(residual + summed + bias_vec, gain_vec, shift_vec)


def norm_back(grad_hidden, normal, inverse_std, gain_vec):
    grad_normal = grad_hidden * gain_vec
    grad_summed = inverse_std * (
        grad_normal
        - jnp.mean(grad_normal, axis=-1, keepdims=True)
        - normal * jnp.mean(grad_normal * normal, axis=-1, keepdims=True)
    )
    return (grad_summed, jnp.sum(grad_hidden * normal, axis=0), jnp.sum(grad_hidden, axis=0))


def combine_soft(earlier, later):
    top_score = jnp.maximum(earlier[0], later[0])
    weight_first = jnp.exp(earlier[0] - top_score)
    weight_second = jnp.exp(later[0] - top_score)
    return (
        top_score,
        earlier[1] * weight_first + later[1] * weight_second,
        earlier[2] * weight_first[..., None] + later[2] * weight_second[..., None],
    )


def general_plan(
    tokens,
    lengths,
    query_weight,
    query_bias,
    key_weight,
    value_weight,
    value_bias,
    conv_kernel,
    out_weight,
    out_bias,
    first_gain,
    first_shift,
    up_weight,
    up_bias,
    down_weight,
    down_bias,
    second_gain,
    second_shift,
    out_grad,
):
    batch, tok_local, width = tokens.shape
    local_width = query_weight.shape[1]
    local_heads = conv_kernel.shape[0]
    head_dim = local_width // local_heads
    score_scale = HEAD_DIM ** (-0.5)
    rows = batch * tok_local
    half_width = CONV // 2
    f32 = jnp.float32
    bf16 = jnp.bfloat16
    position = lax.axis_index("seq") * tok_local + jnp.arange(tok_local, dtype=jnp.int32)
    inside = position[None, :] < lengths[:, None]
    living = inside.astype(f32)
    segment = position[None, :] * LAND // lengths[:, None]
    onehot = (
        (segment[:, :, None] == jnp.arange(LAND, dtype=jnp.int32)[None, None, :])
        & inside[:, :, None]
    ).astype(f32)
    marks_index = jnp.arange(LAND, dtype=jnp.int32)
    upper = ((marks_index[None, :] + 1) * lengths[:, None] + LAND - 1) // LAND
    lower = (marks_index[None, :] * lengths[:, None] + LAND - 1) // LAND
    counts = (upper - lower).astype(f32)
    flat = tokens.reshape(rows, width)
    flat_wide = flat.astype(f32)
    queries = (jnp.dot(flat, query_weight, preferred_element_type=f32) + query_bias).astype(bf16)
    key_vectors = jnp.dot(flat, key_weight, preferred_element_type=f32).astype(bf16)
    values = (
        (jnp.dot(flat, value_weight, preferred_element_type=f32) + value_bias)
        * living.reshape(rows, 1)
    ).astype(bf16)
    query_three = queries.reshape(batch, tok_local, local_width)
    key_three = key_vectors.reshape(batch, tok_local, local_width)
    value_three = values.reshape(batch, tok_local, local_width)
    onehot_low = onehot.astype(bf16)
    query_sum = jnp.einsum("btj,btf->bjf", onehot_low, query_three, preferred_element_type=f32)
    key_sum = jnp.einsum("btj,btf->bjf", onehot_low, key_three, preferred_element_type=f32)
    query_sum, key_sum = lax.psum((query_sum, key_sum), "seq")
    query_marks = (
        (query_sum / counts[:, :, None])
        .reshape(batch, LAND, local_heads, head_dim)
        .transpose(0, 2, 1, 3)
    )
    key_marks = (
        (key_sum / counts[:, :, None])
        .reshape(batch, LAND, local_heads, head_dim)
        .transpose(0, 2, 1, 3)
    )
    (kernel_two, inverse), core_back = jax.vjp(landmark_core, query_marks, key_marks)
    identity = jnp.eye(LAND, dtype=f32)
    deviation = identity - jnp.matmul(kernel_two, inverse, precision=highest)
    proxy_part = jnp.sum(jnp.sqrt(jnp.sum(deviation * deviation, axis=(-2, -1)))) / (batch * HEADS)
    query_heads = query_three.reshape(batch, tok_local, local_heads, head_dim).astype(f32)
    key_heads = key_three.reshape(batch, tok_local, local_heads, head_dim).astype(f32)
    value_heads = value_three.reshape(batch, tok_local, local_heads, head_dim).astype(f32)
    first_scores = (
        jnp.einsum("bthd,bhjd->bhtj", query_heads, key_marks, precision=highest) * score_scale
    )
    kernel_one = jax.nn.softmax(first_scores, axis=-1)
    third_scores = (
        jnp.einsum("bhjd,bthd->bhjt", query_marks, key_heads, precision=highest) * score_scale
    )
    key_alive = inside[:, None, None, :]
    third_scores = jnp.where(key_alive, third_scores, negative)
    local_top = jnp.max(third_scores, axis=-1)
    local_weights = jnp.where(key_alive, jnp.exp(third_scores - local_top[..., None]), 0.0)
    local_total = jnp.sum(local_weights, axis=-1)
    local_mix = jnp.einsum("bhjt,bthd->bhjd", local_weights, value_heads, precision=highest)
    top_score, total_weight, mixed = joined(
        (local_top, local_total, local_mix), "seq", combine_soft
    )
    third_out = mixed / total_weight[..., None]
    carried = jnp.matmul(inverse, third_out, precision=highest)
    nystrom = jnp.einsum("bhtj,bhjd->bthd", kernel_one, carried, precision=highest).reshape(
        batch, tok_local, local_width
    )
    padded_values = with_halo(value_three, (("seq", 1),), half_width)
    kernel_wide = jnp.repeat(conv_kernel, head_dim, axis=0)
    convolved = jnp.zeros((batch, tok_local, local_width), f32)
    for i in range(CONV):
        convolved = (
            convolved + padded_values[:, i : i + tok_local, :].astype(f32) * kernel_wide[:, i]
        )
    attention = (nystrom + convolved).astype(bf16).reshape(rows, local_width)
    out_part = jnp.dot(attention, out_weight, preferred_element_type=f32)
    hidden_one, normal_one, inverse_one = add_norm(
        out_part, flat_wide, out_bias, first_gain, first_shift
    )
    hidden_low = hidden_one.astype(bf16)
    up_value = jnp.dot(hidden_low, up_weight, preferred_element_type=f32) + up_bias
    activated, gelu_back = jax.vjp(lambda z: jax.nn.gelu(z, approximate=False), up_value)
    activated = activated.astype(bf16)
    down_part = jnp.dot(activated, down_weight, preferred_element_type=f32)
    hidden_two, normal_two, inverse_two = add_norm(
        down_part, hidden_one, down_bias, second_gain, second_shift
    )
    output = hidden_two.astype(bf16).reshape(batch, tok_local, width)
    grad_output = out_grad.reshape(rows, width).astype(f32)
    grad_second_total, grad_second_gain, grad_second_shift = norm_back(
        grad_output, normal_two, inverse_two, second_gain
    )
    down_in = grad_second_total.astype(bf16)
    grad_down_bias = jnp.sum(down_in.astype(f32), axis=0)
    grad_down_weight = jnp.einsum("rf,rd->fd", activated, down_in, preferred_element_type=f32)
    grad_activated = jnp.einsum("rd,fd->rf", down_in, down_weight, preferred_element_type=f32)
    up_in = gelu_back(grad_activated)[0].astype(bf16)
    grad_up_bias = jnp.sum(up_in.astype(f32), axis=0)
    grad_up_weight = jnp.einsum("rd,rf->df", hidden_low, up_in, preferred_element_type=f32)
    hidden_part = jnp.einsum("rf,df->rd", up_in, up_weight, preferred_element_type=f32)
    grad_hidden_one = (
        lax.psum(hidden_part.astype(jnp.bfloat16), "tensor").astype(jnp.float32) + grad_second_total
    )
    grad_first_total, grad_first_gain, grad_first_shift = norm_back(
        grad_hidden_one, normal_one, inverse_one, first_gain
    )
    out_in = grad_first_total.astype(bf16)
    grad_out_bias = jnp.sum(out_in.astype(f32), axis=0)
    grad_out_weight = jnp.einsum("rf,rd->fd", attention, out_in, preferred_element_type=f32)
    grad_attention = jnp.einsum(
        "rd,fd->rf", out_in, out_weight, preferred_element_type=f32
    ).reshape(batch, tok_local, local_width)
    padded_grad = with_halo(grad_attention.astype(jnp.bfloat16), (("seq", 1),), half_width).astype(
        grad_attention.dtype
    )
    grad_conv_values = jnp.zeros((batch, tok_local, local_width), f32)
    conv_columns = []
    for i in range(CONV):
        conv_columns.append(
            jnp.sum(
                grad_attention * padded_values[:, i : i + tok_local, :].astype(f32), axis=(0, 1)
            )
        )
        start_index = 2 * half_width - i
        grad_conv_values = (
            grad_conv_values
            + padded_grad[:, start_index : start_index + tok_local, :] * kernel_wide[:, i]
        )
    grad_conv_kernel = (
        jnp.stack(conv_columns, axis=0).reshape(CONV, local_heads, head_dim).sum(axis=-1).T
    )
    grad_nystrom = grad_attention.reshape(batch, tok_local, local_heads, head_dim)
    grad_kernel_one = jnp.einsum("bthd,bhjd->bhtj", grad_nystrom, carried, precision=highest)
    grad_carried_part = jnp.einsum("bhtj,bthd->bhjd", kernel_one, grad_nystrom, precision=highest)
    grad_first_scores = kernel_one * (
        grad_kernel_one - jnp.sum(kernel_one * grad_kernel_one, axis=-1, keepdims=True)
    )
    grad_query_one = (
        jnp.einsum("bhtj,bhjd->bthd", grad_first_scores, key_marks, precision=highest) * score_scale
    )
    grad_key_marks_part = (
        jnp.einsum("bhtj,bthd->bhjd", grad_first_scores, query_heads, precision=highest)
        * score_scale
    )
    grad_carried, grad_key_marks_one = lax.psum((grad_carried_part, grad_key_marks_part), "seq")
    grad_third_out = jnp.matmul(jnp.swapaxes(inverse, -1, -2), grad_carried, precision=highest)
    grad_inverse = jnp.matmul(grad_carried, jnp.swapaxes(third_out, -1, -2), precision=highest)
    grad_query_marks_two, grad_key_marks_two = core_back((jnp.zeros_like(kernel_two), grad_inverse))
    third_prob = local_weights * jnp.exp(local_top - top_score)[..., None] / total_weight[..., None]
    delta_term = jnp.sum(grad_third_out * third_out, axis=-1)
    grad_prob_value = jnp.einsum("bhjd,bthd->bhjt", grad_third_out, value_heads, precision=highest)
    grad_third_scores = third_prob * (grad_prob_value - delta_term[..., None])
    grad_value_three = jnp.einsum("bhjt,bhjd->bthd", third_prob, grad_third_out, precision=highest)
    grad_key_three = (
        jnp.einsum("bhjt,bhjd->bthd", grad_third_scores, query_marks, precision=highest)
        * score_scale
    )
    grad_query_marks_part = (
        jnp.einsum("bhjt,bthd->bhjd", grad_third_scores, key_heads, precision=highest) * score_scale
    )
    grad_query_marks_three = lax.psum(grad_query_marks_part, "seq")
    grad_query_marks = (grad_query_marks_two + grad_query_marks_three) / counts[:, None, :, None]
    grad_key_marks = (grad_key_marks_one + grad_key_marks_two) / counts[:, None, :, None]
    grad_query_marks = grad_query_marks.transpose(0, 2, 1, 3).reshape(batch, LAND, local_width)
    grad_key_marks = grad_key_marks.transpose(0, 2, 1, 3).reshape(batch, LAND, local_width)
    grad_query_seg = jnp.einsum("btj,bjf->btf", onehot, grad_query_marks, precision=highest)
    grad_key_seg = jnp.einsum("btj,bjf->btf", onehot, grad_key_marks, precision=highest)
    query_in = (
        (grad_query_one.reshape(batch, tok_local, local_width) + grad_query_seg)
        .astype(bf16)
        .reshape(rows, local_width)
    )
    key_in = (
        (grad_key_three.reshape(batch, tok_local, local_width) + grad_key_seg)
        .astype(bf16)
        .reshape(rows, local_width)
    )
    value_in = (grad_value_three.reshape(batch, tok_local, local_width) + grad_conv_values).astype(
        bf16
    )
    value_in = jnp.where(inside[:, :, None], value_in, jnp.zeros_like(value_in)).reshape(
        rows, local_width
    )
    grad_query_bias = jnp.sum(query_in.astype(f32), axis=0)
    grad_value_bias = jnp.sum(value_in.astype(f32), axis=0)
    grad_query_weight = jnp.einsum("rd,rf->df", flat, query_in, preferred_element_type=f32)
    grad_key_weight = jnp.einsum("rd,rf->df", flat, key_in, preferred_element_type=f32)
    grad_value_weight = jnp.einsum("rd,rf->df", flat, value_in, preferred_element_type=f32)
    input_part = (
        jnp.einsum("rf,df->rd", query_in, query_weight, preferred_element_type=f32)
        + jnp.einsum("rf,df->rd", key_in, key_weight, preferred_element_type=f32)
        + jnp.einsum("rf,df->rd", value_in, value_weight, preferred_element_type=f32)
    )
    input_sum, proxy_norm = (
        lax.psum(input_part.astype(jnp.bfloat16), "tensor").astype(jnp.float32),
        lax.psum(proxy_part.astype(jnp.bfloat16), "tensor").astype(jnp.float32),
    )
    grad_tokens = (grad_first_total + input_sum).reshape(batch, tok_local, width)
    (
        grad_query_weight,
        grad_key_weight,
        grad_value_weight,
        grad_out_weight,
        grad_up_weight,
        grad_down_weight,
    ) = (
        lax.psum_scatter(grad_query_weight, "seq", scatter_dimension=0, tiled=True),
        lax.psum_scatter(grad_key_weight, "seq", scatter_dimension=0, tiled=True),
        lax.psum_scatter(grad_value_weight, "seq", scatter_dimension=0, tiled=True),
        lax.psum_scatter(grad_out_weight, "seq", scatter_dimension=1, tiled=True),
        lax.psum_scatter(grad_up_weight, "seq", scatter_dimension=0, tiled=True),
        lax.psum_scatter(grad_down_weight, "seq", scatter_dimension=1, tiled=True),
    )
    (
        grad_query_bias,
        grad_value_bias,
        grad_conv_kernel,
        grad_out_bias,
        grad_first_gain,
        grad_first_shift,
        grad_up_bias,
        grad_down_bias,
        grad_second_gain,
        grad_second_shift,
    ) = lax.psum(
        (
            grad_query_bias,
            grad_value_bias,
            grad_conv_kernel,
            grad_out_bias,
            grad_first_gain,
            grad_first_shift,
            grad_up_bias,
            grad_down_bias,
            grad_second_gain,
            grad_second_shift,
        ),
        "seq",
    )
    return (
        output,
        grad_tokens,
        grad_query_weight,
        grad_query_bias,
        grad_key_weight,
        grad_value_weight,
        grad_value_bias,
        grad_conv_kernel,
        grad_out_weight,
        grad_out_bias,
        grad_first_gain,
        grad_first_shift,
        grad_up_weight,
        grad_up_bias,
        grad_down_weight,
        grad_down_bias,
        grad_second_gain,
        grad_second_shift,
        proxy_norm,
    )


MESH = pl.DeviceIdType.MESH
LANES = 2 * HEAD_DIM
f32 = jnp.float32
bf16 = jnp.bfloat16
NN = (1, 0)
NT = (1, 1)
TN = (0, 0)


def dot(a, b, dims=NN):
    return lax.dot_general(
        a, b, (((dims[0],), (dims[1],)), ((), ())), preferred_element_type=f32
    )


def split(x):
    if x.dtype == bf16:
        return (x,)
    top = x.astype(bf16)
    return (top, (x - top.astype(f32)).astype(bf16))


def fine(a, b, dims=NN):
    a, b = split(a), split(b)
    total = dot(a[0], b[0], dims)
    if len(b) > 1:
        total = total + dot(a[0], b[1], dims)
    if len(a) > 1:
        total = total + dot(a[1], b[0], dims)
    return total


def iota(shape, dim):
    return lax.broadcasted_iota(jnp.int32, shape, dim)


def block_mask():
    shape = (LANES, LANES)
    return (iota(shape, 0) < HEAD_DIM) == (iota(shape, 1) < HEAD_DIM)


def eye():
    return jnp.where(iota((LANES, LANES), 0) == iota((LANES, LANES), 1), 1.0, 0.0).astype(f32)


def block_sums(x, same_head):
    ones = jnp.where(same_head, 1.0, 0.0).astype(bf16)
    return jnp.where(same_head, fine(fine(ones, x), ones), 1.0)


def taps_matrix(row, tok):
    return pltpu.roll(jnp.broadcast_to(row, (tok, 2 * tok)), 0, 1, stride=1, stride_axis=0)


def taps_row(taps, head, tok):
    row = taps[pl.ds(head, 1), :]
    return jnp.concatenate([row, jnp.zeros((1, 2 * tok - CONV), f32)], axis=1)


def conv_block(matrices, window):
    first = fine(matrices[0], window)
    second = fine(matrices[1], window)
    return jnp.where(iota(first.shape, 1) < HEAD_DIM, first, second)


def greet(devices):
    barrier = pltpu.get_barrier_semaphore()
    for device in devices:
        pl.semaphore_signal(barrier, inc=1, device_id=device, device_id_type=MESH)
    return barrier


def around(n, me, tensor):
    return [(lax.rem(me + d, n), tensor) for d in range(1, n)]


def others(me, tensor):
    core = tensor + 1 - 2 * (tensor % 2)
    return [(me, core), (me, lax.rem(tensor + 2, 4)), (me, lax.rem(core + 2, 4))]


def paired(y):
    return y[:, :LANES], jnp.concatenate(
        [y[:, LANES : LANES + HEAD_DIM], y[:, HEAD_DIM:LANES]], axis=1
    )


def remote(src, dst, send, recv, device):
    return pltpu.make_async_remote_copy(
        src_ref=src, dst_ref=dst, send_sem=send, recv_sem=recv, device_id=device,
        device_id_type=MESH,
    )


def member_rows(length, total):
    j = iota((LANES, total), 0) % LAND
    t = iota((LANES, total), 1)
    inside = (t * LAND >= j * length) & (t * LAND < (j + 1) * length) & (t < length)
    return jnp.where(inside, 1.0, 0.0).astype(bf16)


def member_columns(length, total):
    j = iota((total, LANES), 1) % LAND
    t = iota((total, LANES), 0)
    inside = (t * LAND >= j * length) & (t * LAND < (j + 1) * length) & (t < length)
    return jnp.where(inside, 1.0, 0.0).astype(bf16)


def segment_counts(length):
    j = iota((LANES, LANES), 0) % LAND
    upper = ((j + 1) * length + LAND - 1) // LAND
    lower = (j * length + LAND - 1) // LAND
    return (upper - lower).astype(f32)


def normal_of(summed):
    middle = jnp.mean(summed, axis=-1, keepdims=True)
    centred = summed - middle
    inverse_std = lax.rsqrt(jnp.mean(centred * centred, axis=-1, keepdims=True) + epsilon)
    return centred * inverse_std, inverse_std


def before_norm(grad, normal, inverse_std, gain):
    grad_normal = grad * gain
    return inverse_std * (
        grad_normal
        - jnp.mean(grad_normal, axis=-1, keepdims=True)
        - normal * jnp.mean(grad_normal * normal, axis=-1, keepdims=True)
    )


def block_rows(t, tok):
    return pl.ds(pl.multiple_of(t * tok, tok), tok)


def settle(ref, sem):
    pltpu.make_async_copy(ref, ref, sem).wait()


class Scatter:
    def __init__(self, index, me, tensor, source, columns, buffers, send, recv, order):
        self.index, self.source, self.columns = index, source, pl.ds(*columns)
        self.first_in, self.held, self.second_in, self.pair, self.last_in, self.cross_in = buffers
        self.block = source.shape[0] // 8
        self.weights = [2**bit for bit in order]
        self.bits = [(me // weight) % 2 for weight in self.weights]
        self.partners = [
            (me + weight * (1 - 2 * bit), tensor) for weight, bit in zip(self.weights, self.bits)
        ]
        self.send, self.recv = send, recv

    def rows(self, slot, bit):
        index = (slot // 2) * self.weights[2] + (slot % 2) * self.weights[1] + bit * self.weights[0]
        return pl.ds(pl.multiple_of(index * self.block, 16), self.block)

    def copy(self, src, dst, k, stage):
        return remote(
            src, dst, self.send.at[self.index, min(k, 1)], self.recv.at[self.index, k],
            self.partners[stage],
        )

    def arrived(self, ref, k):
        settle(ref, self.recv.at[self.index, k])

    def first(self, slots=range(4)):
        for slot in slots:
            source = self.source.at[self.rows(slot, 1 - self.bits[0]), self.columns]
            self.copy(source, self.first_in.at[slot], 0, 0).start()

    def second(self):
        self.arrived(self.first_in, 0)
        for slot in range(4):
            mine = self.source[self.rows(slot, self.bits[0]), self.columns]
            self.held[slot] = self.joined(mine, self.first_in[slot])
        for k in range(2):
            self.copy(self.held.at[2 * k + 1 - self.bits[1]], self.second_in.at[k], 1, 1).start()

    def joined(self, mine, come):
        return (mine.astype(f32) + come.astype(f32)).astype(bf16)

    def third(self):
        self.arrived(self.second_in, 1)
        for k in range(2):
            both = self.held[2 * k + self.bits[1]].astype(f32) + self.second_in[k].astype(f32)
            self.pair[k] = both.astype(bf16)
        self.copy(self.pair.at[1 - self.bits[2]], self.last_in, 2, 2).start()

    def last(self, write):
        self.arrived(self.last_in, 2)
        write(self.pair[self.bits[2]].astype(f32) + self.last_in[...].astype(f32))

    def finish(self):
        settle(self.first_in, self.send.at[self.index, 0])
        settle(self.held.at[pl.ds(0, 3)], self.send.at[self.index, 1])


class Line(Scatter):
    def __init__(self, *args):
        super().__init__(*args)
        z = self.bits[1] + 2 * self.bits[2]
        right = z // 2
        self.end = self.bits[1] == right
        self.inner = self.bits[1] != right
        self.slots = [k * (1 - right) + (3 - k) * right for k in range(4)]
        self.partners[2] = (2 * (3 - z) + self.bits[0], self.partners[0][1])

    def second(self):
        self.arrived(self.first_in, 0)
        for slot in range(4):
            mine = self.source[self.rows(slot, self.bits[0]), self.columns]
            self.held[slot] = self.joined(mine, self.first_in[slot])
        come = (self.second_in.at[0], self.second_in.at[1], self.last_in)
        sends = [
            self.copy(self.held.at[self.slots[3 - k]], come[k], (1, 1, 2)[k], 1)
            for k in range(3)
        ]

        @pl.when(self.end)
        def _():
            for copy in sends:
                copy.start()

    def third(self):
        sends = [
            self.copy(self.pair.at[k], self.cross_in.at[k], 3, 2) for k in range(2)
        ]

        @pl.when(self.inner)
        def _():
            self.arrived(self.second_in, 1)
            for k in range(2):
                self.pair[k] = self.joined(self.held[self.slots[3 - k]], self.second_in[k])
                sends[k].start()

    def fourth(self):
        back = self.copy(self.first_in.at[2], self.first_in.at[3], 4, 1)

        @pl.when(self.inner)
        def _():
            self.arrived(self.cross_in, 3)
            self.first_in[2] = self.joined(self.held[self.slots[0]], self.cross_in[0])
            back.start()

    def last(self, write):
        @pl.when(self.inner)
        def _():
            self.arrived(self.last_in, 2)
            write(
                self.held[self.slots[1]].astype(f32)
                + self.last_in[...].astype(f32)
                + self.cross_in[1].astype(f32)
            )

        @pl.when(self.end)
        def _():
            self.arrived(self.first_in.at[3], 4)
            write(self.held[self.slots[0]].astype(f32) + self.first_in[3].astype(f32))


class Pairs(Scatter):
    def second(self):
        self.arrived(self.first_in, 0)
        width = self.first_in.shape[2]
        for slot in range(4):
            at = self.rows(slot, self.bits[0])
            self.held[slot, :, :width] = self.source[at]
            self.held[slot, :, width : 2 * width] = self.shared[at]
            self.held[slot, :, 2 * width :] = self.first_in[slot]
        for k in range(2):
            self.copy(self.held.at[2 * k + 1 - self.bits[1]], self.second_in.at[k], 1, 1).start()


def scatter_buffers(first, width, block):
    return [
        pltpu.VMEM((4, block, first), bf16),
        pltpu.VMEM((4, block, width), bf16),
        pltpu.VMEM((2, block, width), bf16),
        pltpu.VMEM((2, block, width), bf16),
        pltpu.VMEM((block, width), bf16),
        pltpu.VMEM((2, block, width), bf16),
    ]


def total_of(v):
    return jnp.sum(v, axis=0, keepdims=True)


def packed(block):
    middle = block.shape[-2] // 2
    first, second = block[..., :middle, :HEAD_DIM], block[..., middle:, :HEAD_DIM]
    return jnp.concatenate([first, second], axis=-1)


def unpacked(block):
    return jnp.concatenate([block[..., :HEAD_DIM], block[..., HEAD_DIM:]], axis=-2)


class Ring:
    def __init__(
        self, tensor, peers, parts, core_out, core_in, y_out, y_in, ag_send, ag_recv, sum_send,
        sum_recv,
    ):
        self.tensor, self.place = tensor, tensor % 2
        self.core, self.across, self.far = peers
        self.near_pair = tensor - self.place
        self.far_pair = lax.rem(self.near_pair + 2, 4)
        self.parts, self.core_out, self.core_in = parts, core_out, core_in
        self.y_out, self.y_in = y_out, y_in
        self.ag, self.sums = (ag_send, ag_recv), (sum_send, sum_recv)
        self.copies = {}

    def send(self, name, src, dst, sems, at, device):
        copy = remote(src, dst, sems[0].at[0], sems[1].at[at], device)
        copy.start()
        self.copies[name] = copy

    def share(self, phase, c, held):
        mine = held.at[c, self.tensor]
        self.send((phase, c, "y"), mine, mine, self.ag, (phase, c, 0), self.across)
        self.send((phase, c, "core"), mine, mine, self.ag, (phase, c, 1), self.core)

    def work(self, phase, c, side, value):
        self.parts[phase, c, side] = value.reshape(2, -1, value.shape[1])
        self.core_out[phase, c, side] = self.parts[phase, c, side, 1 - self.place].astype(bf16)
        self.send(
            (phase, c, side), self.core_out.at[phase, c, side], self.core_in.at[phase, c, side],
            self.sums, (phase, c, side), self.core,
        )

    def run(self, phase, held, work):
        for c in range(2):
            self.copies[phase, c, "core"].wait_recv()
            self.work(phase, c, 0, work(c, self.near_pair))
        for c in range(2):
            self.copies[phase, c, "y"].wait_recv()
            other = held.at[c, self.across[1]]
            self.send((phase, c, "pass"), other, other, self.ag, (phase, c, 2), self.core)
            if c == 1:
                self.cross(phase, 0)
            self.copies[phase, c, "pass"].wait_recv()
            self.work(phase, c, 1, work(c, self.far_pair))
        self.cross(phase, 1)

    def cross(self, phase, c):
        self.copies[phase, c, 1].wait_recv()
        both = self.parts[phase, c, 1, self.place] + self.core_in[phase, c, 1].astype(f32)
        self.y_out[phase, c] = both.astype(bf16)
        self.send(
            (phase, c, "sum"), self.y_out.at[phase, c], self.y_in.at[phase, c], self.sums,
            (phase, c, 2), self.across,
        )

    def total(self, phase, c):
        self.copies[phase, c, 0].wait_recv()
        self.copies[phase, c, "sum"].wait_recv()
        return (
            self.parts[phase, c, 0, self.place]
            + self.core_in[phase, c, 0].astype(f32)
            + self.y_in[phase, c].astype(f32)
        )


JOBS = 6
RESULTS = 19


def layer_kernel(
    n, lengths, x_far, wq_far, qb, wk_far, wv_far, vb, taps, out_far, out_bias, gain_one,
    shift_one, up_far, up_bias, down_far, down_bias, gain_two, shift_two, grad_far,
    *rest,
):
    results, rest = rest[:RESULTS], rest[RESULTS:]
    ready, rest = rest[:RESULTS], rest[RESULTS:]
    layer_body(
        n, lengths, x_far, wq_far, qb, wk_far, wv_far, vb, taps, out_far, out_bias, gain_one,
        shift_one, up_far, up_bias, down_far, down_bias, gain_two, shift_two, grad_far, results,
        ready, *rest,
    )


def layer_body(
    n, lengths, x_far, wq_far, qb, wk_far, wv_far, vb, taps, out_far, out_bias, gain_one,
    shift_one, up_far, up_bias, down_far, down_bias, gain_two, shift_two, grad_far, results, ready,
    x, wk, wq, wv, up_weight, down_weight, out_grad, out_weight, out_whole,
    up_turned, down_turned, stage, ks, qs, vs, k1, p3, newton, out_stage, out_single, attn_pair, attn_single,
    pairs_in, singles_in, heads_out, hidden, slope, active, down_in, up_in,
    core_out, core_in, y_out, y_in, core_last, y_last,
    gs, back_stage, back_single, come_pair, come_single, weight_in, out_in, early, early_tensor, tokens_own, tokens_low, source_up,
    source_down, source_out, source_own, source_both, early_out, early_in, late_out, late_in, tokens_whole,
    parts_held,
    *rest,
):
    buffers, sems = rest[: 6 * JOBS], rest[6 * JOBS :]
    (load, send, recv, out_send, out_recv, whole_send, whole_recv, copy_send, copy_recv, ag_send,
     ag_recv, sum_send, sum_recv, grad_send, grad_recv, back_send, back_recv, share_send,
     share_recv, small_send, small_recv, job_send, job_recv, own_send, own_recv, last_send, last_recv,
     store) = sems
    (output, grad_tokens, grad_query, query_bias, grad_key, grad_value, value_bias, conv, grad_out,
     out_bias_grad, first_gain, first_shift, grad_up, up_bias_grad, grad_down, down_bias_grad,
     second_gain, second_shift, proxy) = ready
    stores = []

    def done(*numbers):
        for i in numbers:
            copy = pltpu.make_async_copy(ready[i], results[i], store.at[i])
            copy.start()
            stores.append(copy)

    me = lax.axis_index("seq")
    tensor = lax.axis_index("tensor")
    rows, width = x.shape
    batch = n // 2
    tok = rows // batch
    total = n * tok
    half = CONV // 2
    own, side = me // 2, me % 2
    scale = HEAD_DIM ** (-0.5)
    ring_peers = around(n, me, tensor)
    peers = others(me, tensor)
    core, across, far = peers

    def batch_of(t):
        return lax.rem(t - me + 8, 4)

    def rows_at(t):
        return block_rows(batch_of(t), tok)

    mine = rows_at(tensor)
    at_home = batch_of(tensor) == own
    away = batch_of(tensor) != own
    local = wk.shape[0]
    barrier = greet(ring_peers + peers)
    loads = []
    for i, (source, target) in enumerate((
        (x_far, x), (wk_far, wk), (wq_far, wq), (wv_far, wv),
        (out_far, out_weight), (up_far, up_weight),
        (down_far, down_weight), (grad_far, out_grad),
    )):
        copy = pltpu.make_async_copy(source, target, load.at[i])
        copy.start()
        loads.append(copy)
    hidden_width = up_weight.shape[1]
    span = hidden_width // 2
    jobs = [
        kind(i, me, tensor, source, columns, buffers[6 * i : 6 * i + 6], job_send, job_recv, order)
        for i, (kind, source, columns, order) in enumerate((
            (Line, source_down, (0, span), (0, 1, 2)),
            (Scatter, source_down, (span, span), (1, 0, 2)),
            (Line, source_up, (0, span), (0, 1, 2)),
            (Line, source_up, (span, span), (0, 1, 2)),
            (Scatter, source_out, (0, local), (0, 1, 2)),
            (Pairs, source_own, (0, local), (0, 1, 2)),
        ))
    ]
    job_down, job_up = jobs[0:2], jobs[2:4]
    job_out, job_heads = jobs[4:]
    job_heads.shared = source_both

    owned = (ks, qs, vs)
    offsets = (0, 0, half)
    for padded in (vs, gs):
        padded[0:half] = jnp.zeros((half, LANES), bf16)
        padded[half + total : total + tok] = jnp.zeros((tok - half, LANES), bf16)
    even = side == 0

    seven = pl.ds(0, (n - 1) * tok)

    def spread(i):
        here = pl.ds(pl.multiple_of(offsets[i] + me * tok, 16), tok)
        for d in range(1, n):
            peer = lax.rem(me + d, n)
            copy = remote(
                stage.at[i, peer % 2, block_rows(peer // 2, tok)], owned[i].at[here],
                send.at[i], recv.at[i], (peer, tensor),
            )
            copy.start()
        owned[i][here] = stage[i, side, block_rows(own, tok)]

    loads[0].wait()
    loads[1].wait()
    y = dot(x[...], wk[...], NT)
    stage[0, 0], stage[0, 1] = paired(y.astype(bf16))
    pl.semaphore_wait(barrier, n + 2)
    spread(0)
    loads[2].wait()
    y = dot(x[...], wq[...], NT) + qb[...].reshape(1, local)
    stage[1, 0], stage[1, 1] = paired(y.astype(bf16))
    spread(1)
    loads[3].wait()
    y = dot(x[...], wv[...], NT) + vb[...].reshape(1, local)
    position = me * tok + iota((tok, local), 0)
    y = jnp.concatenate(
        [
            jnp.where(position < lengths[b], y[b * tok : (b + 1) * tok], 0.0)
            for b in range(batch)
        ],
        axis=0,
    )
    stage[2, 0], stage[2, 1] = paired(y.astype(bf16))
    loads[4].wait()
    pair_rows = block_rows(tensor, LANES)
    single_rows = pl.ds(pl.multiple_of(4 * LANES + tensor * HEAD_DIM, HEAD_DIM), HEAD_DIM)
    first, single = out_weight[:LANES], out_weight[LANES:]
    out_whole[pair_rows] = jnp.where(
        even, first, jnp.concatenate([single, first[HEAD_DIM:]], axis=0)
    )
    out_whole[single_rows] = jnp.where(even, single, first[:HEAD_DIM])
    for i, device in enumerate(peers):
        for at in (pair_rows, single_rows):
            part = out_whole.at[at]
            remote(part, part, whole_send.at[0], whole_recv.at[0], device).start()

    length = lengths[own]
    same_head = block_mask()
    identity = eye()
    ones = jnp.where(same_head, 1.0, 0.0).astype(bf16)
    members = member_rows(length, total)
    counts = segment_counts(length)
    matrices = [taps_matrix(taps_row(taps, h, tok), tok) for h in (2 * side, 1)]
    flip = jnp.where(
        iota((2 * tok, 2 * tok), 0) + iota((2 * tok, 2 * tok), 1) == CONV - 1, 1.0, 0.0
    ).astype(bf16)
    reverse = [
        taps_matrix(
            fine(jnp.broadcast_to(taps_row(taps, h, tok), (8, 2 * tok)), flip)[0:1], tok
        )
        for h in (2 * side, 1)
    ]
    for i, w in enumerate((wk, wq, wv)):
        pair, single = w[:LANES], w[LANES:]
        weight_in[i * LANES : (i + 1) * LANES] = jnp.where(
            even, pair, jnp.concatenate([single, pair[HEAD_DIM:]], axis=0)
        )
        start = 3 * LANES + i * HEAD_DIM
        weight_in[start : start + HEAD_DIM] = jnp.where(even, single, pair[:HEAD_DIM])
    for copy in loads[5:]:
        copy.wait()
    up_turned[...] = up_weight[...].T
    down_turned[...] = down_weight[...].T
    settle(ks.at[seven], recv.at[0])
    keys = ks[...]
    key_marks = jnp.where(same_head, dot(members, keys) / counts, 0.0)
    settle(qs.at[seven], send.at[1])
    spread(2)
    settle(qs.at[seven], recv.at[1])
    queries = qs[...]
    query_marks = jnp.where(same_head, dot(members, queries) / counts, 0.0)
    scores = jnp.where(same_head, fine(query_marks, key_marks, NT) * scale, negative)
    weights = jnp.exp(scores - jnp.max(scores, axis=1, keepdims=True))
    kernel_two = weights / jnp.sum(weights, axis=1, keepdims=True)
    inverse = jnp.where(
        same_head, kernel_two.T / block_sums(kernel_two * kernel_two, same_head), 0.0
    )
    def scores_one():
        values = fine(queries, key_marks, NT) * scale
        left = iota(values.shape, 1) < HEAD_DIM
        top_left = jnp.max(jnp.where(left, values, negative), axis=1, keepdims=True)
        top_right = jnp.max(jnp.where(left, negative, values), axis=1, keepdims=True)
        return jnp.exp(values - jnp.where(left, top_left, top_right))

    def scores_three():
        values = fine(keys, query_marks, NT) * scale
        alive = iota(values.shape, 0) < length
        values = jnp.where(alive, values, negative)
        weights = jnp.exp(values - jnp.max(values, axis=0, keepdims=True))
        return jnp.where(alive, weights, 0.0)

    product = fine(kernel_two, inverse)
    for step in range(NS_ITERS):
        if step == 0:
            weights_one = scores_one()
        if step == 1:
            k1[...] = weights_one / fine(weights_one, ones)
        if step == 2:
            weights_three = scores_three()
        if step == 3:
            third_prob = weights_three / jnp.sum(weights_three, axis=0, keepdims=True)
            p3[...] = third_prob
        inner = fine(product, 7.0 * identity - product)
        outer = 13.0 * identity - fine(product, 15.0 * identity - inner)
        newton[5 * step] = inverse
        newton[5 * step + 1] = product
        newton[5 * step + 2] = inner
        newton[5 * step + 3] = outer
        newton[5 * step + 4] = fine(product, kernel_two)
        inverse = 0.25 * fine(inverse, outer)
        product = 0.25 * fine(product, outer)

    deviation = identity - product
    norms = jnp.sqrt(block_sums(deviation * deviation, same_head))
    first, second = norms[0:1, 0:1], norms[LANES - 1 :, LANES - 1 :]
    norm_sum = jnp.where(side == 0, first + second, first) / (batch * HEADS)
    early[7:8] = jnp.broadcast_to(norm_sum, (1, width))

    settle(vs.at[seven], recv.at[2])
    values = vs[half : half + total]
    third_out = jnp.where(same_head, fine(third_prob, values, TN), 0.0)
    carried = fine(inverse, third_out)

    for d in range(1, n + 1):
        peer = lax.rem(me + d, n)
        start = pl.multiple_of(peer * tok, tok)
        nystrom = fine(k1[pl.ds(start, tok)], carried)
        convolved = conv_block(matrices, vs[pl.ds(start, 2 * tok)])
        low = (nystrom + convolved).astype(bf16)
        device = (peer, lax.rem(own + peer, 4))
        if d % 2 == 0:
            source, target = out_stage.at[d - 1], pairs_in.at[tensor]
            source[...] = low
        else:
            source, target = out_single.at[d - 1], singles_in.at[tensor]
            source[...] = packed(low)
        copy = remote(source, target, out_send.at[d % 2], out_recv.at[d % 2], device)
        if d < n:
            copy.start()
            continue
        attn_pair[own] = low
        pl.when(away)(copy.start)

        @pl.when(at_home)
        def _():
            pairs_in[tensor] = low

    three = pl.ds(0, 3)

    def settle_home(ref, some, sem):
        pl.when(away)(lambda: settle(ref, sem))
        pl.when(at_home)(lambda: settle(ref.at[some], sem))

    settle_home(pairs_in, three, out_recv.at[0])
    settle(singles_in, out_recv.at[1])
    settle(out_whole.at[pl.ds(0, 3 * local)], whole_recv.at[0])
    z, side_of_chip = me // 2, tensor % 2
    beside = (me + 1 - 2 * side, tensor)
    def give_tokens(src, dst, i, device):
        remote(src, dst, own_send.at[i // 2], own_recv.at[i], device).start()

    def half_block(b):
        start = pl.multiple_of(b * tok + side_of_chip * (tok // 2), tok // 2)
        return pl.ds(start, tok // 2)

    tokens_own[me, side_of_chip] = x[half_block(own)]
    for k in range(1, 4):
        peer = lax.rem(z + k, 4)
        give_tokens(
            x.at[half_block(peer)], tokens_own.at[me, side_of_chip], 0, (2 * peer + side, tensor)
        )
    half_own = tokens_own.at[me, side_of_chip]
    give_tokens(half_own, half_own, 1, beside)

    def pass_tokens():
        settle(tokens_own.at[pl.ds(0, 3), 0], own_recv.at[0])
        for k in range(1, 4):
            come = tokens_own.at[2 * lax.rem(z + 4 - k, 4) + side, side_of_chip]
            give_tokens(come, come, 1, beside)

    def line(vector):
        return vector[...].reshape(1, vector.shape[0])

    piece = tok // 2
    chunks = range(2)
    ring = Ring(
        tensor, peers, parts_held, core_out, core_in, y_out, y_in, ag_send, ag_recv, sum_send,
        sum_recv,
    )

    def rows_of(c):
        return pl.ds(pl.multiple_of(batch_of(tensor) * tok + c * piece, piece), piece)

    def normed(c):
        at = slice(c * piece, (c + 1) * piece)
        lanes = slice(c * HEAD_DIM, (c + 1) * HEAD_DIM)
        heads = jnp.concatenate(
            [pairs_in[t, at] for t in range(4)] + [singles_in[t, :, lanes] for t in range(4)],
            axis=1,
        )
        branch = dot(heads, out_whole[...])
        first_total = x[rows_of(c)].astype(f32) + (branch + line(out_bias))
        normal, inverse_std = normal_of(first_total)
        whole_row = normal * line(gain_one) + line(shift_one)
        hidden[c, tensor] = whole_row.astype(bf16)
        ring.share(0, c, hidden)
        return normal, inverse_std, whole_row

    def up(c, t):
        at = pl.ds(t, 2)
        value = dot(hidden[c, at].reshape(tok, width), up_weight[...]) + line(up_bias)
        half_erf = 0.5 * (1.0 + lax.erf(value * (0.5**0.5)))
        density = jnp.exp(-0.5 * value * value) * (0.5 / jnp.pi) ** 0.5
        slope[c, at] = (half_erf + value * density).reshape(2, piece, hidden_width)
        low = (value * half_erf).astype(bf16)
        active[c, at] = low.reshape(2, piece, hidden_width)
        return dot(low, down_weight[...])

    def down(c, t):
        at = pl.ds(t, 2)
        grad = dot(down_in[c, at].reshape(tok, width), down_turned[...])
        low = (grad * slope[c, at].reshape(tok, hidden_width)).astype(bf16)
        up_in[c, at] = low.reshape(2, piece, hidden_width)
        return dot(low, up_turned[...])

    after_norm_one = [normed(c) for c in chunks]
    ring.run(0, hidden, up)
    pass_tokens()
    for d in range(1, n):
        if d % 2 == 0:
            source, target = out_stage.at[d - 1], attn_pair.at[own]
        else:
            source, target = out_single.at[d - 1], attn_single.at[own]
        remote(
            source, target, copy_send.at[d % 2], copy_recv.at[d % 2],
            (lax.rem(me + d, n), tensor),
        ).start()

    grads_second, sums_second = [], []
    for c in chunks:
        hidden_one = after_norm_one[c][2]
        second_total = hidden_one + (ring.total(0, c) + line(down_bias))
        normal, inverse_std = normal_of(second_total)
        output[rows_of(c)] = (normal * line(gain_two) + line(shift_two)).astype(bf16)
        grad_output = out_grad[rows_of(c)].astype(f32)
        grad_second = before_norm(grad_output, normal, inverse_std, line(gain_two))
        low = grad_second.astype(bf16)
        down_in[c, tensor] = low
        ring.share(1, c, down_in)
        grads_second.append(grad_second)
        sums_second.append(
            (total_of(grad_output * normal), total_of(grad_output), total_of(low.astype(f32)))
        )
    ring.run(1, down_in, down)
    everything = (rows, width)
    every_hidden = (rows, hidden_width)
    source_down[...] = dot(
        down_in[...].reshape(everything), active[...].reshape(every_hidden), TN
    ).astype(bf16)
    for job in job_down:
        job.first()

    grads_first, sums_first = [], []
    for c in chunks:
        normal, inverse_std, _ = after_norm_one[c]
        grad_hidden = grads_second[c] + ring.total(1, c)
        grad_first = before_norm(grad_hidden, normal, inverse_std, line(gain_one))
        low = grad_first.astype(bf16)
        out_in[rows_of(c)] = low
        heads = dot(low, out_whole[...], NT).astype(bf16)
        at = slice(c * piece, (c + 1) * piece)
        for t in range(4):
            start = 4 * LANES + t * HEAD_DIM
            pair = heads[:, t * LANES : (t + 1) * LANES]
            heads_out[t, 0, at] = pair
            heads_out[t, 1, at] = jnp.concatenate(
                [heads[:, start : start + HEAD_DIM], pair[:, HEAD_DIM:]], axis=1
            )
        b = batch_of(tensor)
        there = pl.ds(pl.multiple_of(half + me * tok + c * piece, 16), piece)
        for t in range(4):
            for k, device in enumerate(((2 * b + side, t), (2 * b + 1 - side, t))):
                copy = remote(
                    heads_out.at[t, k, pl.ds(c * piece, piece)], gs.at[there], grad_send.at[0],
                    grad_recv.at[0], device,
                )
                if k == 1:
                    copy.start()
                else:
                    pl.when((batch_of(tensor) != own) | (tensor != t))(copy.start)
        grads_first.append(grad_first)
        sums_first.append(
            (total_of(grad_hidden * normal), total_of(grad_hidden), total_of(low.astype(f32)))
        )

    @pl.when(at_home)
    def _():
        here = pl.ds(pl.multiple_of(half + me * tok, 16), tok)
        gs[here] = heads_out[tensor, 0]

    source_up[...] = dot(
        hidden[...].reshape(everything), up_in[...].reshape(every_hidden), TN
    ).astype(bf16)
    for i in range(3):
        early[i : i + 1] = sums_second[0][i] + sums_second[1][i]
        early[i + 3 : i + 4] = sums_first[0][i] + sums_first[1][i]
    early[6:7] = dot(jnp.ones((8, rows), bf16), up_in[...].reshape(every_hidden))[0:1]
    early_tensor[tensor] = early[...]
    job_up[0].first(range(2))
    for i, device in enumerate(peers):
        remote(
            early, early_tensor.at[tensor], small_send.at[0], small_recv.at[0], device
        ).start()
    shares = []
    for i, held in enumerate((out_in, output)):
        for j, device in enumerate((across, core)):
            copy = remote(
                held.at[mine], held.at[mine], share_send.at[i], share_recv.at[i, j], device
            )
            copy.start()
            shares.append(copy)
    job_down[0].second()
    job_up[0].first(range(2, 4))
    job_up[1].first()
    settle(tokens_own.at[pl.ds(0, 4), 0], own_recv.at[1])
    half_all = tokens_own.at[:, side_of_chip]
    give_tokens(half_all, half_all, 2, core)

    members = member_columns(length, total)
    def give(i, block):
        low = block.astype(bf16)
        back_stage[i] = low.reshape(n, tok, LANES)
        back_single[i] = packed(low.reshape(n, tok, LANES))
        for d in range(1, n):
            peer = lax.rem(me + d, n)
            source, target = (back_stage, come_pair) if d % 2 == 0 else (back_single, come_single)
            remote(
                source.at[i, peer], target.at[i, own], back_send.at[d % 2],
                back_recv.at[d % 2], (peer, tensor),
            ).start()
        come_pair[i, own] = back_stage[i, me]
        return low

    eight = gs.at[pl.ds(0, total)]
    settle_home(eight, seven, grad_recv.at[0])
    grad = gs[half : half + total]
    kernel_one = k1[...]
    grad_carried = jnp.where(same_head, fine(kernel_one, grad, TN), 0.0)
    grad_third = fine(inverse, grad_carried, TN)
    grad_inverse = fine(grad_carried, third_out, NT)
    settle(early_tensor.at[three], small_recv.at[0])
    by_tensor = early_tensor[0] + early_tensor[1] + early_tensor[2] + early_tensor[3]
    early_out[0] = jnp.where(iota(by_tensor.shape, 0) == 6, early[...], by_tensor)
    smalls_early = []

    def early_next(k):
        if k > 0:
            smalls_early[k - 1].wait_recv()
            early_out[k] = early_out[k - 1] + early_in[k - 1]
        if k < 3:
            copy = remote(
                early_out.at[k], early_in.at[k], small_send.at[1], small_recv.at[1 + k],
                job_out.partners[(k + 1) % 3],
            )
            copy.start()
            smalls_early.append(copy)

    early_next(0)
    job_down[0].third()
    kernel_back = jnp.zeros((LANES, LANES), f32)
    grad_state = grad_inverse
    for step in reversed(range(NS_ITERS)):
        state, product, inner, outer, shifted = [newton[5 * step + i] for i in range(5)]
        grad_outer = 0.25 * fine(state, grad_state, TN)
        partial = (
            fine(grad_outer, inner, NT)
            - 15.0 * grad_outer
            - fine(7.0 * product - inner, grad_outer, TN)
        )
        rest_part = 7.0 * grad_outer - fine(grad_outer, product, NT)
        grad_state = (
            0.25 * fine(grad_state, outer, NT)
            + fine(kernel_two, partial, TN)
            + fine(shifted, rest_part, TN)
        )
        kernel_back = kernel_back + fine(partial + fine(product, rest_part, TN), state, NT)
        if step == NS_ITERS - 1:
            third_prob = p3[...]
            convolved = jnp.concatenate(
                [conv_block(reverse, gs[m * tok : (m + 2) * tok]) for m in range(n)], axis=0
            )
            grad_values = fine(third_prob, grad_third) + convolved
            value_in = give(
                2, jnp.where(iota(grad_values.shape, 0) < length, grad_values, 0.0)
            )
        if step == NS_ITERS - 2:
            grad_one = fine(grad, carried, NT)
            both = kernel_one * grad_one
            first_scores = scale * (both - kernel_one * fine(both, ones))
        if step == NS_ITERS - 3:
            key_one = jnp.where(same_head, fine(first_scores, queries, TN), 0.0)
            delta = fine(jnp.ones((8, LANES), bf16), grad_third * third_out, NT)[0:1]
            third_scores = scale * third_prob * (fine(values, grad_third, NT) - delta)
        if step == NS_ITERS - 4:
            query_three = jnp.where(same_head, fine(third_scores, keys, TN), 0.0)
            key_part = fine(third_scores, query_marks)
            query_part = fine(first_scores, key_marks)
    squares = block_sums(kernel_two * kernel_two, same_head)
    spread_sum = jnp.where(same_head, block_sums(grad_state * newton[0], same_head), 0.0)
    kernel_back = kernel_back + (grad_state.T - 2.0 * kernel_two * spread_sum) / squares
    grad_scores = scale * kernel_two * (
        kernel_back - jnp.sum(kernel_two * kernel_back, axis=1, keepdims=True)
    )
    query_two = fine(grad_scores, key_marks)
    key_two = fine(grad_scores, query_marks, TN)

    key_in = give(0, key_part + fine(members, (key_one + key_two) / counts))
    query_in = give(1, query_part + fine(members, (query_two + query_three) / counts))

    for i, held in enumerate((out_in, output)):
        shares[2 * i].wait_recv()
        block = held.at[rows_at(across[1])]
        copy = remote(block, block, share_send.at[i], share_recv.at[i, 2], core)
        copy.start()
        shares.append(copy)
    job_up[0].second()
    job_down[1].second()
    settle(half_all, own_recv.at[2])
    tokens_all = tokens_own[...].reshape(total, width)
    lanes_own, lanes_both = slice(0, HEAD_DIM), slice(HEAD_DIM, LANES)
    for ref, at in ((source_own, lanes_own), (source_both, lanes_both)):
        grads = jnp.concatenate([key_in[:, at], query_in[:, at], value_in[:, at]], axis=1)
        ref[...] = dot(tokens_all, grads, TN).astype(bf16)
    job_heads.first()
    shares[1].wait_recv()
    shares[4].wait_recv()
    settle(attn_pair.at[three], copy_recv.at[0])
    settle(attn_single, copy_recv.at[1])
    pair, single = attn_pair[...].reshape(rows, LANES), unpacked(attn_single[...])
    single = single.reshape(rows, HEAD_DIM)
    attention = jnp.concatenate(
        [
            jnp.where(even, pair, jnp.concatenate([single, pair[:, HEAD_DIM:]], axis=1)),
            jnp.where(even, single, pair[:, :HEAD_DIM]),
        ],
        axis=1,
    )
    source_out[...] = dot(out_in[...], attention, TN).astype(bf16)
    job_out.first()
    position = iota((tok, tok), 0) + iota((tok, tok), 1)
    upside = jnp.where(position == tok - 1, 1.0, 0.0).astype(bf16)
    lane = iota((tok, LANES), 1)
    conv_rows = []
    for h in range(2):
        inner = (lane < HEAD_DIM) if h == 0 else (lane >= HEAD_DIM)
        table = jnp.zeros((tok, 2 * tok), f32)
        for m in range(n):
            block = gs[half + m * tok : half + (m + 1) * tok]
            block = jnp.where(inner, block, jnp.zeros_like(block))
            table = table + dot(block, vs[m * tok : (m + 2) * tok], NT)
        table = pltpu.roll(fine(upside, table), 0, 1, stride=1, stride_axis=0)
        row = jnp.sum(table, axis=0, keepdims=True)
        row = pltpu.roll(jnp.broadcast_to(row, (8, 2 * tok)), tok + 1, 1)
        conv_rows.append(row[0:1, :LANES])
    late = late_out.at[0]
    late[...] = jnp.zeros(late.shape, f32)
    column = jnp.ones((8, total), bf16)
    for row, v in ((0, query_in), (1, value_in)):
        v = dot(column, v)[0:1]
        late[row : row + 1, 0:LANES] = jnp.where(even, v, 0.0)
        late[row : row + 1, LANES:local] = jnp.where(even, 0.0, v[:, :HEAD_DIM])
    late[2:3, 0:LANES] = jnp.where(even, conv_rows[0], 0.0)
    late[3:4, 0:LANES] = jnp.where(even, conv_rows[1], 0.0)
    late[4:5, 0:LANES] = jnp.where(even, 0.0, conv_rows[0])
    smalls_late = []

    def late_next(k):
        if k > 0:
            smalls_late[k - 1].wait_recv()
            late_out[k] = late_out[k - 1] + late_in[k - 1]
        if k < 3:
            copy = remote(
                late_out.at[k], late_in.at[k], small_send.at[2], small_recv.at[4 + k],
                job_out.partners[(k + 1) % 3],
            )
            copy.start()
            smalls_late.append(copy)

    late_next(0)
    early_next(1)
    job_down[1].third()
    job_down[0].fourth()
    job_up[1].second()
    settle(come_pair.at[:, three], back_recv.at[0])
    settle(come_single, back_recv.at[1])
    singles = []
    for i in range(3):
        tokens_low[:, i * LANES : (i + 1) * LANES] = come_pair[i].reshape(rows, LANES)
        singles.append(unpacked(come_single[i]).reshape(rows, HEAD_DIM))
    tokens_low[:, 3 * LANES :] = jnp.concatenate(singles, axis=1)

    def input_part(t):
        return dot(tokens_low[rows_at(t)], weight_in[...])

    def pass_sum(k, value, device):
        core_last[0, k] = value.astype(bf16)
        copy = remote(
            core_last.at[0, k], core_last.at[1, k], last_send.at[0], last_recv.at[k], device
        )
        copy.start()
        return copy

    middle = pass_sum(1, input_part(far[1]), core)
    near = pass_sum(0, input_part(core[1]), core)
    crossing = input_part(across[1])
    middle.wait_recv()
    y_last[0] = (crossing + core_last[1, 1].astype(f32)).astype(bf16)
    final = remote(y_last.at[0], y_last.at[1], last_send.at[0], last_recv.at[2], across)
    final.start()
    result = input_part(tensor) + jnp.concatenate(grads_first, axis=0)
    late_next(1)
    job_up[0].third()
    job_heads.second()
    early_next(2)
    job_up[1].third()
    job_up[0].fourth()
    near.wait_recv()
    final.wait_recv()
    result = result + core_last[1, 0].astype(f32) + y_last[1].astype(f32)
    tokens_whole[mine] = result.astype(bf16)
    ends = []
    for j, device in enumerate((across, core)):
        copy = remote(
            tokens_whole.at[mine], tokens_whole.at[mine], share_send.at[2], share_recv.at[2, j],
            device,
        )
        copy.start()
        ends.append(copy)
    job_out.second()
    late_next(2)

    def into(ref, k):
        def write(value):
            ref[:, k * span : (k + 1) * span] = value

        return write

    for k, job in enumerate(job_down):
        job.last(into(grad_down, k))
    done(14)
    job_heads.third()
    job_up[1].fourth()
    ends[0].wait_recv()
    block = tokens_whole.at[rows_at(across[1])]
    copy = remote(block, block, share_send.at[2], share_recv.at[2, 2], core)
    copy.start()
    ends.append(copy)
    job_out.third()
    ends[1].wait_recv()
    ends[2].wait_recv()
    grad_tokens[...] = tokens_whole[...].astype(f32)
    done(1)
    early_next(3)
    late_next(3)
    by_seq = early_out[3]
    for ref, row in (
        (second_gain, 0), (second_shift, 1), (down_bias_grad, 2), (first_gain, 3),
        (first_shift, 4), (out_bias_grad, 5), (up_bias_grad, 6),
    ):
        ref[...] = by_seq[row]
    proxy[...] = by_seq[7:8, 0:1]
    by_seq = late_out[3]
    query_bias[...] = by_seq[0, :local]
    value_bias[...] = by_seq[1, :local]
    conv[...] = by_seq[2:5, :CONV]
    shares[3].wait_recv()
    shares[5].wait_recv()
    done(0, 3, 6, 7, 9, 10, 11, 13, 15, 16, 17, 18)
    for k, job in enumerate(job_up):
        job.last(into(grad_up, k))
    done(12)

    def write_heads(result):
        for i, ref in enumerate((grad_key, grad_query, grad_value)):
            mine, both, come = [
                result[:, k * local + i * HEAD_DIM : k * local + (i + 1) * HEAD_DIM]
                for k in range(3)
            ]
            ref[:, :HEAD_DIM] = jnp.where(even, mine, come)
            ref[:, HEAD_DIM:LANES] = both
            ref[:, LANES:] = jnp.where(even, come, mine)

    job_heads.last(write_heads)
    done(2, 4, 5)

    def write_out(value):
        grad_out[...] = value.T

    job_out.last(write_out)
    done(8)
    three_rows = x.at[pl.ds(0, 3 * tok)]
    settle_home(pairs_in, three, out_send.at[0])
    settle_home(eight, seven, grad_send.at[0])
    for ref, sem in (
        (ks.at[seven], send.at[0]), (vs.at[seven], send.at[2]),
        (singles_in, out_send.at[1]), (attn_pair.at[three], copy_send.at[0]),
        (attn_single, copy_send.at[1]),
        (out_whole.at[pl.ds(0, 3 * local)], whole_send.at[0]),
        (out_whole, ag_send.at[0]), (out_whole, sum_send.at[0]),
        (come_pair.at[:, three], back_send.at[0]),
        (come_single, back_send.at[1]), (three_rows, share_send.at[0]),
        (three_rows, share_send.at[1]), (three_rows, share_send.at[2]),
        (early_tensor.at[three], small_send.at[0]), (early_in, small_send.at[1]),
        (late_in, small_send.at[2]), (tokens_own.at[pl.ds(0, n - 1), 0], own_send.at[0]),
        (half_all, own_send.at[1]), (three_rows, last_send.at[0]),
    ):
        settle(ref, sem)
    for job in jobs:
        job.finish()
    for copy in stores:
        copy.wait()


def finish_kernel(*refs):
    come, go, held = [refs[i * RESULTS : (i + 1) * RESULTS] for i in range(3)]
    loads, stores = refs[3 * RESULTS :]
    copies = [
        pltpu.make_async_copy(come[i], held[i], loads.at[i]) for i in range(RESULTS)
    ]
    for copy in copies:
        copy.start()
    outs = []
    for i in range(RESULTS):
        copies[i].wait()
        copy = pltpu.make_async_copy(held[i], go[i], stores.at[i])
        copy.start()
        outs.append(copy)
    for copy in outs:
        copy.wait()


def whole(shape, dtype):
    return jax.ShapeDtypeStruct(shape, dtype)


VMEM = pl.BlockSpec(memory_space=pltpu.VMEM)
SMEM = pl.BlockSpec(memory_space=pltpu.SMEM)
HBM = pl.BlockSpec(memory_space=pl.ANY)


def dma(*shape):
    return pltpu.SemaphoreType.DMA(shape)


def gathered_plan(
    n, tokens, lengths, query_weight, query_bias, key_weight, value_weight, value_bias,
    conv_kernel, out_weight, out_bias, first_gain, first_shift, up_weight, up_bias, down_weight,
    down_bias, second_gain, second_shift, out_grad,
):
    batch, tok, width = tokens.shape
    rows = batch * tok
    local = query_weight.shape[1]
    hidden = up_weight.shape[1]
    total = n * tok
    block = width // n
    piece = tok // 2

    def low(*shape):
        return pltpu.VMEM(shape, bf16)

    def wide(*shape):
        return pltpu.VMEM(shape, f32)

    results = (
        whole((rows, width), bf16),
        whole((rows, width), f32),
        whole((block, local), f32),
        whole((local,), f32),
        whole((block, local), f32),
        whole((block, local), f32),
        whole((local,), f32),
        whole(conv_kernel.shape, f32),
        whole((local, block), f32),
        whole((width,), f32),
        whole((width,), f32),
        whole((width,), f32),
        whole((block, hidden), f32),
        whole((hidden,), f32),
        whole((block, hidden), f32),
        whole((width,), f32),
        whole((width,), f32),
        whole((width,), f32),
        whole((1, 1), f32),
    )
    outs = pl.pallas_call(
        functools.partial(layer_kernel, n),
        out_shape=results,
        in_specs=[SMEM, HBM, HBM, VMEM, HBM, HBM, VMEM, VMEM, HBM, VMEM, VMEM, VMEM, HBM, VMEM, HBM,
                  VMEM, VMEM, VMEM, HBM],
        out_specs=(HBM,) * RESULTS,
        scratch_shapes=[pltpu.VMEM(r.shape, r.dtype) for r in results]
        + [
            low(rows, width), low(local, width), low(local, width), low(local, width),
            low(width, hidden), low(hidden, width), low(rows, width), low(local, width),
            low(width, width), low(hidden, width), low(width, hidden),
            low(3, 2, rows, LANES), low(total, LANES), low(total, LANES), low(total + tok, LANES),
            wide(total, LANES), wide(total, LANES), wide(5 * NS_ITERS, LANES, LANES),
            low(n, tok, LANES), low(n, piece, LANES), low(batch, tok, LANES),
            low(batch, piece, LANES),
            low(4, tok, LANES), low(4, piece, LANES), low(4, 2, tok, LANES),
            low(2, 4, piece, width), wide(2, 4, piece, hidden),
            low(2, 4, piece, hidden), low(2, 4, piece, width), low(2, 4, piece, hidden),
            low(2, 2, 2, piece, width), low(2, 2, 2, piece, width), low(2, 2, piece, width),
            low(2, 2, piece, width), low(2, 2, tok, width), low(2, tok, width),
            low(total + tok, LANES), low(3, n, tok, LANES), low(3, n, tok // 2, LANES),
            low(3, batch, tok, LANES), low(3, batch, tok // 2, LANES), low(3 * local, width),
            low(rows, width), wide(8, width), wide(4, 8, width), low(n, 2, tok // 2, width),
            low(rows, 3 * local), low(width, hidden), low(width, hidden), low(width, local),
            low(width, local), low(width, local), wide(4, 8, width), wide(3, 8, width),
            wide(4, 8, 2 * LANES), wide(3, 8, 2 * LANES), low(rows, width), wide(2, 2, 2, 2, piece, width),
        ]
        + [
            b
            for first, w in (
                *((hidden // 2, hidden // 2),) * 4, (local, local), (local, 3 * local)
            )
            for b in scatter_buffers(first, w, block)
        ]
        + [
            dma(8), dma(3), dma(3), dma(2), dma(2), dma(1), dma(1), dma(2), dma(2), dma(1),
            dma(2, 2, 3), dma(1), dma(2, 2, 3), dma(1), dma(1), dma(2), dma(2), dma(3), dma(3, 3),
            dma(3), dma(7), dma(JOBS, 2), dma(JOBS, 5), dma(2), dma(3), dma(1), dma(3),
            dma(RESULTS),
        ],
        compiler_params=pltpu.CompilerParams(
            collective_id=0, has_side_effects=True, vmem_limit_bytes=56 * 2**20
        ),
        name="layer",
    )(
        lengths, tokens.reshape(rows, width), query_weight.T, query_bias, key_weight.T,
        value_weight.T, value_bias, conv_kernel, out_weight, out_bias, first_gain, first_shift,
        up_weight, up_bias, down_weight, down_bias, second_gain, second_shift,
        out_grad.reshape(rows, width),
    )
    outs = pl.pallas_call(
        finish_kernel,
        out_shape=results,
        in_specs=[HBM] * RESULTS,
        out_specs=(HBM,) * RESULTS,
        scratch_shapes=[pltpu.VMEM(r.shape, r.dtype) for r in results]
        + [dma(RESULTS), dma(RESULTS)],
        compiler_params=pltpu.CompilerParams(vmem_limit_bytes=60 * 2**20),
        name="finish",
    )(*outs)
    return (
        outs[0].reshape(tokens.shape),
        outs[1].reshape(tokens.shape),
        *outs[2:14],
        outs[14].T,
        *outs[15:18],
        outs[18].reshape(()),
    )


def per_device(seq, tensor, *args):
    batch, tok, width = args[0].shape
    heads = args[7].shape[0]
    if seq == 8 and tensor == 4 and batch == 4 and heads == 3 and tok == 128:
        return gathered_plan(seq, *args)
    return general_plan(*args)


def solution(mesh):
    return jax.shard_map(
        functools.partial(per_device, mesh.shape["seq"], mesh.shape["tensor"]),
        mesh=mesh,
        in_specs=(
            P(None, "seq", None),
            P(),
            P(None, "tensor"),
            P("tensor"),
            P(None, "tensor"),
            P(None, "tensor"),
            P("tensor"),
            P("tensor", None),
            P("tensor", None),
            P(),
            P(),
            P(),
            P(None, "tensor"),
            P("tensor"),
            P("tensor", None),
            P(),
            P(),
            P(),
            P(None, "seq", None),
        ),
        out_specs=(
            P(None, "seq", None),
            P(None, "seq", None),
            P("seq", "tensor"),
            P("tensor"),
            P("seq", "tensor"),
            P("seq", "tensor"),
            P("tensor"),
            P("tensor", None),
            P("tensor", "seq"),
            P(),
            P(),
            P(),
            P("seq", "tensor"),
            P("tensor"),
            P("tensor", "seq"),
            P(),
            P(),
            P(),
            P(),
        ),
        check_vma=False,
    )
```

```python
import functools

import jax
import jax.numpy as jnp
from jax import lax
from jax.experimental import pallas as pl
from jax.experimental.pallas import tpu as pltpu
from jax.sharding import PartitionSpec as P

HEADS = 12
HEAD_DIM = 64
LAND = 64
CONV = 33
NS_ITERS = 6


highest = lax.Precision.HIGHEST
epsilon = 1e-05
negative = -1e30


def joined(x, axis, combine):
    everything = jax.tree.map(lambda part: lax.all_gather(part, axis), x)
    first = jax.tree.map(lambda part: part[0], everything)

    def hop(k, so_far):
        return combine(so_far, jax.tree.map(lambda part: part[k], everything))

    return lax.fori_loop(1, lax.axis_size(axis), hop, first)


def with_halo(block, sides, width):
    for axis, dim in sides:
        count = lax.axis_size(axis)
        forward = [(i, i + 1) for i in range(count - 1)]
        backward = [(target, source) for source, target in forward]
        low = lax.ppermute(
            lax.slice_in_dim(block, block.shape[dim] - width, None, axis=dim), axis, forward
        )
        high = lax.ppermute(lax.slice_in_dim(block, 0, width, axis=dim), axis, backward)
        block = jnp.concatenate([low, block, high], axis=dim)
    return block


def newton_inverse(kernel):
    identity = jnp.eye(kernel.shape[-1], dtype=jnp.float32)
    inverse = jnp.swapaxes(kernel, -1, -2) / jnp.sum(kernel * kernel, axis=(-2, -1), keepdims=True)
    for _ in range(NS_ITERS):
        product = jnp.matmul(kernel, inverse, precision=highest)
        inner_term = jnp.matmul(product, 7.0 * identity - product, precision=highest)
        inner_term = jnp.matmul(product, 15.0 * identity - inner_term, precision=highest)
        inverse = 0.25 * jnp.matmul(inverse, 13.0 * identity - inner_term, precision=highest)
    return inverse


def landmark_core(query_marks, key_marks):
    scores = jnp.einsum(
        "bhjd,bhid->bhji", query_marks, key_marks, precision=highest
    ) * HEAD_DIM ** (-0.5)
    kernel_two = jax.nn.softmax(scores, axis=-1)
    return (kernel_two, newton_inverse(kernel_two))


def normalize(summed, gain_vec, shift_vec):
    middle = jnp.mean(summed, axis=-1, keepdims=True)
    centred = summed - middle
    inverse_std = lax.rsqrt(jnp.mean(centred * centred, axis=-1, keepdims=True) + epsilon)
    normal = centred * inverse_std
    return (normal * gain_vec + shift_vec, normal, inverse_std)


def add_norm(partial_sum, residual, bias_vec, gain_vec, shift_vec):
    summed = lax.psum(partial_sum.astype(jnp.bfloat16), "tensor").astype(jnp.float32)
    return normalize(residual + summed + bias_vec, gain_vec, shift_vec)


def norm_back(grad_hidden, normal, inverse_std, gain_vec):
    grad_normal = grad_hidden * gain_vec
    grad_summed = inverse_std * (
        grad_normal
        - jnp.mean(grad_normal, axis=-1, keepdims=True)
        - normal * jnp.mean(grad_normal * normal, axis=-1, keepdims=True)
    )
    return (grad_summed, jnp.sum(grad_hidden * normal, axis=0), jnp.sum(grad_hidden, axis=0))


def combine_soft(earlier, later):
    top_score = jnp.maximum(earlier[0], later[0])
    weight_first = jnp.exp(earlier[0] - top_score)
    weight_second = jnp.exp(later[0] - top_score)
    return (
        top_score,
        earlier[1] * weight_first + later[1] * weight_second,
        earlier[2] * weight_first[..., None] + later[2] * weight_second[..., None],
    )


def general_plan(
    tokens,
    lengths,
    query_weight,
    query_bias,
    key_weight,
    value_weight,
    value_bias,
    conv_kernel,
    out_weight,
    out_bias,
    first_gain,
    first_shift,
    up_weight,
    up_bias,
    down_weight,
    down_bias,
    second_gain,
    second_shift,
    out_grad,
):
    batch, tok_local, width = tokens.shape
    local_width = query_weight.shape[1]
    local_heads = conv_kernel.shape[0]
    head_dim = local_width // local_heads
    score_scale = HEAD_DIM ** (-0.5)
    rows = batch * tok_local
    half_width = CONV // 2
    f32 = jnp.float32
    bf16 = jnp.bfloat16
    position = lax.axis_index("seq") * tok_local + jnp.arange(tok_local, dtype=jnp.int32)
    inside = position[None, :] < lengths[:, None]
    living = inside.astype(f32)
    segment = position[None, :] * LAND // lengths[:, None]
    onehot = (
        (segment[:, :, None] == jnp.arange(LAND, dtype=jnp.int32)[None, None, :])
        & inside[:, :, None]
    ).astype(f32)
    marks_index = jnp.arange(LAND, dtype=jnp.int32)
    upper = ((marks_index[None, :] + 1) * lengths[:, None] + LAND - 1) // LAND
    lower = (marks_index[None, :] * lengths[:, None] + LAND - 1) // LAND
    counts = (upper - lower).astype(f32)
    flat = tokens.reshape(rows, width)
    flat_wide = flat.astype(f32)
    queries = (jnp.dot(flat, query_weight, preferred_element_type=f32) + query_bias).astype(bf16)
    key_vectors = jnp.dot(flat, key_weight, preferred_element_type=f32).astype(bf16)
    values = (
        (jnp.dot(flat, value_weight, preferred_element_type=f32) + value_bias)
        * living.reshape(rows, 1)
    ).astype(bf16)
    query_three = queries.reshape(batch, tok_local, local_width)
    key_three = key_vectors.reshape(batch, tok_local, local_width)
    value_three = values.reshape(batch, tok_local, local_width)
    onehot_low = onehot.astype(bf16)
    query_sum = jnp.einsum("btj,btf->bjf", onehot_low, query_three, preferred_element_type=f32)
    key_sum = jnp.einsum("btj,btf->bjf", onehot_low, key_three, preferred_element_type=f32)
    query_sum, key_sum = lax.psum((query_sum, key_sum), "seq")
    query_marks = (
        (query_sum / counts[:, :, None])
        .reshape(batch, LAND, local_heads, head_dim)
        .transpose(0, 2, 1, 3)
    )
    key_marks = (
        (key_sum / counts[:, :, None])
        .reshape(batch, LAND, local_heads, head_dim)
        .transpose(0, 2, 1, 3)
    )
    (kernel_two, inverse), core_back = jax.vjp(landmark_core, query_marks, key_marks)
    identity = jnp.eye(LAND, dtype=f32)
    deviation = identity - jnp.matmul(kernel_two, inverse, precision=highest)
    proxy_part = jnp.sum(jnp.sqrt(jnp.sum(deviation * deviation, axis=(-2, -1)))) / (batch * HEADS)
    query_heads = query_three.reshape(batch, tok_local, local_heads, head_dim).astype(f32)
    key_heads = key_three.reshape(batch, tok_local, local_heads, head_dim).astype(f32)
    value_heads = value_three.reshape(batch, tok_local, local_heads, head_dim).astype(f32)
    first_scores = (
        jnp.einsum("bthd,bhjd->bhtj", query_heads, key_marks, precision=highest) * score_scale
    )
    kernel_one = jax.nn.softmax(first_scores, axis=-1)
    third_scores = (
        jnp.einsum("bhjd,bthd->bhjt", query_marks, key_heads, precision=highest) * score_scale
    )
    key_alive = inside[:, None, None, :]
    third_scores = jnp.where(key_alive, third_scores, negative)
    local_top = jnp.max(third_scores, axis=-1)
    local_weights = jnp.where(key_alive, jnp.exp(third_scores - local_top[..., None]), 0.0)
    local_total = jnp.sum(local_weights, axis=-1)
    local_mix = jnp.einsum("bhjt,bthd->bhjd", local_weights, value_heads, precision=highest)
    top_score, total_weight, mixed = joined(
        (local_top, local_total, local_mix), "seq", combine_soft
    )
    third_out = mixed / total_weight[..., None]
    carried = jnp.matmul(inverse, third_out, precision=highest)
    nystrom = jnp.einsum("bhtj,bhjd->bthd", kernel_one, carried, precision=highest).reshape(
        batch, tok_local, local_width
    )
    padded_values = with_halo(value_three, (("seq", 1),), half_width)
    kernel_wide = jnp.repeat(conv_kernel, head_dim, axis=0)
    convolved = jnp.zeros((batch, tok_local, local_width), f32)
    for i in range(CONV):
        convolved = (
            convolved + padded_values[:, i : i + tok_local, :].astype(f32) * kernel_wide[:, i]
        )
    attention = (nystrom + convolved).astype(bf16).reshape(rows, local_width)
    out_part = jnp.dot(attention, out_weight, preferred_element_type=f32)
    hidden_one, normal_one, inverse_one = add_norm(
        out_part, flat_wide, out_bias, first_gain, first_shift
    )
    hidden_low = hidden_one.astype(bf16)
    up_value = jnp.dot(hidden_low, up_weight, preferred_element_type=f32) + up_bias
    activated, gelu_back = jax.vjp(lambda z: jax.nn.gelu(z, approximate=False), up_value)
    activated = activated.astype(bf16)
    down_part = jnp.dot(activated, down_weight, preferred_element_type=f32)
    hidden_two, normal_two, inverse_two = add_norm(
        down_part, hidden_one, down_bias, second_gain, second_shift
    )
    output = hidden_two.astype(bf16).reshape(batch, tok_local, width)
    grad_output = out_grad.reshape(rows, width).astype(f32)
    grad_second_total, grad_second_gain, grad_second_shift = norm_back(
        grad_output, normal_two, inverse_two, second_gain
    )
    down_in = grad_second_total.astype(bf16)
    grad_down_bias = jnp.sum(down_in.astype(f32), axis=0)
    grad_down_weight = jnp.einsum("rf,rd->fd", activated, down_in, preferred_element_type=f32)
    grad_activated = jnp.einsum("rd,fd->rf", down_in, down_weight, preferred_element_type=f32)
    up_in = gelu_back(grad_activated)[0].astype(bf16)
    grad_up_bias = jnp.sum(up_in.astype(f32), axis=0)
    grad_up_weight = jnp.einsum("rd,rf->df", hidden_low, up_in, preferred_element_type=f32)
    hidden_part = jnp.einsum("rf,df->rd", up_in, up_weight, preferred_element_type=f32)
    grad_hidden_one = (
        lax.psum(hidden_part.astype(jnp.bfloat16), "tensor").astype(jnp.float32) + grad_second_total
    )
    grad_first_total, grad_first_gain, grad_first_shift = norm_back(
        grad_hidden_one, normal_one, inverse_one, first_gain
    )
    out_in = grad_first_total.astype(bf16)
    grad_out_bias = jnp.sum(out_in.astype(f32), axis=0)
    grad_out_weight = jnp.einsum("rf,rd->fd", attention, out_in, preferred_element_type=f32)
    grad_attention = jnp.einsum(
        "rd,fd->rf", out_in, out_weight, preferred_element_type=f32
    ).reshape(batch, tok_local, local_width)
    padded_grad = with_halo(grad_attention.astype(jnp.bfloat16), (("seq", 1),), half_width).astype(
        grad_attention.dtype
    )
    grad_conv_values = jnp.zeros((batch, tok_local, local_width), f32)
    conv_columns = []
    for i in range(CONV):
        conv_columns.append(
            jnp.sum(
                grad_attention * padded_values[:, i : i + tok_local, :].astype(f32), axis=(0, 1)
            )
        )
        start_index = 2 * half_width - i
        grad_conv_values = (
            grad_conv_values
            + padded_grad[:, start_index : start_index + tok_local, :] * kernel_wide[:, i]
        )
    grad_conv_kernel = (
        jnp.stack(conv_columns, axis=0).reshape(CONV, local_heads, head_dim).sum(axis=-1).T
    )
    grad_nystrom = grad_attention.reshape(batch, tok_local, local_heads, head_dim)
    grad_kernel_one = jnp.einsum("bthd,bhjd->bhtj", grad_nystrom, carried, precision=highest)
    grad_carried_part = jnp.einsum("bhtj,bthd->bhjd", kernel_one, grad_nystrom, precision=highest)
    grad_first_scores = kernel_one * (
        grad_kernel_one - jnp.sum(kernel_one * grad_kernel_one, axis=-1, keepdims=True)
    )
    grad_query_one = (
        jnp.einsum("bhtj,bhjd->bthd", grad_first_scores, key_marks, precision=highest) * score_scale
    )
    grad_key_marks_part = (
        jnp.einsum("bhtj,bthd->bhjd", grad_first_scores, query_heads, precision=highest)
        * score_scale
    )
    grad_carried, grad_key_marks_one = lax.psum((grad_carried_part, grad_key_marks_part), "seq")
    grad_third_out = jnp.matmul(jnp.swapaxes(inverse, -1, -2), grad_carried, precision=highest)
    grad_inverse = jnp.matmul(grad_carried, jnp.swapaxes(third_out, -1, -2), precision=highest)
    grad_query_marks_two, grad_key_marks_two = core_back((jnp.zeros_like(kernel_two), grad_inverse))
    third_prob = local_weights * jnp.exp(local_top - top_score)[..., None] / total_weight[..., None]
    delta_term = jnp.sum(grad_third_out * third_out, axis=-1)
    grad_prob_value = jnp.einsum("bhjd,bthd->bhjt", grad_third_out, value_heads, precision=highest)
    grad_third_scores = third_prob * (grad_prob_value - delta_term[..., None])
    grad_value_three = jnp.einsum("bhjt,bhjd->bthd", third_prob, grad_third_out, precision=highest)
    grad_key_three = (
        jnp.einsum("bhjt,bhjd->bthd", grad_third_scores, query_marks, precision=highest)
        * score_scale
    )
    grad_query_marks_part = (
        jnp.einsum("bhjt,bthd->bhjd", grad_third_scores, key_heads, precision=highest) * score_scale
    )
    grad_query_marks_three = lax.psum(grad_query_marks_part, "seq")
    grad_query_marks = (grad_query_marks_two + grad_query_marks_three) / counts[:, None, :, None]
    grad_key_marks = (grad_key_marks_one + grad_key_marks_two) / counts[:, None, :, None]
    grad_query_marks = grad_query_marks.transpose(0, 2, 1, 3).reshape(batch, LAND, local_width)
    grad_key_marks = grad_key_marks.transpose(0, 2, 1, 3).reshape(batch, LAND, local_width)
    grad_query_seg = jnp.einsum("btj,bjf->btf", onehot, grad_query_marks, precision=highest)
    grad_key_seg = jnp.einsum("btj,bjf->btf", onehot, grad_key_marks, precision=highest)
    query_in = (
        (grad_query_one.reshape(batch, tok_local, local_width) + grad_query_seg)
        .astype(bf16)
        .reshape(rows, local_width)
    )
    key_in = (
        (grad_key_three.reshape(batch, tok_local, local_width) + grad_key_seg)
        .astype(bf16)
        .reshape(rows, local_width)
    )
    value_in = (grad_value_three.reshape(batch, tok_local, local_width) + grad_conv_values).astype(
        bf16
    )
    value_in = jnp.where(inside[:, :, None], value_in, jnp.zeros_like(value_in)).reshape(
        rows, local_width
    )
    grad_query_bias = jnp.sum(query_in.astype(f32), axis=0)
    grad_value_bias = jnp.sum(value_in.astype(f32), axis=0)
    grad_query_weight = jnp.einsum("rd,rf->df", flat, query_in, preferred_element_type=f32)
    grad_key_weight = jnp.einsum("rd,rf->df", flat, key_in, preferred_element_type=f32)
    grad_value_weight = jnp.einsum("rd,rf->df", flat, value_in, preferred_element_type=f32)
    input_part = (
        jnp.einsum("rf,df->rd", query_in, query_weight, preferred_element_type=f32)
        + jnp.einsum("rf,df->rd", key_in, key_weight, preferred_element_type=f32)
        + jnp.einsum("rf,df->rd", value_in, value_weight, preferred_element_type=f32)
    )
    input_sum, proxy_norm = (
        lax.psum(input_part.astype(jnp.bfloat16), "tensor").astype(jnp.float32),
        lax.psum(proxy_part.astype(jnp.bfloat16), "tensor").astype(jnp.float32),
    )
    grad_tokens = (grad_first_total + input_sum).reshape(batch, tok_local, width)
    (
        grad_query_weight,
        grad_key_weight,
        grad_value_weight,
        grad_out_weight,
        grad_up_weight,
        grad_down_weight,
    ) = (
        lax.psum_scatter(grad_query_weight, "seq", scatter_dimension=0, tiled=True),
        lax.psum_scatter(grad_key_weight, "seq", scatter_dimension=0, tiled=True),
        lax.psum_scatter(grad_value_weight, "seq", scatter_dimension=0, tiled=True),
        lax.psum_scatter(grad_out_weight, "seq", scatter_dimension=1, tiled=True),
        lax.psum_scatter(grad_up_weight, "seq", scatter_dimension=0, tiled=True),
        lax.psum_scatter(grad_down_weight, "seq", scatter_dimension=1, tiled=True),
    )
    (
        grad_query_bias,
        grad_value_bias,
        grad_conv_kernel,
        grad_out_bias,
        grad_first_gain,
        grad_first_shift,
        grad_up_bias,
        grad_down_bias,
        grad_second_gain,
        grad_second_shift,
    ) = lax.psum(
        (
            grad_query_bias,
            grad_value_bias,
            grad_conv_kernel,
            grad_out_bias,
            grad_first_gain,
            grad_first_shift,
            grad_up_bias,
            grad_down_bias,
            grad_second_gain,
            grad_second_shift,
        ),
        "seq",
    )
    return (
        output,
        grad_tokens,
        grad_query_weight,
        grad_query_bias,
        grad_key_weight,
        grad_value_weight,
        grad_value_bias,
        grad_conv_kernel,
        grad_out_weight,
        grad_out_bias,
        grad_first_gain,
        grad_first_shift,
        grad_up_weight,
        grad_up_bias,
        grad_down_weight,
        grad_down_bias,
        grad_second_gain,
        grad_second_shift,
        proxy_norm,
    )


MESH = pl.DeviceIdType.MESH
LANES = 2 * HEAD_DIM
f32 = jnp.float32
bf16 = jnp.bfloat16
NN = (1, 0)
NT = (1, 1)
TN = (0, 0)


def dot(a, b, dims=NN):
    return lax.dot_general(
        a, b, (((dims[0],), (dims[1],)), ((), ())), preferred_element_type=f32
    )


def split(x):
    if x.dtype == bf16:
        return (x,)
    top = x.astype(bf16)
    return (top, (x - top.astype(f32)).astype(bf16))


def fine(a, b, dims=NN):
    a, b = split(a), split(b)
    total = dot(a[0], b[0], dims)
    if len(b) > 1:
        total = total + dot(a[0], b[1], dims)
    if len(a) > 1:
        total = total + dot(a[1], b[0], dims)
    return total


def iota(shape, dim):
    return lax.broadcasted_iota(jnp.int32, shape, dim)


def block_mask():
    shape = (LANES, LANES)
    return (iota(shape, 0) < HEAD_DIM) == (iota(shape, 1) < HEAD_DIM)


def eye():
    return jnp.where(iota((LANES, LANES), 0) == iota((LANES, LANES), 1), 1.0, 0.0).astype(f32)


def block_sums(x, same_head):
    ones = jnp.where(same_head, 1.0, 0.0).astype(bf16)
    return jnp.where(same_head, fine(fine(ones, x), ones), 1.0)


def taps_matrix(row, tok):
    return pltpu.roll(jnp.broadcast_to(row, (tok, 2 * tok)), 0, 1, stride=1, stride_axis=0)


def taps_row(taps, head, tok):
    row = taps[pl.ds(head, 1), :]
    return jnp.concatenate([row, jnp.zeros((1, 2 * tok - CONV), f32)], axis=1)


def conv_block(matrices, window):
    first = fine(matrices[0], window)
    second = fine(matrices[1], window)
    return jnp.where(iota(first.shape, 1) < HEAD_DIM, first, second)


def greet(devices):
    barrier = pltpu.get_barrier_semaphore()
    for device in devices:
        pl.semaphore_signal(barrier, inc=1, device_id=device, device_id_type=MESH)
    return barrier


def around(n, me, tensor):
    return [(lax.rem(me + d, n), tensor) for d in range(1, n)]


def others(me, tensor):
    core = tensor + 1 - 2 * (tensor % 2)
    return [(me, core), (me, lax.rem(tensor + 2, 4)), (me, lax.rem(core + 2, 4))]


def paired(y):
    return y[:, :LANES], jnp.concatenate(
        [y[:, LANES : LANES + HEAD_DIM], y[:, HEAD_DIM:LANES]], axis=1
    )


def remote(src, dst, send, recv, device):
    return pltpu.make_async_remote_copy(
        src_ref=src, dst_ref=dst, send_sem=send, recv_sem=recv, device_id=device,
        device_id_type=MESH,
    )


def member_rows(length, total):
    j = iota((LANES, total), 0) % LAND
    t = iota((LANES, total), 1)
    inside = (t * LAND >= j * length) & (t * LAND < (j + 1) * length) & (t < length)
    return jnp.where(inside, 1.0, 0.0).astype(bf16)


def member_columns(length, total):
    j = iota((total, LANES), 1) % LAND
    t = iota((total, LANES), 0)
    inside = (t * LAND >= j * length) & (t * LAND < (j + 1) * length) & (t < length)
    return jnp.where(inside, 1.0, 0.0).astype(bf16)


def segment_counts(length):
    j = iota((LANES, LANES), 0) % LAND
    upper = ((j + 1) * length + LAND - 1) // LAND
    lower = (j * length + LAND - 1) // LAND
    return (upper - lower).astype(f32)


def normal_of(summed):
    middle = jnp.mean(summed, axis=-1, keepdims=True)
    centred = summed - middle
    inverse_std = lax.rsqrt(jnp.mean(centred * centred, axis=-1, keepdims=True) + epsilon)
    return centred * inverse_std, inverse_std


def before_norm(grad, normal, inverse_std, gain):
    grad_normal = grad * gain
    return inverse_std * (
        grad_normal
        - jnp.mean(grad_normal, axis=-1, keepdims=True)
        - normal * jnp.mean(grad_normal * normal, axis=-1, keepdims=True)
    )


def block_rows(t, tok):
    return pl.ds(pl.multiple_of(t * tok, tok), tok)


def settle(ref, sem):
    pltpu.make_async_copy(ref, ref, sem).wait()


class Scatter:
    def __init__(self, index, me, tensor, source, columns, buffers, send, recv, order):
        self.index, self.source, self.columns = index, source, pl.ds(*columns)
        self.first_in, self.held, self.second_in, self.pair, self.last_in, self.cross_in = buffers
        self.block = source.shape[0] // 8
        self.weights = [2**bit for bit in order]
        self.bits = [(me // weight) % 2 for weight in self.weights]
        self.partners = [
            (me + weight * (1 - 2 * bit), tensor) for weight, bit in zip(self.weights, self.bits)
        ]
        self.send, self.recv = send, recv

    def rows(self, slot, bit):
        index = (slot // 2) * self.weights[2] + (slot % 2) * self.weights[1] + bit * self.weights[0]
        return pl.ds(pl.multiple_of(index * self.block, 16), self.block)

    def copy(self, src, dst, k, stage):
        return remote(
            src, dst, self.send.at[self.index, min(k, 1)], self.recv.at[self.index, k],
            self.partners[stage],
        )

    def arrived(self, ref, k):
        settle(ref, self.recv.at[self.index, k])

    def first(self, slots=range(4)):
        for slot in slots:
            source = self.source.at[self.rows(slot, 1 - self.bits[0]), self.columns]
            self.copy(source, self.first_in.at[slot], 0, 0).start()

    def second(self):
        self.arrived(self.first_in, 0)
        for slot in range(4):
            mine = self.source[self.rows(slot, self.bits[0]), self.columns]
            self.held[slot] = self.joined(mine, self.first_in[slot])
        for k in range(2):
            self.copy(self.held.at[2 * k + 1 - self.bits[1]], self.second_in.at[k], 1, 1).start()

    def joined(self, mine, come):
        return (mine.astype(f32) + come.astype(f32)).astype(bf16)

    def third(self):
        self.arrived(self.second_in, 1)
        for k in range(2):
            both = self.held[2 * k + self.bits[1]].astype(f32) + self.second_in[k].astype(f32)
            self.pair[k] = both.astype(bf16)
        self.copy(self.pair.at[1 - self.bits[2]], self.last_in, 2, 2).start()

    def last(self, write):
        self.arrived(self.last_in, 2)
        write(self.pair[self.bits[2]].astype(f32) + self.last_in[...].astype(f32))

    def finish(self):
        settle(self.first_in, self.send.at[self.index, 0])
        settle(self.held.at[pl.ds(0, 3)], self.send.at[self.index, 1])


class Line(Scatter):
    def __init__(self, *args):
        super().__init__(*args)
        z = self.bits[1] + 2 * self.bits[2]
        right = z // 2
        self.end = self.bits[1] == right
        self.inner = self.bits[1] != right
        self.slots = [k * (1 - right) + (3 - k) * right for k in range(4)]
        self.partners[2] = (2 * (3 - z) + self.bits[0], self.partners[0][1])

    def second(self):
        self.arrived(self.first_in, 0)
        for slot in range(4):
            mine = self.source[self.rows(slot, self.bits[0]), self.columns]
            self.held[slot] = self.joined(mine, self.first_in[slot])
        come = (self.second_in.at[0], self.second_in.at[1], self.last_in)
        sends = [
            self.copy(self.held.at[self.slots[3 - k]], come[k], (1, 1, 2)[k], 1)
            for k in range(3)
        ]

        @pl.when(self.end)
        def _():
            for copy in sends:
                copy.start()

    def third(self):
        sends = [
            self.copy(self.pair.at[k], self.cross_in.at[k], 3, 2) for k in range(2)
        ]

        @pl.when(self.inner)
        def _():
            self.arrived(self.second_in, 1)
            for k in range(2):
                self.pair[k] = self.joined(self.held[self.slots[3 - k]], self.second_in[k])
                sends[k].start()

    def fourth(self):
        back = self.copy(self.first_in.at[2], self.first_in.at[3], 4, 1)

        @pl.when(self.inner)
        def _():
            self.arrived(self.cross_in, 3)
            self.first_in[2] = self.joined(self.held[self.slots[0]], self.cross_in[0])
            back.start()

    def last(self, write):
        @pl.when(self.inner)
        def _():
            self.arrived(self.last_in, 2)
            write(
                self.held[self.slots[1]].astype(f32)
                + self.last_in[...].astype(f32)
                + self.cross_in[1].astype(f32)
            )

        @pl.when(self.end)
        def _():
            self.arrived(self.first_in.at[3], 4)
            write(self.held[self.slots[0]].astype(f32) + self.first_in[3].astype(f32))


class Pairs(Scatter):
    def second(self):
        self.arrived(self.first_in, 0)
        width = self.first_in.shape[2]
        for slot in range(4):
            at = self.rows(slot, self.bits[0])
            self.held[slot, :, :width] = self.source[at]
            self.held[slot, :, width : 2 * width] = self.shared[at]
            self.held[slot, :, 2 * width :] = self.first_in[slot]
        for k in range(2):
            self.copy(self.held.at[2 * k + 1 - self.bits[1]], self.second_in.at[k], 1, 1).start()


def scatter_buffers(first, width, block):
    return [
        pltpu.VMEM((4, block, first), bf16),
        pltpu.VMEM((4, block, width), bf16),
        pltpu.VMEM((2, block, width), bf16),
        pltpu.VMEM((2, block, width), bf16),
        pltpu.VMEM((block, width), bf16),
        pltpu.VMEM((2, block, width), bf16),
    ]


def total_of(v):
    return jnp.sum(v, axis=0, keepdims=True)


def packed(block):
    middle = block.shape[-2] // 2
    first, second = block[..., :middle, :HEAD_DIM], block[..., middle:, :HEAD_DIM]
    return jnp.concatenate([first, second], axis=-1)


def unpacked(block):
    return jnp.concatenate([block[..., :HEAD_DIM], block[..., HEAD_DIM:]], axis=-2)


class Ring:
    def __init__(
        self, tensor, peers, parts, core_out, core_in, y_out, y_in, ag_send, ag_recv, sum_send,
        sum_recv,
    ):
        self.tensor, self.place = tensor, tensor % 2
        self.core, self.across, self.far = peers
        self.near_pair = tensor - self.place
        self.far_pair = lax.rem(self.near_pair + 2, 4)
        self.parts, self.core_out, self.core_in = parts, core_out, core_in
        self.y_out, self.y_in = y_out, y_in
        self.ag, self.sums = (ag_send, ag_recv), (sum_send, sum_recv)
        self.copies = {}

    def send(self, name, src, dst, sems, at, device):
        copy = remote(src, dst, sems[0].at[0], sems[1].at[at], device)
        copy.start()
        self.copies[name] = copy

    def share(self, phase, c, held):
        mine = held.at[c, self.tensor]
        self.send((phase, c, "y"), mine, mine, self.ag, (phase, c, 0), self.across)
        self.send((phase, c, "core"), mine, mine, self.ag, (phase, c, 1), self.core)

    def work(self, phase, c, side, value):
        self.parts[phase, c, side] = value.reshape(2, -1, value.shape[1])
        self.core_out[phase, c, side] = self.parts[phase, c, side, 1 - self.place].astype(bf16)
        self.send(
            (phase, c, side), self.core_out.at[phase, c, side], self.core_in.at[phase, c, side],
            self.sums, (phase, c, side), self.core,
        )

    def run(self, phase, held, work):
        for c in range(2):
            self.copies[phase, c, "core"].wait_recv()
            self.work(phase, c, 0, work(c, self.near_pair))
        for c in range(2):
            self.copies[phase, c, "y"].wait_recv()
            other = held.at[c, self.across[1]]
            self.send((phase, c, "pass"), other, other, self.ag, (phase, c, 2), self.core)
            if c == 1:
                self.cross(phase, 0)
            self.copies[phase, c, "pass"].wait_recv()
            self.work(phase, c, 1, work(c, self.far_pair))
        self.cross(phase, 1)

    def cross(self, phase, c):
        self.copies[phase, c, 1].wait_recv()
        both = self.parts[phase, c, 1, self.place] + self.core_in[phase, c, 1].astype(f32)
        self.y_out[phase, c] = both.astype(bf16)
        self.send(
            (phase, c, "sum"), self.y_out.at[phase, c], self.y_in.at[phase, c], self.sums,
            (phase, c, 2), self.across,
        )

    def total(self, phase, c):
        self.copies[phase, c, 0].wait_recv()
        self.copies[phase, c, "sum"].wait_recv()
        return (
            self.parts[phase, c, 0, self.place]
            + self.core_in[phase, c, 0].astype(f32)
            + self.y_in[phase, c].astype(f32)
        )


JOBS = 6
MATRICES = 8
RESULTS = MATRICES + 2
OUTPUTS = 19


def layer_kernel(
    n, lengths, x_far, wq_far, qb, wk_far, wv_far, vb, taps, out_far, out_bias, gain_one,
    shift_one, up_far, up_bias, down_far, down_bias, gain_two, shift_two, grad_far,
    *rest,
):
    results, rest = rest[:RESULTS], rest[RESULTS:]
    ready, rest = rest[:MATRICES], rest[MATRICES:]
    layer_body(
        n, lengths, x_far, wq_far, qb, wk_far, wv_far, vb, taps, out_far, out_bias, gain_one,
        shift_one, up_far, up_bias, down_far, down_bias, gain_two, shift_two, grad_far, results,
        ready, *rest,
    )


def layer_body(
    n, lengths, x_far, wq_far, qb, wk_far, wv_far, vb, taps, out_far, out_bias, gain_one,
    shift_one, up_far, up_bias, down_far, down_bias, gain_two, shift_two, grad_far, results, ready,
    x, wk, wq, wv, up_weight, down_weight, out_grad, out_weight, out_whole,
    up_turned, down_turned, stage, ks, qs, vs, k1, p3, newton, out_stage, out_single, attn_pair, attn_single,
    pairs_in, singles_in, heads_out, hidden, slope, active, down_in, up_in,
    core_out, core_in, y_out, y_in, core_last, y_last,
    gs, back_stage, back_single, come_pair, come_single, weight_in, out_in, early, early_tensor, tokens_own, tokens_low, source_up,
    source_down, source_out, source_own, source_both, early_out, early_in, late_out, late_in, tokens_whole,
    parts_held,
    *rest,
):
    buffers, sems = rest[: 6 * JOBS], rest[6 * JOBS :]
    (load, send, recv, out_send, out_recv, whole_send, whole_recv, copy_send, copy_recv, ag_send,
     ag_recv, sum_send, sum_recv, grad_send, grad_recv, back_send, back_recv, share_send,
     share_recv, small_send, small_recv, job_send, job_recv, own_send, own_recv, last_send, last_recv,
     store) = sems
    output, grad_tokens, grad_query, grad_key, grad_value, grad_out, grad_up, grad_down = ready
    ready = (*ready, early_out.at[3], late_out.at[3])
    stores = []

    def done(*numbers):
        for i in numbers:
            copy = pltpu.make_async_copy(ready[i], results[i], store.at[i])
            copy.start()
            stores.append(copy)

    me = lax.axis_index("seq")
    tensor = lax.axis_index("tensor")
    rows, width = x.shape
    batch = n // 2
    tok = rows // batch
    total = n * tok
    half = CONV // 2
    own, side = me // 2, me % 2
    scale = HEAD_DIM ** (-0.5)
    ring_peers = around(n, me, tensor)
    peers = others(me, tensor)
    core, across, far = peers

    def batch_of(t):
        return lax.rem(t - me + 8, 4)

    def rows_at(t):
        return block_rows(batch_of(t), tok)

    mine = rows_at(tensor)
    at_home = batch_of(tensor) == own
    away = batch_of(tensor) != own
    local = wk.shape[0]
    barrier = greet(ring_peers + peers)
    loads = []
    for i, (source, target) in enumerate((
        (x_far, x), (wk_far, wk), (wq_far, wq), (wv_far, wv),
        (out_far, out_weight), (up_far, up_weight),
        (down_far, down_weight), (grad_far, out_grad),
    )):
        copy = pltpu.make_async_copy(source, target, load.at[i])
        copy.start()
        loads.append(copy)
    hidden_width = up_weight.shape[1]
    span = hidden_width // 2
    jobs = [
        kind(i, me, tensor, source, columns, buffers[6 * i : 6 * i + 6], job_send, job_recv, order)
        for i, (kind, source, columns, order) in enumerate((
            (Line, source_down, (0, span), (0, 1, 2)),
            (Scatter, source_down, (span, span), (1, 0, 2)),
            (Line, source_up, (0, span), (0, 1, 2)),
            (Line, source_up, (span, span), (0, 1, 2)),
            (Scatter, source_out, (0, local), (0, 1, 2)),
            (Pairs, source_own, (0, local), (0, 1, 2)),
        ))
    ]
    job_down, job_up = jobs[0:2], jobs[2:4]
    job_out, job_heads = jobs[4:]
    job_heads.shared = source_both

    owned = (ks, qs, vs)
    offsets = (0, 0, half)
    for padded in (vs, gs):
        padded[0:half] = jnp.zeros((half, LANES), bf16)
        padded[half + total : total + tok] = jnp.zeros((tok - half, LANES), bf16)
    even = side == 0

    seven = pl.ds(0, (n - 1) * tok)

    def spread(i):
        here = pl.ds(pl.multiple_of(offsets[i] + me * tok, 16), tok)
        for d in range(1, n):
            peer = lax.rem(me + d, n)
            copy = remote(
                stage.at[i, peer % 2, block_rows(peer // 2, tok)], owned[i].at[here],
                send.at[i], recv.at[i], (peer, tensor),
            )
            copy.start()
        owned[i][here] = stage[i, side, block_rows(own, tok)]

    loads[0].wait()
    loads[1].wait()
    y = dot(x[...], wk[...], NT)
    stage[0, 0], stage[0, 1] = paired(y.astype(bf16))
    pl.semaphore_wait(barrier, n + 2)
    spread(0)
    loads[2].wait()
    y = dot(x[...], wq[...], NT) + qb[...].reshape(1, local)
    stage[1, 0], stage[1, 1] = paired(y.astype(bf16))
    spread(1)
    loads[3].wait()
    y = dot(x[...], wv[...], NT) + vb[...].reshape(1, local)
    position = me * tok + iota((tok, local), 0)
    y = jnp.concatenate(
        [
            jnp.where(position < lengths[b], y[b * tok : (b + 1) * tok], 0.0)
            for b in range(batch)
        ],
        axis=0,
    )
    stage[2, 0], stage[2, 1] = paired(y.astype(bf16))
    loads[4].wait()
    pair_rows = block_rows(tensor, LANES)
    single_rows = pl.ds(pl.multiple_of(4 * LANES + tensor * HEAD_DIM, HEAD_DIM), HEAD_DIM)
    first, single = out_weight[:LANES], out_weight[LANES:]
    out_whole[pair_rows] = jnp.where(
        even, first, jnp.concatenate([single, first[HEAD_DIM:]], axis=0)
    )
    out_whole[single_rows] = jnp.where(even, single, first[:HEAD_DIM])
    for i, device in enumerate(peers):
        for at in (pair_rows, single_rows):
            part = out_whole.at[at]
            remote(part, part, whole_send.at[0], whole_recv.at[0], device).start()

    length = lengths[own]
    same_head = block_mask()
    identity = eye()
    ones = jnp.where(same_head, 1.0, 0.0).astype(bf16)
    members = member_rows(length, total)
    counts = segment_counts(length)
    matrices = [taps_matrix(taps_row(taps, h, tok), tok) for h in (2 * side, 1)]
    flip = jnp.where(
        iota((2 * tok, 2 * tok), 0) + iota((2 * tok, 2 * tok), 1) == CONV - 1, 1.0, 0.0
    ).astype(bf16)
    reverse = [
        taps_matrix(
            fine(jnp.broadcast_to(taps_row(taps, h, tok), (8, 2 * tok)), flip)[0:1], tok
        )
        for h in (2 * side, 1)
    ]
    for i, w in enumerate((wk, wq, wv)):
        pair, single = w[:LANES], w[LANES:]
        weight_in[i * LANES : (i + 1) * LANES] = jnp.where(
            even, pair, jnp.concatenate([single, pair[HEAD_DIM:]], axis=0)
        )
        start = 3 * LANES + i * HEAD_DIM
        weight_in[start : start + HEAD_DIM] = jnp.where(even, single, pair[:HEAD_DIM])
    for copy in loads[5:]:
        copy.wait()
    up_turned[...] = up_weight[...].T
    down_turned[...] = down_weight[...].T
    settle(ks.at[seven], recv.at[0])
    keys = ks[...]
    key_marks = jnp.where(same_head, dot(members, keys) / counts, 0.0)
    settle(qs.at[seven], send.at[1])
    spread(2)
    settle(qs.at[seven], recv.at[1])
    queries = qs[...]
    query_marks = jnp.where(same_head, dot(members, queries) / counts, 0.0)
    scores = jnp.where(same_head, fine(query_marks, key_marks, NT) * scale, negative)
    weights = jnp.exp(scores - jnp.max(scores, axis=1, keepdims=True))
    kernel_two = weights / jnp.sum(weights, axis=1, keepdims=True)
    inverse = jnp.where(
        same_head, kernel_two.T / block_sums(kernel_two * kernel_two, same_head), 0.0
    )
    def scores_one():
        values = fine(queries, key_marks, NT) * scale
        left = iota(values.shape, 1) < HEAD_DIM
        top_left = jnp.max(jnp.where(left, values, negative), axis=1, keepdims=True)
        top_right = jnp.max(jnp.where(left, negative, values), axis=1, keepdims=True)
        return jnp.exp(values - jnp.where(left, top_left, top_right))

    def scores_three():
        values = fine(keys, query_marks, NT) * scale
        alive = iota(values.shape, 0) < length
        values = jnp.where(alive, values, negative)
        weights = jnp.exp(values - jnp.max(values, axis=0, keepdims=True))
        return jnp.where(alive, weights, 0.0)

    product = fine(kernel_two, inverse)
    for step in range(NS_ITERS):
        if step == 0:
            weights_one = scores_one()
        if step == 1:
            k1[...] = weights_one / fine(weights_one, ones)
        if step == 2:
            weights_three = scores_three()
        if step == 3:
            third_prob = weights_three / jnp.sum(weights_three, axis=0, keepdims=True)
            p3[...] = third_prob
        inner = fine(product, 7.0 * identity - product)
        outer = 13.0 * identity - fine(product, 15.0 * identity - inner)
        newton[5 * step] = inverse
        newton[5 * step + 1] = product
        newton[5 * step + 2] = inner
        newton[5 * step + 3] = outer
        newton[5 * step + 4] = fine(product, kernel_two)
        inverse = 0.25 * fine(inverse, outer)
        product = 0.25 * fine(product, outer)

    deviation = identity - product
    norms = jnp.sqrt(block_sums(deviation * deviation, same_head))
    first, second = norms[0:1, 0:1], norms[LANES - 1 :, LANES - 1 :]
    norm_sum = jnp.where(side == 0, first + second, first) / (batch * HEADS)
    early[7:8] = jnp.broadcast_to(norm_sum, (1, width))

    settle(vs.at[seven], recv.at[2])
    values = vs[half : half + total]
    third_out = jnp.where(same_head, fine(third_prob, values, TN), 0.0)
    carried = fine(inverse, third_out)

    for d in range(1, n + 1):
        peer = lax.rem(me + d, n)
        start = pl.multiple_of(peer * tok, tok)
        nystrom = fine(k1[pl.ds(start, tok)], carried)
        convolved = conv_block(matrices, vs[pl.ds(start, 2 * tok)])
        low = (nystrom + convolved).astype(bf16)
        device = (peer, lax.rem(own + peer, 4))
        if d % 2 == 0:
            source, target = out_stage.at[d - 1], pairs_in.at[tensor]
            source[...] = low
        else:
            source, target = out_single.at[d - 1], singles_in.at[tensor]
            source[...] = packed(low)
        copy = remote(source, target, out_send.at[d % 2], out_recv.at[d % 2], device)
        if d < n:
            copy.start()
            continue
        attn_pair[own] = low
        pl.when(away)(copy.start)

        @pl.when(at_home)
        def _():
            pairs_in[tensor] = low

    three = pl.ds(0, 3)

    def settle_home(ref, some, sem):
        pl.when(away)(lambda: settle(ref, sem))
        pl.when(at_home)(lambda: settle(ref.at[some], sem))

    settle_home(pairs_in, three, out_recv.at[0])
    settle(singles_in, out_recv.at[1])
    settle(out_whole.at[pl.ds(0, 3 * local)], whole_recv.at[0])
    z, side_of_chip = me // 2, tensor % 2
    beside = (me + 1 - 2 * side, tensor)
    def give_tokens(src, dst, i, device):
        remote(src, dst, own_send.at[i // 2], own_recv.at[i], device).start()

    def half_block(b):
        start = pl.multiple_of(b * tok + side_of_chip * (tok // 2), tok // 2)
        return pl.ds(start, tok // 2)

    tokens_own[me, side_of_chip] = x[half_block(own)]
    for k in range(1, 4):
        peer = lax.rem(z + k, 4)
        give_tokens(
            x.at[half_block(peer)], tokens_own.at[me, side_of_chip], 0, (2 * peer + side, tensor)
        )
    half_own = tokens_own.at[me, side_of_chip]
    give_tokens(half_own, half_own, 1, beside)

    def pass_tokens():
        settle(tokens_own.at[pl.ds(0, 3), 0], own_recv.at[0])
        for k in range(1, 4):
            come = tokens_own.at[2 * lax.rem(z + 4 - k, 4) + side, side_of_chip]
            give_tokens(come, come, 1, beside)

    def line(vector):
        return vector[...].reshape(1, vector.shape[0])

    piece = tok // 2
    chunks = range(2)
    ring = Ring(
        tensor, peers, parts_held, core_out, core_in, y_out, y_in, ag_send, ag_recv, sum_send,
        sum_recv,
    )

    def rows_of(c):
        return pl.ds(pl.multiple_of(batch_of(tensor) * tok + c * piece, piece), piece)

    def normed(c):
        at = slice(c * piece, (c + 1) * piece)
        lanes = slice(c * HEAD_DIM, (c + 1) * HEAD_DIM)
        heads = jnp.concatenate(
            [pairs_in[t, at] for t in range(4)] + [singles_in[t, :, lanes] for t in range(4)],
            axis=1,
        )
        branch = dot(heads, out_whole[...])
        first_total = x[rows_of(c)].astype(f32) + (branch + line(out_bias))
        normal, inverse_std = normal_of(first_total)
        whole_row = normal * line(gain_one) + line(shift_one)
        hidden[c, tensor] = whole_row.astype(bf16)
        ring.share(0, c, hidden)
        return normal, inverse_std, whole_row

    def up(c, t):
        at = pl.ds(t, 2)
        value = dot(hidden[c, at].reshape(tok, width), up_weight[...]) + line(up_bias)
        half_erf = 0.5 * (1.0 + lax.erf(value * (0.5**0.5)))
        density = jnp.exp(-0.5 * value * value) * (0.5 / jnp.pi) ** 0.5
        slope[c, at] = (half_erf + value * density).reshape(2, piece, hidden_width)
        low = (value * half_erf).astype(bf16)
        active[c, at] = low.reshape(2, piece, hidden_width)
        return dot(low, down_weight[...])

    def down(c, t):
        at = pl.ds(t, 2)
        grad = dot(down_in[c, at].reshape(tok, width), down_turned[...])
        low = (grad * slope[c, at].reshape(tok, hidden_width)).astype(bf16)
        up_in[c, at] = low.reshape(2, piece, hidden_width)
        return dot(low, up_turned[...])

    after_norm_one = [normed(c) for c in chunks]
    ring.run(0, hidden, up)
    pass_tokens()
    for d in range(1, n):
        if d % 2 == 0:
            source, target = out_stage.at[d - 1], attn_pair.at[own]
        else:
            source, target = out_single.at[d - 1], attn_single.at[own]
        remote(
            source, target, copy_send.at[d % 2], copy_recv.at[d % 2],
            (lax.rem(me + d, n), tensor),
        ).start()

    grads_second, sums_second = [], []
    for c in chunks:
        hidden_one = after_norm_one[c][2]
        second_total = hidden_one + (ring.total(0, c) + line(down_bias))
        normal, inverse_std = normal_of(second_total)
        output[rows_of(c)] = (normal * line(gain_two) + line(shift_two)).astype(bf16)
        grad_output = out_grad[rows_of(c)].astype(f32)
        grad_second = before_norm(grad_output, normal, inverse_std, line(gain_two))
        low = grad_second.astype(bf16)
        down_in[c, tensor] = low
        ring.share(1, c, down_in)
        grads_second.append(grad_second)
        sums_second.append(
            (total_of(grad_output * normal), total_of(grad_output), total_of(low.astype(f32)))
        )
    ring.run(1, down_in, down)
    everything = (rows, width)
    every_hidden = (rows, hidden_width)
    source_down[...] = dot(
        down_in[...].reshape(everything), active[...].reshape(every_hidden), TN
    ).astype(bf16)
    for job in job_down:
        job.first()

    grads_first, sums_first = [], []
    for c in chunks:
        normal, inverse_std, _ = after_norm_one[c]
        grad_hidden = grads_second[c] + ring.total(1, c)
        grad_first = before_norm(grad_hidden, normal, inverse_std, line(gain_one))
        low = grad_first.astype(bf16)
        out_in[rows_of(c)] = low
        heads = dot(low, out_whole[...], NT).astype(bf16)
        at = slice(c * piece, (c + 1) * piece)
        for t in range(4):
            start = 4 * LANES + t * HEAD_DIM
            pair = heads[:, t * LANES : (t + 1) * LANES]
            heads_out[t, 0, at] = pair
            heads_out[t, 1, at] = jnp.concatenate(
                [heads[:, start : start + HEAD_DIM], pair[:, HEAD_DIM:]], axis=1
            )
        b = batch_of(tensor)
        there = pl.ds(pl.multiple_of(half + me * tok + c * piece, 16), piece)
        for t in range(4):
            for k, device in enumerate(((2 * b + side, t), (2 * b + 1 - side, t))):
                copy = remote(
                    heads_out.at[t, k, pl.ds(c * piece, piece)], gs.at[there], grad_send.at[0],
                    grad_recv.at[0], device,
                )
                if k == 1:
                    copy.start()
                else:
                    pl.when((batch_of(tensor) != own) | (tensor != t))(copy.start)
        grads_first.append(grad_first)
        sums_first.append(
            (total_of(grad_hidden * normal), total_of(grad_hidden), total_of(low.astype(f32)))
        )

    @pl.when(at_home)
    def _():
        here = pl.ds(pl.multiple_of(half + me * tok, 16), tok)
        gs[here] = heads_out[tensor, 0]

    source_up[...] = dot(
        hidden[...].reshape(everything), up_in[...].reshape(every_hidden), TN
    ).astype(bf16)
    for i in range(3):
        early[i : i + 1] = sums_second[0][i] + sums_second[1][i]
        early[i + 3 : i + 4] = sums_first[0][i] + sums_first[1][i]
    early[6:7] = dot(jnp.ones((8, rows), bf16), up_in[...].reshape(every_hidden))[0:1]
    early_tensor[tensor] = early[...]
    job_up[0].first(range(2))
    for i, device in enumerate(peers):
        remote(
            early, early_tensor.at[tensor], small_send.at[0], small_recv.at[0], device
        ).start()
    shares = []
    for i, held in enumerate((out_in, output)):
        for j, device in enumerate((across, core)):
            copy = remote(
                held.at[mine], held.at[mine], share_send.at[i], share_recv.at[i, j], device
            )
            copy.start()
            shares.append(copy)
    job_down[0].second()
    job_up[0].first(range(2, 4))
    job_up[1].first()
    settle(tokens_own.at[pl.ds(0, 4), 0], own_recv.at[1])
    half_all = tokens_own.at[:, side_of_chip]
    give_tokens(half_all, half_all, 2, core)

    members = member_columns(length, total)
    def give(i, block):
        low = block.astype(bf16)
        back_stage[i] = low.reshape(n, tok, LANES)
        back_single[i] = packed(low.reshape(n, tok, LANES))
        for d in range(1, n):
            peer = lax.rem(me + d, n)
            source, target = (back_stage, come_pair) if d % 2 == 0 else (back_single, come_single)
            remote(
                source.at[i, peer], target.at[i, own], back_send.at[d % 2],
                back_recv.at[d % 2], (peer, tensor),
            ).start()
        come_pair[i, own] = back_stage[i, me]
        return low

    eight = gs.at[pl.ds(0, total)]
    settle_home(eight, seven, grad_recv.at[0])
    grad = gs[half : half + total]
    kernel_one = k1[...]
    grad_carried = jnp.where(same_head, fine(kernel_one, grad, TN), 0.0)
    grad_third = fine(inverse, grad_carried, TN)
    grad_inverse = fine(grad_carried, third_out, NT)
    settle(early_tensor.at[three], small_recv.at[0])
    by_tensor = early_tensor[0] + early_tensor[1] + early_tensor[2] + early_tensor[3]
    early_out[0] = jnp.where(iota(by_tensor.shape, 0) == 6, early[...], by_tensor)
    smalls_early = []

    def early_next(k):
        if k > 0:
            smalls_early[k - 1].wait_recv()
            early_out[k] = early_out[k - 1] + early_in[k - 1]
        if k < 3:
            copy = remote(
                early_out.at[k], early_in.at[k], small_send.at[1], small_recv.at[1 + k],
                job_out.partners[(k + 1) % 3],
            )
            copy.start()
            smalls_early.append(copy)

    early_next(0)
    job_down[0].third()
    kernel_back = jnp.zeros((LANES, LANES), f32)
    grad_state = grad_inverse
    for step in reversed(range(NS_ITERS)):
        state, product, inner, outer, shifted = [newton[5 * step + i] for i in range(5)]
        grad_outer = 0.25 * fine(state, grad_state, TN)
        partial = (
            fine(grad_outer, inner, NT)
            - 15.0 * grad_outer
            - fine(7.0 * product - inner, grad_outer, TN)
        )
        rest_part = 7.0 * grad_outer - fine(grad_outer, product, NT)
        grad_state = (
            0.25 * fine(grad_state, outer, NT)
            + fine(kernel_two, partial, TN)
            + fine(shifted, rest_part, TN)
        )
        kernel_back = kernel_back + fine(partial + fine(product, rest_part, TN), state, NT)
        if step == NS_ITERS - 1:
            third_prob = p3[...]
            convolved = jnp.concatenate(
                [conv_block(reverse, gs[m * tok : (m + 2) * tok]) for m in range(n)], axis=0
            )
            grad_values = fine(third_prob, grad_third) + convolved
            value_in = give(
                2, jnp.where(iota(grad_values.shape, 0) < length, grad_values, 0.0)
            )
        if step == NS_ITERS - 2:
            grad_one = fine(grad, carried, NT)
            both = kernel_one * grad_one
            first_scores = scale * (both - kernel_one * fine(both, ones))
        if step == NS_ITERS - 3:
            key_one = jnp.where(same_head, fine(first_scores, queries, TN), 0.0)
            delta = fine(jnp.ones((8, LANES), bf16), grad_third * third_out, NT)[0:1]
            third_scores = scale * third_prob * (fine(values, grad_third, NT) - delta)
        if step == NS_ITERS - 4:
            query_three = jnp.where(same_head, fine(third_scores, keys, TN), 0.0)
            key_part = fine(third_scores, query_marks)
            query_part = fine(first_scores, key_marks)
    squares = block_sums(kernel_two * kernel_two, same_head)
    spread_sum = jnp.where(same_head, block_sums(grad_state * newton[0], same_head), 0.0)
    kernel_back = kernel_back + (grad_state.T - 2.0 * kernel_two * spread_sum) / squares
    grad_scores = scale * kernel_two * (
        kernel_back - jnp.sum(kernel_two * kernel_back, axis=1, keepdims=True)
    )
    query_two = fine(grad_scores, key_marks)
    key_two = fine(grad_scores, query_marks, TN)

    key_in = give(0, key_part + fine(members, (key_one + key_two) / counts))
    query_in = give(1, query_part + fine(members, (query_two + query_three) / counts))

    for i, held in enumerate((out_in, output)):
        shares[2 * i].wait_recv()
        block = held.at[rows_at(across[1])]
        copy = remote(block, block, share_send.at[i], share_recv.at[i, 2], core)
        copy.start()
        shares.append(copy)
    job_up[0].second()
    job_down[1].second()
    settle(half_all, own_recv.at[2])
    tokens_all = tokens_own[...].reshape(total, width)
    lanes_own, lanes_both = slice(0, HEAD_DIM), slice(HEAD_DIM, LANES)
    for ref, at in ((source_own, lanes_own), (source_both, lanes_both)):
        grads = jnp.concatenate([key_in[:, at], query_in[:, at], value_in[:, at]], axis=1)
        ref[...] = dot(tokens_all, grads, TN).astype(bf16)
    job_heads.first()
    shares[1].wait_recv()
    shares[4].wait_recv()
    settle(attn_pair.at[three], copy_recv.at[0])
    settle(attn_single, copy_recv.at[1])
    pair, single = attn_pair[...].reshape(rows, LANES), unpacked(attn_single[...])
    single = single.reshape(rows, HEAD_DIM)
    attention = jnp.concatenate(
        [
            jnp.where(even, pair, jnp.concatenate([single, pair[:, HEAD_DIM:]], axis=1)),
            jnp.where(even, single, pair[:, :HEAD_DIM]),
        ],
        axis=1,
    )
    source_out[...] = dot(out_in[...], attention, TN).astype(bf16)
    job_out.first()
    position = iota((tok, tok), 0) + iota((tok, tok), 1)
    upside = jnp.where(position == tok - 1, 1.0, 0.0).astype(bf16)
    lane = iota((tok, LANES), 1)
    conv_rows = []
    for h in range(2):
        inner = (lane < HEAD_DIM) if h == 0 else (lane >= HEAD_DIM)
        table = jnp.zeros((tok, 2 * tok), f32)
        for m in range(n):
            block = gs[half + m * tok : half + (m + 1) * tok]
            block = jnp.where(inner, block, jnp.zeros_like(block))
            table = table + dot(block, vs[m * tok : (m + 2) * tok], NT)
        table = pltpu.roll(fine(upside, table), 0, 1, stride=1, stride_axis=0)
        row = jnp.sum(table, axis=0, keepdims=True)
        row = pltpu.roll(jnp.broadcast_to(row, (8, 2 * tok)), tok + 1, 1)
        conv_rows.append(row[0:1, :LANES])
    late = late_out.at[0]
    late[...] = jnp.zeros(late.shape, f32)
    column = jnp.ones((8, total), bf16)
    for row, v in ((0, query_in), (1, value_in)):
        v = dot(column, v)[0:1]
        late[row : row + 1, 0:LANES] = jnp.where(even, v, 0.0)
        late[row : row + 1, LANES:local] = jnp.where(even, 0.0, v[:, :HEAD_DIM])
    late[2:3, 0:LANES] = jnp.where(even, conv_rows[0], 0.0)
    late[3:4, 0:LANES] = jnp.where(even, conv_rows[1], 0.0)
    late[4:5, 0:LANES] = jnp.where(even, 0.0, conv_rows[0])
    smalls_late = []

    def late_next(k):
        if k > 0:
            smalls_late[k - 1].wait_recv()
            late_out[k] = late_out[k - 1] + late_in[k - 1]
        if k < 3:
            copy = remote(
                late_out.at[k], late_in.at[k], small_send.at[2], small_recv.at[4 + k],
                job_out.partners[(k + 1) % 3],
            )
            copy.start()
            smalls_late.append(copy)

    late_next(0)
    early_next(1)
    job_down[1].third()
    job_down[0].fourth()
    job_up[1].second()
    settle(come_pair.at[:, three], back_recv.at[0])
    settle(come_single, back_recv.at[1])
    singles = []
    for i in range(3):
        tokens_low[:, i * LANES : (i + 1) * LANES] = come_pair[i].reshape(rows, LANES)
        singles.append(unpacked(come_single[i]).reshape(rows, HEAD_DIM))
    tokens_low[:, 3 * LANES :] = jnp.concatenate(singles, axis=1)

    def input_part(t):
        return dot(tokens_low[rows_at(t)], weight_in[...])

    def pass_sum(k, value, device):
        core_last[0, k] = value.astype(bf16)
        copy = remote(
            core_last.at[0, k], core_last.at[1, k], last_send.at[0], last_recv.at[k], device
        )
        copy.start()
        return copy

    middle = pass_sum(1, input_part(far[1]), core)
    near = pass_sum(0, input_part(core[1]), core)
    crossing = input_part(across[1])
    middle.wait_recv()
    y_last[0] = (crossing + core_last[1, 1].astype(f32)).astype(bf16)
    final = remote(y_last.at[0], y_last.at[1], last_send.at[0], last_recv.at[2], across)
    final.start()
    result = input_part(tensor) + jnp.concatenate(grads_first, axis=0)
    late_next(1)
    job_up[0].third()
    job_heads.second()
    early_next(2)
    job_up[1].third()
    job_up[0].fourth()
    near.wait_recv()
    final.wait_recv()
    result = result + core_last[1, 0].astype(f32) + y_last[1].astype(f32)
    tokens_whole[mine] = result.astype(bf16)
    ends = []
    for j, device in enumerate((across, core)):
        copy = remote(
            tokens_whole.at[mine], tokens_whole.at[mine], share_send.at[2], share_recv.at[2, j],
            device,
        )
        copy.start()
        ends.append(copy)
    job_out.second()
    late_next(2)

    def into(ref, k):
        def write(value):
            ref[:, k * span : (k + 1) * span] = value

        return write

    for k, job in enumerate(job_down):
        job.last(into(grad_down, k))
    done(7)
    job_heads.third()
    job_up[1].fourth()
    ends[0].wait_recv()
    block = tokens_whole.at[rows_at(across[1])]
    copy = remote(block, block, share_send.at[2], share_recv.at[2, 2], core)
    copy.start()
    ends.append(copy)
    job_out.third()
    ends[1].wait_recv()
    ends[2].wait_recv()
    grad_tokens[...] = tokens_whole[...].astype(f32)
    done(1)
    early_next(3)
    late_next(3)
    shares[3].wait_recv()
    shares[5].wait_recv()
    done(0, 8, 9)
    for k, job in enumerate(job_up):
        job.last(into(grad_up, k))
    done(6)

    def write_heads(result):
        for i, ref in enumerate((grad_key, grad_query, grad_value)):
            mine, both, come = [
                result[:, k * local + i * HEAD_DIM : k * local + (i + 1) * HEAD_DIM]
                for k in range(3)
            ]
            ref[:, :HEAD_DIM] = jnp.where(even, mine, come)
            ref[:, HEAD_DIM:LANES] = both
            ref[:, LANES:] = jnp.where(even, come, mine)

    job_heads.last(write_heads)
    done(2, 3, 4)

    def write_out(value):
        grad_out[...] = value.T

    job_out.last(write_out)
    done(5)
    three_rows = x.at[pl.ds(0, 3 * tok)]
    settle_home(pairs_in, three, out_send.at[0])
    settle_home(eight, seven, grad_send.at[0])
    for ref, sem in (
        (ks.at[seven], send.at[0]), (vs.at[seven], send.at[2]),
        (singles_in, out_send.at[1]), (attn_pair.at[three], copy_send.at[0]),
        (attn_single, copy_send.at[1]),
        (out_whole.at[pl.ds(0, 3 * local)], whole_send.at[0]),
        (out_whole, ag_send.at[0]), (out_whole, sum_send.at[0]),
        (come_pair.at[:, three], back_send.at[0]),
        (come_single, back_send.at[1]), (three_rows, share_send.at[0]),
        (three_rows, share_send.at[1]), (three_rows, share_send.at[2]),
        (early_tensor.at[three], small_send.at[0]), (early_in, small_send.at[1]),
        (late_in, small_send.at[2]), (tokens_own.at[pl.ds(0, n - 1), 0], own_send.at[0]),
        (half_all, own_send.at[1]), (three_rows, last_send.at[0]),
    ):
        settle(ref, sem)
    for job in jobs:
        job.finish()
    for copy in stores:
        copy.wait()


def finish_kernel(*refs):
    come, refs = refs[:RESULTS], refs[RESULTS:]
    go, refs = refs[:OUTPUTS], refs[OUTPUTS:]
    held, refs = refs[:RESULTS], refs[RESULTS:]
    (query_bias, value_bias, conv, out_bias, first_gain, first_shift, up_bias, down_bias,
     second_gain, second_shift, proxy, loads, stores) = refs
    early, late = held[MATRICES:]
    small = (query_bias, value_bias, conv, out_bias, first_gain, first_shift, up_bias, down_bias,
             second_gain, second_shift, proxy)
    places = (0, 1, 2, 4, 5, 8, 12, 14)
    other = [i for i in range(OUTPUTS) if i not in places]
    copies = [
        pltpu.make_async_copy(come[i], held[i], loads.at[i]) for i in range(RESULTS)
    ]
    for copy in copies:
        copy.start()
    outs = []

    def store(i, source):
        copy = pltpu.make_async_copy(source, go[i], stores.at[i])
        copy.start()
        outs.append(copy)

    copies[MATRICES].wait()
    copies[MATRICES + 1].wait()
    for ref, row in (
        (second_gain, 0), (second_shift, 1), (down_bias, 2), (first_gain, 3), (first_shift, 4),
        (out_bias, 5), (up_bias, 6),
    ):
        ref[...] = early[row]
    proxy[...] = early[7:8, 0:1]
    local = query_bias.shape[0]
    query_bias[...] = late[0, :local]
    value_bias[...] = late[1, :local]
    conv[...] = late[2:5, :CONV]
    for i, ref in zip(other, small):
        store(i, ref)
    for k, i in enumerate(places):
        copies[k].wait()
        store(i, held[k])
    for copy in outs:
        copy.wait()


def whole(shape, dtype):
    return jax.ShapeDtypeStruct(shape, dtype)


VMEM = pl.BlockSpec(memory_space=pltpu.VMEM)
SMEM = pl.BlockSpec(memory_space=pltpu.SMEM)
HBM = pl.BlockSpec(memory_space=pl.ANY)


def dma(*shape):
    return pltpu.SemaphoreType.DMA(shape)


def gathered_plan(
    n, tokens, lengths, query_weight, query_bias, key_weight, value_weight, value_bias,
    conv_kernel, out_weight, out_bias, first_gain, first_shift, up_weight, up_bias, down_weight,
    down_bias, second_gain, second_shift, out_grad,
):
    batch, tok, width = tokens.shape
    rows = batch * tok
    local = query_weight.shape[1]
    hidden = up_weight.shape[1]
    total = n * tok
    block = width // n
    piece = tok // 2

    def low(*shape):
        return pltpu.VMEM(shape, bf16)

    def wide(*shape):
        return pltpu.VMEM(shape, f32)

    results = (
        whole((rows, width), bf16),
        whole((rows, width), f32),
        whole((block, local), f32),
        whole((local,), f32),
        whole((block, local), f32),
        whole((block, local), f32),
        whole((local,), f32),
        whole(conv_kernel.shape, f32),
        whole((local, block), f32),
        whole((width,), f32),
        whole((width,), f32),
        whole((width,), f32),
        whole((block, hidden), f32),
        whole((hidden,), f32),
        whole((block, hidden), f32),
        whole((width,), f32),
        whole((width,), f32),
        whole((width,), f32),
        whole((1, 1), f32),
    )
    places = (0, 1, 2, 4, 5, 8, 12, 14)
    parts = [results[i] for i in places]
    sums = [whole((8, width), f32), whole((8, 2 * LANES), f32)]
    outs = pl.pallas_call(
        functools.partial(layer_kernel, n),
        out_shape=(*parts, *sums),
        in_specs=[SMEM, HBM, HBM, VMEM, HBM, HBM, VMEM, VMEM, HBM, VMEM, VMEM, VMEM, HBM, VMEM, HBM,
                  VMEM, VMEM, VMEM, HBM],
        out_specs=(HBM,) * RESULTS,
        scratch_shapes=[pltpu.VMEM(r.shape, r.dtype) for r in parts]
        + [
            low(rows, width), low(local, width), low(local, width), low(local, width),
            low(width, hidden), low(hidden, width), low(rows, width), low(local, width),
            low(width, width), low(hidden, width), low(width, hidden),
            low(3, 2, rows, LANES), low(total, LANES), low(total, LANES), low(total + tok, LANES),
            wide(total, LANES), wide(total, LANES), wide(5 * NS_ITERS, LANES, LANES),
            low(n, tok, LANES), low(n, piece, LANES), low(batch, tok, LANES),
            low(batch, piece, LANES),
            low(4, tok, LANES), low(4, piece, LANES), low(4, 2, tok, LANES),
            low(2, 4, piece, width), wide(2, 4, piece, hidden),
            low(2, 4, piece, hidden), low(2, 4, piece, width), low(2, 4, piece, hidden),
            low(2, 2, 2, piece, width), low(2, 2, 2, piece, width), low(2, 2, piece, width),
            low(2, 2, piece, width), low(2, 2, tok, width), low(2, tok, width),
            low(total + tok, LANES), low(3, n, tok, LANES), low(3, n, tok // 2, LANES),
            low(3, batch, tok, LANES), low(3, batch, tok // 2, LANES), low(3 * local, width),
            low(rows, width), wide(8, width), wide(4, 8, width), low(n, 2, tok // 2, width),
            low(rows, 3 * local), low(width, hidden), low(width, hidden), low(width, local),
            low(width, local), low(width, local), wide(4, 8, width), wide(3, 8, width),
            wide(4, 8, 2 * LANES), wide(3, 8, 2 * LANES), low(rows, width), wide(2, 2, 2, 2, piece, width),
        ]
        + [
            b
            for first, w in (
                *((hidden // 2, hidden // 2),) * 4, (local, local), (local, 3 * local)
            )
            for b in scatter_buffers(first, w, block)
        ]
        + [
            dma(8), dma(3), dma(3), dma(2), dma(2), dma(1), dma(1), dma(2), dma(2), dma(1),
            dma(2, 2, 3), dma(1), dma(2, 2, 3), dma(1), dma(1), dma(2), dma(2), dma(3), dma(3, 3),
            dma(3), dma(7), dma(JOBS, 2), dma(JOBS, 5), dma(2), dma(3), dma(1), dma(3),
            dma(RESULTS),
        ],
        compiler_params=pltpu.CompilerParams(
            collective_id=0, has_side_effects=True, vmem_limit_bytes=56 * 2**20
        ),
        name="layer",
    )(
        lengths, tokens.reshape(rows, width), query_weight.T, query_bias, key_weight.T,
        value_weight.T, value_bias, conv_kernel, out_weight, out_bias, first_gain, first_shift,
        up_weight, up_bias, down_weight, down_bias, second_gain, second_shift,
        out_grad.reshape(rows, width),
    )
    outs = pl.pallas_call(
        finish_kernel,
        out_shape=results,
        in_specs=[HBM] * RESULTS,
        out_specs=(HBM,) * OUTPUTS,
        scratch_shapes=[pltpu.VMEM(r.shape, r.dtype) for r in (*parts, *sums)]
        + [pltpu.VMEM(results[i].shape, f32) for i in range(OUTPUTS) if i not in places]
        + [dma(RESULTS), dma(OUTPUTS)],
        compiler_params=pltpu.CompilerParams(vmem_limit_bytes=60 * 2**20),
        name="finish",
    )(*outs)
    return (
        outs[0].reshape(tokens.shape),
        outs[1].reshape(tokens.shape),
        *outs[2:14],
        outs[14].T,
        *outs[15:18],
        outs[18].reshape(()),
    )


def per_device(seq, tensor, *args):
    batch, tok, width = args[0].shape
    heads = args[7].shape[0]
    if seq == 8 and tensor == 4 and batch == 4 and heads == 3 and tok == 128:
        return gathered_plan(seq, *args)
    return general_plan(*args)


def solution(mesh):
    return jax.shard_map(
        functools.partial(per_device, mesh.shape["seq"], mesh.shape["tensor"]),
        mesh=mesh,
        in_specs=(
            P(None, "seq", None),
            P(),
            P(None, "tensor"),
            P("tensor"),
            P(None, "tensor"),
            P(None, "tensor"),
            P("tensor"),
            P("tensor", None),
            P("tensor", None),
            P(),
            P(),
            P(),
            P(None, "tensor"),
            P("tensor"),
            P("tensor", None),
            P(),
            P(),
            P(),
            P(None, "seq", None),
        ),
        out_specs=(
            P(None, "seq", None),
            P(None, "seq", None),
            P("seq", "tensor"),
            P("tensor"),
            P("seq", "tensor"),
            P("seq", "tensor"),
            P("tensor"),
            P("tensor", None),
            P("tensor", "seq"),
            P(),
            P(),
            P(),
            P("seq", "tensor"),
            P("tensor"),
            P("tensor", "seq"),
            P(),
            P(),
            P(),
            P(),
        ),
        check_vma=False,
    )
```

```python
import functools

import jax
import jax.numpy as jnp
from jax import lax
from jax.experimental import pallas as pl
from jax.experimental.pallas import tpu as pltpu
from jax.sharding import PartitionSpec as P

HEADS = 12
HEAD_DIM = 64
LAND = 64
CONV = 33
NS_ITERS = 6


highest = lax.Precision.HIGHEST
epsilon = 1e-05
negative = -1e30


def joined(x, axis, combine):
    everything = jax.tree.map(lambda part: lax.all_gather(part, axis), x)
    first = jax.tree.map(lambda part: part[0], everything)

    def hop(k, so_far):
        return combine(so_far, jax.tree.map(lambda part: part[k], everything))

    return lax.fori_loop(1, lax.axis_size(axis), hop, first)


def with_halo(block, sides, width):
    for axis, dim in sides:
        count = lax.axis_size(axis)
        forward = [(i, i + 1) for i in range(count - 1)]
        backward = [(target, source) for source, target in forward]
        low = lax.ppermute(
            lax.slice_in_dim(block, block.shape[dim] - width, None, axis=dim), axis, forward
        )
        high = lax.ppermute(lax.slice_in_dim(block, 0, width, axis=dim), axis, backward)
        block = jnp.concatenate([low, block, high], axis=dim)
    return block


def newton_inverse(kernel):
    identity = jnp.eye(kernel.shape[-1], dtype=jnp.float32)
    inverse = jnp.swapaxes(kernel, -1, -2) / jnp.sum(kernel * kernel, axis=(-2, -1), keepdims=True)
    for _ in range(NS_ITERS):
        product = jnp.matmul(kernel, inverse, precision=highest)
        inner_term = jnp.matmul(product, 7.0 * identity - product, precision=highest)
        inner_term = jnp.matmul(product, 15.0 * identity - inner_term, precision=highest)
        inverse = 0.25 * jnp.matmul(inverse, 13.0 * identity - inner_term, precision=highest)
    return inverse


def landmark_core(query_marks, key_marks):
    scores = jnp.einsum(
        "bhjd,bhid->bhji", query_marks, key_marks, precision=highest
    ) * HEAD_DIM ** (-0.5)
    kernel_two = jax.nn.softmax(scores, axis=-1)
    return (kernel_two, newton_inverse(kernel_two))


def normalize(summed, gain_vec, shift_vec):
    middle = jnp.mean(summed, axis=-1, keepdims=True)
    centred = summed - middle
    inverse_std = lax.rsqrt(jnp.mean(centred * centred, axis=-1, keepdims=True) + epsilon)
    normal = centred * inverse_std
    return (normal * gain_vec + shift_vec, normal, inverse_std)


def add_norm(partial_sum, residual, bias_vec, gain_vec, shift_vec):
    summed = lax.psum(partial_sum.astype(jnp.bfloat16), "tensor").astype(jnp.float32)
    return normalize(residual + summed + bias_vec, gain_vec, shift_vec)


def norm_back(grad_hidden, normal, inverse_std, gain_vec):
    grad_normal = grad_hidden * gain_vec
    grad_summed = inverse_std * (
        grad_normal
        - jnp.mean(grad_normal, axis=-1, keepdims=True)
        - normal * jnp.mean(grad_normal * normal, axis=-1, keepdims=True)
    )
    return (grad_summed, jnp.sum(grad_hidden * normal, axis=0), jnp.sum(grad_hidden, axis=0))


def combine_soft(earlier, later):
    top_score = jnp.maximum(earlier[0], later[0])
    weight_first = jnp.exp(earlier[0] - top_score)
    weight_second = jnp.exp(later[0] - top_score)
    return (
        top_score,
        earlier[1] * weight_first + later[1] * weight_second,
        earlier[2] * weight_first[..., None] + later[2] * weight_second[..., None],
    )


def general_plan(
    tokens,
    lengths,
    query_weight,
    query_bias,
    key_weight,
    value_weight,
    value_bias,
    conv_kernel,
    out_weight,
    out_bias,
    first_gain,
    first_shift,
    up_weight,
    up_bias,
    down_weight,
    down_bias,
    second_gain,
    second_shift,
    out_grad,
):
    batch, tok_local, width = tokens.shape
    local_width = query_weight.shape[1]
    local_heads = conv_kernel.shape[0]
    head_dim = local_width // local_heads
    score_scale = HEAD_DIM ** (-0.5)
    rows = batch * tok_local
    half_width = CONV // 2
    f32 = jnp.float32
    bf16 = jnp.bfloat16
    position = lax.axis_index("seq") * tok_local + jnp.arange(tok_local, dtype=jnp.int32)
    inside = position[None, :] < lengths[:, None]
    living = inside.astype(f32)
    segment = position[None, :] * LAND // lengths[:, None]
    onehot = (
        (segment[:, :, None] == jnp.arange(LAND, dtype=jnp.int32)[None, None, :])
        & inside[:, :, None]
    ).astype(f32)
    marks_index = jnp.arange(LAND, dtype=jnp.int32)
    upper = ((marks_index[None, :] + 1) * lengths[:, None] + LAND - 1) // LAND
    lower = (marks_index[None, :] * lengths[:, None] + LAND - 1) // LAND
    counts = (upper - lower).astype(f32)
    flat = tokens.reshape(rows, width)
    flat_wide = flat.astype(f32)
    queries = (jnp.dot(flat, query_weight, preferred_element_type=f32) + query_bias).astype(bf16)
    key_vectors = jnp.dot(flat, key_weight, preferred_element_type=f32).astype(bf16)
    values = (
        (jnp.dot(flat, value_weight, preferred_element_type=f32) + value_bias)
        * living.reshape(rows, 1)
    ).astype(bf16)
    query_three = queries.reshape(batch, tok_local, local_width)
    key_three = key_vectors.reshape(batch, tok_local, local_width)
    value_three = values.reshape(batch, tok_local, local_width)
    onehot_low = onehot.astype(bf16)
    query_sum = jnp.einsum("btj,btf->bjf", onehot_low, query_three, preferred_element_type=f32)
    key_sum = jnp.einsum("btj,btf->bjf", onehot_low, key_three, preferred_element_type=f32)
    query_sum, key_sum = lax.psum((query_sum, key_sum), "seq")
    query_marks = (
        (query_sum / counts[:, :, None])
        .reshape(batch, LAND, local_heads, head_dim)
        .transpose(0, 2, 1, 3)
    )
    key_marks = (
        (key_sum / counts[:, :, None])
        .reshape(batch, LAND, local_heads, head_dim)
        .transpose(0, 2, 1, 3)
    )
    (kernel_two, inverse), core_back = jax.vjp(landmark_core, query_marks, key_marks)
    identity = jnp.eye(LAND, dtype=f32)
    deviation = identity - jnp.matmul(kernel_two, inverse, precision=highest)
    proxy_part = jnp.sum(jnp.sqrt(jnp.sum(deviation * deviation, axis=(-2, -1)))) / (batch * HEADS)
    query_heads = query_three.reshape(batch, tok_local, local_heads, head_dim).astype(f32)
    key_heads = key_three.reshape(batch, tok_local, local_heads, head_dim).astype(f32)
    value_heads = value_three.reshape(batch, tok_local, local_heads, head_dim).astype(f32)
    first_scores = (
        jnp.einsum("bthd,bhjd->bhtj", query_heads, key_marks, precision=highest) * score_scale
    )
    kernel_one = jax.nn.softmax(first_scores, axis=-1)
    third_scores = (
        jnp.einsum("bhjd,bthd->bhjt", query_marks, key_heads, precision=highest) * score_scale
    )
    key_alive = inside[:, None, None, :]
    third_scores = jnp.where(key_alive, third_scores, negative)
    local_top = jnp.max(third_scores, axis=-1)
    local_weights = jnp.where(key_alive, jnp.exp(third_scores - local_top[..., None]), 0.0)
    local_total = jnp.sum(local_weights, axis=-1)
    local_mix = jnp.einsum("bhjt,bthd->bhjd", local_weights, value_heads, precision=highest)
    top_score, total_weight, mixed = joined(
        (local_top, local_total, local_mix), "seq", combine_soft
    )
    third_out = mixed / total_weight[..., None]
    carried = jnp.matmul(inverse, third_out, precision=highest)
    nystrom = jnp.einsum("bhtj,bhjd->bthd", kernel_one, carried, precision=highest).reshape(
        batch, tok_local, local_width
    )
    padded_values = with_halo(value_three, (("seq", 1),), half_width)
    kernel_wide = jnp.repeat(conv_kernel, head_dim, axis=0)
    convolved = jnp.zeros((batch, tok_local, local_width), f32)
    for i in range(CONV):
        convolved = (
            convolved + padded_values[:, i : i + tok_local, :].astype(f32) * kernel_wide[:, i]
        )
    attention = (nystrom + convolved).astype(bf16).reshape(rows, local_width)
    out_part = jnp.dot(attention, out_weight, preferred_element_type=f32)
    hidden_one, normal_one, inverse_one = add_norm(
        out_part, flat_wide, out_bias, first_gain, first_shift
    )
    hidden_low = hidden_one.astype(bf16)
    up_value = jnp.dot(hidden_low, up_weight, preferred_element_type=f32) + up_bias
    activated, gelu_back = jax.vjp(lambda z: jax.nn.gelu(z, approximate=False), up_value)
    activated = activated.astype(bf16)
    down_part = jnp.dot(activated, down_weight, preferred_element_type=f32)
    hidden_two, normal_two, inverse_two = add_norm(
        down_part, hidden_one, down_bias, second_gain, second_shift
    )
    output = hidden_two.astype(bf16).reshape(batch, tok_local, width)
    grad_output = out_grad.reshape(rows, width).astype(f32)
    grad_second_total, grad_second_gain, grad_second_shift = norm_back(
        grad_output, normal_two, inverse_two, second_gain
    )
    down_in = grad_second_total.astype(bf16)
    grad_down_bias = jnp.sum(down_in.astype(f32), axis=0)
    grad_down_weight = jnp.einsum("rf,rd->fd", activated, down_in, preferred_element_type=f32)
    grad_activated = jnp.einsum("rd,fd->rf", down_in, down_weight, preferred_element_type=f32)
    up_in = gelu_back(grad_activated)[0].astype(bf16)
    grad_up_bias = jnp.sum(up_in.astype(f32), axis=0)
    grad_up_weight = jnp.einsum("rd,rf->df", hidden_low, up_in, preferred_element_type=f32)
    hidden_part = jnp.einsum("rf,df->rd", up_in, up_weight, preferred_element_type=f32)
    grad_hidden_one = (
        lax.psum(hidden_part.astype(jnp.bfloat16), "tensor").astype(jnp.float32) + grad_second_total
    )
    grad_first_total, grad_first_gain, grad_first_shift = norm_back(
        grad_hidden_one, normal_one, inverse_one, first_gain
    )
    out_in = grad_first_total.astype(bf16)
    grad_out_bias = jnp.sum(out_in.astype(f32), axis=0)
    grad_out_weight = jnp.einsum("rf,rd->fd", attention, out_in, preferred_element_type=f32)
    grad_attention = jnp.einsum(
        "rd,fd->rf", out_in, out_weight, preferred_element_type=f32
    ).reshape(batch, tok_local, local_width)
    padded_grad = with_halo(grad_attention.astype(jnp.bfloat16), (("seq", 1),), half_width).astype(
        grad_attention.dtype
    )
    grad_conv_values = jnp.zeros((batch, tok_local, local_width), f32)
    conv_columns = []
    for i in range(CONV):
        conv_columns.append(
            jnp.sum(
                grad_attention * padded_values[:, i : i + tok_local, :].astype(f32), axis=(0, 1)
            )
        )
        start_index = 2 * half_width - i
        grad_conv_values = (
            grad_conv_values
            + padded_grad[:, start_index : start_index + tok_local, :] * kernel_wide[:, i]
        )
    grad_conv_kernel = (
        jnp.stack(conv_columns, axis=0).reshape(CONV, local_heads, head_dim).sum(axis=-1).T
    )
    grad_nystrom = grad_attention.reshape(batch, tok_local, local_heads, head_dim)
    grad_kernel_one = jnp.einsum("bthd,bhjd->bhtj", grad_nystrom, carried, precision=highest)
    grad_carried_part = jnp.einsum("bhtj,bthd->bhjd", kernel_one, grad_nystrom, precision=highest)
    grad_first_scores = kernel_one * (
        grad_kernel_one - jnp.sum(kernel_one * grad_kernel_one, axis=-1, keepdims=True)
    )
    grad_query_one = (
        jnp.einsum("bhtj,bhjd->bthd", grad_first_scores, key_marks, precision=highest) * score_scale
    )
    grad_key_marks_part = (
        jnp.einsum("bhtj,bthd->bhjd", grad_first_scores, query_heads, precision=highest)
        * score_scale
    )
    grad_carried, grad_key_marks_one = lax.psum((grad_carried_part, grad_key_marks_part), "seq")
    grad_third_out = jnp.matmul(jnp.swapaxes(inverse, -1, -2), grad_carried, precision=highest)
    grad_inverse = jnp.matmul(grad_carried, jnp.swapaxes(third_out, -1, -2), precision=highest)
    grad_query_marks_two, grad_key_marks_two = core_back((jnp.zeros_like(kernel_two), grad_inverse))
    third_prob = local_weights * jnp.exp(local_top - top_score)[..., None] / total_weight[..., None]
    delta_term = jnp.sum(grad_third_out * third_out, axis=-1)
    grad_prob_value = jnp.einsum("bhjd,bthd->bhjt", grad_third_out, value_heads, precision=highest)
    grad_third_scores = third_prob * (grad_prob_value - delta_term[..., None])
    grad_value_three = jnp.einsum("bhjt,bhjd->bthd", third_prob, grad_third_out, precision=highest)
    grad_key_three = (
        jnp.einsum("bhjt,bhjd->bthd", grad_third_scores, query_marks, precision=highest)
        * score_scale
    )
    grad_query_marks_part = (
        jnp.einsum("bhjt,bthd->bhjd", grad_third_scores, key_heads, precision=highest) * score_scale
    )
    grad_query_marks_three = lax.psum(grad_query_marks_part, "seq")
    grad_query_marks = (grad_query_marks_two + grad_query_marks_three) / counts[:, None, :, None]
    grad_key_marks = (grad_key_marks_one + grad_key_marks_two) / counts[:, None, :, None]
    grad_query_marks = grad_query_marks.transpose(0, 2, 1, 3).reshape(batch, LAND, local_width)
    grad_key_marks = grad_key_marks.transpose(0, 2, 1, 3).reshape(batch, LAND, local_width)
    grad_query_seg = jnp.einsum("btj,bjf->btf", onehot, grad_query_marks, precision=highest)
    grad_key_seg = jnp.einsum("btj,bjf->btf", onehot, grad_key_marks, precision=highest)
    query_in = (
        (grad_query_one.reshape(batch, tok_local, local_width) + grad_query_seg)
        .astype(bf16)
        .reshape(rows, local_width)
    )
    key_in = (
        (grad_key_three.reshape(batch, tok_local, local_width) + grad_key_seg)
        .astype(bf16)
        .reshape(rows, local_width)
    )
    value_in = (grad_value_three.reshape(batch, tok_local, local_width) + grad_conv_values).astype(
        bf16
    )
    value_in = jnp.where(inside[:, :, None], value_in, jnp.zeros_like(value_in)).reshape(
        rows, local_width
    )
    grad_query_bias = jnp.sum(query_in.astype(f32), axis=0)
    grad_value_bias = jnp.sum(value_in.astype(f32), axis=0)
    grad_query_weight = jnp.einsum("rd,rf->df", flat, query_in, preferred_element_type=f32)
    grad_key_weight = jnp.einsum("rd,rf->df", flat, key_in, preferred_element_type=f32)
    grad_value_weight = jnp.einsum("rd,rf->df", flat, value_in, preferred_element_type=f32)
    input_part = (
        jnp.einsum("rf,df->rd", query_in, query_weight, preferred_element_type=f32)
        + jnp.einsum("rf,df->rd", key_in, key_weight, preferred_element_type=f32)
        + jnp.einsum("rf,df->rd", value_in, value_weight, preferred_element_type=f32)
    )
    input_sum, proxy_norm = (
        lax.psum(input_part.astype(jnp.bfloat16), "tensor").astype(jnp.float32),
        lax.psum(proxy_part.astype(jnp.bfloat16), "tensor").astype(jnp.float32),
    )
    grad_tokens = (grad_first_total + input_sum).reshape(batch, tok_local, width)
    (
        grad_query_weight,
        grad_key_weight,
        grad_value_weight,
        grad_out_weight,
        grad_up_weight,
        grad_down_weight,
    ) = (
        lax.psum_scatter(grad_query_weight, "seq", scatter_dimension=0, tiled=True),
        lax.psum_scatter(grad_key_weight, "seq", scatter_dimension=0, tiled=True),
        lax.psum_scatter(grad_value_weight, "seq", scatter_dimension=0, tiled=True),
        lax.psum_scatter(grad_out_weight, "seq", scatter_dimension=1, tiled=True),
        lax.psum_scatter(grad_up_weight, "seq", scatter_dimension=0, tiled=True),
        lax.psum_scatter(grad_down_weight, "seq", scatter_dimension=1, tiled=True),
    )
    (
        grad_query_bias,
        grad_value_bias,
        grad_conv_kernel,
        grad_out_bias,
        grad_first_gain,
        grad_first_shift,
        grad_up_bias,
        grad_down_bias,
        grad_second_gain,
        grad_second_shift,
    ) = lax.psum(
        (
            grad_query_bias,
            grad_value_bias,
            grad_conv_kernel,
            grad_out_bias,
            grad_first_gain,
            grad_first_shift,
            grad_up_bias,
            grad_down_bias,
            grad_second_gain,
            grad_second_shift,
        ),
        "seq",
    )
    return (
        output,
        grad_tokens,
        grad_query_weight,
        grad_query_bias,
        grad_key_weight,
        grad_value_weight,
        grad_value_bias,
        grad_conv_kernel,
        grad_out_weight,
        grad_out_bias,
        grad_first_gain,
        grad_first_shift,
        grad_up_weight,
        grad_up_bias,
        grad_down_weight,
        grad_down_bias,
        grad_second_gain,
        grad_second_shift,
        proxy_norm,
    )


MESH = pl.DeviceIdType.MESH
LANES = 2 * HEAD_DIM
f32 = jnp.float32
bf16 = jnp.bfloat16
NN = (1, 0)
NT = (1, 1)
TN = (0, 0)


def dot(a, b, dims=NN):
    return lax.dot_general(
        a, b, (((dims[0],), (dims[1],)), ((), ())), preferred_element_type=f32
    )


def split(x):
    if x.dtype == bf16:
        return (x,)
    top = x.astype(bf16)
    return (top, (x - top.astype(f32)).astype(bf16))


def fine(a, b, dims=NN):
    a, b = split(a), split(b)
    total = dot(a[0], b[0], dims)
    if len(b) > 1:
        total = total + dot(a[0], b[1], dims)
    if len(a) > 1:
        total = total + dot(a[1], b[0], dims)
    return total


def iota(shape, dim):
    return lax.broadcasted_iota(jnp.int32, shape, dim)


def block_mask():
    shape = (LANES, LANES)
    return (iota(shape, 0) < HEAD_DIM) == (iota(shape, 1) < HEAD_DIM)


def eye():
    return jnp.where(iota((LANES, LANES), 0) == iota((LANES, LANES), 1), 1.0, 0.0).astype(f32)


def block_sums(x, same_head):
    ones = jnp.where(same_head, 1.0, 0.0).astype(bf16)
    return jnp.where(same_head, fine(fine(ones, x), ones), 1.0)


def taps_matrix(row, tok):
    return pltpu.roll(jnp.broadcast_to(row, (tok, 2 * tok)), 0, 1, stride=1, stride_axis=0)


def taps_row(taps, head, tok):
    row = taps[pl.ds(head, 1), :]
    return jnp.concatenate([row, jnp.zeros((1, 2 * tok - CONV), f32)], axis=1)


def conv_block(matrices, window):
    first = fine(matrices[0], window)
    second = fine(matrices[1], window)
    return jnp.where(iota(first.shape, 1) < HEAD_DIM, first, second)


def greet(devices):
    barrier = pltpu.get_barrier_semaphore()
    for device in devices:
        pl.semaphore_signal(barrier, inc=1, device_id=device, device_id_type=MESH)
    return barrier


def around(n, me, tensor):
    return [(lax.rem(me + d, n), tensor) for d in range(1, n)]


def others(me, tensor):
    core = tensor + 1 - 2 * (tensor % 2)
    return [(me, core), (me, lax.rem(tensor + 2, 4)), (me, lax.rem(core + 2, 4))]


def paired(y):
    return y[:, :LANES], jnp.concatenate(
        [y[:, LANES : LANES + HEAD_DIM], y[:, HEAD_DIM:LANES]], axis=1
    )


def remote(src, dst, send, recv, device):
    return pltpu.make_async_remote_copy(
        src_ref=src, dst_ref=dst, send_sem=send, recv_sem=recv, device_id=device,
        device_id_type=MESH,
    )


def member_rows(length, total):
    j = iota((LANES, total), 0) % LAND
    t = iota((LANES, total), 1)
    inside = (t * LAND >= j * length) & (t * LAND < (j + 1) * length) & (t < length)
    return jnp.where(inside, 1.0, 0.0).astype(bf16)


def member_columns(length, total):
    j = iota((total, LANES), 1) % LAND
    t = iota((total, LANES), 0)
    inside = (t * LAND >= j * length) & (t * LAND < (j + 1) * length) & (t < length)
    return jnp.where(inside, 1.0, 0.0).astype(bf16)


def segment_counts(length):
    j = iota((LANES, LANES), 0) % LAND
    upper = ((j + 1) * length + LAND - 1) // LAND
    lower = (j * length + LAND - 1) // LAND
    return (upper - lower).astype(f32)


def normal_of(summed):
    middle = jnp.mean(summed, axis=-1, keepdims=True)
    centred = summed - middle
    inverse_std = lax.rsqrt(jnp.mean(centred * centred, axis=-1, keepdims=True) + epsilon)
    return centred * inverse_std, inverse_std


def before_norm(grad, normal, inverse_std, gain):
    grad_normal = grad * gain
    return inverse_std * (
        grad_normal
        - jnp.mean(grad_normal, axis=-1, keepdims=True)
        - normal * jnp.mean(grad_normal * normal, axis=-1, keepdims=True)
    )


def block_rows(t, tok):
    return pl.ds(pl.multiple_of(t * tok, tok), tok)


def settle(ref, sem):
    pltpu.make_async_copy(ref, ref, sem).wait()


class Scatter:
    def __init__(self, index, me, tensor, source, columns, buffers, send, recv, order):
        self.index, self.source, self.columns = index, source, pl.ds(*columns)
        self.first_in, self.held, self.second_in, self.pair, self.last_in, self.cross_in = buffers
        self.block = source.shape[0] // 8
        self.weights = [2**bit for bit in order]
        self.bits = [(me // weight) % 2 for weight in self.weights]
        self.partners = [
            (me + weight * (1 - 2 * bit), tensor) for weight, bit in zip(self.weights, self.bits)
        ]
        self.send, self.recv = send, recv

    def rows(self, slot, bit):
        index = (slot // 2) * self.weights[2] + (slot % 2) * self.weights[1] + bit * self.weights[0]
        return pl.ds(pl.multiple_of(index * self.block, 16), self.block)

    def copy(self, src, dst, k, stage):
        return remote(
            src, dst, self.send.at[self.index, min(k, 1)], self.recv.at[self.index, k],
            self.partners[stage],
        )

    def arrived(self, ref, k):
        settle(ref, self.recv.at[self.index, k])

    def first(self, slots=range(4)):
        for slot in slots:
            source = self.source.at[self.rows(slot, 1 - self.bits[0]), self.columns]
            self.copy(source, self.first_in.at[slot], 0, 0).start()

    def second(self):
        self.arrived(self.first_in, 0)
        for slot in range(4):
            mine = self.source[self.rows(slot, self.bits[0]), self.columns]
            self.held[slot] = self.joined(mine, self.first_in[slot])
        for k in range(2):
            self.copy(self.held.at[2 * k + 1 - self.bits[1]], self.second_in.at[k], 1, 1).start()

    def joined(self, mine, come):
        return (mine.astype(f32) + come.astype(f32)).astype(bf16)

    def third(self):
        self.arrived(self.second_in, 1)
        for k in range(2):
            both = self.held[2 * k + self.bits[1]].astype(f32) + self.second_in[k].astype(f32)
            self.pair[k] = both.astype(bf16)
        self.copy(self.pair.at[1 - self.bits[2]], self.last_in, 2, 2).start()

    def last(self, write):
        self.arrived(self.last_in, 2)
        write(self.pair[self.bits[2]].astype(f32) + self.last_in[...].astype(f32))

    def finish(self):
        settle(self.first_in, self.send.at[self.index, 0])
        settle(self.held.at[pl.ds(0, 3)], self.send.at[self.index, 1])


class Line(Scatter):
    def __init__(self, *args):
        super().__init__(*args)
        z = self.bits[1] + 2 * self.bits[2]
        right = z // 2
        self.end = self.bits[1] == right
        self.inner = self.bits[1] != right
        self.slots = [k * (1 - right) + (3 - k) * right for k in range(4)]
        self.partners[2] = (2 * (3 - z) + self.bits[0], self.partners[0][1])

    def second(self):
        self.arrived(self.first_in, 0)
        for slot in range(4):
            mine = self.source[self.rows(slot, self.bits[0]), self.columns]
            self.held[slot] = self.joined(mine, self.first_in[slot])
        come = (self.second_in.at[0], self.second_in.at[1], self.last_in)
        sends = [
            self.copy(self.held.at[self.slots[3 - k]], come[k], (1, 1, 2)[k], 1)
            for k in range(3)
        ]

        @pl.when(self.end)
        def _():
            for copy in sends:
                copy.start()

    def third(self):
        sends = [
            self.copy(self.pair.at[k], self.cross_in.at[k], 3, 2) for k in range(2)
        ]

        @pl.when(self.inner)
        def _():
            self.arrived(self.second_in, 1)
            for k in range(2):
                self.pair[k] = self.joined(self.held[self.slots[3 - k]], self.second_in[k])
                sends[k].start()

    def fourth(self):
        back = self.copy(self.first_in.at[2], self.first_in.at[3], 4, 1)

        @pl.when(self.inner)
        def _():
            self.arrived(self.cross_in, 3)
            self.first_in[2] = self.joined(self.held[self.slots[0]], self.cross_in[0])
            back.start()

    def last(self, write):
        @pl.when(self.inner)
        def _():
            self.arrived(self.last_in, 2)
            write(
                self.held[self.slots[1]].astype(f32)
                + self.last_in[...].astype(f32)
                + self.cross_in[1].astype(f32)
            )

        @pl.when(self.end)
        def _():
            self.arrived(self.first_in.at[3], 4)
            write(self.held[self.slots[0]].astype(f32) + self.first_in[3].astype(f32))


class Pairs(Scatter):
    def second(self):
        self.arrived(self.first_in, 0)
        width = self.first_in.shape[2]
        for slot in range(4):
            at = self.rows(slot, self.bits[0])
            self.held[slot, :, :width] = self.source[at]
            self.held[slot, :, width : 2 * width] = self.shared[at]
            self.held[slot, :, 2 * width :] = self.first_in[slot]
        for k in range(2):
            self.copy(self.held.at[2 * k + 1 - self.bits[1]], self.second_in.at[k], 1, 1).start()


def scatter_buffers(first, width, block):
    return [
        pltpu.VMEM((4, block, first), bf16),
        pltpu.VMEM((4, block, width), bf16),
        pltpu.VMEM((2, block, width), bf16),
        pltpu.VMEM((2, block, width), bf16),
        pltpu.VMEM((block, width), bf16),
        pltpu.VMEM((2, block, width), bf16),
    ]


def total_of(v):
    return jnp.sum(v, axis=0, keepdims=True)


def packed(block):
    middle = block.shape[-2] // 2
    first, second = block[..., :middle, :HEAD_DIM], block[..., middle:, :HEAD_DIM]
    return jnp.concatenate([first, second], axis=-1)


def unpacked(block):
    return jnp.concatenate([block[..., :HEAD_DIM], block[..., HEAD_DIM:]], axis=-2)


class Ring:
    def __init__(
        self, tensor, peers, parts, core_out, core_in, y_out, y_in, ag_send, ag_recv, sum_send,
        sum_recv,
    ):
        self.tensor, self.place = tensor, tensor % 2
        self.core, self.across, self.far = peers
        self.near_pair = tensor - self.place
        self.far_pair = lax.rem(self.near_pair + 2, 4)
        self.parts, self.core_out, self.core_in = parts, core_out, core_in
        self.y_out, self.y_in = y_out, y_in
        self.ag, self.sums = (ag_send, ag_recv), (sum_send, sum_recv)
        self.copies = {}

    def send(self, name, src, dst, sems, at, device):
        copy = remote(src, dst, sems[0].at[0], sems[1].at[at], device)
        copy.start()
        self.copies[name] = copy

    def share(self, phase, c, held):
        mine = held.at[c, self.tensor]
        self.send((phase, c, "y"), mine, mine, self.ag, (phase, c, 0), self.across)
        self.send((phase, c, "core"), mine, mine, self.ag, (phase, c, 1), self.core)

    def work(self, phase, c, side, value):
        self.parts[phase, c, side] = value.reshape(2, -1, value.shape[1])
        self.core_out[phase, c, side] = self.parts[phase, c, side, 1 - self.place].astype(bf16)
        self.send(
            (phase, c, side), self.core_out.at[phase, c, side], self.core_in.at[phase, c, side],
            self.sums, (phase, c, side), self.core,
        )

    def run(self, phase, held, work):
        for c in range(2):
            self.copies[phase, c, "core"].wait_recv()
            self.work(phase, c, 0, work(c, self.near_pair))
        for c in range(2):
            self.copies[phase, c, "y"].wait_recv()
            other = held.at[c, self.across[1]]
            self.send((phase, c, "pass"), other, other, self.ag, (phase, c, 2), self.core)
            if c == 1:
                self.cross(phase, 0)
            self.copies[phase, c, "pass"].wait_recv()
            self.work(phase, c, 1, work(c, self.far_pair))
        self.cross(phase, 1)

    def cross(self, phase, c):
        self.copies[phase, c, 1].wait_recv()
        both = self.parts[phase, c, 1, self.place] + self.core_in[phase, c, 1].astype(f32)
        self.y_out[phase, c] = both.astype(bf16)
        self.send(
            (phase, c, "sum"), self.y_out.at[phase, c], self.y_in.at[phase, c], self.sums,
            (phase, c, 2), self.across,
        )

    def total(self, phase, c):
        self.copies[phase, c, 0].wait_recv()
        self.copies[phase, c, "sum"].wait_recv()
        return (
            self.parts[phase, c, 0, self.place]
            + self.core_in[phase, c, 0].astype(f32)
            + self.y_in[phase, c].astype(f32)
        )


JOBS = 6
MATRICES = 8
RESULTS = MATRICES + 2
OUTPUTS = 19
ORDER = (4, 3, 5, 2, 6, 1, 7)


def layer_kernel(
    n, lengths, x_far, wq_far, qb, wk_far, wv_far, vb, taps, out_far, out_bias, gain_one,
    shift_one, up_far, up_bias, down_far, down_bias, gain_two, shift_two, grad_far,
    *rest,
):
    results, rest = rest[:RESULTS], rest[RESULTS:]
    ready, rest = rest[:MATRICES], rest[MATRICES:]
    layer_body(
        n, lengths, x_far, wq_far, qb, wk_far, wv_far, vb, taps, out_far, out_bias, gain_one,
        shift_one, up_far, up_bias, down_far, down_bias, gain_two, shift_two, grad_far, results,
        ready, *rest,
    )


def layer_body(
    n, lengths, x_far, wq_far, qb, wk_far, wv_far, vb, taps, out_far, out_bias, gain_one,
    shift_one, up_far, up_bias, down_far, down_bias, gain_two, shift_two, grad_far, results, ready,
    x, wk, wq, wv, up_weight, down_weight, out_grad, out_weight, out_whole,
    up_turned, down_turned, stage, ks, qs, vs, k1, p3, newton, out_stage, out_single, attn_pair, attn_single,
    pairs_in, singles_in, heads_out, hidden, slope, active, down_in, up_in,
    core_out, core_in, y_out, y_in, core_last, y_last,
    gs, back_stage, back_single, come_pair, come_single, weight_in, out_in, early, early_tensor, tokens_own, tokens_low, source_up,
    source_down, source_out, source_own, source_both, early_out, early_in, late_out, late_in, tokens_whole,
    parts_held,
    *rest,
):
    buffers, sems = rest[: 6 * JOBS], rest[6 * JOBS :]
    (load, send, recv, out_send, out_recv, whole_send, whole_recv, copy_send, copy_recv, ag_send,
     ag_recv, sum_send, sum_recv, grad_send, grad_recv, back_send, back_recv, share_send,
     share_recv, small_send, small_recv, job_send, job_recv, own_send, own_recv, last_send, last_recv,
     store) = sems
    output, grad_tokens, grad_query, grad_key, grad_value, grad_out, grad_up, grad_down = ready
    ready = (*ready, early_out.at[3], late_out.at[3])
    stores = []

    def done(*numbers):
        for i in numbers:
            copy = pltpu.make_async_copy(ready[i], results[i], store.at[i])
            copy.start()
            stores.append(copy)

    me = lax.axis_index("seq")
    tensor = lax.axis_index("tensor")
    rows, width = x.shape
    batch = n // 2
    tok = rows // batch
    total = n * tok
    half = CONV // 2
    own, side = me // 2, me % 2
    scale = HEAD_DIM ** (-0.5)
    ring_peers = around(n, me, tensor)
    peers = others(me, tensor)
    core, across, far = peers

    def batch_of(t):
        return lax.rem(t - me + 8, 4)

    def rows_at(t):
        return block_rows(batch_of(t), tok)

    mine = rows_at(tensor)
    at_home = batch_of(tensor) == own
    away = batch_of(tensor) != own
    local = wk.shape[0]
    barrier = greet(ring_peers + peers)
    loads = []
    for i, (source, target) in enumerate((
        (x_far, x), (wk_far, wk), (wq_far, wq), (wv_far, wv),
        (out_far, out_weight), (up_far, up_weight),
        (down_far, down_weight), (grad_far, out_grad),
    )):
        copy = pltpu.make_async_copy(source, target, load.at[i])
        copy.start()
        loads.append(copy)
    hidden_width = up_weight.shape[1]
    span = hidden_width // 2
    jobs = [
        kind(i, me, tensor, source, columns, buffers[6 * i : 6 * i + 6], job_send, job_recv, order)
        for i, (kind, source, columns, order) in enumerate((
            (Line, source_down, (0, span), (0, 1, 2)),
            (Scatter, source_down, (span, span), (1, 0, 2)),
            (Line, source_up, (0, span), (0, 1, 2)),
            (Line, source_up, (span, span), (0, 1, 2)),
            (Scatter, source_out, (0, local), (0, 1, 2)),
            (Pairs, source_own, (0, local), (0, 1, 2)),
        ))
    ]
    job_down, job_up = jobs[0:2], jobs[2:4]
    job_out, job_heads = jobs[4:]
    job_heads.shared = source_both

    owned = (ks, qs, vs)
    offsets = (0, 0, half)
    for padded in (vs, gs):
        padded[0:half] = jnp.zeros((half, LANES), bf16)
        padded[half + total : total + tok] = jnp.zeros((tok - half, LANES), bf16)
    even = side == 0

    seven = pl.ds(0, (n - 1) * tok)

    def spread(i):
        here = pl.ds(pl.multiple_of(offsets[i] + me * tok, 16), tok)
        for d in ORDER:
            peer = lax.rem(me + d, n)
            copy = remote(
                stage.at[i, peer % 2, block_rows(peer // 2, tok)], owned[i].at[here],
                send.at[i], recv.at[i], (peer, tensor),
            )
            copy.start()
        owned[i][here] = stage[i, side, block_rows(own, tok)]

    loads[0].wait()
    loads[1].wait()
    y = dot(x[...], wk[...], NT)
    stage[0, 0], stage[0, 1] = paired(y.astype(bf16))
    pl.semaphore_wait(barrier, n + 2)
    spread(0)
    loads[2].wait()
    y = dot(x[...], wq[...], NT) + qb[...].reshape(1, local)
    stage[1, 0], stage[1, 1] = paired(y.astype(bf16))
    spread(1)
    loads[3].wait()
    y = dot(x[...], wv[...], NT) + vb[...].reshape(1, local)
    position = me * tok + iota((tok, local), 0)
    y = jnp.concatenate(
        [
            jnp.where(position < lengths[b], y[b * tok : (b + 1) * tok], 0.0)
            for b in range(batch)
        ],
        axis=0,
    )
    stage[2, 0], stage[2, 1] = paired(y.astype(bf16))
    loads[4].wait()
    pair_rows = block_rows(tensor, LANES)
    single_rows = pl.ds(pl.multiple_of(4 * LANES + tensor * HEAD_DIM, HEAD_DIM), HEAD_DIM)
    first, single = out_weight[:LANES], out_weight[LANES:]
    out_whole[pair_rows] = jnp.where(
        even, first, jnp.concatenate([single, first[HEAD_DIM:]], axis=0)
    )
    out_whole[single_rows] = jnp.where(even, single, first[:HEAD_DIM])
    for i, device in enumerate(peers):
        for at in (pair_rows, single_rows):
            part = out_whole.at[at]
            remote(part, part, whole_send.at[0], whole_recv.at[0], device).start()

    length = lengths[own]
    same_head = block_mask()
    identity = eye()
    ones = jnp.where(same_head, 1.0, 0.0).astype(bf16)
    members = member_rows(length, total)
    counts = segment_counts(length)
    matrices = [taps_matrix(taps_row(taps, h, tok), tok) for h in (2 * side, 1)]
    flip = jnp.where(
        iota((2 * tok, 2 * tok), 0) + iota((2 * tok, 2 * tok), 1) == CONV - 1, 1.0, 0.0
    ).astype(bf16)
    reverse = [
        taps_matrix(
            fine(jnp.broadcast_to(taps_row(taps, h, tok), (8, 2 * tok)), flip)[0:1], tok
        )
        for h in (2 * side, 1)
    ]
    for i, w in enumerate((wk, wq, wv)):
        pair, single = w[:LANES], w[LANES:]
        weight_in[i * LANES : (i + 1) * LANES] = jnp.where(
            even, pair, jnp.concatenate([single, pair[HEAD_DIM:]], axis=0)
        )
        start = 3 * LANES + i * HEAD_DIM
        weight_in[start : start + HEAD_DIM] = jnp.where(even, single, pair[:HEAD_DIM])
    for copy in loads[5:]:
        copy.wait()
    up_turned[...] = up_weight[...].T
    down_turned[...] = down_weight[...].T
    settle(ks.at[seven], recv.at[0])
    keys = ks[...]
    key_marks = jnp.where(same_head, dot(members, keys) / counts, 0.0)
    settle(qs.at[seven], send.at[1])
    spread(2)
    settle(qs.at[seven], recv.at[1])
    queries = qs[...]
    query_marks = jnp.where(same_head, dot(members, queries) / counts, 0.0)
    scores = jnp.where(same_head, fine(query_marks, key_marks, NT) * scale, negative)
    weights = jnp.exp(scores - jnp.max(scores, axis=1, keepdims=True))
    kernel_two = weights / jnp.sum(weights, axis=1, keepdims=True)
    inverse = jnp.where(
        same_head, kernel_two.T / block_sums(kernel_two * kernel_two, same_head), 0.0
    )
    def scores_one():
        values = fine(queries, key_marks, NT) * scale
        left = iota(values.shape, 1) < HEAD_DIM
        top_left = jnp.max(jnp.where(left, values, negative), axis=1, keepdims=True)
        top_right = jnp.max(jnp.where(left, negative, values), axis=1, keepdims=True)
        return jnp.exp(values - jnp.where(left, top_left, top_right))

    def scores_three():
        values = fine(keys, query_marks, NT) * scale
        alive = iota(values.shape, 0) < length
        values = jnp.where(alive, values, negative)
        weights = jnp.exp(values - jnp.max(values, axis=0, keepdims=True))
        return jnp.where(alive, weights, 0.0)

    product = fine(kernel_two, inverse)
    for step in range(NS_ITERS):
        if step == 0:
            weights_one = scores_one()
        if step == 1:
            k1[...] = weights_one / fine(weights_one, ones)
        if step == 2:
            weights_three = scores_three()
        if step == 3:
            third_prob = weights_three / jnp.sum(weights_three, axis=0, keepdims=True)
            p3[...] = third_prob
        inner = fine(product, 7.0 * identity - product)
        outer = 13.0 * identity - fine(product, 15.0 * identity - inner)
        newton[5 * step] = inverse
        newton[5 * step + 1] = product
        newton[5 * step + 2] = inner
        newton[5 * step + 3] = outer
        newton[5 * step + 4] = fine(product, kernel_two)
        inverse = 0.25 * fine(inverse, outer)
        product = 0.25 * fine(product, outer)

    deviation = identity - product
    norms = jnp.sqrt(block_sums(deviation * deviation, same_head))
    first, second = norms[0:1, 0:1], norms[LANES - 1 :, LANES - 1 :]
    norm_sum = jnp.where(side == 0, first + second, first) / (batch * HEADS)
    early[7:8] = jnp.broadcast_to(norm_sum, (1, width))

    settle(vs.at[seven], recv.at[2])
    values = vs[half : half + total]
    third_out = jnp.where(same_head, fine(third_prob, values, TN), 0.0)
    carried = fine(inverse, third_out)

    for d in (*ORDER, n):
        peer = lax.rem(me + d, n)
        start = pl.multiple_of(peer * tok, tok)
        nystrom = fine(k1[pl.ds(start, tok)], carried)
        convolved = conv_block(matrices, vs[pl.ds(start, 2 * tok)])
        low = (nystrom + convolved).astype(bf16)
        device = (peer, lax.rem(own + peer, 4))
        if d % 2 == 0:
            source, target = out_stage.at[d - 1], pairs_in.at[tensor]
            source[...] = low
        else:
            source, target = out_single.at[d - 1], singles_in.at[tensor]
            source[...] = packed(low)
        copy = remote(source, target, out_send.at[d % 2], out_recv.at[d % 2], device)
        if d < n:
            copy.start()
            continue
        attn_pair[own] = low
        pl.when(away)(copy.start)

        @pl.when(at_home)
        def _():
            pairs_in[tensor] = low

    three = pl.ds(0, 3)

    def settle_home(ref, some, sem):
        pl.when(away)(lambda: settle(ref, sem))
        pl.when(at_home)(lambda: settle(ref.at[some], sem))

    settle_home(pairs_in, three, out_recv.at[0])
    settle(singles_in, out_recv.at[1])
    settle(out_whole.at[pl.ds(0, 3 * local)], whole_recv.at[0])
    z, side_of_chip = me // 2, tensor % 2
    beside = (me + 1 - 2 * side, tensor)
    def give_tokens(src, dst, i, device):
        remote(src, dst, own_send.at[i // 2], own_recv.at[i], device).start()

    def half_block(b):
        start = pl.multiple_of(b * tok + side_of_chip * (tok // 2), tok // 2)
        return pl.ds(start, tok // 2)

    tokens_own[me, side_of_chip] = x[half_block(own)]
    for k in range(1, 4):
        peer = lax.rem(z + k, 4)
        give_tokens(
            x.at[half_block(peer)], tokens_own.at[me, side_of_chip], 0, (2 * peer + side, tensor)
        )
    half_own = tokens_own.at[me, side_of_chip]
    give_tokens(half_own, half_own, 1, beside)

    def pass_tokens():
        settle(tokens_own.at[pl.ds(0, 3), 0], own_recv.at[0])
        for k in range(1, 4):
            come = tokens_own.at[2 * lax.rem(z + 4 - k, 4) + side, side_of_chip]
            give_tokens(come, come, 1, beside)

    def line(vector):
        return vector[...].reshape(1, vector.shape[0])

    piece = tok // 2
    chunks = range(2)
    ring = Ring(
        tensor, peers, parts_held, core_out, core_in, y_out, y_in, ag_send, ag_recv, sum_send,
        sum_recv,
    )

    def rows_of(c):
        return pl.ds(pl.multiple_of(batch_of(tensor) * tok + c * piece, piece), piece)

    def normed(c):
        at = slice(c * piece, (c + 1) * piece)
        lanes = slice(c * HEAD_DIM, (c + 1) * HEAD_DIM)
        heads = jnp.concatenate(
            [pairs_in[t, at] for t in range(4)] + [singles_in[t, :, lanes] for t in range(4)],
            axis=1,
        )
        branch = dot(heads, out_whole[...])
        first_total = x[rows_of(c)].astype(f32) + (branch + line(out_bias))
        normal, inverse_std = normal_of(first_total)
        whole_row = normal * line(gain_one) + line(shift_one)
        hidden[c, tensor] = whole_row.astype(bf16)
        ring.share(0, c, hidden)
        return normal, inverse_std, whole_row

    def up(c, t):
        at = pl.ds(t, 2)
        value = dot(hidden[c, at].reshape(tok, width), up_weight[...]) + line(up_bias)
        half_erf = 0.5 * (1.0 + lax.erf(value * (0.5**0.5)))
        density = jnp.exp(-0.5 * value * value) * (0.5 / jnp.pi) ** 0.5
        slope[c, at] = (half_erf + value * density).reshape(2, piece, hidden_width)
        low = (value * half_erf).astype(bf16)
        active[c, at] = low.reshape(2, piece, hidden_width)
        return dot(low, down_weight[...])

    def down(c, t):
        at = pl.ds(t, 2)
        grad = dot(down_in[c, at].reshape(tok, width), down_turned[...])
        low = (grad * slope[c, at].reshape(tok, hidden_width)).astype(bf16)
        up_in[c, at] = low.reshape(2, piece, hidden_width)
        return dot(low, up_turned[...])

    after_norm_one = [normed(c) for c in chunks]
    ring.run(0, hidden, up)
    pass_tokens()
    for d in range(1, n):
        if d % 2 == 0:
            source, target = out_stage.at[d - 1], attn_pair.at[own]
        else:
            source, target = out_single.at[d - 1], attn_single.at[own]
        remote(
            source, target, copy_send.at[d % 2], copy_recv.at[d % 2],
            (lax.rem(me + d, n), tensor),
        ).start()

    grads_second, sums_second = [], []
    for c in chunks:
        hidden_one = after_norm_one[c][2]
        second_total = hidden_one + (ring.total(0, c) + line(down_bias))
        normal, inverse_std = normal_of(second_total)
        output[rows_of(c)] = (normal * line(gain_two) + line(shift_two)).astype(bf16)
        grad_output = out_grad[rows_of(c)].astype(f32)
        grad_second = before_norm(grad_output, normal, inverse_std, line(gain_two))
        low = grad_second.astype(bf16)
        down_in[c, tensor] = low
        ring.share(1, c, down_in)
        grads_second.append(grad_second)
        sums_second.append(
            (total_of(grad_output * normal), total_of(grad_output), total_of(low.astype(f32)))
        )
    ring.run(1, down_in, down)
    everything = (rows, width)
    every_hidden = (rows, hidden_width)
    source_down[...] = dot(
        down_in[...].reshape(everything), active[...].reshape(every_hidden), TN
    ).astype(bf16)
    for job in job_down:
        job.first()

    grads_first, sums_first = [], []
    for c in chunks:
        normal, inverse_std, _ = after_norm_one[c]
        grad_hidden = grads_second[c] + ring.total(1, c)
        grad_first = before_norm(grad_hidden, normal, inverse_std, line(gain_one))
        low = grad_first.astype(bf16)
        out_in[rows_of(c)] = low
        heads = dot(low, out_whole[...], NT).astype(bf16)
        at = slice(c * piece, (c + 1) * piece)
        for t in range(4):
            start = 4 * LANES + t * HEAD_DIM
            pair = heads[:, t * LANES : (t + 1) * LANES]
            heads_out[t, 0, at] = pair
            heads_out[t, 1, at] = jnp.concatenate(
                [heads[:, start : start + HEAD_DIM], pair[:, HEAD_DIM:]], axis=1
            )
        b = batch_of(tensor)
        there = pl.ds(pl.multiple_of(half + me * tok + c * piece, 16), piece)
        for t in range(4):
            for k, device in enumerate(((2 * b + side, t), (2 * b + 1 - side, t))):
                copy = remote(
                    heads_out.at[t, k, pl.ds(c * piece, piece)], gs.at[there], grad_send.at[0],
                    grad_recv.at[0], device,
                )
                if k == 1:
                    copy.start()
                else:
                    pl.when((batch_of(tensor) != own) | (tensor != t))(copy.start)
        grads_first.append(grad_first)
        sums_first.append(
            (total_of(grad_hidden * normal), total_of(grad_hidden), total_of(low.astype(f32)))
        )

    @pl.when(at_home)
    def _():
        here = pl.ds(pl.multiple_of(half + me * tok, 16), tok)
        gs[here] = heads_out[tensor, 0]

    source_up[...] = dot(
        hidden[...].reshape(everything), up_in[...].reshape(every_hidden), TN
    ).astype(bf16)
    for i in range(3):
        early[i : i + 1] = sums_second[0][i] + sums_second[1][i]
        early[i + 3 : i + 4] = sums_first[0][i] + sums_first[1][i]
    early[6:7] = dot(jnp.ones((8, rows), bf16), up_in[...].reshape(every_hidden))[0:1]
    early_tensor[tensor] = early[...]
    job_up[0].first(range(2))
    for i, device in enumerate(peers):
        remote(
            early, early_tensor.at[tensor], small_send.at[0], small_recv.at[0], device
        ).start()
    shares = []
    for i, held in enumerate((out_in, output)):
        for j, device in enumerate((across, core)):
            copy = remote(
                held.at[mine], held.at[mine], share_send.at[i], share_recv.at[i, j], device
            )
            copy.start()
            shares.append(copy)
    job_down[0].second()
    job_up[0].first(range(2, 4))
    job_up[1].first()
    settle(tokens_own.at[pl.ds(0, 4), 0], own_recv.at[1])
    half_all = tokens_own.at[:, side_of_chip]
    give_tokens(half_all, half_all, 2, core)

    members = member_columns(length, total)
    def give(i, block):
        low = block.astype(bf16)
        back_stage[i] = low.reshape(n, tok, LANES)
        back_single[i] = packed(low.reshape(n, tok, LANES))
        for d in ORDER:
            peer = lax.rem(me + d, n)
            source, target = (back_stage, come_pair) if d % 2 == 0 else (back_single, come_single)
            remote(
                source.at[i, peer], target.at[i, own], back_send.at[d % 2],
                back_recv.at[d % 2], (peer, tensor),
            ).start()
        come_pair[i, own] = back_stage[i, me]
        return low

    eight = gs.at[pl.ds(0, total)]
    settle_home(eight, seven, grad_recv.at[0])
    grad = gs[half : half + total]
    kernel_one = k1[...]
    grad_carried = jnp.where(same_head, fine(kernel_one, grad, TN), 0.0)
    grad_third = fine(inverse, grad_carried, TN)
    grad_inverse = fine(grad_carried, third_out, NT)
    settle(early_tensor.at[three], small_recv.at[0])
    by_tensor = early_tensor[0] + early_tensor[1] + early_tensor[2] + early_tensor[3]
    early_out[0] = jnp.where(iota(by_tensor.shape, 0) == 6, early[...], by_tensor)
    smalls_early = []

    def early_next(k):
        if k > 0:
            smalls_early[k - 1].wait_recv()
            early_out[k] = early_out[k - 1] + early_in[k - 1]
        if k < 3:
            copy = remote(
                early_out.at[k], early_in.at[k], small_send.at[1], small_recv.at[1 + k],
                job_out.partners[(k + 1) % 3],
            )
            copy.start()
            smalls_early.append(copy)

    early_next(0)
    job_down[0].third()
    kernel_back = jnp.zeros((LANES, LANES), f32)
    grad_state = grad_inverse
    for step in reversed(range(NS_ITERS)):
        state, product, inner, outer, shifted = [newton[5 * step + i] for i in range(5)]
        grad_outer = 0.25 * fine(state, grad_state, TN)
        partial = (
            fine(grad_outer, inner, NT)
            - 15.0 * grad_outer
            - fine(7.0 * product - inner, grad_outer, TN)
        )
        rest_part = 7.0 * grad_outer - fine(grad_outer, product, NT)
        grad_state = (
            0.25 * fine(grad_state, outer, NT)
            + fine(kernel_two, partial, TN)
            + fine(shifted, rest_part, TN)
        )
        kernel_back = kernel_back + fine(partial + fine(product, rest_part, TN), state, NT)
        if step == NS_ITERS - 1:
            third_prob = p3[...]
            convolved = jnp.concatenate(
                [conv_block(reverse, gs[m * tok : (m + 2) * tok]) for m in range(n)], axis=0
            )
            grad_values = fine(third_prob, grad_third) + convolved
            value_in = give(
                2, jnp.where(iota(grad_values.shape, 0) < length, grad_values, 0.0)
            )
        if step == NS_ITERS - 2:
            grad_one = fine(grad, carried, NT)
            both = kernel_one * grad_one
            first_scores = scale * (both - kernel_one * fine(both, ones))
        if step == NS_ITERS - 3:
            key_one = jnp.where(same_head, fine(first_scores, queries, TN), 0.0)
            delta = fine(jnp.ones((8, LANES), bf16), grad_third * third_out, NT)[0:1]
            third_scores = scale * third_prob * (fine(values, grad_third, NT) - delta)
        if step == NS_ITERS - 4:
            query_three = jnp.where(same_head, fine(third_scores, keys, TN), 0.0)
            key_part = fine(third_scores, query_marks)
            query_part = fine(first_scores, key_marks)
    squares = block_sums(kernel_two * kernel_two, same_head)
    spread_sum = jnp.where(same_head, block_sums(grad_state * newton[0], same_head), 0.0)
    kernel_back = kernel_back + (grad_state.T - 2.0 * kernel_two * spread_sum) / squares
    grad_scores = scale * kernel_two * (
        kernel_back - jnp.sum(kernel_two * kernel_back, axis=1, keepdims=True)
    )
    query_two = fine(grad_scores, key_marks)
    key_two = fine(grad_scores, query_marks, TN)

    key_in = give(0, key_part + fine(members, (key_one + key_two) / counts))
    query_in = give(1, query_part + fine(members, (query_two + query_three) / counts))

    for i, held in enumerate((out_in, output)):
        shares[2 * i].wait_recv()
        block = held.at[rows_at(across[1])]
        copy = remote(block, block, share_send.at[i], share_recv.at[i, 2], core)
        copy.start()
        shares.append(copy)
    job_up[0].second()
    job_down[1].second()
    settle(half_all, own_recv.at[2])
    tokens_all = tokens_own[...].reshape(total, width)
    lanes_own, lanes_both = slice(0, HEAD_DIM), slice(HEAD_DIM, LANES)
    for ref, at in ((source_own, lanes_own), (source_both, lanes_both)):
        grads = jnp.concatenate([key_in[:, at], query_in[:, at], value_in[:, at]], axis=1)
        ref[...] = dot(tokens_all, grads, TN).astype(bf16)
    job_heads.first()
    shares[1].wait_recv()
    shares[4].wait_recv()
    settle(attn_pair.at[three], copy_recv.at[0])
    settle(attn_single, copy_recv.at[1])
    pair, single = attn_pair[...].reshape(rows, LANES), unpacked(attn_single[...])
    single = single.reshape(rows, HEAD_DIM)
    attention = jnp.concatenate(
        [
            jnp.where(even, pair, jnp.concatenate([single, pair[:, HEAD_DIM:]], axis=1)),
            jnp.where(even, single, pair[:, :HEAD_DIM]),
        ],
        axis=1,
    )
    source_out[...] = dot(out_in[...], attention, TN).astype(bf16)
    job_out.first()
    position = iota((tok, tok), 0) + iota((tok, tok), 1)
    upside = jnp.where(position == tok - 1, 1.0, 0.0).astype(bf16)
    lane = iota((tok, LANES), 1)
    conv_rows = []
    for h in range(2):
        inner = (lane < HEAD_DIM) if h == 0 else (lane >= HEAD_DIM)
        table = jnp.zeros((tok, 2 * tok), f32)
        for m in range(n):
            block = gs[half + m * tok : half + (m + 1) * tok]
            block = jnp.where(inner, block, jnp.zeros_like(block))
            table = table + dot(block, vs[m * tok : (m + 2) * tok], NT)
        table = pltpu.roll(fine(upside, table), 0, 1, stride=1, stride_axis=0)
        row = jnp.sum(table, axis=0, keepdims=True)
        row = pltpu.roll(jnp.broadcast_to(row, (8, 2 * tok)), tok + 1, 1)
        conv_rows.append(row[0:1, :LANES])
    late = late_out.at[0]
    late[...] = jnp.zeros(late.shape, f32)
    column = jnp.ones((8, total), bf16)
    for row, v in ((0, query_in), (1, value_in)):
        v = dot(column, v)[0:1]
        late[row : row + 1, 0:LANES] = jnp.where(even, v, 0.0)
        late[row : row + 1, LANES:local] = jnp.where(even, 0.0, v[:, :HEAD_DIM])
    late[2:3, 0:LANES] = jnp.where(even, conv_rows[0], 0.0)
    late[3:4, 0:LANES] = jnp.where(even, conv_rows[1], 0.0)
    late[4:5, 0:LANES] = jnp.where(even, 0.0, conv_rows[0])
    smalls_late = []

    def late_next(k):
        if k > 0:
            smalls_late[k - 1].wait_recv()
            late_out[k] = late_out[k - 1] + late_in[k - 1]
        if k < 3:
            copy = remote(
                late_out.at[k], late_in.at[k], small_send.at[2], small_recv.at[4 + k],
                job_out.partners[(k + 1) % 3],
            )
            copy.start()
            smalls_late.append(copy)

    late_next(0)
    early_next(1)
    job_down[1].third()
    job_down[0].fourth()
    job_up[1].second()
    settle(come_pair.at[:, three], back_recv.at[0])
    settle(come_single, back_recv.at[1])
    singles = []
    for i in range(3):
        tokens_low[:, i * LANES : (i + 1) * LANES] = come_pair[i].reshape(rows, LANES)
        singles.append(unpacked(come_single[i]).reshape(rows, HEAD_DIM))
    tokens_low[:, 3 * LANES :] = jnp.concatenate(singles, axis=1)

    def input_part(t):
        return dot(tokens_low[rows_at(t)], weight_in[...])

    def pass_sum(k, value, device):
        core_last[0, k] = value.astype(bf16)
        copy = remote(
            core_last.at[0, k], core_last.at[1, k], last_send.at[0], last_recv.at[k], device
        )
        copy.start()
        return copy

    middle = pass_sum(1, input_part(far[1]), core)
    near = pass_sum(0, input_part(core[1]), core)
    crossing = input_part(across[1])
    middle.wait_recv()
    y_last[0] = (crossing + core_last[1, 1].astype(f32)).astype(bf16)
    final = remote(y_last.at[0], y_last.at[1], last_send.at[0], last_recv.at[2], across)
    final.start()
    result = input_part(tensor) + jnp.concatenate(grads_first, axis=0)
    late_next(1)
    job_up[0].third()
    job_heads.second()
    early_next(2)
    job_up[1].third()
    job_up[0].fourth()
    near.wait_recv()
    final.wait_recv()
    result = result + core_last[1, 0].astype(f32) + y_last[1].astype(f32)
    tokens_whole[mine] = result.astype(bf16)
    ends = []
    for j, device in enumerate((across, core)):
        copy = remote(
            tokens_whole.at[mine], tokens_whole.at[mine], share_send.at[2], share_recv.at[2, j],
            device,
        )
        copy.start()
        ends.append(copy)
    job_out.second()
    late_next(2)

    def into(ref, k):
        def write(value):
            ref[:, k * span : (k + 1) * span] = value

        return write

    for k, job in enumerate(job_down):
        job.last(into(grad_down, k))
    done(7)
    job_heads.third()
    job_up[1].fourth()
    ends[0].wait_recv()
    block = tokens_whole.at[rows_at(across[1])]
    copy = remote(block, block, share_send.at[2], share_recv.at[2, 2], core)
    copy.start()
    ends.append(copy)
    job_out.third()
    ends[1].wait_recv()
    ends[2].wait_recv()
    grad_tokens[...] = tokens_whole[...].astype(f32)
    done(1)
    early_next(3)
    late_next(3)
    shares[3].wait_recv()
    shares[5].wait_recv()
    done(0, 8, 9)
    for k, job in enumerate(job_up):
        job.last(into(grad_up, k))
    done(6)

    def write_heads(result):
        for i, ref in enumerate((grad_key, grad_query, grad_value)):
            mine, both, come = [
                result[:, k * local + i * HEAD_DIM : k * local + (i + 1) * HEAD_DIM]
                for k in range(3)
            ]
            ref[:, :HEAD_DIM] = jnp.where(even, mine, come)
            ref[:, HEAD_DIM:LANES] = both
            ref[:, LANES:] = jnp.where(even, come, mine)

    job_heads.last(write_heads)
    done(2, 3, 4)

    def write_out(value):
        grad_out[...] = value.T

    job_out.last(write_out)
    done(5)
    three_rows = x.at[pl.ds(0, 3 * tok)]
    settle_home(pairs_in, three, out_send.at[0])
    settle_home(eight, seven, grad_send.at[0])
    for ref, sem in (
        (ks.at[seven], send.at[0]), (vs.at[seven], send.at[2]),
        (singles_in, out_send.at[1]), (attn_pair.at[three], copy_send.at[0]),
        (attn_single, copy_send.at[1]),
        (out_whole.at[pl.ds(0, 3 * local)], whole_send.at[0]),
        (out_whole, ag_send.at[0]), (out_whole, sum_send.at[0]),
        (come_pair.at[:, three], back_send.at[0]),
        (come_single, back_send.at[1]), (three_rows, share_send.at[0]),
        (three_rows, share_send.at[1]), (three_rows, share_send.at[2]),
        (early_tensor.at[three], small_send.at[0]), (early_in, small_send.at[1]),
        (late_in, small_send.at[2]), (tokens_own.at[pl.ds(0, n - 1), 0], own_send.at[0]),
        (half_all, own_send.at[1]), (three_rows, last_send.at[0]),
    ):
        settle(ref, sem)
    for job in jobs:
        job.finish()
    for copy in stores:
        copy.wait()


def finish_kernel(*refs):
    come, refs = refs[:RESULTS], refs[RESULTS:]
    go, refs = refs[:OUTPUTS], refs[OUTPUTS:]
    held, refs = refs[:RESULTS], refs[RESULTS:]
    (query_bias, value_bias, conv, out_bias, first_gain, first_shift, up_bias, down_bias,
     second_gain, second_shift, proxy, loads, stores) = refs
    early, late = held[MATRICES:]
    small = (query_bias, value_bias, conv, out_bias, first_gain, first_shift, up_bias, down_bias,
             second_gain, second_shift, proxy)
    places = (0, 1, 2, 4, 5, 8, 12, 14)
    other = [i for i in range(OUTPUTS) if i not in places]
    copies = [
        pltpu.make_async_copy(come[i], held[i], loads.at[i]) for i in range(RESULTS)
    ]
    for copy in copies:
        copy.start()
    outs = []

    def store(i, source):
        copy = pltpu.make_async_copy(source, go[i], stores.at[i])
        copy.start()
        outs.append(copy)

    copies[MATRICES].wait()
    copies[MATRICES + 1].wait()
    for ref, row in (
        (second_gain, 0), (second_shift, 1), (down_bias, 2), (first_gain, 3), (first_shift, 4),
        (out_bias, 5), (up_bias, 6),
    ):
        ref[...] = early[row]
    proxy[...] = early[7:8, 0:1]
    local = query_bias.shape[0]
    query_bias[...] = late[0, :local]
    value_bias[...] = late[1, :local]
    conv[...] = late[2:5, :CONV]
    for i, ref in zip(other, small):
        store(i, ref)
    for k, i in enumerate(places):
        copies[k].wait()
        store(i, held[k])
    for copy in outs:
        copy.wait()


def whole(shape, dtype):
    return jax.ShapeDtypeStruct(shape, dtype)


VMEM = pl.BlockSpec(memory_space=pltpu.VMEM)
SMEM = pl.BlockSpec(memory_space=pltpu.SMEM)
HBM = pl.BlockSpec(memory_space=pl.ANY)


def dma(*shape):
    return pltpu.SemaphoreType.DMA(shape)


def gathered_plan(
    n, tokens, lengths, query_weight, query_bias, key_weight, value_weight, value_bias,
    conv_kernel, out_weight, out_bias, first_gain, first_shift, up_weight, up_bias, down_weight,
    down_bias, second_gain, second_shift, out_grad,
):
    batch, tok, width = tokens.shape
    rows = batch * tok
    local = query_weight.shape[1]
    hidden = up_weight.shape[1]
    total = n * tok
    block = width // n
    piece = tok // 2

    def low(*shape):
        return pltpu.VMEM(shape, bf16)

    def wide(*shape):
        return pltpu.VMEM(shape, f32)

    results = (
        whole((rows, width), bf16),
        whole((rows, width), f32),
        whole((block, local), f32),
        whole((local,), f32),
        whole((block, local), f32),
        whole((block, local), f32),
        whole((local,), f32),
        whole(conv_kernel.shape, f32),
        whole((local, block), f32),
        whole((width,), f32),
        whole((width,), f32),
        whole((width,), f32),
        whole((block, hidden), f32),
        whole((hidden,), f32),
        whole((block, hidden), f32),
        whole((width,), f32),
        whole((width,), f32),
        whole((width,), f32),
        whole((1, 1), f32),
    )
    places = (0, 1, 2, 4, 5, 8, 12, 14)
    parts = [results[i] for i in places]
    sums = [whole((8, width), f32), whole((8, 2 * LANES), f32)]
    outs = pl.pallas_call(
        functools.partial(layer_kernel, n),
        out_shape=(*parts, *sums),
        in_specs=[SMEM, HBM, HBM, VMEM, HBM, HBM, VMEM, VMEM, HBM, VMEM, VMEM, VMEM, HBM, VMEM, HBM,
                  VMEM, VMEM, VMEM, HBM],
        out_specs=(HBM,) * RESULTS,
        scratch_shapes=[pltpu.VMEM(r.shape, r.dtype) for r in parts]
        + [
            low(rows, width), low(local, width), low(local, width), low(local, width),
            low(width, hidden), low(hidden, width), low(rows, width), low(local, width),
            low(width, width), low(hidden, width), low(width, hidden),
            low(3, 2, rows, LANES), low(total, LANES), low(total, LANES), low(total + tok, LANES),
            wide(total, LANES), wide(total, LANES), wide(5 * NS_ITERS, LANES, LANES),
            low(n, tok, LANES), low(n, piece, LANES), low(batch, tok, LANES),
            low(batch, piece, LANES),
            low(4, tok, LANES), low(4, piece, LANES), low(4, 2, tok, LANES),
            low(2, 4, piece, width), wide(2, 4, piece, hidden),
            low(2, 4, piece, hidden), low(2, 4, piece, width), low(2, 4, piece, hidden),
            low(2, 2, 2, piece, width), low(2, 2, 2, piece, width), low(2, 2, piece, width),
            low(2, 2, piece, width), low(2, 2, tok, width), low(2, tok, width),
            low(total + tok, LANES), low(3, n, tok, LANES), low(3, n, tok // 2, LANES),
            low(3, batch, tok, LANES), low(3, batch, tok // 2, LANES), low(3 * local, width),
            low(rows, width), wide(8, width), wide(4, 8, width), low(n, 2, tok // 2, width),
            low(rows, 3 * local), low(width, hidden), low(width, hidden), low(width, local),
            low(width, local), low(width, local), wide(4, 8, width), wide(3, 8, width),
            wide(4, 8, 2 * LANES), wide(3, 8, 2 * LANES), low(rows, width), wide(2, 2, 2, 2, piece, width),
        ]
        + [
            b
            for first, w in (
                *((hidden // 2, hidden // 2),) * 4, (local, local), (local, 3 * local)
            )
            for b in scatter_buffers(first, w, block)
        ]
        + [
            dma(8), dma(3), dma(3), dma(2), dma(2), dma(1), dma(1), dma(2), dma(2), dma(1),
            dma(2, 2, 3), dma(1), dma(2, 2, 3), dma(1), dma(1), dma(2), dma(2), dma(3), dma(3, 3),
            dma(3), dma(7), dma(JOBS, 2), dma(JOBS, 5), dma(2), dma(3), dma(1), dma(3),
            dma(RESULTS),
        ],
        compiler_params=pltpu.CompilerParams(
            collective_id=0, has_side_effects=True, vmem_limit_bytes=56 * 2**20
        ),
        name="layer",
    )(
        lengths, tokens.reshape(rows, width), query_weight.T, query_bias, key_weight.T,
        value_weight.T, value_bias, conv_kernel, out_weight, out_bias, first_gain, first_shift,
        up_weight, up_bias, down_weight, down_bias, second_gain, second_shift,
        out_grad.reshape(rows, width),
    )
    outs = pl.pallas_call(
        finish_kernel,
        out_shape=results,
        in_specs=[HBM] * RESULTS,
        out_specs=(HBM,) * OUTPUTS,
        scratch_shapes=[pltpu.VMEM(r.shape, r.dtype) for r in (*parts, *sums)]
        + [pltpu.VMEM(results[i].shape, f32) for i in range(OUTPUTS) if i not in places]
        + [dma(RESULTS), dma(OUTPUTS)],
        compiler_params=pltpu.CompilerParams(vmem_limit_bytes=60 * 2**20),
        name="finish",
    )(*outs)
    return (
        outs[0].reshape(tokens.shape),
        outs[1].reshape(tokens.shape),
        *outs[2:14],
        outs[14].T,
        *outs[15:18],
        outs[18].reshape(()),
    )


def per_device(seq, tensor, *args):
    batch, tok, width = args[0].shape
    heads = args[7].shape[0]
    if seq == 8 and tensor == 4 and batch == 4 and heads == 3 and tok == 128:
        return gathered_plan(seq, *args)
    return general_plan(*args)


def solution(mesh):
    return jax.shard_map(
        functools.partial(per_device, mesh.shape["seq"], mesh.shape["tensor"]),
        mesh=mesh,
        in_specs=(
            P(None, "seq", None),
            P(),
            P(None, "tensor"),
            P("tensor"),
            P(None, "tensor"),
            P(None, "tensor"),
            P("tensor"),
            P("tensor", None),
            P("tensor", None),
            P(),
            P(),
            P(),
            P(None, "tensor"),
            P("tensor"),
            P("tensor", None),
            P(),
            P(),
            P(),
            P(None, "seq", None),
        ),
        out_specs=(
            P(None, "seq", None),
            P(None, "seq", None),
            P("seq", "tensor"),
            P("tensor"),
            P("seq", "tensor"),
            P("seq", "tensor"),
            P("tensor"),
            P("tensor", None),
            P("tensor", "seq"),
            P(),
            P(),
            P(),
            P("seq", "tensor"),
            P("tensor"),
            P("tensor", "seq"),
            P(),
            P(),
            P(),
            P(),
        ),
        check_vma=False,
    )
```

```python
import functools

import jax
import jax.numpy as jnp
from jax import lax
from jax.experimental import pallas as pl
from jax.experimental.pallas import tpu as pltpu
from jax.sharding import PartitionSpec as P

HEADS = 12
HEAD_DIM = 64
LAND = 64
CONV = 33
NS_ITERS = 6


highest = lax.Precision.HIGHEST
epsilon = 1e-05
negative = -1e30


def joined(x, axis, combine):
    everything = jax.tree.map(lambda part: lax.all_gather(part, axis), x)
    first = jax.tree.map(lambda part: part[0], everything)

    def hop(k, so_far):
        return combine(so_far, jax.tree.map(lambda part: part[k], everything))

    return lax.fori_loop(1, lax.axis_size(axis), hop, first)


def with_halo(block, sides, width):
    for axis, dim in sides:
        count = lax.axis_size(axis)
        forward = [(i, i + 1) for i in range(count - 1)]
        backward = [(target, source) for source, target in forward]
        low = lax.ppermute(
            lax.slice_in_dim(block, block.shape[dim] - width, None, axis=dim), axis, forward
        )
        high = lax.ppermute(lax.slice_in_dim(block, 0, width, axis=dim), axis, backward)
        block = jnp.concatenate([low, block, high], axis=dim)
    return block


def newton_inverse(kernel):
    identity = jnp.eye(kernel.shape[-1], dtype=jnp.float32)
    inverse = jnp.swapaxes(kernel, -1, -2) / jnp.sum(kernel * kernel, axis=(-2, -1), keepdims=True)
    for _ in range(NS_ITERS):
        product = jnp.matmul(kernel, inverse, precision=highest)
        inner_term = jnp.matmul(product, 7.0 * identity - product, precision=highest)
        inner_term = jnp.matmul(product, 15.0 * identity - inner_term, precision=highest)
        inverse = 0.25 * jnp.matmul(inverse, 13.0 * identity - inner_term, precision=highest)
    return inverse


def landmark_core(query_marks, key_marks):
    scores = jnp.einsum(
        "bhjd,bhid->bhji", query_marks, key_marks, precision=highest
    ) * HEAD_DIM ** (-0.5)
    kernel_two = jax.nn.softmax(scores, axis=-1)
    return (kernel_two, newton_inverse(kernel_two))


def normalize(summed, gain_vec, shift_vec):
    middle = jnp.mean(summed, axis=-1, keepdims=True)
    centred = summed - middle
    inverse_std = lax.rsqrt(jnp.mean(centred * centred, axis=-1, keepdims=True) + epsilon)
    normal = centred * inverse_std
    return (normal * gain_vec + shift_vec, normal, inverse_std)


def add_norm(partial_sum, residual, bias_vec, gain_vec, shift_vec):
    summed = lax.psum(partial_sum.astype(jnp.bfloat16), "tensor").astype(jnp.float32)
    return normalize(residual + summed + bias_vec, gain_vec, shift_vec)


def norm_back(grad_hidden, normal, inverse_std, gain_vec):
    grad_normal = grad_hidden * gain_vec
    grad_summed = inverse_std * (
        grad_normal
        - jnp.mean(grad_normal, axis=-1, keepdims=True)
        - normal * jnp.mean(grad_normal * normal, axis=-1, keepdims=True)
    )
    return (grad_summed, jnp.sum(grad_hidden * normal, axis=0), jnp.sum(grad_hidden, axis=0))


def combine_soft(earlier, later):
    top_score = jnp.maximum(earlier[0], later[0])
    weight_first = jnp.exp(earlier[0] - top_score)
    weight_second = jnp.exp(later[0] - top_score)
    return (
        top_score,
        earlier[1] * weight_first + later[1] * weight_second,
        earlier[2] * weight_first[..., None] + later[2] * weight_second[..., None],
    )


def general_plan(
    tokens,
    lengths,
    query_weight,
    query_bias,
    key_weight,
    value_weight,
    value_bias,
    conv_kernel,
    out_weight,
    out_bias,
    first_gain,
    first_shift,
    up_weight,
    up_bias,
    down_weight,
    down_bias,
    second_gain,
    second_shift,
    out_grad,
):
    batch, tok_local, width = tokens.shape
    local_width = query_weight.shape[1]
    local_heads = conv_kernel.shape[0]
    head_dim = local_width // local_heads
    score_scale = HEAD_DIM ** (-0.5)
    rows = batch * tok_local
    half_width = CONV // 2
    f32 = jnp.float32
    bf16 = jnp.bfloat16
    position = lax.axis_index("seq") * tok_local + jnp.arange(tok_local, dtype=jnp.int32)
    inside = position[None, :] < lengths[:, None]
    living = inside.astype(f32)
    segment = position[None, :] * LAND // lengths[:, None]
    onehot = (
        (segment[:, :, None] == jnp.arange(LAND, dtype=jnp.int32)[None, None, :])
        & inside[:, :, None]
    ).astype(f32)
    marks_index = jnp.arange(LAND, dtype=jnp.int32)
    upper = ((marks_index[None, :] + 1) * lengths[:, None] + LAND - 1) // LAND
    lower = (marks_index[None, :] * lengths[:, None] + LAND - 1) // LAND
    counts = (upper - lower).astype(f32)
    flat = tokens.reshape(rows, width)
    flat_wide = flat.astype(f32)
    queries = (jnp.dot(flat, query_weight, preferred_element_type=f32) + query_bias).astype(bf16)
    key_vectors = jnp.dot(flat, key_weight, preferred_element_type=f32).astype(bf16)
    values = (
        (jnp.dot(flat, value_weight, preferred_element_type=f32) + value_bias)
        * living.reshape(rows, 1)
    ).astype(bf16)
    query_three = queries.reshape(batch, tok_local, local_width)
    key_three = key_vectors.reshape(batch, tok_local, local_width)
    value_three = values.reshape(batch, tok_local, local_width)
    onehot_low = onehot.astype(bf16)
    query_sum = jnp.einsum("btj,btf->bjf", onehot_low, query_three, preferred_element_type=f32)
    key_sum = jnp.einsum("btj,btf->bjf", onehot_low, key_three, preferred_element_type=f32)
    query_sum, key_sum = lax.psum((query_sum, key_sum), "seq")
    query_marks = (
        (query_sum / counts[:, :, None])
        .reshape(batch, LAND, local_heads, head_dim)
        .transpose(0, 2, 1, 3)
    )
    key_marks = (
        (key_sum / counts[:, :, None])
        .reshape(batch, LAND, local_heads, head_dim)
        .transpose(0, 2, 1, 3)
    )
    (kernel_two, inverse), core_back = jax.vjp(landmark_core, query_marks, key_marks)
    identity = jnp.eye(LAND, dtype=f32)
    deviation = identity - jnp.matmul(kernel_two, inverse, precision=highest)
    proxy_part = jnp.sum(jnp.sqrt(jnp.sum(deviation * deviation, axis=(-2, -1)))) / (batch * HEADS)
    query_heads = query_three.reshape(batch, tok_local, local_heads, head_dim).astype(f32)
    key_heads = key_three.reshape(batch, tok_local, local_heads, head_dim).astype(f32)
    value_heads = value_three.reshape(batch, tok_local, local_heads, head_dim).astype(f32)
    first_scores = (
        jnp.einsum("bthd,bhjd->bhtj", query_heads, key_marks, precision=highest) * score_scale
    )
    kernel_one = jax.nn.softmax(first_scores, axis=-1)
    third_scores = (
        jnp.einsum("bhjd,bthd->bhjt", query_marks, key_heads, precision=highest) * score_scale
    )
    key_alive = inside[:, None, None, :]
    third_scores = jnp.where(key_alive, third_scores, negative)
    local_top = jnp.max(third_scores, axis=-1)
    local_weights = jnp.where(key_alive, jnp.exp(third_scores - local_top[..., None]), 0.0)
    local_total = jnp.sum(local_weights, axis=-1)
    local_mix = jnp.einsum("bhjt,bthd->bhjd", local_weights, value_heads, precision=highest)
    top_score, total_weight, mixed = joined(
        (local_top, local_total, local_mix), "seq", combine_soft
    )
    third_out = mixed / total_weight[..., None]
    carried = jnp.matmul(inverse, third_out, precision=highest)
    nystrom = jnp.einsum("bhtj,bhjd->bthd", kernel_one, carried, precision=highest).reshape(
        batch, tok_local, local_width
    )
    padded_values = with_halo(value_three, (("seq", 1),), half_width)
    kernel_wide = jnp.repeat(conv_kernel, head_dim, axis=0)
    convolved = jnp.zeros((batch, tok_local, local_width), f32)
    for i in range(CONV):
        convolved = (
            convolved + padded_values[:, i : i + tok_local, :].astype(f32) * kernel_wide[:, i]
        )
    attention = (nystrom + convolved).astype(bf16).reshape(rows, local_width)
    out_part = jnp.dot(attention, out_weight, preferred_element_type=f32)
    hidden_one, normal_one, inverse_one = add_norm(
        out_part, flat_wide, out_bias, first_gain, first_shift
    )
    hidden_low = hidden_one.astype(bf16)
    up_value = jnp.dot(hidden_low, up_weight, preferred_element_type=f32) + up_bias
    activated, gelu_back = jax.vjp(lambda z: jax.nn.gelu(z, approximate=False), up_value)
    activated = activated.astype(bf16)
    down_part = jnp.dot(activated, down_weight, preferred_element_type=f32)
    hidden_two, normal_two, inverse_two = add_norm(
        down_part, hidden_one, down_bias, second_gain, second_shift
    )
    output = hidden_two.astype(bf16).reshape(batch, tok_local, width)
    grad_output = out_grad.reshape(rows, width).astype(f32)
    grad_second_total, grad_second_gain, grad_second_shift = norm_back(
        grad_output, normal_two, inverse_two, second_gain
    )
    down_in = grad_second_total.astype(bf16)
    grad_down_bias = jnp.sum(down_in.astype(f32), axis=0)
    grad_down_weight = jnp.einsum("rf,rd->fd", activated, down_in, preferred_element_type=f32)
    grad_activated = jnp.einsum("rd,fd->rf", down_in, down_weight, preferred_element_type=f32)
    up_in = gelu_back(grad_activated)[0].astype(bf16)
    grad_up_bias = jnp.sum(up_in.astype(f32), axis=0)
    grad_up_weight = jnp.einsum("rd,rf->df", hidden_low, up_in, preferred_element_type=f32)
    hidden_part = jnp.einsum("rf,df->rd", up_in, up_weight, preferred_element_type=f32)
    grad_hidden_one = (
        lax.psum(hidden_part.astype(jnp.bfloat16), "tensor").astype(jnp.float32) + grad_second_total
    )
    grad_first_total, grad_first_gain, grad_first_shift = norm_back(
        grad_hidden_one, normal_one, inverse_one, first_gain
    )
    out_in = grad_first_total.astype(bf16)
    grad_out_bias = jnp.sum(out_in.astype(f32), axis=0)
    grad_out_weight = jnp.einsum("rf,rd->fd", attention, out_in, preferred_element_type=f32)
    grad_attention = jnp.einsum(
        "rd,fd->rf", out_in, out_weight, preferred_element_type=f32
    ).reshape(batch, tok_local, local_width)
    padded_grad = with_halo(grad_attention.astype(jnp.bfloat16), (("seq", 1),), half_width).astype(
        grad_attention.dtype
    )
    grad_conv_values = jnp.zeros((batch, tok_local, local_width), f32)
    conv_columns = []
    for i in range(CONV):
        conv_columns.append(
            jnp.sum(
                grad_attention * padded_values[:, i : i + tok_local, :].astype(f32), axis=(0, 1)
            )
        )
        start_index = 2 * half_width - i
        grad_conv_values = (
            grad_conv_values
            + padded_grad[:, start_index : start_index + tok_local, :] * kernel_wide[:, i]
        )
    grad_conv_kernel = (
        jnp.stack(conv_columns, axis=0).reshape(CONV, local_heads, head_dim).sum(axis=-1).T
    )
    grad_nystrom = grad_attention.reshape(batch, tok_local, local_heads, head_dim)
    grad_kernel_one = jnp.einsum("bthd,bhjd->bhtj", grad_nystrom, carried, precision=highest)
    grad_carried_part = jnp.einsum("bhtj,bthd->bhjd", kernel_one, grad_nystrom, precision=highest)
    grad_first_scores = kernel_one * (
        grad_kernel_one - jnp.sum(kernel_one * grad_kernel_one, axis=-1, keepdims=True)
    )
    grad_query_one = (
        jnp.einsum("bhtj,bhjd->bthd", grad_first_scores, key_marks, precision=highest) * score_scale
    )
    grad_key_marks_part = (
        jnp.einsum("bhtj,bthd->bhjd", grad_first_scores, query_heads, precision=highest)
        * score_scale
    )
    grad_carried, grad_key_marks_one = lax.psum((grad_carried_part, grad_key_marks_part), "seq")
    grad_third_out = jnp.matmul(jnp.swapaxes(inverse, -1, -2), grad_carried, precision=highest)
    grad_inverse = jnp.matmul(grad_carried, jnp.swapaxes(third_out, -1, -2), precision=highest)
    grad_query_marks_two, grad_key_marks_two = core_back((jnp.zeros_like(kernel_two), grad_inverse))
    third_prob = local_weights * jnp.exp(local_top - top_score)[..., None] / total_weight[..., None]
    delta_term = jnp.sum(grad_third_out * third_out, axis=-1)
    grad_prob_value = jnp.einsum("bhjd,bthd->bhjt", grad_third_out, value_heads, precision=highest)
    grad_third_scores = third_prob * (grad_prob_value - delta_term[..., None])
    grad_value_three = jnp.einsum("bhjt,bhjd->bthd", third_prob, grad_third_out, precision=highest)
    grad_key_three = (
        jnp.einsum("bhjt,bhjd->bthd", grad_third_scores, query_marks, precision=highest)
        * score_scale
    )
    grad_query_marks_part = (
        jnp.einsum("bhjt,bthd->bhjd", grad_third_scores, key_heads, precision=highest) * score_scale
    )
    grad_query_marks_three = lax.psum(grad_query_marks_part, "seq")
    grad_query_marks = (grad_query_marks_two + grad_query_marks_three) / counts[:, None, :, None]
    grad_key_marks = (grad_key_marks_one + grad_key_marks_two) / counts[:, None, :, None]
    grad_query_marks = grad_query_marks.transpose(0, 2, 1, 3).reshape(batch, LAND, local_width)
    grad_key_marks = grad_key_marks.transpose(0, 2, 1, 3).reshape(batch, LAND, local_width)
    grad_query_seg = jnp.einsum("btj,bjf->btf", onehot, grad_query_marks, precision=highest)
    grad_key_seg = jnp.einsum("btj,bjf->btf", onehot, grad_key_marks, precision=highest)
    query_in = (
        (grad_query_one.reshape(batch, tok_local, local_width) + grad_query_seg)
        .astype(bf16)
        .reshape(rows, local_width)
    )
    key_in = (
        (grad_key_three.reshape(batch, tok_local, local_width) + grad_key_seg)
        .astype(bf16)
        .reshape(rows, local_width)
    )
    value_in = (grad_value_three.reshape(batch, tok_local, local_width) + grad_conv_values).astype(
        bf16
    )
    value_in = jnp.where(inside[:, :, None], value_in, jnp.zeros_like(value_in)).reshape(
        rows, local_width
    )
    grad_query_bias = jnp.sum(query_in.astype(f32), axis=0)
    grad_value_bias = jnp.sum(value_in.astype(f32), axis=0)
    grad_query_weight = jnp.einsum("rd,rf->df", flat, query_in, preferred_element_type=f32)
    grad_key_weight = jnp.einsum("rd,rf->df", flat, key_in, preferred_element_type=f32)
    grad_value_weight = jnp.einsum("rd,rf->df", flat, value_in, preferred_element_type=f32)
    input_part = (
        jnp.einsum("rf,df->rd", query_in, query_weight, preferred_element_type=f32)
        + jnp.einsum("rf,df->rd", key_in, key_weight, preferred_element_type=f32)
        + jnp.einsum("rf,df->rd", value_in, value_weight, preferred_element_type=f32)
    )
    input_sum, proxy_norm = (
        lax.psum(input_part.astype(jnp.bfloat16), "tensor").astype(jnp.float32),
        lax.psum(proxy_part.astype(jnp.bfloat16), "tensor").astype(jnp.float32),
    )
    grad_tokens = (grad_first_total + input_sum).reshape(batch, tok_local, width)
    (
        grad_query_weight,
        grad_key_weight,
        grad_value_weight,
        grad_out_weight,
        grad_up_weight,
        grad_down_weight,
    ) = (
        lax.psum_scatter(grad_query_weight, "seq", scatter_dimension=0, tiled=True),
        lax.psum_scatter(grad_key_weight, "seq", scatter_dimension=0, tiled=True),
        lax.psum_scatter(grad_value_weight, "seq", scatter_dimension=0, tiled=True),
        lax.psum_scatter(grad_out_weight, "seq", scatter_dimension=1, tiled=True),
        lax.psum_scatter(grad_up_weight, "seq", scatter_dimension=0, tiled=True),
        lax.psum_scatter(grad_down_weight, "seq", scatter_dimension=1, tiled=True),
    )
    (
        grad_query_bias,
        grad_value_bias,
        grad_conv_kernel,
        grad_out_bias,
        grad_first_gain,
        grad_first_shift,
        grad_up_bias,
        grad_down_bias,
        grad_second_gain,
        grad_second_shift,
    ) = lax.psum(
        (
            grad_query_bias,
            grad_value_bias,
            grad_conv_kernel,
            grad_out_bias,
            grad_first_gain,
            grad_first_shift,
            grad_up_bias,
            grad_down_bias,
            grad_second_gain,
            grad_second_shift,
        ),
        "seq",
    )
    return (
        output,
        grad_tokens,
        grad_query_weight,
        grad_query_bias,
        grad_key_weight,
        grad_value_weight,
        grad_value_bias,
        grad_conv_kernel,
        grad_out_weight,
        grad_out_bias,
        grad_first_gain,
        grad_first_shift,
        grad_up_weight,
        grad_up_bias,
        grad_down_weight,
        grad_down_bias,
        grad_second_gain,
        grad_second_shift,
        proxy_norm,
    )


MESH = pl.DeviceIdType.MESH
LANES = 2 * HEAD_DIM
f32 = jnp.float32
bf16 = jnp.bfloat16
NN = (1, 0)
NT = (1, 1)
TN = (0, 0)


def dot(a, b, dims=NN):
    return lax.dot_general(
        a, b, (((dims[0],), (dims[1],)), ((), ())), preferred_element_type=f32
    )


def split(x):
    if x.dtype == bf16:
        return (x,)
    top = x.astype(bf16)
    return (top, (x - top.astype(f32)).astype(bf16))


def fine(a, b, dims=NN):
    a, b = split(a), split(b)
    total = dot(a[0], b[0], dims)
    if len(b) > 1:
        total = total + dot(a[0], b[1], dims)
    if len(a) > 1:
        total = total + dot(a[1], b[0], dims)
    return total


def iota(shape, dim):
    return lax.broadcasted_iota(jnp.int32, shape, dim)


def block_mask():
    shape = (LANES, LANES)
    return (iota(shape, 0) < HEAD_DIM) == (iota(shape, 1) < HEAD_DIM)


def eye():
    return jnp.where(iota((LANES, LANES), 0) == iota((LANES, LANES), 1), 1.0, 0.0).astype(f32)


def block_sums(x, same_head):
    ones = jnp.where(same_head, 1.0, 0.0).astype(bf16)
    return jnp.where(same_head, fine(fine(ones, x), ones), 1.0)


def taps_matrix(row, tok):
    return pltpu.roll(jnp.broadcast_to(row, (tok, 2 * tok)), 0, 1, stride=1, stride_axis=0)


def taps_row(taps, head, tok):
    row = taps[pl.ds(head, 1), :]
    return jnp.concatenate([row, jnp.zeros((1, 2 * tok - CONV), f32)], axis=1)


def conv_block(matrices, window):
    first = fine(matrices[0], window)
    second = fine(matrices[1], window)
    return jnp.where(iota(first.shape, 1) < HEAD_DIM, first, second)


def greet(devices):
    barrier = pltpu.get_barrier_semaphore()
    for device in devices:
        pl.semaphore_signal(barrier, inc=1, device_id=device, device_id_type=MESH)
    return barrier


def around(n, me, tensor):
    return [(lax.rem(me + d, n), tensor) for d in range(1, n)]


def others(me, tensor):
    core = tensor + 1 - 2 * (tensor % 2)
    return [(me, core), (me, lax.rem(tensor + 2, 4)), (me, lax.rem(core + 2, 4))]


def paired(y):
    return y[:, :LANES], jnp.concatenate(
        [y[:, LANES : LANES + HEAD_DIM], y[:, HEAD_DIM:LANES]], axis=1
    )


def remote(src, dst, send, recv, device):
    return pltpu.make_async_remote_copy(
        src_ref=src, dst_ref=dst, send_sem=send, recv_sem=recv, device_id=device,
        device_id_type=MESH,
    )


def member_rows(length, total):
    j = iota((LANES, total), 0) % LAND
    t = iota((LANES, total), 1)
    inside = (t * LAND >= j * length) & (t * LAND < (j + 1) * length) & (t < length)
    return jnp.where(inside, 1.0, 0.0).astype(bf16)


def member_columns(length, total):
    j = iota((total, LANES), 1) % LAND
    t = iota((total, LANES), 0)
    inside = (t * LAND >= j * length) & (t * LAND < (j + 1) * length) & (t < length)
    return jnp.where(inside, 1.0, 0.0).astype(bf16)


def segment_counts(length):
    j = iota((LANES, LANES), 0) % LAND
    upper = ((j + 1) * length + LAND - 1) // LAND
    lower = (j * length + LAND - 1) // LAND
    return (upper - lower).astype(f32)


def normal_of(summed):
    middle = jnp.mean(summed, axis=-1, keepdims=True)
    centred = summed - middle
    inverse_std = lax.rsqrt(jnp.mean(centred * centred, axis=-1, keepdims=True) + epsilon)
    return centred * inverse_std, inverse_std


def before_norm(grad, normal, inverse_std, gain):
    grad_normal = grad * gain
    return inverse_std * (
        grad_normal
        - jnp.mean(grad_normal, axis=-1, keepdims=True)
        - normal * jnp.mean(grad_normal * normal, axis=-1, keepdims=True)
    )


def block_rows(t, tok):
    return pl.ds(pl.multiple_of(t * tok, tok), tok)


def settle(ref, sem):
    pltpu.make_async_copy(ref, ref, sem).wait()


class Scatter:
    def __init__(self, index, me, tensor, source, columns, buffers, send, recv, order):
        self.index, self.source, self.columns = index, source, pl.ds(*columns)
        self.first_in, self.held, self.second_in, self.pair, self.last_in, self.cross_in = buffers
        self.block = source.shape[0] // 8
        self.weights = [2**bit for bit in order]
        self.bits = [(me // weight) % 2 for weight in self.weights]
        self.partners = [
            (me + weight * (1 - 2 * bit), tensor) for weight, bit in zip(self.weights, self.bits)
        ]
        self.send, self.recv = send, recv

    def rows(self, slot, bit):
        index = (slot // 2) * self.weights[2] + (slot % 2) * self.weights[1] + bit * self.weights[0]
        return pl.ds(pl.multiple_of(index * self.block, 16), self.block)

    def copy(self, src, dst, k, stage):
        return remote(
            src, dst, self.send.at[self.index, min(k, 1)], self.recv.at[self.index, k],
            self.partners[stage],
        )

    def arrived(self, ref, k):
        settle(ref, self.recv.at[self.index, k])

    def first(self, slots=range(4)):
        for slot in slots:
            source = self.source.at[self.rows(slot, 1 - self.bits[0]), self.columns]
            self.copy(source, self.first_in.at[slot], 0, 0).start()

    def second(self):
        self.arrived(self.first_in, 0)
        for slot in range(4):
            mine = self.source[self.rows(slot, self.bits[0]), self.columns]
            self.held[slot] = self.joined(mine, self.first_in[slot])
        for k in range(2):
            self.copy(self.held.at[2 * k + 1 - self.bits[1]], self.second_in.at[k], 1, 1).start()

    def joined(self, mine, come):
        return (mine.astype(f32) + come.astype(f32)).astype(bf16)

    def third(self):
        self.arrived(self.second_in, 1)
        for k in range(2):
            both = self.held[2 * k + self.bits[1]].astype(f32) + self.second_in[k].astype(f32)
            self.pair[k] = both.astype(bf16)
        self.copy(self.pair.at[1 - self.bits[2]], self.last_in, 2, 2).start()

    def last(self, write):
        self.arrived(self.last_in, 2)
        write(self.pair[self.bits[2]].astype(f32) + self.last_in[...].astype(f32))

    def finish(self):
        settle(self.first_in, self.send.at[self.index, 0])
        settle(self.held.at[pl.ds(0, 3)], self.send.at[self.index, 1])


class Line(Scatter):
    def __init__(self, *args):
        super().__init__(*args)
        z = self.bits[1] + 2 * self.bits[2]
        right = z // 2
        self.end = self.bits[1] == right
        self.inner = self.bits[1] != right
        self.slots = [k * (1 - right) + (3 - k) * right for k in range(4)]
        self.partners[2] = (2 * (3 - z) + self.bits[0], self.partners[0][1])

    def second(self):
        self.arrived(self.first_in, 0)
        for slot in range(4):
            mine = self.source[self.rows(slot, self.bits[0]), self.columns]
            self.held[slot] = self.joined(mine, self.first_in[slot])
        come = (self.second_in.at[0], self.second_in.at[1], self.last_in)
        sends = [
            self.copy(self.held.at[self.slots[3 - k]], come[k], (1, 1, 2)[k], 1)
            for k in range(3)
        ]

        @pl.when(self.end)
        def _():
            for copy in sends:
                copy.start()

    def third(self):
        sends = [
            self.copy(self.pair.at[k], self.cross_in.at[k], 3, 2) for k in range(2)
        ]

        @pl.when(self.inner)
        def _():
            self.arrived(self.second_in, 1)
            for k in range(2):
                self.pair[k] = self.joined(self.held[self.slots[3 - k]], self.second_in[k])
                sends[k].start()

    def fourth(self):
        back = self.copy(self.first_in.at[2], self.first_in.at[3], 4, 1)

        @pl.when(self.inner)
        def _():
            self.arrived(self.cross_in, 3)
            self.first_in[2] = self.joined(self.held[self.slots[0]], self.cross_in[0])
            back.start()

    def last(self, write):
        @pl.when(self.inner)
        def _():
            self.arrived(self.last_in, 2)
            write(
                self.held[self.slots[1]].astype(f32)
                + self.last_in[...].astype(f32)
                + self.cross_in[1].astype(f32)
            )

        @pl.when(self.end)
        def _():
            self.arrived(self.first_in.at[3], 4)
            write(self.held[self.slots[0]].astype(f32) + self.first_in[3].astype(f32))


class Pairs(Scatter):
    def second(self):
        self.arrived(self.first_in, 0)
        width = self.first_in.shape[2]
        for slot in range(4):
            at = self.rows(slot, self.bits[0])
            self.held[slot, :, :width] = self.source[at]
            self.held[slot, :, width : 2 * width] = self.shared[at]
            self.held[slot, :, 2 * width :] = self.first_in[slot]
        for k in range(2):
            self.copy(self.held.at[2 * k + 1 - self.bits[1]], self.second_in.at[k], 1, 1).start()


def scatter_buffers(first, width, block):
    return [
        pltpu.VMEM((4, block, first), bf16),
        pltpu.VMEM((4, block, width), bf16),
        pltpu.VMEM((2, block, width), bf16),
        pltpu.VMEM((2, block, width), bf16),
        pltpu.VMEM((block, width), bf16),
        pltpu.VMEM((2, block, width), bf16),
    ]


def total_of(v):
    return jnp.sum(v, axis=0, keepdims=True)


def packed(block):
    middle = block.shape[-2] // 2
    first, second = block[..., :middle, :HEAD_DIM], block[..., middle:, :HEAD_DIM]
    return jnp.concatenate([first, second], axis=-1)


def unpacked(block):
    return jnp.concatenate([block[..., :HEAD_DIM], block[..., HEAD_DIM:]], axis=-2)


class Ring:
    def __init__(
        self, tensor, peers, parts, core_out, core_in, y_out, y_in, ag_send, ag_recv, sum_send,
        sum_recv,
    ):
        self.tensor, self.place = tensor, tensor % 2
        self.core, self.across, self.far = peers
        self.near_pair = tensor - self.place
        self.far_pair = lax.rem(self.near_pair + 2, 4)
        self.parts, self.core_out, self.core_in = parts, core_out, core_in
        self.y_out, self.y_in = y_out, y_in
        self.ag, self.sums = (ag_send, ag_recv), (sum_send, sum_recv)
        self.copies = {}

    def send(self, name, src, dst, sems, at, device):
        copy = remote(src, dst, sems[0].at[0], sems[1].at[at], device)
        copy.start()
        self.copies[name] = copy

    def share(self, phase, c, held):
        mine = held.at[c, self.tensor]
        self.send((phase, c, "y"), mine, mine, self.ag, (phase, c, 0), self.across)
        self.send((phase, c, "core"), mine, mine, self.ag, (phase, c, 1), self.core)

    def work(self, phase, c, side, value):
        self.parts[phase, c, side] = value.reshape(2, -1, value.shape[1])
        self.core_out[phase, c, side] = self.parts[phase, c, side, 1 - self.place].astype(bf16)
        self.send(
            (phase, c, side), self.core_out.at[phase, c, side], self.core_in.at[phase, c, side],
            self.sums, (phase, c, side), self.core,
        )

    def run(self, phase, held, work):
        for c in range(2):
            self.copies[phase, c, "core"].wait_recv()
            self.work(phase, c, 0, work(c, self.near_pair))
        for c in range(2):
            self.copies[phase, c, "y"].wait_recv()
            other = held.at[c, self.across[1]]
            self.send((phase, c, "pass"), other, other, self.ag, (phase, c, 2), self.core)
            if c == 1:
                self.cross(phase, 0)
            self.copies[phase, c, "pass"].wait_recv()
            self.work(phase, c, 1, work(c, self.far_pair))
        self.cross(phase, 1)

    def cross(self, phase, c):
        self.copies[phase, c, 1].wait_recv()
        both = self.parts[phase, c, 1, self.place] + self.core_in[phase, c, 1].astype(f32)
        self.y_out[phase, c] = both.astype(bf16)
        self.send(
            (phase, c, "sum"), self.y_out.at[phase, c], self.y_in.at[phase, c], self.sums,
            (phase, c, 2), self.across,
        )

    def total(self, phase, c):
        self.copies[phase, c, 0].wait_recv()
        self.copies[phase, c, "sum"].wait_recv()
        return (
            self.parts[phase, c, 0, self.place]
            + self.core_in[phase, c, 0].astype(f32)
            + self.y_in[phase, c].astype(f32)
        )


JOBS = 6
MATRICES = 8
RESULTS = MATRICES + 2
OUTPUTS = 19
ORDER = (4, 3, 5, 2, 6, 1, 7)


def layer_kernel(
    n, lengths, x_far, wq_far, qb, wk_far, wv_far, vb, taps, out_far, out_bias, gain_one,
    shift_one, up_far, up_bias, down_far, down_bias, gain_two, shift_two, grad_far,
    *rest,
):
    results, rest = rest[:RESULTS], rest[RESULTS:]
    ready, rest = rest[:MATRICES], rest[MATRICES:]
    layer_body(
        n, lengths, x_far, wq_far, qb, wk_far, wv_far, vb, taps, out_far, out_bias, gain_one,
        shift_one, up_far, up_bias, down_far, down_bias, gain_two, shift_two, grad_far, results,
        ready, *rest,
    )


def layer_body(
    n, lengths, x_far, wq_far, qb, wk_far, wv_far, vb, taps, out_far, out_bias, gain_one,
    shift_one, up_far, up_bias, down_far, down_bias, gain_two, shift_two, grad_far, results, ready,
    x, wk, wq, wv, up_weight, down_weight, out_grad, out_weight, out_whole,
    up_turned, down_turned, stage, ks, qs, vs, k1, p3, newton, out_stage, out_single, attn_pair, attn_single,
    pairs_in, singles_in, heads_out, hidden, slope, active, down_in, up_in,
    core_out, core_in, y_out, y_in, core_last, y_last,
    gs, back_stage, back_single, come_pair, come_single, weight_in, out_in, early, early_tensor, tokens_own, tokens_low, source_up,
    source_down, source_out, source_own, source_both, early_out, early_in, late_out, late_in, tokens_whole,
    parts_held,
    *rest,
):
    buffers, sems = rest[: 6 * JOBS], rest[6 * JOBS :]
    (load, send, recv, out_send, out_recv, whole_send, whole_recv, copy_send, copy_recv, ag_send,
     ag_recv, sum_send, sum_recv, grad_send, grad_recv, back_send, back_recv, share_send,
     share_recv, small_send, small_recv, job_send, job_recv, own_send, own_recv, last_send, last_recv,
     store) = sems
    output, grad_tokens, grad_query, grad_key, grad_value, grad_out, grad_up, grad_down = ready
    ready = (*ready, early_out.at[3], late_out.at[3])
    stores = []

    def done(*numbers):
        for i in numbers:
            copy = pltpu.make_async_copy(ready[i], results[i], store.at[i])
            copy.start()
            stores.append(copy)

    me = lax.axis_index("seq")
    tensor = lax.axis_index("tensor")
    rows, width = x.shape
    batch = n // 2
    tok = rows // batch
    total = n * tok
    half = CONV // 2
    own, side = me // 2, me % 2
    scale = HEAD_DIM ** (-0.5)
    ring_peers = around(n, me, tensor)
    peers = others(me, tensor)
    core, across, far = peers

    def batch_of(t):
        return lax.rem(t - me + 8, 4)

    def rows_at(t):
        return block_rows(batch_of(t), tok)

    mine = rows_at(tensor)
    at_home = batch_of(tensor) == own
    away = batch_of(tensor) != own
    local = wk.shape[0]
    barrier = greet(ring_peers + peers)
    loads = []
    for i, (source, target) in enumerate((
        (x_far, x), (wk_far, wk), (wq_far, wq), (wv_far, wv),
        (out_far, out_weight), (up_far, up_weight),
        (down_far, down_weight), (grad_far, out_grad),
    )):
        copy = pltpu.make_async_copy(source, target, load.at[i])
        if i < 5:
            copy.start()
        loads.append(copy)
    hidden_width = up_weight.shape[1]
    span = hidden_width // 2
    jobs = [
        kind(i, me, tensor, source, columns, buffers[6 * i : 6 * i + 6], job_send, job_recv, order)
        for i, (kind, source, columns, order) in enumerate((
            (Line, source_down, (0, span), (0, 1, 2)),
            (Scatter, source_down, (span, span), (1, 0, 2)),
            (Line, source_up, (0, span), (0, 1, 2)),
            (Line, source_up, (span, span), (0, 1, 2)),
            (Scatter, source_out, (0, local), (0, 1, 2)),
            (Pairs, source_own, (0, local), (0, 1, 2)),
        ))
    ]
    job_down, job_up = jobs[0:2], jobs[2:4]
    job_out, job_heads = jobs[4:]
    job_heads.shared = source_both

    owned = (ks, qs, vs)
    offsets = (0, 0, half)
    for padded in (vs, gs):
        padded[0:half] = jnp.zeros((half, LANES), bf16)
        padded[half + total : total + tok] = jnp.zeros((tok - half, LANES), bf16)
    even = side == 0

    seven = pl.ds(0, (n - 1) * tok)

    def spread(i):
        here = pl.ds(pl.multiple_of(offsets[i] + me * tok, 16), tok)
        for d in ORDER:
            peer = lax.rem(me + d, n)
            copy = remote(
                stage.at[i, peer % 2, block_rows(peer // 2, tok)], owned[i].at[here],
                send.at[i], recv.at[i], (peer, tensor),
            )
            copy.start()
        owned[i][here] = stage[i, side, block_rows(own, tok)]

    loads[0].wait()
    loads[1].wait()
    y = dot(x[...], wk[...], NT)
    stage[0, 0], stage[0, 1] = paired(y.astype(bf16))
    pl.semaphore_wait(barrier, n + 2)
    spread(0)
    for copy in loads[5:]:
        copy.start()
    loads[2].wait()
    y = dot(x[...], wq[...], NT) + qb[...].reshape(1, local)
    stage[1, 0], stage[1, 1] = paired(y.astype(bf16))
    spread(1)
    loads[3].wait()
    y = dot(x[...], wv[...], NT) + vb[...].reshape(1, local)
    position = me * tok + iota((tok, local), 0)
    y = jnp.concatenate(
        [
            jnp.where(position < lengths[b], y[b * tok : (b + 1) * tok], 0.0)
            for b in range(batch)
        ],
        axis=0,
    )
    stage[2, 0], stage[2, 1] = paired(y.astype(bf16))
    loads[4].wait()
    pair_rows = block_rows(tensor, LANES)
    single_rows = pl.ds(pl.multiple_of(4 * LANES + tensor * HEAD_DIM, HEAD_DIM), HEAD_DIM)
    first, single = out_weight[:LANES], out_weight[LANES:]
    out_whole[pair_rows] = jnp.where(
        even, first, jnp.concatenate([single, first[HEAD_DIM:]], axis=0)
    )
    out_whole[single_rows] = jnp.where(even, single, first[:HEAD_DIM])
    for i, device in enumerate(peers):
        for at in (pair_rows, single_rows):
            part = out_whole.at[at]
            remote(part, part, whole_send.at[0], whole_recv.at[0], device).start()

    length = lengths[own]
    same_head = block_mask()
    identity = eye()
    ones = jnp.where(same_head, 1.0, 0.0).astype(bf16)
    members = member_rows(length, total)
    counts = segment_counts(length)
    matrices = [taps_matrix(taps_row(taps, h, tok), tok) for h in (2 * side, 1)]
    flip = jnp.where(
        iota((2 * tok, 2 * tok), 0) + iota((2 * tok, 2 * tok), 1) == CONV - 1, 1.0, 0.0
    ).astype(bf16)
    reverse = [
        taps_matrix(
            fine(jnp.broadcast_to(taps_row(taps, h, tok), (8, 2 * tok)), flip)[0:1], tok
        )
        for h in (2 * side, 1)
    ]
    for i, w in enumerate((wk, wq, wv)):
        pair, single = w[:LANES], w[LANES:]
        weight_in[i * LANES : (i + 1) * LANES] = jnp.where(
            even, pair, jnp.concatenate([single, pair[HEAD_DIM:]], axis=0)
        )
        start = 3 * LANES + i * HEAD_DIM
        weight_in[start : start + HEAD_DIM] = jnp.where(even, single, pair[:HEAD_DIM])
    for copy in loads[5:]:
        copy.wait()
    up_turned[...] = up_weight[...].T
    down_turned[...] = down_weight[...].T
    settle(ks.at[seven], recv.at[0])
    keys = ks[...]
    key_marks = jnp.where(same_head, dot(members, keys) / counts, 0.0)
    settle(qs.at[seven], send.at[1])
    spread(2)
    settle(qs.at[seven], recv.at[1])
    queries = qs[...]
    query_marks = jnp.where(same_head, dot(members, queries) / counts, 0.0)
    scores = jnp.where(same_head, fine(query_marks, key_marks, NT) * scale, negative)
    weights = jnp.exp(scores - jnp.max(scores, axis=1, keepdims=True))
    kernel_two = weights / jnp.sum(weights, axis=1, keepdims=True)
    inverse = jnp.where(
        same_head, kernel_two.T / block_sums(kernel_two * kernel_two, same_head), 0.0
    )
    def scores_one():
        values = fine(queries, key_marks, NT) * scale
        left = iota(values.shape, 1) < HEAD_DIM
        top_left = jnp.max(jnp.where(left, values, negative), axis=1, keepdims=True)
        top_right = jnp.max(jnp.where(left, negative, values), axis=1, keepdims=True)
        return jnp.exp(values - jnp.where(left, top_left, top_right))

    def scores_three():
        values = fine(keys, query_marks, NT) * scale
        alive = iota(values.shape, 0) < length
        values = jnp.where(alive, values, negative)
        weights = jnp.exp(values - jnp.max(values, axis=0, keepdims=True))
        return jnp.where(alive, weights, 0.0)

    product = fine(kernel_two, inverse)
    for step in range(NS_ITERS):
        if step == 0:
            weights_one = scores_one()
        if step == 1:
            k1[...] = weights_one / fine(weights_one, ones)
        if step == 2:
            weights_three = scores_three()
        if step == 3:
            third_prob = weights_three / jnp.sum(weights_three, axis=0, keepdims=True)
            p3[...] = third_prob
        inner = fine(product, 7.0 * identity - product)
        outer = 13.0 * identity - fine(product, 15.0 * identity - inner)
        newton[5 * step] = inverse
        newton[5 * step + 1] = product
        newton[5 * step + 2] = inner
        newton[5 * step + 3] = outer
        newton[5 * step + 4] = fine(product, kernel_two)
        inverse = 0.25 * fine(inverse, outer)
        product = 0.25 * fine(product, outer)

    deviation = identity - product
    norms = jnp.sqrt(block_sums(deviation * deviation, same_head))
    first, second = norms[0:1, 0:1], norms[LANES - 1 :, LANES - 1 :]
    norm_sum = jnp.where(side == 0, first + second, first) / (batch * HEADS)
    early[7:8] = jnp.broadcast_to(norm_sum, (1, width))

    settle(vs.at[seven], recv.at[2])
    values = vs[half : half + total]
    third_out = jnp.where(same_head, fine(third_prob, values, TN), 0.0)
    carried = fine(inverse, third_out)

    for d in (*ORDER, n):
        peer = lax.rem(me + d, n)
        start = pl.multiple_of(peer * tok, tok)
        nystrom = fine(k1[pl.ds(start, tok)], carried)
        convolved = conv_block(matrices, vs[pl.ds(start, 2 * tok)])
        low = (nystrom + convolved).astype(bf16)
        device = (peer, lax.rem(own + peer, 4))
        if d % 2 == 0:
            source, target = out_stage.at[d - 1], pairs_in.at[tensor]
            source[...] = low
        else:
            source, target = out_single.at[d - 1], singles_in.at[tensor]
            source[...] = packed(low)
        copy = remote(source, target, out_send.at[d % 2], out_recv.at[d % 2], device)
        if d < n:
            copy.start()
            continue
        attn_pair[own] = low
        pl.when(away)(copy.start)

        @pl.when(at_home)
        def _():
            pairs_in[tensor] = low

    three = pl.ds(0, 3)

    def settle_home(ref, some, sem):
        pl.when(away)(lambda: settle(ref, sem))
        pl.when(at_home)(lambda: settle(ref.at[some], sem))

    settle_home(pairs_in, three, out_recv.at[0])
    settle(singles_in, out_recv.at[1])
    settle(out_whole.at[pl.ds(0, 3 * local)], whole_recv.at[0])
    z, side_of_chip = me // 2, tensor % 2
    beside = (me + 1 - 2 * side, tensor)
    def give_tokens(src, dst, i, device):
        remote(src, dst, own_send.at[i // 2], own_recv.at[i], device).start()

    def half_block(b):
        start = pl.multiple_of(b * tok + side_of_chip * (tok // 2), tok // 2)
        return pl.ds(start, tok // 2)

    tokens_own[me, side_of_chip] = x[half_block(own)]
    for k in range(1, 4):
        peer = lax.rem(z + k, 4)
        give_tokens(
            x.at[half_block(peer)], tokens_own.at[me, side_of_chip], 0, (2 * peer + side, tensor)
        )
    half_own = tokens_own.at[me, side_of_chip]
    give_tokens(half_own, half_own, 1, beside)

    def pass_tokens():
        settle(tokens_own.at[pl.ds(0, 3), 0], own_recv.at[0])
        for k in range(1, 4):
            come = tokens_own.at[2 * lax.rem(z + 4 - k, 4) + side, side_of_chip]
            give_tokens(come, come, 1, beside)

    def line(vector):
        return vector[...].reshape(1, vector.shape[0])

    piece = tok // 2
    chunks = range(2)
    ring = Ring(
        tensor, peers, parts_held, core_out, core_in, y_out, y_in, ag_send, ag_recv, sum_send,
        sum_recv,
    )

    def rows_of(c):
        return pl.ds(pl.multiple_of(batch_of(tensor) * tok + c * piece, piece), piece)

    def normed(c):
        at = slice(c * piece, (c + 1) * piece)
        lanes = slice(c * HEAD_DIM, (c + 1) * HEAD_DIM)
        heads = jnp.concatenate(
            [pairs_in[t, at] for t in range(4)] + [singles_in[t, :, lanes] for t in range(4)],
            axis=1,
        )
        branch = dot(heads, out_whole[...])
        first_total = x[rows_of(c)].astype(f32) + (branch + line(out_bias))
        normal, inverse_std = normal_of(first_total)
        whole_row = normal * line(gain_one) + line(shift_one)
        hidden[c, tensor] = whole_row.astype(bf16)
        ring.share(0, c, hidden)
        return normal, inverse_std, whole_row

    def up(c, t):
        at = pl.ds(t, 2)
        value = dot(hidden[c, at].reshape(tok, width), up_weight[...]) + line(up_bias)
        half_erf = 0.5 * (1.0 + lax.erf(value * (0.5**0.5)))
        density = jnp.exp(-0.5 * value * value) * (0.5 / jnp.pi) ** 0.5
        slope[c, at] = (half_erf + value * density).reshape(2, piece, hidden_width)
        low = (value * half_erf).astype(bf16)
        active[c, at] = low.reshape(2, piece, hidden_width)
        return dot(low, down_weight[...])

    def down(c, t):
        at = pl.ds(t, 2)
        grad = dot(down_in[c, at].reshape(tok, width), down_turned[...])
        low = (grad * slope[c, at].reshape(tok, hidden_width)).astype(bf16)
        up_in[c, at] = low.reshape(2, piece, hidden_width)
        return dot(low, up_turned[...])

    after_norm_one = [normed(c) for c in chunks]
    ring.run(0, hidden, up)
    pass_tokens()
    for d in range(1, n):
        if d % 2 == 0:
            source, target = out_stage.at[d - 1], attn_pair.at[own]
        else:
            source, target = out_single.at[d - 1], attn_single.at[own]
        remote(
            source, target, copy_send.at[d % 2], copy_recv.at[d % 2],
            (lax.rem(me + d, n), tensor),
        ).start()

    grads_second, sums_second = [], []
    for c in chunks:
        hidden_one = after_norm_one[c][2]
        second_total = hidden_one + (ring.total(0, c) + line(down_bias))
        normal, inverse_std = normal_of(second_total)
        output[rows_of(c)] = (normal * line(gain_two) + line(shift_two)).astype(bf16)
        grad_output = out_grad[rows_of(c)].astype(f32)
        grad_second = before_norm(grad_output, normal, inverse_std, line(gain_two))
        low = grad_second.astype(bf16)
        down_in[c, tensor] = low
        ring.share(1, c, down_in)
        grads_second.append(grad_second)
        sums_second.append(
            (total_of(grad_output * normal), total_of(grad_output), total_of(low.astype(f32)))
        )
    ring.run(1, down_in, down)
    everything = (rows, width)
    every_hidden = (rows, hidden_width)
    source_down[...] = dot(
        down_in[...].reshape(everything), active[...].reshape(every_hidden), TN
    ).astype(bf16)
    for job in job_down:
        job.first()

    grads_first, sums_first = [], []
    for c in chunks:
        normal, inverse_std, _ = after_norm_one[c]
        grad_hidden = grads_second[c] + ring.total(1, c)
        grad_first = before_norm(grad_hidden, normal, inverse_std, line(gain_one))
        low = grad_first.astype(bf16)
        out_in[rows_of(c)] = low
        heads = dot(low, out_whole[...], NT).astype(bf16)
        at = slice(c * piece, (c + 1) * piece)
        for t in range(4):
            start = 4 * LANES + t * HEAD_DIM
            pair = heads[:, t * LANES : (t + 1) * LANES]
            heads_out[t, 0, at] = pair
            heads_out[t, 1, at] = jnp.concatenate(
                [heads[:, start : start + HEAD_DIM], pair[:, HEAD_DIM:]], axis=1
            )
        b = batch_of(tensor)
        there = pl.ds(pl.multiple_of(half + me * tok + c * piece, 16), piece)
        for t in range(4):
            for k, device in enumerate(((2 * b + side, t), (2 * b + 1 - side, t))):
                copy = remote(
                    heads_out.at[t, k, pl.ds(c * piece, piece)], gs.at[there], grad_send.at[0],
                    grad_recv.at[0], device,
                )
                if k == 1:
                    copy.start()
                else:
                    pl.when((batch_of(tensor) != own) | (tensor != t))(copy.start)
        grads_first.append(grad_first)
        sums_first.append(
            (total_of(grad_hidden * normal), total_of(grad_hidden), total_of(low.astype(f32)))
        )

    @pl.when(at_home)
    def _():
        here = pl.ds(pl.multiple_of(half + me * tok, 16), tok)
        gs[here] = heads_out[tensor, 0]

    source_up[...] = dot(
        hidden[...].reshape(everything), up_in[...].reshape(every_hidden), TN
    ).astype(bf16)
    for i in range(3):
        early[i : i + 1] = sums_second[0][i] + sums_second[1][i]
        early[i + 3 : i + 4] = sums_first[0][i] + sums_first[1][i]
    early[6:7] = dot(jnp.ones((8, rows), bf16), up_in[...].reshape(every_hidden))[0:1]
    early_tensor[tensor] = early[...]
    job_up[0].first(range(2))
    for i, device in enumerate(peers):
        remote(
            early, early_tensor.at[tensor], small_send.at[0], small_recv.at[0], device
        ).start()
    shares = []
    for i, held in enumerate((out_in, output)):
        for j, device in enumerate((across, core)):
            copy = remote(
                held.at[mine], held.at[mine], share_send.at[i], share_recv.at[i, j], device
            )
            copy.start()
            shares.append(copy)
    job_down[0].second()
    job_up[0].first(range(2, 4))
    job_up[1].first()
    settle(tokens_own.at[pl.ds(0, 4), 0], own_recv.at[1])
    half_all = tokens_own.at[:, side_of_chip]
    give_tokens(half_all, half_all, 2, core)

    members = member_columns(length, total)
    def give(i, block):
        low = block.astype(bf16)
        back_stage[i] = low.reshape(n, tok, LANES)
        back_single[i] = packed(low.reshape(n, tok, LANES))
        for d in ORDER:
            peer = lax.rem(me + d, n)
            source, target = (back_stage, come_pair) if d % 2 == 0 else (back_single, come_single)
            remote(
                source.at[i, peer], target.at[i, own], back_send.at[d % 2],
                back_recv.at[d % 2], (peer, tensor),
            ).start()
        come_pair[i, own] = back_stage[i, me]
        return low

    eight = gs.at[pl.ds(0, total)]
    settle_home(eight, seven, grad_recv.at[0])
    grad = gs[half : half + total]
    kernel_one = k1[...]
    grad_carried = jnp.where(same_head, fine(kernel_one, grad, TN), 0.0)
    grad_third = fine(inverse, grad_carried, TN)
    grad_inverse = fine(grad_carried, third_out, NT)
    settle(early_tensor.at[three], small_recv.at[0])
    by_tensor = early_tensor[0] + early_tensor[1] + early_tensor[2] + early_tensor[3]
    early_out[0] = jnp.where(iota(by_tensor.shape, 0) == 6, early[...], by_tensor)
    smalls_early = []

    def early_next(k):
        if k > 0:
            smalls_early[k - 1].wait_recv()
            early_out[k] = early_out[k - 1] + early_in[k - 1]
        if k < 3:
            copy = remote(
                early_out.at[k], early_in.at[k], small_send.at[1], small_recv.at[1 + k],
                job_out.partners[(k + 1) % 3],
            )
            copy.start()
            smalls_early.append(copy)

    early_next(0)
    job_down[0].third()
    kernel_back = jnp.zeros((LANES, LANES), f32)
    grad_state = grad_inverse
    for step in reversed(range(NS_ITERS)):
        state, product, inner, outer, shifted = [newton[5 * step + i] for i in range(5)]
        grad_outer = 0.25 * fine(state, grad_state, TN)
        partial = (
            fine(grad_outer, inner, NT)
            - 15.0 * grad_outer
            - fine(7.0 * product - inner, grad_outer, TN)
        )
        rest_part = 7.0 * grad_outer - fine(grad_outer, product, NT)
        grad_state = (
            0.25 * fine(grad_state, outer, NT)
            + fine(kernel_two, partial, TN)
            + fine(shifted, rest_part, TN)
        )
        kernel_back = kernel_back + fine(partial + fine(product, rest_part, TN), state, NT)
        if step == NS_ITERS - 1:
            third_prob = p3[...]
            convolved = jnp.concatenate(
                [conv_block(reverse, gs[m * tok : (m + 2) * tok]) for m in range(n)], axis=0
            )
            grad_values = fine(third_prob, grad_third) + convolved
            value_in = give(
                2, jnp.where(iota(grad_values.shape, 0) < length, grad_values, 0.0)
            )
        if step == NS_ITERS - 2:
            grad_one = fine(grad, carried, NT)
            both = kernel_one * grad_one
            first_scores = scale * (both - kernel_one * fine(both, ones))
        if step == NS_ITERS - 3:
            key_one = jnp.where(same_head, fine(first_scores, queries, TN), 0.0)
            delta = fine(jnp.ones((8, LANES), bf16), grad_third * third_out, NT)[0:1]
            third_scores = scale * third_prob * (fine(values, grad_third, NT) - delta)
        if step == NS_ITERS - 4:
            query_three = jnp.where(same_head, fine(third_scores, keys, TN), 0.0)
            key_part = fine(third_scores, query_marks)
            query_part = fine(first_scores, key_marks)
    squares = block_sums(kernel_two * kernel_two, same_head)
    spread_sum = jnp.where(same_head, block_sums(grad_state * newton[0], same_head), 0.0)
    kernel_back = kernel_back + (grad_state.T - 2.0 * kernel_two * spread_sum) / squares
    grad_scores = scale * kernel_two * (
        kernel_back - jnp.sum(kernel_two * kernel_back, axis=1, keepdims=True)
    )
    query_two = fine(grad_scores, key_marks)
    key_two = fine(grad_scores, query_marks, TN)

    key_in = give(0, key_part + fine(members, (key_one + key_two) / counts))
    query_in = give(1, query_part + fine(members, (query_two + query_three) / counts))

    for i, held in enumerate((out_in, output)):
        shares[2 * i].wait_recv()
        block = held.at[rows_at(across[1])]
        copy = remote(block, block, share_send.at[i], share_recv.at[i, 2], core)
        copy.start()
        shares.append(copy)
    job_up[0].second()
    job_down[1].second()
    settle(half_all, own_recv.at[2])
    tokens_all = tokens_own[...].reshape(total, width)
    lanes_own, lanes_both = slice(0, HEAD_DIM), slice(HEAD_DIM, LANES)
    for ref, at in ((source_own, lanes_own), (source_both, lanes_both)):
        grads = jnp.concatenate([key_in[:, at], query_in[:, at], value_in[:, at]], axis=1)
        ref[...] = dot(tokens_all, grads, TN).astype(bf16)
    job_heads.first()
    shares[1].wait_recv()
    shares[4].wait_recv()
    settle(attn_pair.at[three], copy_recv.at[0])
    settle(attn_single, copy_recv.at[1])
    pair, single = attn_pair[...].reshape(rows, LANES), unpacked(attn_single[...])
    single = single.reshape(rows, HEAD_DIM)
    attention = jnp.concatenate(
        [
            jnp.where(even, pair, jnp.concatenate([single, pair[:, HEAD_DIM:]], axis=1)),
            jnp.where(even, single, pair[:, :HEAD_DIM]),
        ],
        axis=1,
    )
    source_out[...] = dot(out_in[...], attention, TN).astype(bf16)
    job_out.first()
    position = iota((tok, tok), 0) + iota((tok, tok), 1)
    upside = jnp.where(position == tok - 1, 1.0, 0.0).astype(bf16)
    lane = iota((tok, LANES), 1)
    conv_rows = []
    for h in range(2):
        inner = (lane < HEAD_DIM) if h == 0 else (lane >= HEAD_DIM)
        table = jnp.zeros((tok, 2 * tok), f32)
        for m in range(n):
            block = gs[half + m * tok : half + (m + 1) * tok]
            block = jnp.where(inner, block, jnp.zeros_like(block))
            table = table + dot(block, vs[m * tok : (m + 2) * tok], NT)
        table = pltpu.roll(fine(upside, table), 0, 1, stride=1, stride_axis=0)
        row = jnp.sum(table, axis=0, keepdims=True)
        row = pltpu.roll(jnp.broadcast_to(row, (8, 2 * tok)), tok + 1, 1)
        conv_rows.append(row[0:1, :LANES])
    late = late_out.at[0]
    late[...] = jnp.zeros(late.shape, f32)
    column = jnp.ones((8, total), bf16)
    for row, v in ((0, query_in), (1, value_in)):
        v = dot(column, v)[0:1]
        late[row : row + 1, 0:LANES] = jnp.where(even, v, 0.0)
        late[row : row + 1, LANES:local] = jnp.where(even, 0.0, v[:, :HEAD_DIM])
    late[2:3, 0:LANES] = jnp.where(even, conv_rows[0], 0.0)
    late[3:4, 0:LANES] = jnp.where(even, conv_rows[1], 0.0)
    late[4:5, 0:LANES] = jnp.where(even, 0.0, conv_rows[0])
    smalls_late = []

    def late_next(k):
        if k > 0:
            smalls_late[k - 1].wait_recv()
            late_out[k] = late_out[k - 1] + late_in[k - 1]
        if k < 3:
            copy = remote(
                late_out.at[k], late_in.at[k], small_send.at[2], small_recv.at[4 + k],
                job_out.partners[(k + 1) % 3],
            )
            copy.start()
            smalls_late.append(copy)

    late_next(0)
    early_next(1)
    job_down[1].third()
    job_down[0].fourth()
    job_up[1].second()
    settle(come_pair.at[:, three], back_recv.at[0])
    settle(come_single, back_recv.at[1])
    singles = []
    for i in range(3):
        tokens_low[:, i * LANES : (i + 1) * LANES] = come_pair[i].reshape(rows, LANES)
        singles.append(unpacked(come_single[i]).reshape(rows, HEAD_DIM))
    tokens_low[:, 3 * LANES :] = jnp.concatenate(singles, axis=1)

    def input_part(t):
        return dot(tokens_low[rows_at(t)], weight_in[...])

    def pass_sum(k, value, device):
        core_last[0, k] = value.astype(bf16)
        copy = remote(
            core_last.at[0, k], core_last.at[1, k], last_send.at[0], last_recv.at[k], device
        )
        copy.start()
        return copy

    middle = pass_sum(1, input_part(far[1]), core)
    near = pass_sum(0, input_part(core[1]), core)
    crossing = input_part(across[1])
    middle.wait_recv()
    y_last[0] = (crossing + core_last[1, 1].astype(f32)).astype(bf16)
    final = remote(y_last.at[0], y_last.at[1], last_send.at[0], last_recv.at[2], across)
    final.start()
    result = input_part(tensor) + jnp.concatenate(grads_first, axis=0)
    late_next(1)
    job_up[0].third()
    job_heads.second()
    early_next(2)
    job_up[1].third()
    job_up[0].fourth()
    near.wait_recv()
    final.wait_recv()
    result = result + core_last[1, 0].astype(f32) + y_last[1].astype(f32)
    tokens_whole[mine] = result.astype(bf16)
    ends = []
    for j, device in enumerate((across, core)):
        copy = remote(
            tokens_whole.at[mine], tokens_whole.at[mine], share_send.at[2], share_recv.at[2, j],
            device,
        )
        copy.start()
        ends.append(copy)
    job_out.second()
    late_next(2)

    def into(ref, k):
        def write(value):
            ref[:, k * span : (k + 1) * span] = value

        return write

    for k, job in enumerate(job_down):
        job.last(into(grad_down, k))
    done(7)
    job_heads.third()
    job_up[1].fourth()
    ends[0].wait_recv()
    block = tokens_whole.at[rows_at(across[1])]
    copy = remote(block, block, share_send.at[2], share_recv.at[2, 2], core)
    copy.start()
    ends.append(copy)
    job_out.third()
    ends[1].wait_recv()
    ends[2].wait_recv()
    grad_tokens[...] = tokens_whole[...].astype(f32)
    done(1)
    early_next(3)
    late_next(3)
    shares[3].wait_recv()
    shares[5].wait_recv()
    done(0, 8, 9)
    for k, job in enumerate(job_up):
        job.last(into(grad_up, k))
    done(6)

    def write_heads(result):
        for i, ref in enumerate((grad_key, grad_query, grad_value)):
            mine, both, come = [
                result[:, k * local + i * HEAD_DIM : k * local + (i + 1) * HEAD_DIM]
                for k in range(3)
            ]
            ref[:, :HEAD_DIM] = jnp.where(even, mine, come)
            ref[:, HEAD_DIM:LANES] = both
            ref[:, LANES:] = jnp.where(even, come, mine)

    job_heads.last(write_heads)
    done(2, 3, 4)

    def write_out(value):
        grad_out[...] = value.T

    job_out.last(write_out)
    done(5)
    three_rows = x.at[pl.ds(0, 3 * tok)]
    settle_home(pairs_in, three, out_send.at[0])
    settle_home(eight, seven, grad_send.at[0])
    for ref, sem in (
        (ks.at[seven], send.at[0]), (vs.at[seven], send.at[2]),
        (singles_in, out_send.at[1]), (attn_pair.at[three], copy_send.at[0]),
        (attn_single, copy_send.at[1]),
        (out_whole.at[pl.ds(0, 3 * local)], whole_send.at[0]),
        (out_whole, ag_send.at[0]), (out_whole, sum_send.at[0]),
        (come_pair.at[:, three], back_send.at[0]),
        (come_single, back_send.at[1]), (three_rows, share_send.at[0]),
        (three_rows, share_send.at[1]), (three_rows, share_send.at[2]),
        (early_tensor.at[three], small_send.at[0]), (early_in, small_send.at[1]),
        (late_in, small_send.at[2]), (tokens_own.at[pl.ds(0, n - 1), 0], own_send.at[0]),
        (half_all, own_send.at[1]), (three_rows, last_send.at[0]),
    ):
        settle(ref, sem)
    for job in jobs:
        job.finish()
    for copy in stores:
        copy.wait()


def finish_kernel(*refs):
    come, refs = refs[:RESULTS], refs[RESULTS:]
    go, refs = refs[:OUTPUTS], refs[OUTPUTS:]
    held, refs = refs[:RESULTS], refs[RESULTS:]
    (query_bias, value_bias, conv, out_bias, first_gain, first_shift, up_bias, down_bias,
     second_gain, second_shift, proxy, loads, stores) = refs
    early, late = held[MATRICES:]
    small = (query_bias, value_bias, conv, out_bias, first_gain, first_shift, up_bias, down_bias,
             second_gain, second_shift, proxy)
    places = (0, 1, 2, 4, 5, 8, 12, 14)
    other = [i for i in range(OUTPUTS) if i not in places]
    copies = [
        pltpu.make_async_copy(come[i], held[i], loads.at[i]) for i in range(RESULTS)
    ]
    for copy in copies:
        copy.start()
    outs = []

    def store(i, source):
        copy = pltpu.make_async_copy(source, go[i], stores.at[i])
        copy.start()
        outs.append(copy)

    copies[MATRICES].wait()
    copies[MATRICES + 1].wait()
    for ref, row in (
        (second_gain, 0), (second_shift, 1), (down_bias, 2), (first_gain, 3), (first_shift, 4),
        (out_bias, 5), (up_bias, 6),
    ):
        ref[...] = early[row]
    proxy[...] = early[7:8, 0:1]
    local = query_bias.shape[0]
    query_bias[...] = late[0, :local]
    value_bias[...] = late[1, :local]
    conv[...] = late[2:5, :CONV]
    for i, ref in zip(other, small):
        store(i, ref)
    for k, i in enumerate(places):
        copies[k].wait()
        store(i, held[k])
    for copy in outs:
        copy.wait()


def whole(shape, dtype):
    return jax.ShapeDtypeStruct(shape, dtype)


VMEM = pl.BlockSpec(memory_space=pltpu.VMEM)
SMEM = pl.BlockSpec(memory_space=pltpu.SMEM)
HBM = pl.BlockSpec(memory_space=pl.ANY)


def dma(*shape):
    return pltpu.SemaphoreType.DMA(shape)


def gathered_plan(
    n, tokens, lengths, query_weight, query_bias, key_weight, value_weight, value_bias,
    conv_kernel, out_weight, out_bias, first_gain, first_shift, up_weight, up_bias, down_weight,
    down_bias, second_gain, second_shift, out_grad,
):
    batch, tok, width = tokens.shape
    rows = batch * tok
    local = query_weight.shape[1]
    hidden = up_weight.shape[1]
    total = n * tok
    block = width // n
    piece = tok // 2

    def low(*shape):
        return pltpu.VMEM(shape, bf16)

    def wide(*shape):
        return pltpu.VMEM(shape, f32)

    results = (
        whole((rows, width), bf16),
        whole((rows, width), f32),
        whole((block, local), f32),
        whole((local,), f32),
        whole((block, local), f32),
        whole((block, local), f32),
        whole((local,), f32),
        whole(conv_kernel.shape, f32),
        whole((local, block), f32),
        whole((width,), f32),
        whole((width,), f32),
        whole((width,), f32),
        whole((block, hidden), f32),
        whole((hidden,), f32),
        whole((block, hidden), f32),
        whole((width,), f32),
        whole((width,), f32),
        whole((width,), f32),
        whole((1, 1), f32),
    )
    places = (0, 1, 2, 4, 5, 8, 12, 14)
    parts = [results[i] for i in places]
    sums = [whole((8, width), f32), whole((8, 2 * LANES), f32)]
    outs = pl.pallas_call(
        functools.partial(layer_kernel, n),
        out_shape=(*parts, *sums),
        in_specs=[SMEM, HBM, HBM, VMEM, HBM, HBM, VMEM, VMEM, HBM, VMEM, VMEM, VMEM, HBM, VMEM, HBM,
                  VMEM, VMEM, VMEM, HBM],
        out_specs=(HBM,) * RESULTS,
        scratch_shapes=[pltpu.VMEM(r.shape, r.dtype) for r in parts]
        + [
            low(rows, width), low(local, width), low(local, width), low(local, width),
            low(width, hidden), low(hidden, width), low(rows, width), low(local, width),
            low(width, width), low(hidden, width), low(width, hidden),
            low(3, 2, rows, LANES), low(total, LANES), low(total, LANES), low(total + tok, LANES),
            wide(total, LANES), wide(total, LANES), wide(5 * NS_ITERS, LANES, LANES),
            low(n, tok, LANES), low(n, piece, LANES), low(batch, tok, LANES),
            low(batch, piece, LANES),
            low(4, tok, LANES), low(4, piece, LANES), low(4, 2, tok, LANES),
            low(2, 4, piece, width), wide(2, 4, piece, hidden),
            low(2, 4, piece, hidden), low(2, 4, piece, width), low(2, 4, piece, hidden),
            low(2, 2, 2, piece, width), low(2, 2, 2, piece, width), low(2, 2, piece, width),
            low(2, 2, piece, width), low(2, 2, tok, width), low(2, tok, width),
            low(total + tok, LANES), low(3, n, tok, LANES), low(3, n, tok // 2, LANES),
            low(3, batch, tok, LANES), low(3, batch, tok // 2, LANES), low(3 * local, width),
            low(rows, width), wide(8, width), wide(4, 8, width), low(n, 2, tok // 2, width),
            low(rows, 3 * local), low(width, hidden), low(width, hidden), low(width, local),
            low(width, local), low(width, local), wide(4, 8, width), wide(3, 8, width),
            wide(4, 8, 2 * LANES), wide(3, 8, 2 * LANES), low(rows, width), wide(2, 2, 2, 2, piece, width),
        ]
        + [
            b
            for first, w in (
                *((hidden // 2, hidden // 2),) * 4, (local, local), (local, 3 * local)
            )
            for b in scatter_buffers(first, w, block)
        ]
        + [
            dma(8), dma(3), dma(3), dma(2), dma(2), dma(1), dma(1), dma(2), dma(2), dma(1),
            dma(2, 2, 3), dma(1), dma(2, 2, 3), dma(1), dma(1), dma(2), dma(2), dma(3), dma(3, 3),
            dma(3), dma(7), dma(JOBS, 2), dma(JOBS, 5), dma(2), dma(3), dma(1), dma(3),
            dma(RESULTS),
        ],
        compiler_params=pltpu.CompilerParams(
            collective_id=0, has_side_effects=True, vmem_limit_bytes=56 * 2**20
        ),
        name="layer",
    )(
        lengths, tokens.reshape(rows, width), query_weight.T, query_bias, key_weight.T,
        value_weight.T, value_bias, conv_kernel, out_weight, out_bias, first_gain, first_shift,
        up_weight, up_bias, down_weight, down_bias, second_gain, second_shift,
        out_grad.reshape(rows, width),
    )
    outs = pl.pallas_call(
        finish_kernel,
        out_shape=results,
        in_specs=[HBM] * RESULTS,
        out_specs=(HBM,) * OUTPUTS,
        scratch_shapes=[pltpu.VMEM(r.shape, r.dtype) for r in (*parts, *sums)]
        + [pltpu.VMEM(results[i].shape, f32) for i in range(OUTPUTS) if i not in places]
        + [dma(RESULTS), dma(OUTPUTS)],
        compiler_params=pltpu.CompilerParams(vmem_limit_bytes=60 * 2**20),
        name="finish",
    )(*outs)
    return (
        outs[0].reshape(tokens.shape),
        outs[1].reshape(tokens.shape),
        *outs[2:14],
        outs[14].T,
        *outs[15:18],
        outs[18].reshape(()),
    )


def per_device(seq, tensor, *args):
    batch, tok, width = args[0].shape
    heads = args[7].shape[0]
    if seq == 8 and tensor == 4 and batch == 4 and heads == 3 and tok == 128:
        return gathered_plan(seq, *args)
    return general_plan(*args)


def solution(mesh):
    return jax.shard_map(
        functools.partial(per_device, mesh.shape["seq"], mesh.shape["tensor"]),
        mesh=mesh,
        in_specs=(
            P(None, "seq", None),
            P(),
            P(None, "tensor"),
            P("tensor"),
            P(None, "tensor"),
            P(None, "tensor"),
            P("tensor"),
            P("tensor", None),
            P("tensor", None),
            P(),
            P(),
            P(),
            P(None, "tensor"),
            P("tensor"),
            P("tensor", None),
            P(),
            P(),
            P(),
            P(None, "seq", None),
        ),
        out_specs=(
            P(None, "seq", None),
            P(None, "seq", None),
            P("seq", "tensor"),
            P("tensor"),
            P("seq", "tensor"),
            P("seq", "tensor"),
            P("tensor"),
            P("tensor", None),
            P("tensor", "seq"),
            P(),
            P(),
            P(),
            P("seq", "tensor"),
            P("tensor"),
            P("tensor", "seq"),
            P(),
            P(),
            P(),
            P(),
        ),
        check_vma=False,
    )
```
